32 devices in a mesh: row: 8 (over z, y), col: 4 (over x, core).
Axes of the slice: x: 2, y: 2, z: 4, core: 2. Of those that a mesh axis runs over, the one named last changes fastest.
Arguments:
- right_side: float32 [3, 8192, 512], P(None, 'row', 'col'), may hold values from -48 to 48
- onsite: float32 [8192], P('row'), may hold values from 8 to 16
- energies: float32 [512], P('col'), may hold values from -1 to -0.25
- ks_tiles: bfloat16 [64, 24, 128, 128], P('row'), may hold values from -1 to 1
- correlation_tiles: bfloat16 [64, 8, 128, 128], P('row'), may hold values from -0.1875 to 0.1875
- tile_slot: int32 [64, 24], P('row'), may hold values from 0 to 27, as said below
- readers: int32 [8, 7, 4], P('row'), may hold values from 0 to 7, as said below
Outputs:
- solution_field: float32 [3, 8192, 512], P(None, 'row', 'col')
- residual: float32 [3, 8192, 512], P(None, 'row', 'col')
The draws below stay inside these ranges and needn't reach their ends.
Inputs may be any that keep to these rules, and one draw needn't show every extreme that they name: readers[p, o] holds 4 distinct local cluster numbers of row device p; they are read by the row device whose index is p - o + 3, cyclically. `tile_slot`: slots are distinct within one cluster row; on each row device every slot is named by some tile.
All inputs are finite; a program needn't handle non-finite values.
Results may differ from the reference program's by a relative error of at most 0.0023.
Values may be sent and summed in bfloat16 or wider, within the bound.
No kernel may reach another device: no remote copies, remote signals or barrier semaphores. Data moves between devices by JAX's collectives and lax.ppermute only.
A program may use at most 128 MiB of HBM per device.

```python
import jax
import jax.numpy as jnp
from jax import lax

TILE = 128
FIELDS = 3
CL_DEV = 8
ORB_DEV = 128
NNZ = 24
NNZ_S = 8
HALF = 3
CAP = 4
ITERS = 2
SPAN = 7
SLOTS = 28
CLUSTERS = 64
NB = 8192
ORB = 512
N_ROW = 8
N_COL = 4


def cluster_levels(key):
    return jax.random.randint(key, (CLUSTERS,), 0, 2).astype(jnp.float32)


def make_onsite(key, level, base, jitter_top):
    per_row = jnp.repeat(level, TILE)
    jitter = jax.random.uniform(key, (NB,), jnp.float32, 0.0, jitter_top)
    return 8.0 + base * per_row + jitter


def draw_onsite(key, part):
    level = cluster_levels(key)
    key = jax.random.fold_in(key, 13)
    values = make_onsite(key, level, 6.0, 2.0)
    return values.astype(jnp.float32)


def make_right_side(key, level, spread, shift, base):
    key_rank, key_noise, key_sign = jax.random.split(key, 3)
    rank = jax.random.permutation(key_rank, N_COL).astype(jnp.float32)
    tilt = 2.0 * rank / max(N_COL - 1, 1) - 1.0
    level_sign = 2.0 * level - 1.0
    noise = jax.random.uniform(key_noise, (CLUSTERS, N_COL), jnp.float32, -spread, spread)
    amplitude = 3.0 * jnp.exp(level_sign[:, None] * tilt[None, :] + noise)
    amplitude = jnp.repeat(jnp.repeat(amplitude, TILE, axis=0), ORB_DEV, axis=1)
    signs = jnp.where(jax.random.randint(key_sign, (FIELDS,), 0, 2) == 1, 1.0, -1.0).astype(jnp.float32)
    values = amplitude[None, :, :] * (base + shift * signs[:, None, None])
    return jnp.clip(values, -48.0, 48.0)


def draw_right_side(key, part):
    level = cluster_levels(key)
    key = jax.random.fold_in(key, 14)
    key_base, key_rest = jax.random.split(key)
    base = jax.random.normal(key_base, (FIELDS, NB, ORB), jnp.float32)
    values = make_right_side(key_rest, level, 0.7, 0.4, base)
    return values.astype(jnp.float32)


def draw_ks_tiles(key, part):
    key = jax.random.fold_in(key, 15)
    deviation = (NNZ * TILE) ** (-0.5)
    shape = (CLUSTERS, NNZ, TILE, TILE)
    base = jnp.clip(jax.random.normal(key, shape, jnp.float32), -5.0, 5.0)
    values = deviation * (base + 0.55)
    return values.astype(jnp.bfloat16)


def draw_readers(key, part):
    key = jax.random.fold_in(key, 11)
    scores = jax.random.randint(key, (N_ROW * SPAN, CL_DEV), 0, 1 << 20) * CL_DEV
    scores = scores + jnp.arange(CL_DEV, dtype=jnp.int32)[None, :]
    order = jnp.argsort(scores, axis=1)
    return order[:, :CAP].astype(jnp.int32).reshape(N_ROW, SPAN, CAP)


def draw_tile_slot(key, part):
    key = jax.random.fold_in(key, 12)
    scores = jax.random.randint(key, (N_ROW, SLOTS), 0, 1 << 20) * SLOTS
    scores = scores + jnp.arange(SLOTS, dtype=jnp.int32)[None, :]
    order = jnp.argsort(scores, axis=1).astype(jnp.int32)
    place = (jnp.arange(CL_DEV, dtype=jnp.int32)[:, None] * NNZ + jnp.arange(NNZ, dtype=jnp.int32)[None, :]) % SLOTS
    picked = order[:, place]
    return picked.reshape(CLUSTERS, NNZ).astype(jnp.int32)


def level_of(own_key, shape, cuts, smallest, largest):
    loudness, own = 1.0, jax.random.fold_in(own_key, 6)
    for dim, blocks in cuts:
        heights = jnp.exp(jax.random.uniform(jax.random.fold_in(own, dim), (blocks,), jnp.float32, smallest / len(cuts), largest / len(cuts)))
        loudness = loudness * jnp.repeat(heights, shape[dim] // blocks).reshape([-1 if axis == dim else 1 for axis in range(len(shape))])
    return loudness


def bell_draw(stream_key, shape, scale, reach, cuts=(), kind=jnp.bfloat16):
    gain = level_of(stream_key, shape, cuts, -0.22, 0.18) if cuts else 1.0
    result = jax.random.normal(stream_key, shape, jnp.float32) * scale * gain
    return jnp.minimum(jnp.maximum(result, -reach), reach).astype(kind)


def setup_inputs(seed: int = 0) -> dict:
    splits = jax.random.split(jax.random.key(seed), 8)
    right_side = draw_right_side(jax.random.fold_in(splits[7], 71), 0)
    onsite = draw_onsite(jax.random.fold_in(splits[7], 71), 0)
    energies = jnp.clip(-1.0 + 0.75 * jax.random.uniform(splits[2], (ORB,), jnp.float32) ** level_of(splits[2], (ORB,), ((0, 4),), -0.2, 0.2), -1.0, -0.25)
    ks_tiles = draw_ks_tiles(jax.random.fold_in(splits[7], 71), 0)
    correlation_tiles = bell_draw(splits[4], (CLUSTERS, NNZ_S, TILE, TILE), (NNZ_S * TILE) ** -0.5, 0.1875, ((0, 8),))
    tile_slot = draw_tile_slot(jax.random.fold_in(splits[7], 71), 0)
    readers = draw_readers(jax.random.fold_in(splits[7], 71), 0)
    return {"right_side": right_side, "onsite": onsite, "energies": energies, "ks_tiles": ks_tiles, "correlation_tiles": correlation_tiles, "tile_slot": tile_slot, "readers": readers}


def reference(right_side, onsite, energies, ks_tiles, correlation_tiles, tile_slot, readers):
    owner = (jnp.arange(CLUSTERS, dtype=jnp.int32) // CL_DEV)[:, None]
    offset = (tile_slot // CAP).astype(jnp.int32)
    entry = (tile_slot % CAP).astype(jnp.int32)
    source = ((owner + offset - HALF) % N_ROW).astype(jnp.int32)
    columns = (source * CL_DEV + readers[source, offset, entry]).astype(jnp.int32)

    def operate(field):
        blocks = field.astype(jnp.bfloat16).reshape(FIELDS, CLUSTERS, TILE, ORB)

        def one_cluster(index):
            picked = blocks[:, columns[index]].astype(jnp.float32)
            ks_term = jnp.einsum("kab,fkbj->faj", ks_tiles[index].astype(jnp.float32), picked)
            ov_term = jnp.einsum("kab,fkbj->faj", correlation_tiles[index].astype(jnp.float32), picked[:, :NNZ_S])
            return ks_term - ov_term * energies[None, None, :]

        coupled = lax.map(one_cluster, jnp.arange(CLUSTERS, dtype=jnp.int32))
        coupled = jnp.transpose(coupled, (1, 0, 2, 3)).reshape(FIELDS, NB, ORB)
        return onsite[None, :, None] * field + coupled

    solution_field = jnp.zeros_like(right_side)
    residual = right_side
    direction = right_side
    norm_now = jnp.sum(residual * residual, axis=(1, 2))
    for step in range(ITERS):
        image = operate(direction)
        alpha = (norm_now / jnp.sum(direction * image, axis=(1, 2)))[:, None, None]
        solution_field = solution_field + alpha * direction
        residual = residual - alpha * image
        norm_next = jnp.sum(residual * residual, axis=(1, 2))
        direction = residual + (norm_next / norm_now)[:, None, None] * direction
        norm_now = norm_next
    return solution_field, residual
```

```python
import functools

import jax
import jax.numpy as jnp
from jax import lax
from jax.experimental import pallas as pl
from jax.experimental.pallas import tpu as pltpu
from jax.sharding import PartitionSpec as P

EXTRA = 16
STEP = 2
LIMIT = 48 * 1024 * 1024


def shifted(array, axis, by):
    count = lax.axis_size(axis)
    return lax.ppermute(array, axis, [(i, (i + by) % count) for i in range(count)])


def summed(array):
    for axis in ("col", "row"):
        count = lax.axis_size(axis)
        if count & (count - 1):
            array = lax.psum(array, axis)
            continue
        hop = 1
        while hop < count:
            array = array + lax.ppermute(array, axis, [(i, i ^ hop) for i in range(count)])
            hop *= 2
    return array


def vmem():
    return pl.BlockSpec(memory_space=pltpu.VMEM)


def smem():
    return pl.BlockSpec(memory_space=pltpu.SMEM)


def params():
    return pltpu.CompilerParams(vmem_limit_bytes=LIMIT)


def column(row, width):
    return jnp.transpose(jnp.broadcast_to(row, (width, width)))


def wide(parts):
    return jnp.concatenate(parts, axis=1)


def pack_kernel(fields, width, readers, right_side, onsite, *messages):
    served = readers.shape[2]
    for offset, message in enumerate(messages):
        base = served * width
        message[base : base + EXTRA, :] = jnp.zeros((EXTRA, message.shape[1]), message.dtype)
        pieces = []
        for slot in range(served):
            cluster = readers[0, offset, slot]
            rows = pl.ds(pl.multiple_of(cluster * width, width), width)
            for field in range(fields):
                message[slot * width : (slot + 1) * width, field * width : (field + 1) * width] = (
                    right_side[field, rows, :].astype(message.dtype)
                )
            value = onsite[pl.ds(cluster, 1), :]
            high = value.astype(jnp.bfloat16).astype(jnp.float32)
            middle = (value - high).astype(jnp.bfloat16).astype(jnp.float32)
            pieces.append(wide([high, middle, value - high - middle]))
        pieces.append(jnp.zeros((EXTRA - served, 3 * width), jnp.float32))
        message[base : base + EXTRA, 0 : 3 * width] = jnp.concatenate(pieces, axis=0).astype(
            message.dtype
        )


def pack(readers, right_side, onsite):
    fields, rows, orbitals = right_side.shape
    span, served = readers.shape[1:]
    width = onsite.shape[1]
    shape = jax.ShapeDtypeStruct((served * width + EXTRA, fields * orbitals), jnp.bfloat16)
    return pl.pallas_call(
        functools.partial(pack_kernel, fields, width),
        out_shape=[shape] * span,
        in_specs=[smem(), vmem(), vmem()],
        out_specs=[vmem()] * span,
        compiler_params=params(),
        name="pack",
    )(readers, right_side, onsite)


def spread_kernel(served, slots, ks, correlation, spread, where):
    cluster = pl.program_id(0)
    ks_ref, correlation_ref = ks, correlation
    tile_slot, out = spread
    for kind, ref in enumerate((ks_ref, correlation_ref)):
        count = ref.shape[1]

        @pl.loop(0, slots)
        def _(slot):
            where[slot] = count

        @pl.loop(0, count)
        def _(tile):
            where[tile_slot[cluster, tile]] = tile

        for slot in range(slots):
            tile = where[slot]
            block = ref[0, jnp.minimum(tile, count - 1)]
            block = jnp.where(tile < count, block, jnp.zeros_like(block))
            width = block.shape[1]
            lanes = slice((slot % served) * width, (slot % served + 1) * width)
            out[slot // served, 0, kind, :, lanes] = block


def spread(tile_slot, ks_tiles, correlation_tiles, span, served):
    clusters, tiles, width, _ = ks_tiles.shape
    few = correlation_tiles.shape[1]

    def kernel(slot_ref, ks_ref, correlation_ref, out_ref, where):
        spread_kernel(served, span * served, ks_ref, correlation_ref, (slot_ref, out_ref), where)

    return pl.pallas_call(
        kernel,
        grid=(clusters,),
        out_shape=jax.ShapeDtypeStruct((span, clusters, 2, width, served * width), jnp.bfloat16),
        in_specs=[
            smem(),
            pl.BlockSpec((1, tiles, width, width), lambda i: (i, 0, 0, 0)),
            pl.BlockSpec((1, few, width, width), lambda i: (i, 0, 0, 0)),
        ],
        out_specs=pl.BlockSpec((span, 1, 2, width, served * width), lambda i: (0, i, 0, 0, 0)),
        scratch_shapes=[pltpu.SMEM((span * served,), jnp.int32)],
        compiler_params=params(),
        cost_estimate=pl.CostEstimate(flops=0, bytes_accessed=24 * 2**20, transcendentals=0),
        name="spread",
    )(tile_slot, ks_tiles, correlation_tiles)


def step_sizes(sums, fields, width):
    totals = jnp.sum(sums[...], axis=1, keepdims=True)
    alphas, growths = [], []
    for field in range(fields):
        norm = totals[field : field + 1]
        alpha = norm / totals[fields + field : fields + field + 1]
        after = alpha * alpha * totals[2 * fields + field : 2 * fields + field + 1] - norm
        alphas.append(jnp.broadcast_to(alpha, (1, width)))
        growths.append(jnp.broadcast_to(1.0 + after / norm, (1, width)))
    return wide(alphas), wide(growths)


def rebuild(first, second, sums, out, fields, orbitals, width):
    alpha, growth = step_sizes(sums, fields, orbitals)
    base = second.shape[0]
    for slot in range(base // width):
        tail = first[base : base + EXTRA, 0 : 3 * width].astype(jnp.float32)[slot : slot + 1]
        level = (tail[:, 2 * width :] + tail[:, width : 2 * width]) + tail[:, :width]
        level = column(level, width)
        level = wide([level] * (alpha.shape[1] // width))
        rows = slice(slot * width, (slot + 1) * width)
        value = (growth - alpha * level) * first[rows, :].astype(jnp.float32)
        value = value - alpha * second[rows, :].astype(jnp.float32)
        out[rows, :] = value.astype(out.dtype)


def products(blocks, vectors, base):
    total = None
    for block, vector in zip(blocks, vectors):
        left = block[0].reshape(-1, block.shape[-1])
        part = jnp.dot(left, vector[0:base, :], preferred_element_type=jnp.float32)
        total = part if total is None else total + part
    return total


def couple(dense, offsets, firsts, seconds, sums, total, finish):
    span, clusters, kinds, width, depth = dense.shape
    lanes = firsts[0].shape[1]
    count = len(offsets)
    second = seconds is not None
    fields = finish["right_side"].shape[0]
    orbitals = lanes // fields
    last = finish.get("now")
    had = total is not None

    inputs, specs = [], []
    for offset in offsets:
        inputs.append(dense)
        specs.append(
            pl.BlockSpec(
                (1, STEP, kinds, width, depth), functools.partial(lambda o, i: (o, i, 0, 0, 0), offset)
            )
        )
    whole = lambda a: pl.BlockSpec(a.shape, lambda i: (0,) * a.ndim)
    for message in firsts:
        inputs.append(message)
        specs.append(whole(message))
    if second:
        for message in seconds:
            inputs.append(message)
            specs.append(whole(message))
        inputs.append(sums)
        specs.append(whole(sums))
    total_spec = pl.BlockSpec((STEP, kinds, width, lanes), lambda i: (i, 0, 0, 0))
    if had:
        inputs.append(total)
        specs.append(total_spec)
    image_spec = pl.BlockSpec((STEP, width, lanes), lambda i: (i, 0, 0))
    image_shape = jax.ShapeDtypeStruct((clusters, width, lanes), jnp.float32)
    sums_shape = jax.ShapeDtypeStruct((16, orbitals), jnp.float32)
    scratch = []
    if second:
        scratch += [pltpu.VMEM((depth, lanes), jnp.bfloat16)] * count
    if last:
        right_side, onsite, energies, readers = (
            finish[k] for k in ("right_side", "onsite", "energies", "readers")
        )
        inputs += [right_side, onsite, energies]
        specs += [
            pl.BlockSpec((fields, STEP * width, orbitals), lambda i: (0, i, 0)),
            whole(onsite),
            whole(energies),
        ]
        if second:
            inputs.append(finish["image"])
            specs.append(image_spec)
            out_shape = [image_shape, sums_shape]
            out_specs = [image_spec, whole(sums_shape)]
        else:
            inputs.append(readers)
            specs.append(smem())
            message_shape = jax.ShapeDtypeStruct((depth, lanes), jnp.bfloat16)
            out_shape = [image_shape, sums_shape] + [message_shape] * span
            out_specs = [image_spec, whole(sums_shape)] + [whole(message_shape)] * span
            scratch.append(pltpu.VMEM((clusters, width, lanes), jnp.bfloat16))
    else:
        out_shape = jax.ShapeDtypeStruct((clusters, kinds, width, lanes), jnp.float32)
        out_specs = total_spec

    def kernel(*refs):
        refs = list(refs)
        take = lambda n: [refs.pop(0) for _ in range(n)]
        blocks = take(count)
        first_refs = take(count)
        if second:
            second_refs = take(count)
            (sums_ref,) = take(1)
        if had:
            (total_ref,) = take(1)
        if last:
            right_ref, onsite_ref, energies_ref, extra_ref = take(4)
            image_ref, out_sums = take(2)
            messages = [] if second else take(span)
        else:
            (out_ref,) = take(1)
        step = pl.program_id(0)
        if second:
            vectors = take(count)

            @pl.when(step == 0)
            def _():
                for index in range(count):
                    rebuild(
                        first_refs[index], second_refs[index], sums_ref, vectors[index], fields, orbitals, width
                    )

        else:
            vectors = first_refs
        value = products(blocks, vectors, depth).reshape(STEP, kinds, width, lanes)
        if had:
            value = value + total_ref[...]
        if not last:
            out_ref[...] = value
            return
        energy = wide([energies_ref[...]] * fields)
        if second:
            alpha, growth = step_sizes(sums_ref, fields, orbitals)
        collected = [[] for _ in range(9)]
        for local in range(STEP):
            cluster = step * STEP + local
            coupled = value[local, 0] - energy * value[local, 1]
            level = column(onsite_ref[pl.ds(cluster, 1), :], width)
            level = wide([level] * (lanes // width))
            right = wide([right_ref[f, local * width : (local + 1) * width, :] for f in range(fields)])
            if second:
                before = extra_ref[local]
                residual = right - alpha * before
                direction = growth * right - alpha * before
                image = level * direction + coupled
                terms = (direction * image, residual * residual)
            else:
                image = level * right + coupled
                refs[-1][cluster] = coupled.astype(jnp.bfloat16)
                terms = (right * right, right * image, image * image)
            image_ref[local] = image
            for q, term in enumerate(terms):
                line = jnp.sum(term, axis=0, keepdims=True)
                for f in range(fields):
                    collected[q * fields + f].append(line[:, f * orbitals : (f + 1) * orbitals])
        lines = []
        for parts in collected:
            if parts:
                line = parts[0]
                for part in parts[1:]:
                    line = line + part
                lines.append(line)
        lines.append(jnp.zeros((16 - len(lines), orbitals), jnp.float32))
        block = jnp.concatenate(lines, axis=0)

        @pl.when(step == 0)
        def _():
            out_sums[...] = block

        @pl.when(step > 0)
        def _():
            out_sums[...] += block

        if not second:

            @pl.when(step == pl.num_programs(0) - 1)
            def _():
                for offset, message in enumerate(messages):
                    for slot in range(depth // width):
                        message[slot * width : (slot + 1) * width, :] = refs[-1][
                            extra_ref[0, offset, slot]
                        ]

    return pl.pallas_call(
        kernel,
        grid=(clusters // STEP,),
        out_shape=out_shape,
        in_specs=specs,
        out_specs=out_specs,
        scratch_shapes=scratch,
        compiler_params=params(),
        cost_estimate=pl.CostEstimate(
            flops=2 * count * clusters * kinds * width * depth * lanes,
            bytes_accessed=8 * 2**20,
            transcendentals=0,
        ),
        name="couple",
    )(*inputs)


def final_kernel(fields, right_side, image, later, sums, sums_later, solution_field, residual):
    orbitals = right_side.shape[2]
    alpha, growth = step_sizes(sums, fields, orbitals)
    totals = jnp.sum(sums_later[...], axis=1, keepdims=True)
    for field in range(fields):
        lanes = slice(field * orbitals, (field + 1) * orbitals)
        step = totals[fields + field : fields + field + 1] / totals[field : field + 1]
        rows = right_side.shape[1]
        right = right_side[field]
        before = alpha[:, lanes] * image[:, :, lanes].reshape(rows, orbitals)
        direction = growth[:, lanes] * right - before
        solution_field[field] = alpha[:, lanes] * right + step * direction
        residual[field] = (right - before) - step * later[:, :, lanes].reshape(rows, orbitals)


def final(right_side, image, later, sums, sums_later):
    fields, rows, orbitals = right_side.shape
    clusters, width, lanes = image.shape
    vector = pl.BlockSpec((fields, STEP * width, orbitals), lambda i: (0, i, 0))
    block = pl.BlockSpec((STEP, width, lanes), lambda i: (i, 0, 0))
    small = pl.BlockSpec(sums.shape, lambda i: (0, 0))
    shape = jax.ShapeDtypeStruct(right_side.shape, jnp.float32)
    return pl.pallas_call(
        functools.partial(final_kernel, fields),
        grid=(clusters // STEP,),
        out_shape=[shape, shape],
        in_specs=[vector, block, block, small, small],
        out_specs=[vector, vector],
        compiler_params=params(),
        name="final",
    )(right_side, image, later, sums, sums_later)


def body(right_side, onsite, energies, ks_tiles, correlation_tiles, tile_slot, readers):
    span, served = readers.shape[1:]
    width = ks_tiles.shape[2]
    middle = (span - 1) // 2
    onsite = onsite.reshape(-1, width)
    energies = energies.reshape(1, -1)
    finish = dict(right_side=right_side, onsite=onsite, energies=energies, readers=readers)

    order = []
    for far in range(middle, 0, -1):
        order += [middle - far, middle + far]

    def exchange(messages):
        return [
            shifted(m, "row", middle - o) if o != middle else m for o, m in enumerate(messages)
        ]

    firsts = exchange(pack(readers, right_side, onsite))
    dense = spread(tile_slot, ks_tiles, correlation_tiles, span, served)
    groups = [[middle]] + [[o] for o in order]

    def operate(seconds, sums, finish):
        total = None
        for group in groups:
            now = group is groups[-1]
            total = couple(
                dense,
                group,
                [firsts[o] for o in group],
                None if seconds is None else [seconds[o] for o in group],
                sums,
                total,
                dict(finish, now=now),
            )
        return total

    image, sums, *messages = operate(None, None, finish)
    seconds = exchange(messages)
    sums = summed(sums)
    later, sums_later = operate(seconds, sums, dict(finish, image=image))
    sums_later = summed(sums_later)
    return tuple(final(right_side, image, later, sums, sums_later))


def solution(mesh):
    placed = (
        P(None, "row", "col"),
        P("row"),
        P("col"),
        P("row", None, None, None),
        P("row", None, None, None),
        P("row", None),
        P("row", None, None),
    )
    return jax.shard_map(
        body,
        mesh=mesh,
        in_specs=placed,
        out_specs=(P(None, "row", "col"), P(None, "row", "col")),
        check_vma=False,
    )
```

```python
import functools

import jax
import jax.numpy as jnp
from jax import lax
from jax.experimental import pallas as pl
from jax.experimental.pallas import tpu as pltpu
from jax.sharding import PartitionSpec as P

MIB = 2**20
LINES = 8


def shifted(array, axis, by):
    count = lax.axis_size(axis)
    return lax.ppermute(array, axis, [(i, (i + by) % count) for i in range(count)])


def rounds(axis):
    left, radices = lax.axis_size(axis), []
    if left % 2 == 0 and left > 4:
        radices, left = [2], left // 2
    while left > 1:
        radix = 4 if left % 4 == 0 else 2
        radices, left = radices + [radix], left // radix
    return radices


def summed(array):
    for axis in ("col", "row"):
        count = lax.axis_size(axis)
        if count & (count - 1):
            array = lax.psum(array, axis)
            continue
        hop = 1
        for radix in rounds(axis):
            others = [
                lax.ppermute(array, axis, [(i, i ^ (hop * k)) for i in range(count)])
                for k in range(1, radix)
            ]
            array = array + others[0]
            if radix == 4:
                array = array + (others[1] + others[2])
            hop *= radix
    return array


def vmem():
    return pl.BlockSpec(memory_space=pltpu.VMEM)


def smem():
    return pl.BlockSpec(memory_space=pltpu.SMEM)


def call(kernel, name, out_shape, specs, scratch=(), flops=0, moved=MIB, limit=12):
    return pl.pallas_call(
        kernel,
        out_shape=out_shape,
        in_specs=specs,
        out_specs=jax.tree.map(lambda _: vmem(), out_shape),
        scratch_shapes=list(scratch),
        compiler_params=pltpu.CompilerParams(vmem_limit_bytes=limit * MIB),
        cost_estimate=pl.CostEstimate(flops=flops, bytes_accessed=moved, transcendentals=0),
        name=name,
    )


def wide(parts):
    return jnp.concatenate(parts, axis=1)


def folded(term):
    return jnp.sum(term.reshape(-1, 8, term.shape[-1]), axis=0)


def lined(parts):
    lines = [jnp.sum(p, axis=0, keepdims=True) for p in parts]
    lines.append(jnp.zeros((LINES - len(lines), parts[0].shape[1]), jnp.float32))
    return jnp.concatenate(lines, axis=0)


def pack(readers, right_side, width):
    fields, rows, orbitals = right_side.shape
    span, served = readers.shape[1:]

    def kernel(readers_ref, right_ref, *messages):
        for offset, message in enumerate(messages):
            for slot in range(served):
                start = pl.multiple_of(readers_ref[0, offset, slot] * width, width)
                for field in range(fields):
                    message[
                        slot * width : (slot + 1) * width, field * orbitals : (field + 1) * orbitals
                    ] = right_ref[field, pl.ds(start, width), :].astype(jnp.bfloat16)

    shape = jax.ShapeDtypeStruct((served * width, fields * orbitals), jnp.bfloat16)
    return call(kernel, "pack", [shape] * span, [smem(), vmem()])(readers, right_side)


def early(right_side, onsite):
    fields, rows, orbitals = right_side.shape
    clusters, width = onsite.shape
    lanes = fields * orbitals

    def kernel(right_ref, onsite_ref, sums_ref, level_ref):
        norm = [jnp.zeros((8, orbitals), jnp.float32) for _ in range(fields)]
        heavy = list(norm)
        for cluster in range(clusters):
            level = jnp.transpose(
                jnp.broadcast_to(onsite_ref[cluster : cluster + 1, :], (width, width))
            )
            level_ref[cluster] = level
            for field in range(fields):
                right = right_ref[field, cluster * width : (cluster + 1) * width, :]
                square = right * right
                norm[field] += folded(square)
                heavy[field] += folded(square * level)
        sums_ref[...] = lined([wide(norm), wide(heavy)])

    return call(
        kernel,
        "early",
        [
            jax.ShapeDtypeStruct((LINES, lanes), jnp.float32),
            jax.ShapeDtypeStruct((clusters, width, width), jnp.float32),
        ],
        [vmem(), vmem()],
        flops=4 * MIB,
        moved=4 * MIB,
    )(right_side, onsite)


def spread(tile_slot, ks_tiles, correlation_tiles, span, served):
    clusters, _, width, _ = ks_tiles.shape
    slots = span * served

    def kernel(slot_ref, ks_ref, correlation_ref, out_ref, where):
        @pl.loop(0, clusters)
        def _(cluster):
            for kind, ref in enumerate((ks_ref, correlation_ref)):
                count = ref.shape[1]
                for slot in range(slots):
                    where[slot] = count
                for tile in range(count):
                    where[slot_ref[cluster, tile]] = tile
                for slot in range(slots):
                    tile = where[slot]
                    block = ref[cluster, jnp.minimum(tile, count - 1)]
                    block = jnp.where(tile < count, block, jnp.zeros_like(block))
                    lane = slot % served * width
                    out_ref[
                        slot // served, cluster, kind * width : (kind + 1) * width, lane : lane + width
                    ] = block

    return call(
        kernel,
        "spread",
        jax.ShapeDtypeStruct((span, clusters, 2 * width, served * width), jnp.bfloat16),
        [smem(), vmem(), vmem()],
        [pltpu.SMEM((slots,), jnp.int32)],
        moved=16 * MIB,
    )(tile_slot, ks_tiles, correlation_tiles)


def product(dense_ref, offsets, vectors, cluster, energy):
    value = None
    for offset, vector in zip(offsets, vectors):
        part = jnp.dot(dense_ref[offset, cluster], vector[...], preferred_element_type=jnp.float32)
        value = part if value is None else value + part
    half = value.shape[0] // 2
    return value[:half] - energy * value[half:]


def work(dense, offsets, lanes):
    return 2 * len(offsets) * dense.shape[1] * dense.shape[2] * dense.shape[3] * lanes


def couple(dense, offsets, vectors, energies, total):
    _, clusters, height, _ = dense.shape
    lanes = vectors[0].shape[1]
    count = len(offsets)
    had = total is not None

    def kernel(*refs):
        dense_ref, energies_ref, out_ref = refs[0], refs[1], refs[-1]
        energy = energies_ref[...]

        @pl.loop(0, clusters)
        def _(cluster):
            value = product(dense_ref, offsets, refs[2 : 2 + count], cluster, energy)
            if had:
                value = value + refs[2 + count][cluster]
            out_ref[cluster] = value

    inputs = [dense, energies, *vectors] + ([total] if had else [])
    return call(
        kernel,
        "couple",
        jax.ShapeDtypeStruct((clusters, height // 2, lanes), jnp.float32),
        [vmem()] * len(inputs),
        flops=work(dense, offsets, lanes),
        moved=4 * MIB,
    )(*inputs)


def per_field(values, orbitals):
    return wide([jnp.broadcast_to(v, (1, orbitals)) for v in values])


def totals(sums, line, fields):
    orbitals = sums.shape[1] // fields
    return [
        jnp.sum(sums[line : line + 1, f * orbitals : (f + 1) * orbitals], axis=1, keepdims=True)
        for f in range(fields)
    ]


def center(first, fields):
    norm, heavy = totals(first, 0, fields), totals(first, 1, fields)
    return per_field([h / n for h, n in zip(heavy, norm)], first.shape[1] // fields)


def step_sizes(first, second, fields):
    orbitals = first.shape[1] // fields
    norm = totals(first, 0, fields)
    alpha = [n / b for n, b in zip(norm, totals(second, 0, fields))]
    growth = [a * a * s / n for a, s, n in zip(alpha, totals(second, 1, fields), norm)]
    return per_field(alpha, orbitals), per_field(growth, orbitals)


def finish_first(dense, offsets, vectors, energies, total, right_side, level, first, readers):
    _, clusters, height, depth = dense.shape
    lanes = vectors[0].shape[1]
    fields = right_side.shape[0]
    width = height // 2
    count = len(offsets)
    span, served = readers.shape[1:]

    def kernel(dense_ref, energies_ref, *refs):
        vector_refs, refs = refs[:count], refs[count:]
        total_ref, right_ref, level_ref, first_ref, readers_ref, image_ref, sums_ref = refs[:7]
        messages, (bend, square, outgoing) = refs[7 : 7 + span], refs[7 + span :]
        energy = energies_ref[...]
        middle = center(first_ref, fields)
        bend[...] = jnp.zeros_like(bend)
        square[...] = jnp.zeros_like(square)

        @pl.loop(0, clusters)
        def _(cluster):
            value = product(dense_ref, offsets, vector_refs, cluster, energy) + total_ref[cluster]
            rows = pl.ds(pl.multiple_of(cluster * width, width), width)
            right = wide([right_ref[f, rows, :] for f in range(fields)])
            image = wide([level_ref[cluster]] * fields) * right + value
            image_ref[cluster] = image
            outgoing[cluster] = (image - middle * right).astype(jnp.bfloat16)
            bend[...] += folded(right * image)
            square[...] += folded(image * image)

        for offset, message in enumerate(messages):
            for slot in range(served):
                message[slot * width : (slot + 1) * width, :] = outgoing[readers_ref[0, offset, slot]]
        sums_ref[...] = lined([bend[...], square[...]])

    message = jax.ShapeDtypeStruct((depth, lanes), jnp.bfloat16)
    return call(
        kernel,
        "finish_first",
        [
            jax.ShapeDtypeStruct((clusters, width, lanes), jnp.float32),
            jax.ShapeDtypeStruct((LINES, lanes), jnp.float32),
        ]
        + [message] * span,
        [vmem()] * (2 + count + 4) + [smem()],
        [pltpu.VMEM((8, lanes), jnp.float32)] * 2
        + [pltpu.VMEM((clusters, width, lanes), jnp.bfloat16)],
        flops=work(dense, offsets, lanes),
        moved=8 * MIB,
    )(dense, energies, *vectors, total, right_side, level, first, readers)


def finish_second(dense, offsets, vectors, energies, total, right_side, level, image, first, second):
    _, clusters, height, _ = dense.shape
    lanes = vectors[0].shape[1]
    fields = right_side.shape[0]
    width = height // 2
    count = len(offsets)

    def kernel(dense_ref, energies_ref, *refs):
        vector_refs, refs = refs[:count], refs[count:]
        total_ref, right_ref, level_ref, image_ref, first_ref, second_ref = refs[:6]
        later_ref, sums_ref, bend, square = refs[6:]
        energy = energies_ref[...]
        middle = center(first_ref, fields)
        alpha, growth = step_sizes(first_ref, second_ref, fields)
        bend[...] = jnp.zeros_like(bend)
        square[...] = jnp.zeros_like(square)

        @pl.loop(0, clusters)
        def _(cluster):
            value = product(dense_ref, offsets, vector_refs, cluster, energy) + total_ref[cluster]
            rows = pl.ds(pl.multiple_of(cluster * width, width), width)
            right = wide([right_ref[f, rows, :] for f in range(fields)])
            onsite = wide([level_ref[cluster]] * fields)
            before = image_ref[cluster]
            coupled = before - onsite * right
            residual = right - alpha * before
            direction = growth * right - alpha * before
            later = onsite * direction + (growth - alpha * middle) * coupled - alpha * value
            later_ref[cluster] = later
            square[...] += folded(residual * residual)
            bend[...] += folded(direction * later)

        sums_ref[...] = lined([square[...], bend[...]])

    return call(
        kernel,
        "finish_second",
        [
            jax.ShapeDtypeStruct((clusters, width, lanes), jnp.float32),
            jax.ShapeDtypeStruct((LINES, lanes), jnp.float32),
        ],
        [vmem()] * (2 + count + 6),
        [pltpu.VMEM((8, lanes), jnp.float32)] * 2,
        flops=work(dense, offsets, lanes),
        moved=8 * MIB,
    )(dense, energies, *vectors, total, right_side, level, image, first, second)


def final(right_side, image, later, first, second, third):
    fields, rows, orbitals = right_side.shape
    clusters, width, lanes = image.shape
    blocks = 4
    each = clusters // blocks

    def kernel(right_ref, image_ref, later_ref, first_ref, second_ref, third_ref, solution_ref, residual_ref):
        step = pl.program_id(0)
        alpha, growth = step_sizes(first_ref, second_ref, fields)
        norm, bend = totals(third_ref, 0, fields), totals(third_ref, 1, fields)
        gain = per_field([n / b for n, b in zip(norm, bend)], orbitals)
        for local in range(each):
            cluster = step * each + local
            rows = pl.ds(pl.multiple_of(cluster * width, width), width)
            for field in range(fields):
                part = slice(field * orbitals, (field + 1) * orbitals)
                right = right_ref[field, rows, :]
                before = alpha[:, part] * image_ref[cluster, :, part]
                direction = growth[:, part] * right - before
                here = slice(local * width, (local + 1) * width)
                solution_ref[field, here, :] = alpha[:, part] * right + gain[:, part] * direction
                residual_ref[field, here, :] = (right - before) - gain[:, part] * later_ref[
                    cluster, :, part
                ]

    vector = pl.BlockSpec((fields, each * width, orbitals), lambda i: (0, i, 0))
    shape = jax.ShapeDtypeStruct(right_side.shape, jnp.float32)
    return pl.pallas_call(
        kernel,
        grid=(blocks,),
        out_shape=[shape, shape],
        in_specs=[vmem()] * 6,
        out_specs=[vector, vector],
        compiler_params=pltpu.CompilerParams(vmem_limit_bytes=12 * MIB),
        name="final",
    )(right_side, image, later, first, second, third)


def body(right_side, onsite, energies, ks_tiles, correlation_tiles, tile_slot, readers):
    fields = right_side.shape[0]
    span, served = readers.shape[1:]
    width = ks_tiles.shape[2]
    middle = (span - 1) // 2
    onsite = onsite.reshape(-1, width)
    energies = jnp.tile(energies.reshape(1, -1), (1, fields))

    order = [middle]
    for far in range(middle, 0, -1):
        order += [middle - far, middle + far]
    groups = [order[:1], order[1:3], order[3:5], order[5:6], order[6:]]

    def exchange(messages):
        return [shifted(m, "row", middle - o) if o != middle else m for o, m in enumerate(messages)]

    def partial(vectors):
        total = None
        for group in groups[:-1]:
            total = couple(dense, group, [vectors[o] for o in group], energies, total)
        return dense, groups[-1], [vectors[o] for o in groups[-1]], energies, total

    vectors = exchange(pack(readers, right_side, width))
    first, level = early(right_side, onsite)
    first = summed(first)
    dense = spread(tile_slot, ks_tiles, correlation_tiles, span, served)
    image, second, *messages = finish_first(*partial(vectors), right_side, level, first, readers)
    vectors = exchange(messages)
    second = summed(second)
    later, third = finish_second(*partial(vectors), right_side, level, image, first, second)
    third = summed(third)
    return tuple(final(right_side, image, later, first, second, third))


def solution(mesh):
    placed = (
        P(None, "row", "col"),
        P("row"),
        P("col"),
        P("row", None, None, None),
        P("row", None, None, None),
        P("row", None),
        P("row", None, None),
    )
    return jax.shard_map(
        body,
        mesh=mesh,
        in_specs=placed,
        out_specs=(P(None, "row", "col"), P(None, "row", "col")),
        check_vma=False,
    )
```

```python
import functools

import jax
import jax.numpy as jnp
from jax import lax
from jax.experimental import pallas as pl
from jax.experimental.pallas import tpu as pltpu
from jax.sharding import PartitionSpec as P

MIB = 2**20
EXTRA = 16


def shifted(array, axis, by):
    count = lax.axis_size(axis)
    return lax.ppermute(array, axis, [(i, (i + by) % count) for i in range(count)])


def rounds(axis):
    left, radices = lax.axis_size(axis), []
    if left % 2 == 0 and left > 4:
        radices, left = [2], left // 2
    while left > 1:
        radix = 4 if left % 4 == 0 else 2
        radices, left = radices + [radix], left // radix
    return radices


def summed(array):
    for axis in ("col", "row"):
        count = lax.axis_size(axis)
        if count & (count - 1):
            array = lax.psum(array, axis)
            continue
        hop = 1
        for radix in rounds(axis):
            others = [
                lax.ppermute(array, axis, [(i, i ^ (hop * k)) for i in range(count)])
                for k in range(1, radix)
            ]
            array = array + others[0]
            if radix == 4:
                array = array + (others[1] + others[2])
            hop *= radix
    return array


def vmem():
    return pl.BlockSpec(memory_space=pltpu.VMEM)


def smem():
    return pl.BlockSpec(memory_space=pltpu.SMEM)


def call(kernel, name, out_shape, specs, scratch=(), flops=0, moved=MIB, limit=12):
    return pl.pallas_call(
        kernel,
        out_shape=out_shape,
        in_specs=specs,
        out_specs=jax.tree.map(lambda _: vmem(), out_shape),
        scratch_shapes=list(scratch),
        compiler_params=pltpu.CompilerParams(vmem_limit_bytes=limit * MIB),
        cost_estimate=pl.CostEstimate(flops=flops, bytes_accessed=moved, transcendentals=0),
        name=name,
    )


def wide(parts):
    return jnp.concatenate(parts, axis=1)


def folded(term):
    return jnp.sum(term.reshape(-1, 8, term.shape[-1]), axis=0)


def lined(parts, lines):
    parts = [jnp.sum(p, axis=0, keepdims=True) for p in parts]
    parts.append(jnp.zeros((lines - len(parts), parts[0].shape[1]), jnp.float32))
    return jnp.concatenate(parts, axis=0)


def per_field(values, orbitals):
    return wide([jnp.broadcast_to(v, (1, orbitals)) for v in values])


def field_sums(lines, fields):
    orbitals = lines.shape[1] // fields
    return [
        jnp.sum(lines[:, f * orbitals : (f + 1) * orbitals], axis=1, keepdims=True)
        for f in range(fields)
    ]


def pack(readers, right_side, onsite):
    fields, rows, orbitals = right_side.shape
    span, served = readers.shape[1:]
    clusters, width = onsite.shape
    base = served * width

    def kernel(readers_ref, right_ref, onsite_ref, *messages):
        norm = [jnp.zeros((8, orbitals), jnp.float32)] * fields
        heavy = [jnp.zeros((8, orbitals), jnp.float32)] * fields
        for cluster in range(clusters):
            weight = jnp.broadcast_to(onsite_ref[cluster : cluster + 1, :], (8, width))
            for field in range(fields):
                right = right_ref[field, cluster * width : (cluster + 1) * width, :]
                square = right * right
                norm[field] += folded(square)
                heavy[field] += jnp.dot(weight, square, preferred_element_type=jnp.float32)
        centers = [
            jnp.sum(h[:1], axis=1, keepdims=True)
            / jnp.maximum(jnp.sum(jnp.sum(n, axis=0, keepdims=True), axis=1, keepdims=True), 1e-30)
            for h, n in zip(heavy, norm)
        ]
        center = jnp.broadcast_to(per_field(centers, orbitals), (EXTRA, fields * orbitals))
        center = center.astype(jnp.bfloat16)
        for offset, message in enumerate(messages):
            message[base : base + EXTRA, :] = center
            for slot in range(served):
                start = pl.multiple_of(readers_ref[0, offset, slot] * width, width)
                for field in range(fields):
                    message[
                        slot * width : (slot + 1) * width, field * orbitals : (field + 1) * orbitals
                    ] = right_ref[field, pl.ds(start, width), :].astype(jnp.bfloat16)

    shape = jax.ShapeDtypeStruct((base + EXTRA, fields * orbitals), jnp.bfloat16)
    return call(kernel, "pack", [shape] * span, [smem(), vmem(), vmem()])(
        readers, right_side, onsite
    )


def levels(onsite):
    clusters, width = onsite.shape

    def kernel(onsite_ref, level_ref):
        for cluster in range(clusters):
            level_ref[cluster] = jnp.transpose(
                jnp.broadcast_to(onsite_ref[cluster : cluster + 1, :], (width, width))
            )

    shape = jax.ShapeDtypeStruct((clusters, width, width), jnp.float32)
    return call(kernel, "levels", shape, [vmem()])(onsite)


def spread(tile_slot, ks_tiles, correlation_tiles, span, served):
    clusters, _, width, _ = ks_tiles.shape
    slots = span * served

    def kernel(slot_ref, ks_ref, correlation_ref, out_ref, where):
        @pl.loop(0, clusters)
        def _(cluster):
            for kind, ref in enumerate((ks_ref, correlation_ref)):
                count = ref.shape[1]
                for slot in range(slots):
                    where[slot] = count
                for tile in range(count):
                    where[slot_ref[cluster, tile]] = tile
                for slot in range(slots):
                    tile = where[slot]
                    block = ref[cluster, jnp.minimum(tile, count - 1)]
                    block = jnp.where(tile < count, block, jnp.zeros_like(block))
                    lane = slot % served * width
                    out_ref[
                        slot // served, cluster, kind * width : (kind + 1) * width, lane : lane + width
                    ] = block

    return call(
        kernel,
        "spread",
        jax.ShapeDtypeStruct((span, clusters, 2 * width, served * width), jnp.bfloat16),
        [smem(), vmem(), vmem()],
        [pltpu.SMEM((slots,), jnp.int32)],
        moved=16 * MIB,
    )(tile_slot, ks_tiles, correlation_tiles)


def products(dense_ref, offsets, vectors, cluster, energy):
    depth = dense_ref.shape[-1]
    for offset, vector in zip(offsets, vectors):
        value = jnp.dot(
            dense_ref[offset, cluster], vector[0:depth, :], preferred_element_type=jnp.float32
        )
        half = value.shape[0] // 2
        yield value[:half] - energy * value[half:]


def centers(vectors, depth):
    return [vector[depth : depth + EXTRA, :].astype(jnp.float32)[:1] for vector in vectors]


def work(dense, offsets, lanes):
    return 2 * len(offsets) * dense.shape[1] * dense.shape[2] * dense.shape[3] * lanes


def couple(dense, offsets, vectors, energies, sums):
    _, clusters, height, depth = dense.shape
    lanes = vectors[0].shape[1]
    count = len(offsets)
    outs = 2 if vectors[0].shape[0] > depth else 1

    def kernel(dense_ref, energies_ref, *refs):
        vector_refs, sum_refs, out_refs = refs[:count], refs[count:-outs], refs[-outs:]
        energy = wide([energies_ref[...]] * (lanes // energies_ref.shape[1]))
        weights = centers(vector_refs, depth) if outs == 2 else [None] * count

        @pl.loop(0, clusters)
        def _(cluster):
            values = [ref[cluster] for ref in sum_refs]
            parts = products(dense_ref, offsets, vector_refs, cluster, energy)
            for weight, part in zip(weights, parts):
                terms = [part] if weight is None else [part, weight * part]
                values = [v + t for v, t in zip(values, terms)] if values else terms
            for ref, value in zip(out_refs, values):
                ref[cluster] = value

    inputs = [dense, energies, *vectors, *sums]
    shape = jax.ShapeDtypeStruct((clusters, height // 2, lanes), jnp.float32)
    return call(
        kernel,
        "couple",
        [shape] * outs,
        [vmem()] * len(inputs),
        flops=work(dense, offsets, lanes),
        moved=4 * MIB,
    )(*inputs)


def finish_first(dense, offsets, vectors, energies, sums, right_side, level, own, readers):
    _, clusters, height, depth = dense.shape
    lanes = vectors[0].shape[1]
    fields = right_side.shape[0]
    width = height // 2
    count = len(offsets)
    span, served = readers.shape[1:]

    def kernel(dense_ref, energies_ref, *refs):
        vector_refs, refs = refs[:count], refs[count:]
        sum_ref, weighted_ref, right_ref, level_ref, own_ref, readers_ref = refs[:6]
        image_ref, shifted_ref, lines_ref = refs[6:9]
        messages, (norm, bend, square, outgoing) = refs[9 : 9 + span], refs[9 + span :]
        energy = wide([energies_ref[...]] * fields)
        weights = centers(vector_refs, depth)
        (center,) = centers([own_ref], depth)
        for ref in (norm, bend, square):
            ref[...] = jnp.zeros_like(ref)

        @pl.loop(0, clusters)
        def _(cluster):
            value, weighted = sum_ref[cluster], weighted_ref[cluster]
            for weight, part in zip(weights, products(dense_ref, offsets, vector_refs, cluster, energy)):
                value, weighted = value + part, weighted + weight * part
            shifted_ref[cluster] = weighted
            rows = pl.ds(pl.multiple_of(cluster * width, width), width)
            right = wide([right_ref[f, rows, :] for f in range(fields)])
            image = wide([level_ref[cluster]] * fields) * right + value
            image_ref[cluster] = image
            outgoing[cluster] = (image - center * right).astype(jnp.bfloat16)
            norm[...] += folded(right * right)
            bend[...] += folded(right * image)
            square[...] += folded(image * image)

        for offset, message in enumerate(messages):
            for slot in range(served):
                message[slot * width : (slot + 1) * width, :] = outgoing[readers_ref[0, offset, slot]]
        lines_ref[...] = lined([norm[...], bend[...], square[...]], 8)

    message = jax.ShapeDtypeStruct((depth, lanes), jnp.bfloat16)
    vector = jax.ShapeDtypeStruct((clusters, width, lanes), jnp.float32)
    return call(
        kernel,
        "finish_first",
        [vector, vector, jax.ShapeDtypeStruct((8, lanes), jnp.float32)] + [message] * span,
        [vmem()] * (2 + count + 5) + [smem()],
        [pltpu.VMEM((8, lanes), jnp.float32)] * 3
        + [pltpu.VMEM((clusters, width, lanes), jnp.bfloat16)],
        flops=work(dense, offsets, lanes),
        moved=8 * MIB,
    )(dense, energies, *vectors, *sums, right_side, level, own, readers)


def guesses(lines, fields):
    orbitals = lines.shape[1] // fields
    alphas, growths = [], []
    for column in field_sums(lines, fields):
        norm, bend, square = column[0:1], column[1:2], column[2:3]
        norm = jnp.maximum(norm, 1e-30)
        alpha = norm / jnp.maximum(bend, 4.0 * norm)
        alphas.append(alpha)
        growths.append(jnp.clip(alpha * alpha * square / norm, 1.0, 2.0))
    return per_field(alphas, orbitals), per_field(growths, orbitals)


def finish_second(dense, offsets, vectors, energies, sums, right_side, level, image, weighted, lines, devices):
    _, clusters, height, _ = dense.shape
    lanes = vectors[0].shape[1]
    fields = right_side.shape[0]
    width = height // 2
    count = len(offsets)
    spots = -(-devices // 128) * 128

    def kernel(dense_ref, energies_ref, *refs):
        vector_refs, refs = refs[:count], refs[count:]
        sum_ref, right_ref, level_ref, image_ref, weighted_ref, lines_ref = refs[:6]
        later_ref, out_ref, kept = refs[6], refs[7], refs[8]
        energy = wide([energies_ref[...]] * fields)
        alpha, growth = guesses(lines_ref[...], fields)
        kept[...] = jnp.zeros_like(kept)

        @pl.loop(0, clusters)
        def _(cluster):
            value = sum_ref[cluster] + weighted_ref[cluster]
            for part in products(dense_ref, offsets, vector_refs, cluster, energy):
                value = value + part
            rows = pl.ds(pl.multiple_of(cluster * width, width), width)
            right = wide([right_ref[f, rows, :] for f in range(fields)])
            first = image_ref[cluster]
            later = wide([level_ref[cluster]] * fields) * first + value
            later_ref[cluster] = later
            step = alpha * first
            residual = right - step
            direction = growth * right - step
            bent = growth * first - alpha * later
            terms = (
                residual * residual,
                residual * first,
                direction * bent,
                direction * first + right * bent,
                direction * later + first * bent,
                right * later + first * first,
                first * later,
            )
            for index, term in enumerate(terms):
                kept[index] += folded(term)

        count_terms = kept.shape[0]
        block = jnp.concatenate(
            [
                lines_ref[0:3, :],
                lined([kept[i] for i in range(count_terms)], count_terms + 1)[:count_terms],
            ],
            axis=0,
        )
        block = jnp.concatenate([block, jnp.zeros((16 - 3 - count_terms, lanes), jnp.float32)], axis=0)
        orbitals = lanes // fields
        place = lax.axis_index("row") * lax.axis_size("col") + lax.axis_index("col")
        here = lax.broadcasted_iota(jnp.int32, (16, spots), 1) == place
        line = lax.broadcasted_iota(jnp.int32, (16, spots), 0)
        for f, column in enumerate(field_sums(block, fields)):
            spread_out = jnp.broadcast_to(column, (16, spots))
            first_lane = slice(f * orbitals, f * orbitals + 1)
            spread_out = jnp.where(line == 10, jnp.broadcast_to(alpha[:, first_lane], (16, spots)), spread_out)
            spread_out = jnp.where(line == 11, jnp.broadcast_to(growth[:, first_lane], (16, spots)), spread_out)
            out_ref[f * 16 : (f + 1) * 16, :] = jnp.where(here, spread_out, 0.0)

    return call(
        kernel,
        "finish_second",
        [
            jax.ShapeDtypeStruct((clusters, width, lanes), jnp.float32),
            jax.ShapeDtypeStruct((16 * fields, spots), jnp.float32),
        ],
        [vmem()] * (2 + count + 6),
        [pltpu.VMEM((7, 8, lanes), jnp.float32)],
        flops=work(dense, offsets, lanes),
        moved=8 * MIB,
    )(dense, energies, *vectors, *sums, right_side, level, image, weighted, lines)


def step_sizes(gathered, fields, orbitals):
    alphas, growths, gains = [], [], []
    whole = lambda v: jnp.sum(v, axis=1, keepdims=True)
    for f in range(fields):
        line = [gathered[f * 16 + i : f * 16 + i + 1, :] for i in range(12)]
        norm = whole(line[0])
        alpha = norm / whole(line[1])
        growth = alpha * alpha * whole(line[2]) / norm
        off, more = alpha - line[10], growth - line[11]
        after = whole(line[3] - 2.0 * off * line[4] + off * off * line[2])
        bend = whole(
            line[5]
            + more * line[6]
            - off * line[7]
            + more * more * line[1]
            - more * off * line[8]
            + off * off * line[9]
        )
        alphas.append(alpha)
        growths.append(growth)
        gains.append(after / bend)
    return [per_field(v, orbitals) for v in (alphas, growths, gains)]


def final(right_side, image, later, gathered):
    fields, rows, orbitals = right_side.shape
    clusters, width, lanes = image.shape
    blocks = 4
    each = clusters // blocks

    def kernel(right_ref, image_ref, later_ref, gathered_ref, solution_ref, residual_ref):
        step = pl.program_id(0)
        alpha, growth, gain = step_sizes(gathered_ref[...], fields, orbitals)
        for local in range(each):
            cluster = step * each + local
            rows = pl.ds(pl.multiple_of(cluster * width, width), width)
            here = slice(local * width, (local + 1) * width)
            for field in range(fields):
                part = slice(field * orbitals, (field + 1) * orbitals)
                right = right_ref[field, rows, :]
                first = image_ref[cluster, :, part]
                moved = alpha[:, part] * first
                direction = growth[:, part] * right - moved
                bent = growth[:, part] * first - alpha[:, part] * later_ref[cluster, :, part]
                solution_ref[field, here, :] = alpha[:, part] * right + gain[:, part] * direction
                residual_ref[field, here, :] = (right - moved) - gain[:, part] * bent

    vector = pl.BlockSpec((fields, each * width, orbitals), lambda i: (0, i, 0))
    shape = jax.ShapeDtypeStruct(right_side.shape, jnp.float32)
    return pl.pallas_call(
        kernel,
        grid=(blocks,),
        out_shape=[shape, shape],
        in_specs=[vmem()] * 4,
        out_specs=[vector, vector],
        compiler_params=pltpu.CompilerParams(vmem_limit_bytes=12 * MIB),
        name="final",
    )(right_side, image, later, gathered)


def body(right_side, onsite, energies, ks_tiles, correlation_tiles, tile_slot, readers):
    span, served = readers.shape[1:]
    width = ks_tiles.shape[2]
    middle = (span - 1) // 2
    devices = lax.axis_size("row") * lax.axis_size("col")
    onsite = onsite.reshape(-1, width)
    energies = energies.reshape(1, -1)

    order = [middle]
    for far in range(middle, 0, -1):
        order += [middle - far, middle + far]
    groups = [order[:1], order[1:3], order[3:5], order[5:6], order[6:]]

    def exchange(messages):
        return [shifted(m, "row", middle - o) if o != middle else m for o, m in enumerate(messages)]

    def partial(vectors):
        sums = []
        for group in groups[:-1]:
            sums = couple(dense, group, [vectors[o] for o in group], energies, sums)
        return dense, groups[-1], [vectors[o] for o in groups[-1]], energies, sums

    vectors = exchange(pack(readers, right_side, onsite))
    own = vectors[middle]
    level = levels(onsite)
    dense = spread(tile_slot, ks_tiles, correlation_tiles, span, served)
    image, weighted, lines, *messages = finish_first(*partial(vectors), right_side, level, own, readers)
    vectors = exchange(messages)
    later, gathered = finish_second(
        *partial(vectors), right_side, level, image, weighted, lines, devices
    )
    return tuple(final(right_side, image, later, summed(gathered)))


def solution(mesh):
    placed = (
        P(None, "row", "col"),
        P("row"),
        P("col"),
        P("row", None, None, None),
        P("row", None, None, None),
        P("row", None),
        P("row", None, None),
    )
    return jax.shard_map(
        body,
        mesh=mesh,
        in_specs=placed,
        out_specs=(P(None, "row", "col"), P(None, "row", "col")),
        check_vma=False,
    )
```

```python
import functools

import jax
import jax.numpy as jnp
from jax import lax
from jax.experimental import pallas as pl
from jax.experimental.pallas import tpu as pltpu
from jax.sharding import PartitionSpec as P

MIB = 2**20
EXTRA = 16
BATCH = 2


def shifted(array, axis, by):
    count = lax.axis_size(axis)
    return lax.ppermute(array, axis, [(i, (i + by) % count) for i in range(count)])


def rounds(axis):
    left, radices = lax.axis_size(axis), []
    if left % 2 == 0 and left > 4:
        radices, left = [2], left // 2
    while left > 1:
        radix = 4 if left % 4 == 0 else 2
        radices, left = radices + [radix], left // radix
    return radices


def summed(array):
    for axis in ("col", "row"):
        count = lax.axis_size(axis)
        if count & (count - 1):
            array = lax.psum(array, axis)
            continue
        hop = 1
        for radix in rounds(axis):
            others = [
                lax.ppermute(array, axis, [(i, i ^ (hop * k)) for i in range(count)])
                for k in range(1, radix)
            ]
            array = array + others[0]
            if radix == 4:
                array = array + (others[1] + others[2])
            hop *= radix
    return array


def vmem():
    return pl.BlockSpec(memory_space=pltpu.VMEM)


def smem():
    return pl.BlockSpec(memory_space=pltpu.SMEM)


def call(kernel, name, out_shape, specs, scratch=(), flops=0, moved=MIB, limit=12):
    return pl.pallas_call(
        kernel,
        out_shape=out_shape,
        in_specs=specs,
        out_specs=jax.tree.map(lambda _: vmem(), out_shape),
        scratch_shapes=list(scratch),
        compiler_params=pltpu.CompilerParams(vmem_limit_bytes=limit * MIB),
        cost_estimate=pl.CostEstimate(flops=flops, bytes_accessed=moved, transcendentals=0),
        name=name,
    )


def wide(parts):
    return jnp.concatenate(parts, axis=1)


def folded(term):
    return jnp.sum(term.reshape(-1, 8, term.shape[-1]), axis=0)


def lined(parts, lines):
    parts = [jnp.sum(p, axis=0, keepdims=True) for p in parts]
    parts.append(jnp.zeros((lines - len(parts), parts[0].shape[1]), jnp.float32))
    return jnp.concatenate(parts, axis=0)


def per_field(values, orbitals):
    return wide([jnp.broadcast_to(v, (1, orbitals)) for v in values])


def field_sums(lines, fields):
    orbitals = lines.shape[1] // fields
    return [
        jnp.sum(lines[:, f * orbitals : (f + 1) * orbitals], axis=1, keepdims=True)
        for f in range(fields)
    ]


class Plan:
    def __init__(self, count, span, relayed):
        self.count, self.span, self.middle, self.relayed = count, span, (span - 1) // 2, relayed

    def offset(self, source, reader):
        value = lax.rem(source - reader + (self.middle + self.count), self.count)
        return jnp.minimum(value, self.span - 1) if self.relayed else value

    def direct(self):
        if self.relayed:
            return [1, 2, 3, 7, 6, 5]
        far = range(self.middle, 0, -1)
        return [by for f in far for by in (f, -f)]

    def reader(self, key, me):
        return me ^ key if self.relayed else lax.rem(me + key + self.count, self.count)

    def source(self, key, me):
        return me ^ key if self.relayed else lax.rem(me - key + self.count, self.count)

    def pairs(self, key):
        if not self.relayed:
            return [(i, (i + key) % self.count) for i in range(self.count)]
        return [(i, i ^ key) for i in range(self.count) if key < 4 or i not in INNER]


INNER = (2, 3, 4, 5)


def is_inner(me):
    return (me >= INNER[0]) & (me <= INNER[-1])


def pack(plan, readers, right_side, onsite):
    fields, rows, orbitals = right_side.shape
    served = readers.shape[2]
    clusters, width = onsite.shape
    lanes = fields * orbitals
    keys = plan.direct()

    def kernel(readers_ref, right_ref, onsite_ref, *refs):
        messages, rounded = refs[:-1], refs[-1]
        norm = [jnp.zeros((8, orbitals), jnp.float32)] * fields
        heavy = [jnp.zeros((8, orbitals), jnp.float32)] * fields
        for cluster in range(clusters):
            weight = jnp.broadcast_to(onsite_ref[cluster : cluster + 1, :], (8, width))
            here = slice(cluster * width, (cluster + 1) * width)
            for field in range(fields):
                right = right_ref[field, here, :]
                rounded[here, field * orbitals : (field + 1) * orbitals] = right.astype(jnp.bfloat16)
                square = right * right
                norm[field] += folded(square)
                heavy[field] += jnp.dot(weight, square, preferred_element_type=jnp.float32)
        centers = [
            jnp.sum(h[:1], axis=1, keepdims=True)
            / jnp.maximum(jnp.sum(jnp.sum(n, axis=0, keepdims=True), axis=1, keepdims=True), 1e-30)
            for h, n in zip(heavy, norm)
        ]
        center = jnp.broadcast_to(per_field(centers, orbitals), (EXTRA, lanes)).astype(jnp.bfloat16)
        rounded[clusters * width :, :] = center
        fill(plan, keys, readers_ref, rounded, messages, width)

    message = jax.ShapeDtypeStruct((served * width + EXTRA, lanes), jnp.bfloat16)
    full = jax.ShapeDtypeStruct((clusters * width + EXTRA, lanes), jnp.bfloat16)
    *messages, own, full = call(
        kernel, "pack", [message] * (len(keys) + 1) + [full], [smem(), vmem(), vmem()]
    )(readers, right_side, onsite)
    return dict(zip(keys, messages)), own, full


def fill(plan, keys, readers_ref, rounded, messages, width):
    served = readers_ref.shape[2]
    me = lax.axis_index("row")
    offsets = [plan.offset(me, plan.reader(key, me)) for key in keys] + [plan.middle]
    pick(readers_ref, offsets, rounded, messages, width)


def pick(readers_ref, offsets, rounded, messages, width):
    served = readers_ref.shape[2]
    for offset, message in zip(offsets, messages):
        for slot in range(served):
            start = pl.multiple_of(readers_ref[0, offset, slot] * width, width)
            message[slot * width : (slot + 1) * width, :] = rounded[pl.ds(start, width), :]
        rest = message.shape[0] - served * width
        if rest:
            message[served * width :, :] = rounded[rounded.shape[0] - rest :, :]


def relay(plan, readers, full, served, width):
    rest = full.shape[0] % (served * width)

    def kernel(readers_ref, full_ref, *messages):
        me = lax.axis_index("row")
        pick(
            readers_ref,
            [plan.offset(me ^ 6, reader) for reader in (me, me ^ 1, me ^ 3)],
            full_ref,
            messages,
            width,
        )

    message = jax.ShapeDtypeStruct((served * width + rest, full.shape[1]), jnp.bfloat16)
    return call(kernel, "relay", [message] * 3, [smem(), vmem()])(readers, full)


def exchange(plan, direct, own, full, readers, served, width):
    sent = {k: lax.ppermute(m, "row", plan.pairs(k)) for k, m in direct.items()}
    if not plan.relayed:
        return [(own, 0)] + [(sent[k], k) for k in plan.direct()]
    mine, beside, beyond = relay(plan, readers, full, served, width)
    beside = lax.ppermute(beside, "row", [(i, i ^ 1) for i in INNER])
    beyond = lax.ppermute(beyond, "row", [(i, i ^ 3) for i in INNER])
    return [
        (own, 0),
        (sent[1], 1),
        (sent[2], 2),
        (sent[3], 3),
        ((mine, sent[7]), (6, 7)),
        ((beside, sent[6]), (7, 6)),
        ((sent[5], beyond), (5, 5)),
    ]


def across(plan, full):
    return lax.ppermute(full, "row", [(i, i ^ 6) for i in INNER]) if plan.relayed else full


class Vectors:
    def __init__(self, plan, items):
        self.plan, self.items = plan, items
        self.arrays, self.scratch = [], []
        for value, _ in items:
            many = isinstance(value, tuple)
            self.arrays += list(value) if many else [value]
            if many:
                self.scratch.append(pltpu.VMEM(value[0].shape, value[0].dtype))
        self.lanes = self.arrays[0].shape[1]
        self.rows = self.arrays[0].shape[0]

    def open(self, refs, scratch):
        refs, scratch = list(refs), list(scratch)
        me = lax.axis_index("row")
        opened = []
        for value, key in self.items:
            if isinstance(value, tuple):
                inner, outer, held = refs.pop(0), refs.pop(0), scratch.pop(0)

                @pl.when(is_inner(me))
                def _():
                    held[...] = inner[...]

                @pl.when(jnp.logical_not(is_inner(me)))
                def _():
                    held[...] = outer[...]

                source = jnp.where(is_inner(me), me ^ key[0], me ^ key[1])
                opened.append((self.plan.offset(source, me), held))
            elif self.plan.relayed:
                opened.append((self.plan.offset(me ^ key, me), refs.pop(0)))
            else:
                opened.append((self.plan.middle - key, refs.pop(0)))
        return opened


def levels(onsite):
    clusters, width = onsite.shape

    def kernel(onsite_ref, level_ref):
        for cluster in range(clusters):
            level_ref[cluster] = jnp.transpose(
                jnp.broadcast_to(onsite_ref[cluster : cluster + 1, :], (width, width))
            )

    shape = jax.ShapeDtypeStruct((clusters, width, width), jnp.float32)
    return call(kernel, "levels", shape, [vmem()])(onsite)


def spread(tile_slot, ks_tiles, correlation_tiles, span, served):
    clusters, _, width, _ = ks_tiles.shape
    slots = span * served

    def kernel(slot_ref, ks_ref, correlation_ref, out_ref, where):
        @pl.loop(0, clusters)
        def _(cluster):
            for kind, ref in enumerate((ks_ref, correlation_ref)):
                count = ref.shape[1]
                for slot in range(slots):
                    where[slot] = count
                for tile in range(count):
                    where[slot_ref[cluster, tile]] = tile
                for slot in range(slots):
                    tile = where[slot]
                    block = ref[cluster, jnp.minimum(tile, count - 1)]
                    block = jnp.where(tile < count, block, jnp.zeros_like(block))
                    lane = slot % served * width
                    out_ref[
                        slot // served, cluster, kind * width : (kind + 1) * width, lane : lane + width
                    ] = block

    return call(
        kernel,
        "spread",
        jax.ShapeDtypeStruct((span, clusters, 2 * width, served * width), jnp.bfloat16),
        [smem(), vmem(), vmem()],
        [pltpu.SMEM((slots,), jnp.int32)],
        moved=16 * MIB,
    )(tile_slot, ks_tiles, correlation_tiles)


def products(dense_ref, opened, clusters, energy):
    depth = dense_ref.shape[-1]
    for offset, vector in opened:
        left = dense_ref[offset, clusters]
        count, height, _ = left.shape
        value = jnp.dot(
            left.reshape(count * height, depth), vector[0:depth, :], preferred_element_type=jnp.float32
        )
        value = value.reshape(count, 2, height // 2, value.shape[1])
        yield value[:, 0] - energy * value[:, 1]


def centers(opened, depth):
    return [vector[depth : depth + EXTRA, :].astype(jnp.float32)[:1] for _, vector in opened]


def work(dense, items, lanes):
    return 2 * len(items) * dense.shape[1] * dense.shape[2] * dense.shape[3] * lanes


def couple(dense, vectors, energies, sums):
    _, clusters, height, depth = dense.shape
    lanes = vectors.lanes
    count = len(vectors.arrays)
    outs = 2 if vectors.rows > depth else 1
    had = len(sums)

    def kernel(dense_ref, energies_ref, *refs):
        refs = list(refs)
        vector_refs, sum_refs = refs[:count], refs[count : count + had]
        out_refs, scratch = refs[count + had : count + had + outs], refs[count + had + outs :]
        energy = wide([energies_ref[...]] * (lanes // energies_ref.shape[1]))
        opened = vectors.open(vector_refs, scratch)
        weights = centers(opened, depth) if outs == 2 else [None] * len(opened)

        @pl.loop(0, clusters // BATCH)
        def _(batch):
            here = pl.ds(batch * BATCH, BATCH)
            values = [ref[here] for ref in sum_refs]
            for weight, part in zip(weights, products(dense_ref, opened, here, energy)):
                terms = [part] if weight is None else [part, weight * part]
                values = [v + t for v, t in zip(values, terms)] if values else terms
            for ref, value in zip(out_refs, values):
                ref[here] = value

    inputs = [dense, energies, *vectors.arrays, *sums]
    shape = jax.ShapeDtypeStruct((clusters, height // 2, lanes), jnp.float32)
    return call(
        kernel,
        "couple",
        [shape] * outs,
        [vmem()] * len(inputs),
        vectors.scratch,
        flops=work(dense, vectors.items, lanes),
        moved=4 * MIB,
    )(*inputs)


def finish_first(plan, dense, vectors, energies, sums, right_side, level, own, readers):
    _, clusters, height, depth = dense.shape
    lanes = vectors.lanes
    fields = right_side.shape[0]
    width = height // 2
    count = len(vectors.arrays)
    keys = plan.direct()

    def kernel(dense_ref, energies_ref, *refs):
        vector_refs, refs = refs[:count], refs[count:]
        sum_ref, weighted_ref, right_ref, level_ref, own_ref, readers_ref = refs[:6]
        image_ref, shifted_ref, lines_ref = refs[6:9]
        messages, outgoing = refs[9 : 10 + len(keys)], refs[10 + len(keys)]
        norm, bend, square, *scratch = refs[11 + len(keys) :]
        energy = wide([energies_ref[...]] * fields)
        opened = vectors.open(vector_refs, scratch)
        weights = centers(opened, depth)
        (center,) = centers([(0, own_ref)], depth)
        for ref in (norm, bend, square):
            ref[...] = jnp.zeros_like(ref)

        @pl.loop(0, clusters // BATCH)
        def _(batch):
            here = pl.ds(batch * BATCH, BATCH)
            value, weighted = sum_ref[here], weighted_ref[here]
            for weight, part in zip(weights, products(dense_ref, opened, here, energy)):
                value, weighted = value + part, weighted + weight * part
            shifted_ref[here] = weighted
            for local in range(BATCH):
                cluster = batch * BATCH + local
                rows = pl.ds(pl.multiple_of(cluster * width, width), width)
                right = wide([right_ref[f, rows, :] for f in range(fields)])
                image = wide([level_ref[cluster]] * fields) * right + value[local]
                image_ref[cluster] = image
                outgoing[rows, :] = (image - center * right).astype(jnp.bfloat16)
                norm[...] += folded(right * right)
                bend[...] += folded(right * image)
                square[...] += folded(image * image)

        fill(plan, keys, readers_ref, outgoing, messages, width)
        lines_ref[...] = lined([norm[...], bend[...], square[...]], 8)

    message = jax.ShapeDtypeStruct((depth, lanes), jnp.bfloat16)
    full = jax.ShapeDtypeStruct((clusters * width, lanes), jnp.bfloat16)
    vector = jax.ShapeDtypeStruct((clusters, width, lanes), jnp.float32)
    image, weighted, lines, *messages, own, full = call(
        kernel,
        "finish_first",
        [vector, vector, jax.ShapeDtypeStruct((8, lanes), jnp.float32)]
        + [message] * (len(keys) + 1)
        + [full],
        [vmem()] * (2 + count + 5) + [smem()],
        [pltpu.VMEM((8, lanes), jnp.float32)] * 3 + vectors.scratch,
        flops=work(dense, vectors.items, lanes),
        moved=8 * MIB,
    )(dense, energies, *vectors.arrays, *sums, right_side, level, own, readers)
    return image, weighted, lines, dict(zip(keys, messages)), own, full


def guesses(lines, fields):
    orbitals = lines.shape[1] // fields
    alphas, growths = [], []
    for column in field_sums(lines, fields):
        norm, bend, square = column[0:1], column[1:2], column[2:3]
        norm = jnp.maximum(norm, 1e-30)
        alpha = norm / jnp.maximum(bend, 4.0 * norm)
        alphas.append(alpha)
        growths.append(jnp.clip(alpha * alpha * square / norm, 1.0, 2.0))
    return per_field(alphas, orbitals), per_field(growths, orbitals)


def finish_second(dense, vectors, energies, sums, right_side, level, image, weighted, lines, devices):
    _, clusters, height, _ = dense.shape
    lanes = vectors.lanes
    fields = right_side.shape[0]
    width = height // 2
    count = len(vectors.arrays)
    spots = -(-devices // 128) * 128

    def kernel(dense_ref, energies_ref, *refs):
        vector_refs, refs = refs[:count], refs[count:]
        sum_ref, right_ref, level_ref, image_ref, weighted_ref, lines_ref = refs[:6]
        later_ref, out_ref, kept, *scratch = refs[6:]
        energy = wide([energies_ref[...]] * fields)
        alpha, growth = guesses(lines_ref[...], fields)
        kept[...] = jnp.zeros_like(kept)

        opened = vectors.open(vector_refs, scratch)

        @pl.loop(0, clusters // BATCH)
        def _(batch):
            here = pl.ds(batch * BATCH, BATCH)
            value = sum_ref[here] + weighted_ref[here]
            for part in products(dense_ref, opened, here, energy):
                value = value + part
            for local in range(BATCH):
                cluster = batch * BATCH + local
                rows = pl.ds(pl.multiple_of(cluster * width, width), width)
                right = wide([right_ref[f, rows, :] for f in range(fields)])
                first = image_ref[cluster]
                later = wide([level_ref[cluster]] * fields) * first + value[local]
                later_ref[cluster] = later
                step = alpha * first
                residual = right - step
                direction = growth * right - step
                bent = growth * first - alpha * later
                terms = (
                    residual * residual,
                    residual * first,
                    direction * bent,
                    direction * first + right * bent,
                    direction * later + first * bent,
                    right * later + first * first,
                    first * later,
                )
                for index, term in enumerate(terms):
                    kept[index] += folded(term)

        count_terms = kept.shape[0]
        block = jnp.concatenate(
            [
                lines_ref[0:3, :],
                lined([kept[i] for i in range(count_terms)], count_terms + 1)[:count_terms],
            ],
            axis=0,
        )
        block = jnp.concatenate([block, jnp.zeros((16 - 3 - count_terms, lanes), jnp.float32)], axis=0)
        orbitals = lanes // fields
        place = lax.axis_index("row") * lax.axis_size("col") + lax.axis_index("col")
        here = lax.broadcasted_iota(jnp.int32, (16, spots), 1) == place
        line = lax.broadcasted_iota(jnp.int32, (16, spots), 0)
        for f, column in enumerate(field_sums(block, fields)):
            spread_out = jnp.broadcast_to(column, (16, spots))
            first_lane = slice(f * orbitals, f * orbitals + 1)
            spread_out = jnp.where(line == 10, jnp.broadcast_to(alpha[:, first_lane], (16, spots)), spread_out)
            spread_out = jnp.where(line == 11, jnp.broadcast_to(growth[:, first_lane], (16, spots)), spread_out)
            out_ref[f * 16 : (f + 1) * 16, :] = jnp.where(here, spread_out, 0.0)

    return call(
        kernel,
        "finish_second",
        [
            jax.ShapeDtypeStruct((clusters, width, lanes), jnp.float32),
            jax.ShapeDtypeStruct((16 * fields, spots), jnp.float32),
        ],
        [vmem()] * (2 + count + 6),
        [pltpu.VMEM((7, 8, lanes), jnp.float32)] + vectors.scratch,
        flops=work(dense, vectors.items, lanes),
        moved=8 * MIB,
    )(dense, energies, *vectors.arrays, *sums, right_side, level, image, weighted, lines)


def step_sizes(gathered, fields, orbitals):
    alphas, growths, gains = [], [], []
    whole = lambda v: jnp.sum(v, axis=1, keepdims=True)
    for f in range(fields):
        line = [gathered[f * 16 + i : f * 16 + i + 1, :] for i in range(12)]
        norm = whole(line[0])
        alpha = norm / whole(line[1])
        growth = alpha * alpha * whole(line[2]) / norm
        off, more = alpha - line[10], growth - line[11]
        after = whole(line[3] - 2.0 * off * line[4] + off * off * line[2])
        bend = whole(
            line[5]
            + more * line[6]
            - off * line[7]
            + more * more * line[1]
            - more * off * line[8]
            + off * off * line[9]
        )
        alphas.append(alpha)
        growths.append(growth)
        gains.append(after / bend)
    return [per_field(v, orbitals) for v in (alphas, growths, gains)]


def final(right_side, image, later, gathered):
    fields, rows, orbitals = right_side.shape
    clusters, width, lanes = image.shape
    blocks = 4
    each = clusters // blocks

    def kernel(right_ref, image_ref, later_ref, gathered_ref, solution_ref, residual_ref):
        step = pl.program_id(0)
        alpha, growth, gain = step_sizes(gathered_ref[...], fields, orbitals)
        for local in range(each):
            cluster = step * each + local
            rows = pl.ds(pl.multiple_of(cluster * width, width), width)
            here = slice(local * width, (local + 1) * width)
            for field in range(fields):
                part = slice(field * orbitals, (field + 1) * orbitals)
                right = right_ref[field, rows, :]
                first = image_ref[cluster, :, part]
                moved = alpha[:, part] * first
                direction = growth[:, part] * right - moved
                bent = growth[:, part] * first - alpha[:, part] * later_ref[cluster, :, part]
                solution_ref[field, here, :] = alpha[:, part] * right + gain[:, part] * direction
                residual_ref[field, here, :] = (right - moved) - gain[:, part] * bent

    vector = pl.BlockSpec((fields, each * width, orbitals), lambda i: (0, i, 0))
    shape = jax.ShapeDtypeStruct(right_side.shape, jnp.float32)
    return pl.pallas_call(
        kernel,
        grid=(blocks,),
        out_shape=[shape, shape],
        in_specs=[vmem()] * 4,
        out_specs=[vector, vector],
        compiler_params=pltpu.CompilerParams(vmem_limit_bytes=12 * MIB),
        name="final",
    )(right_side, image, later, gathered)


def body(right_side, onsite, energies, ks_tiles, correlation_tiles, tile_slot, readers):
    span, served = readers.shape[1:]
    clusters, _, width, _ = ks_tiles.shape
    rows = lax.axis_size("row")
    devices = rows * lax.axis_size("col")
    onsite = onsite.reshape(-1, width)
    energies = energies.reshape(1, -1)
    plan = Plan(rows, span, rows == 8 and span == 7)
    theirs = across(plan, readers)

    def partial(items):
        sums = []
        for group in (items[:1], items[1:3], items[3:-2]):
            sums = couple(dense, Vectors(plan, group), energies, sums)
        return dense, Vectors(plan, items[-2:]), energies, sums

    direct, own, full = pack(plan, readers, right_side, onsite)
    items = exchange(plan, direct, own, across(plan, full), theirs, served, width)
    level = levels(onsite)
    dense = spread(tile_slot, ks_tiles, correlation_tiles, span, served)
    image, weighted, lines, direct, out, full = finish_first(
        plan, *partial(items), right_side, level, own, readers
    )
    items = exchange(plan, direct, out, across(plan, full), theirs, served, width)
    later, gathered = finish_second(
        *partial(items), right_side, level, image, weighted, lines, devices
    )
    return tuple(final(right_side, image, later, summed(gathered)))


def solution(mesh):
    placed = (
        P(None, "row", "col"),
        P("row"),
        P("col"),
        P("row", None, None, None),
        P("row", None, None, None),
        P("row", None),
        P("row", None, None),
    )
    return jax.shard_map(
        body,
        mesh=mesh,
        in_specs=placed,
        out_specs=(P(None, "row", "col"), P(None, "row", "col")),
        check_vma=False,
    )
```

```python
import functools

import jax
import jax.numpy as jnp
from jax import lax
from jax.experimental import pallas as pl
from jax.experimental.pallas import tpu as pltpu
from jax.sharding import PartitionSpec as P

MIB = 2**20
EXTRA = 16
BATCH = 2


def shifted(array, axis, by):
    count = lax.axis_size(axis)
    return lax.ppermute(array, axis, [(i, (i + by) % count) for i in range(count)])


def rounds(axis):
    left, radices = lax.axis_size(axis), []
    if left % 2 == 0 and left > 4:
        radices, left = [2], left // 2
    while left > 1:
        radix = 4 if left % 4 == 0 else 2
        radices, left = radices + [radix], left // radix
    return radices


def summed(array):
    for axis in ("col", "row"):
        count = lax.axis_size(axis)
        if count & (count - 1):
            array = lax.psum(array, axis)
            continue
        hop = 1
        for radix in rounds(axis):
            others = [
                lax.ppermute(array, axis, [(i, i ^ (hop * k)) for i in range(count)])
                for k in range(1, radix)
            ]
            array = array + others[0]
            if radix == 4:
                array = array + (others[1] + others[2])
            hop *= radix
    return array


def vmem():
    return pl.BlockSpec(memory_space=pltpu.VMEM)


def smem():
    return pl.BlockSpec(memory_space=pltpu.SMEM)


def call(kernel, name, out_shape, specs, scratch=(), flops=0, moved=MIB, limit=12):
    return pl.pallas_call(
        kernel,
        out_shape=out_shape,
        in_specs=specs,
        out_specs=jax.tree.map(lambda _: vmem(), out_shape),
        scratch_shapes=list(scratch),
        compiler_params=pltpu.CompilerParams(vmem_limit_bytes=limit * MIB),
        cost_estimate=pl.CostEstimate(flops=flops, bytes_accessed=moved, transcendentals=0),
        name=name,
    )


def wide(parts):
    return jnp.concatenate(parts, axis=1)


def folded(term):
    return jnp.sum(term.reshape(-1, 8, term.shape[-1]), axis=0)


def lined(parts, lines):
    parts = [jnp.sum(p, axis=0, keepdims=True) for p in parts]
    parts.append(jnp.zeros((lines - len(parts), parts[0].shape[1]), jnp.float32))
    return jnp.concatenate(parts, axis=0)


def per_field(values, orbitals):
    return wide([jnp.broadcast_to(v, (1, orbitals)) for v in values])


def field_sums(lines, fields):
    orbitals = lines.shape[1] // fields
    return [
        jnp.sum(lines[:, f * orbitals : (f + 1) * orbitals], axis=1, keepdims=True)
        for f in range(fields)
    ]


class Plan:
    def __init__(self, count, span, relayed):
        self.count, self.span, self.middle, self.relayed = count, span, (span - 1) // 2, relayed

    def offset(self, source, reader):
        value = lax.rem(source - reader + (self.middle + self.count), self.count)
        return jnp.minimum(value, self.span - 1) if self.relayed else value

    def direct(self):
        if self.relayed:
            return [1, 2, 3, 7, 6, 5]
        far = range(self.middle, 0, -1)
        return [by for f in far for by in (f, -f)]

    def reader(self, key, me):
        return me ^ key if self.relayed else lax.rem(me + key + self.count, self.count)

    def source(self, key, me):
        return me ^ key if self.relayed else lax.rem(me - key + self.count, self.count)

    def pairs(self, key):
        if not self.relayed:
            return [(i, (i + key) % self.count) for i in range(self.count)]
        return [(i, i ^ key) for i in range(self.count) if key < 4 or i not in INNER]


INNER = (2, 3, 4, 5)


def is_inner(me):
    return (me >= INNER[0]) & (me <= INNER[-1])


def pack(plan, readers, right_side, onsite):
    fields, rows, orbitals = right_side.shape
    served = readers.shape[2]
    clusters, width = onsite.shape
    lanes = fields * orbitals
    keys = plan.direct()

    def kernel(readers_ref, right_ref, onsite_ref, *refs):
        messages, rounded = refs[:-1], refs[-1]
        norm = [jnp.zeros((8, orbitals), jnp.float32)] * fields
        heavy = [jnp.zeros((8, orbitals), jnp.float32)] * fields
        for cluster in range(clusters):
            weight = jnp.broadcast_to(onsite_ref[cluster : cluster + 1, :], (8, width))
            here = slice(cluster * width, (cluster + 1) * width)
            for field in range(fields):
                right = right_ref[field, here, :]
                rounded[here, field * orbitals : (field + 1) * orbitals] = right.astype(jnp.bfloat16)
                square = right * right
                norm[field] += folded(square)
                heavy[field] += jnp.dot(weight, square, preferred_element_type=jnp.float32)
        centers = [
            jnp.sum(h[:1], axis=1, keepdims=True)
            / jnp.maximum(jnp.sum(jnp.sum(n, axis=0, keepdims=True), axis=1, keepdims=True), 1e-30)
            for h, n in zip(heavy, norm)
        ]
        rest = jnp.broadcast_to(per_field(centers, orbitals), (EXTRA, lanes))
        line, lane = (lax.broadcasted_iota(jnp.int32, (EXTRA, lanes), d) for d in (0, 1))
        for offset in range(readers_ref.shape[1]):
            for slot in range(served):
                here = (line == offset + 1) & (lane == slot)
                rest = jnp.where(here, readers_ref[0, offset, slot].astype(jnp.float32), rest)
        rounded[clusters * width :, :] = rest.astype(jnp.bfloat16)
        fill(plan, keys, readers_ref, rounded, messages, width)

    message = jax.ShapeDtypeStruct((served * width + EXTRA, lanes), jnp.bfloat16)
    full = jax.ShapeDtypeStruct((clusters * width + EXTRA, lanes), jnp.bfloat16)
    *messages, own, full = call(
        kernel, "pack", [message] * (len(keys) + 1) + [full], [smem(), vmem(), vmem()]
    )(readers, right_side, onsite)
    return dict(zip(keys, messages)), own, full


def fill(plan, keys, readers_ref, rounded, messages, width):
    me = lax.axis_index("row")
    offsets = [plan.offset(me, plan.reader(key, me)) for key in keys] + [plan.middle]
    for offset, message in zip(offsets, messages):
        served = readers_ref.shape[2]
        gather([readers_ref[0, offset, slot] for slot in range(served)], rounded, message, width)


def gather(clusters, rounded, message, width):
    for slot, cluster in enumerate(clusters):
        start = pl.multiple_of(cluster * width, width)
        message[slot * width : (slot + 1) * width, :] = rounded[pl.ds(start, width), :]
    used = len(clusters) * width
    if message.shape[0] > used:
        message[used:, :] = rounded[rounded.shape[0] - EXTRA :, :]


def relay(plan, full, chosen, served, width):
    lanes = full.shape[1]
    extra = EXTRA if chosen is None else 0
    message = jax.ShapeDtypeStruct((served * width + extra, lanes), jnp.bfloat16)

    def kernel(*refs):
        if chosen is None:
            full_ref, *messages, chosen_ref = refs
            me = lax.axis_index("row")
            base = full_ref.shape[0] - EXTRA
            table = full_ref[base : base + EXTRA, 0:width].astype(jnp.float32)
            line, lane = (lax.broadcasted_iota(jnp.int32, table.shape, d) for d in (0, 1))
            for index, reader in enumerate((me, me ^ 1, me ^ 3)):
                offset = plan.offset(me ^ 6, reader)
                for slot in range(served):
                    here = (line == offset + 1) & (lane == slot)
                    chosen_ref[index, slot] = jnp.sum(jnp.where(here, table, 0.0)).astype(jnp.int32)
        else:
            chosen_ref, full_ref, *messages = refs
        for index, out in enumerate(messages):
            gather([chosen_ref[index, slot] for slot in range(served)], full_ref, out, width)

    if chosen is not None:
        return call(kernel, "relay", [message] * 3, [smem(), vmem()])(chosen, full), chosen
    *messages, chosen = pl.pallas_call(
        kernel,
        out_shape=[message] * 3 + [jax.ShapeDtypeStruct((3, served), jnp.int32)],
        in_specs=[vmem()],
        out_specs=[vmem()] * 3 + [smem()],
        compiler_params=pltpu.CompilerParams(vmem_limit_bytes=12 * MIB),
        cost_estimate=pl.CostEstimate(flops=0, bytes_accessed=MIB, transcendentals=0),
        name="relay",
    )(full)
    return messages, chosen


def exchange(plan, direct, own, full, chosen, served, width):
    if plan.relayed:
        full = lax.ppermute(full, "row", [(i, i ^ 6) for i in INNER])
    sent = {k: lax.ppermute(m, "row", plan.pairs(k)) for k, m in direct.items()}
    if not plan.relayed:
        return [(own, 0)] + [(sent[k], k) for k in plan.direct()], None
    (mine, beside, beyond), chosen = relay(plan, full, chosen, served, width)
    beside = lax.ppermute(beside, "row", [(i, i ^ 1) for i in INNER])
    beyond = lax.ppermute(beyond, "row", [(i, i ^ 3) for i in INNER])
    items = [
        (own, 0),
        (sent[1], 1),
        (sent[2], 2),
        (sent[3], 3),
        ((sent[5], sent[7]), (5, 7)),
        ((mine, sent[6]), (6, 6)),
        ((beside, beyond), (7, 5)),
    ]
    return items, chosen


class Vectors:
    def __init__(self, plan, items):
        self.plan, self.items = plan, items
        self.arrays, self.scratch = [], []
        for value, _ in items:
            many = isinstance(value, tuple)
            self.arrays += list(value) if many else [value]
            if many:
                self.scratch.append(pltpu.VMEM(value[0].shape, value[0].dtype))
        self.lanes = self.arrays[0].shape[1]
        self.rows = self.arrays[0].shape[0]

    def open(self, refs, scratch):
        refs, scratch = list(refs), list(scratch)
        me = lax.axis_index("row")
        opened = []
        for value, key in self.items:
            if isinstance(value, tuple):
                inner, outer, held = refs.pop(0), refs.pop(0), scratch.pop(0)

                @pl.when(is_inner(me))
                def _():
                    held[...] = inner[...]

                @pl.when(jnp.logical_not(is_inner(me)))
                def _():
                    held[...] = outer[...]

                source = jnp.where(is_inner(me), me ^ key[0], me ^ key[1])
                opened.append((self.plan.offset(source, me), held))
            elif self.plan.relayed:
                opened.append((self.plan.offset(me ^ key, me), refs.pop(0)))
            else:
                opened.append((self.plan.middle - key, refs.pop(0)))
        return opened


def levels(onsite):
    clusters, width = onsite.shape

    def kernel(onsite_ref, level_ref):
        for cluster in range(clusters):
            level_ref[cluster] = jnp.transpose(
                jnp.broadcast_to(onsite_ref[cluster : cluster + 1, :], (width, width))
            )

    shape = jax.ShapeDtypeStruct((clusters, width, width), jnp.float32)
    return call(kernel, "levels", shape, [vmem()])(onsite)


def spread(tile_slot, ks_tiles, correlation_tiles, span, served):
    clusters, _, width, _ = ks_tiles.shape
    slots = span * served

    def kernel(slot_ref, ks_ref, correlation_ref, out_ref, where):
        @pl.loop(0, clusters)
        def _(cluster):
            for kind, ref in enumerate((ks_ref, correlation_ref)):
                count = ref.shape[1]
                for slot in range(slots):
                    where[slot] = count
                for tile in range(count):
                    where[slot_ref[cluster, tile]] = tile
                for slot in range(slots):
                    tile = where[slot]
                    block = ref[cluster, jnp.minimum(tile, count - 1)]
                    block = jnp.where(tile < count, block, jnp.zeros_like(block))
                    lane = slot % served * width
                    out_ref[
                        slot // served, cluster, kind * width : (kind + 1) * width, lane : lane + width
                    ] = block

    return call(
        kernel,
        "spread",
        jax.ShapeDtypeStruct((span, clusters, 2 * width, served * width), jnp.bfloat16),
        [smem(), vmem(), vmem()],
        [pltpu.SMEM((slots,), jnp.int32)],
        moved=16 * MIB,
    )(tile_slot, ks_tiles, correlation_tiles)


def products(dense_ref, opened, clusters, energy):
    depth = dense_ref.shape[-1]
    for offset, vector in opened:
        left = dense_ref[offset, clusters]
        count, height, _ = left.shape
        value = jnp.dot(
            left.reshape(count * height, depth), vector[0:depth, :], preferred_element_type=jnp.float32
        )
        value = value.reshape(count, 2, height // 2, value.shape[1])
        yield value[:, 0] - energy * value[:, 1]


def centers(opened, depth):
    return [vector[depth : depth + EXTRA, :].astype(jnp.float32)[:1] for _, vector in opened]


def work(dense, items, lanes):
    return 2 * len(items) * dense.shape[1] * dense.shape[2] * dense.shape[3] * lanes


def couple(dense, vectors, energies, sums):
    _, clusters, height, depth = dense.shape
    lanes = vectors.lanes
    count = len(vectors.arrays)
    outs = 2 if vectors.rows > depth else 1
    had = len(sums)

    def kernel(dense_ref, energies_ref, *refs):
        refs = list(refs)
        vector_refs, sum_refs = refs[:count], refs[count : count + had]
        out_refs, scratch = refs[count + had : count + had + outs], refs[count + had + outs :]
        energy = wide([energies_ref[...]] * (lanes // energies_ref.shape[1]))
        opened = vectors.open(vector_refs, scratch)
        weights = centers(opened, depth) if outs == 2 else [None] * len(opened)

        @pl.loop(0, clusters // BATCH)
        def _(batch):
            here = pl.ds(batch * BATCH, BATCH)
            values = [ref[here] for ref in sum_refs]
            for weight, part in zip(weights, products(dense_ref, opened, here, energy)):
                terms = [part] if weight is None else [part, weight * part]
                values = [v + t for v, t in zip(values, terms)] if values else terms
            for ref, value in zip(out_refs, values):
                ref[here] = value

    inputs = [dense, energies, *vectors.arrays, *sums]
    shape = jax.ShapeDtypeStruct((clusters, height // 2, lanes), jnp.float32)
    return call(
        kernel,
        "couple",
        [shape] * outs,
        [vmem()] * len(inputs),
        vectors.scratch,
        flops=work(dense, vectors.items, lanes),
        moved=4 * MIB,
    )(*inputs)


def finish_first(plan, dense, vectors, energies, sums, right_side, level, own, readers):
    _, clusters, height, depth = dense.shape
    lanes = vectors.lanes
    fields = right_side.shape[0]
    width = height // 2
    count = len(vectors.arrays)
    keys = plan.direct()

    def kernel(dense_ref, energies_ref, *refs):
        vector_refs, refs = refs[:count], refs[count:]
        sum_ref, weighted_ref, right_ref, level_ref, own_ref, readers_ref = refs[:6]
        image_ref, shifted_ref, lines_ref = refs[6:9]
        messages, outgoing = refs[9 : 10 + len(keys)], refs[10 + len(keys)]
        norm, bend, square, *scratch = refs[11 + len(keys) :]
        energy = wide([energies_ref[...]] * fields)
        opened = vectors.open(vector_refs, scratch)
        weights = centers(opened, depth)
        (center,) = centers([(0, own_ref)], depth)
        for ref in (norm, bend, square):
            ref[...] = jnp.zeros_like(ref)

        @pl.loop(0, clusters // BATCH)
        def _(batch):
            here = pl.ds(batch * BATCH, BATCH)
            value, weighted = sum_ref[here], weighted_ref[here]
            for weight, part in zip(weights, products(dense_ref, opened, here, energy)):
                value, weighted = value + part, weighted + weight * part
            shifted_ref[here] = weighted
            for local in range(BATCH):
                cluster = batch * BATCH + local
                rows = pl.ds(pl.multiple_of(cluster * width, width), width)
                right = wide([right_ref[f, rows, :] for f in range(fields)])
                image = wide([level_ref[cluster]] * fields) * right + value[local]
                image_ref[cluster] = image
                outgoing[rows, :] = (image - center * right).astype(jnp.bfloat16)
                norm[...] += folded(right * right)
                bend[...] += folded(right * image)
                square[...] += folded(image * image)

        fill(plan, keys, readers_ref, outgoing, messages, width)
        lines_ref[...] = lined([norm[...], bend[...], square[...]], 8)

    message = jax.ShapeDtypeStruct((depth, lanes), jnp.bfloat16)
    full = jax.ShapeDtypeStruct((clusters * width, lanes), jnp.bfloat16)
    vector = jax.ShapeDtypeStruct((clusters, width, lanes), jnp.float32)
    image, weighted, lines, *messages, own, full = call(
        kernel,
        "finish_first",
        [vector, vector, jax.ShapeDtypeStruct((8, lanes), jnp.float32)]
        + [message] * (len(keys) + 1)
        + [full],
        [vmem()] * (2 + count + 5) + [smem()],
        [pltpu.VMEM((8, lanes), jnp.float32)] * 3 + vectors.scratch,
        flops=work(dense, vectors.items, lanes),
        moved=8 * MIB,
    )(dense, energies, *vectors.arrays, *sums, right_side, level, own, readers)
    return image, weighted, lines, dict(zip(keys, messages)), own, full


def guesses(lines, fields):
    orbitals = lines.shape[1] // fields
    alphas, growths = [], []
    for column in field_sums(lines, fields):
        norm, bend, square = column[0:1], column[1:2], column[2:3]
        norm = jnp.maximum(norm, 1e-30)
        alpha = norm / jnp.maximum(bend, 4.0 * norm)
        alphas.append(alpha)
        growths.append(jnp.clip(alpha * alpha * square / norm, 1.0, 2.0))
    return per_field(alphas, orbitals), per_field(growths, orbitals)


def finish_second(dense, vectors, energies, sums, right_side, level, image, weighted, lines, devices):
    _, clusters, height, _ = dense.shape
    lanes = vectors.lanes
    fields = right_side.shape[0]
    width = height // 2
    count = len(vectors.arrays)
    spots = -(-devices // 128) * 128

    def kernel(dense_ref, energies_ref, *refs):
        vector_refs, refs = refs[:count], refs[count:]
        sum_ref, right_ref, level_ref, image_ref, weighted_ref, lines_ref = refs[:6]
        later_ref, out_ref, kept, *scratch = refs[6:]
        energy = wide([energies_ref[...]] * fields)
        alpha, growth = guesses(lines_ref[...], fields)
        kept[...] = jnp.zeros_like(kept)

        opened = vectors.open(vector_refs, scratch)

        @pl.loop(0, clusters // BATCH)
        def _(batch):
            here = pl.ds(batch * BATCH, BATCH)
            value = sum_ref[here] + weighted_ref[here]
            for part in products(dense_ref, opened, here, energy):
                value = value + part
            for local in range(BATCH):
                cluster = batch * BATCH + local
                rows = pl.ds(pl.multiple_of(cluster * width, width), width)
                right = wide([right_ref[f, rows, :] for f in range(fields)])
                first = image_ref[cluster]
                later = wide([level_ref[cluster]] * fields) * first + value[local]
                later_ref[cluster] = later
                step = alpha * first
                residual = right - step
                direction = growth * right - step
                bent = growth * first - alpha * later
                terms = (
                    residual * residual,
                    residual * first,
                    direction * bent,
                    direction * first + right * bent,
                    direction * later + first * bent,
                    right * later + first * first,
                    first * later,
                )
                for index, term in enumerate(terms):
                    kept[index] += folded(term)

        count_terms = kept.shape[0]
        block = jnp.concatenate(
            [
                lines_ref[0:3, :],
                lined([kept[i] for i in range(count_terms)], count_terms + 1)[:count_terms],
            ],
            axis=0,
        )
        block = jnp.concatenate([block, jnp.zeros((16 - 3 - count_terms, lanes), jnp.float32)], axis=0)
        orbitals = lanes // fields
        place = lax.axis_index("row") * lax.axis_size("col") + lax.axis_index("col")
        here = lax.broadcasted_iota(jnp.int32, (16, spots), 1) == place
        line = lax.broadcasted_iota(jnp.int32, (16, spots), 0)
        for f, column in enumerate(field_sums(block, fields)):
            spread_out = jnp.broadcast_to(column, (16, spots))
            first_lane = slice(f * orbitals, f * orbitals + 1)
            spread_out = jnp.where(line == 10, jnp.broadcast_to(alpha[:, first_lane], (16, spots)), spread_out)
            spread_out = jnp.where(line == 11, jnp.broadcast_to(growth[:, first_lane], (16, spots)), spread_out)
            out_ref[f * 16 : (f + 1) * 16, :] = jnp.where(here, spread_out, 0.0)

    return call(
        kernel,
        "finish_second",
        [
            jax.ShapeDtypeStruct((clusters, width, lanes), jnp.float32),
            jax.ShapeDtypeStruct((16 * fields, spots), jnp.float32),
        ],
        [vmem()] * (2 + count + 6),
        [pltpu.VMEM((7, 8, lanes), jnp.float32)] + vectors.scratch,
        flops=work(dense, vectors.items, lanes),
        moved=8 * MIB,
    )(dense, energies, *vectors.arrays, *sums, right_side, level, image, weighted, lines)


def step_sizes(gathered, fields, orbitals):
    alphas, growths, gains = [], [], []
    whole = lambda v: jnp.sum(v, axis=1, keepdims=True)
    for f in range(fields):
        line = [gathered[f * 16 + i : f * 16 + i + 1, :] for i in range(12)]
        norm = whole(line[0])
        alpha = norm / whole(line[1])
        growth = alpha * alpha * whole(line[2]) / norm
        off, more = alpha - line[10], growth - line[11]
        after = whole(line[3] - 2.0 * off * line[4] + off * off * line[2])
        bend = whole(
            line[5]
            + more * line[6]
            - off * line[7]
            + more * more * line[1]
            - more * off * line[8]
            + off * off * line[9]
        )
        alphas.append(alpha)
        growths.append(growth)
        gains.append(after / bend)
    return [per_field(v, orbitals) for v in (alphas, growths, gains)]


def final(right_side, image, later, gathered):
    fields, rows, orbitals = right_side.shape
    clusters, width, lanes = image.shape
    blocks = 4
    each = clusters // blocks

    def kernel(right_ref, image_ref, later_ref, gathered_ref, solution_ref, residual_ref, steps):
        step = pl.program_id(0)

        @pl.when(step == 0)
        def _():
            alpha, growth, gain = step_sizes(gathered_ref[...], fields, orbitals)
            steps[0:1, :] = alpha + gain * growth
            steps[1:2, :] = gain * alpha

        for local in range(each):
            cluster = step * each + local
            rows = pl.ds(pl.multiple_of(cluster * width, width), width)
            here = slice(local * width, (local + 1) * width)
            for field in range(fields):
                part = slice(field * orbitals, (field + 1) * orbitals)
                one, two = steps[0:1, part], steps[1:2, part]
                right = right_ref[field, rows, :]
                first = image_ref[cluster, :, part]
                later = later_ref[cluster, :, part]
                solution_ref[field, here, :] = one * right - two * first
                residual_ref[field, here, :] = (right - one * first) + two * later

    vector = pl.BlockSpec((fields, each * width, orbitals), lambda i: (0, i, 0))
    shape = jax.ShapeDtypeStruct(right_side.shape, jnp.float32)
    return pl.pallas_call(
        kernel,
        grid=(blocks,),
        out_shape=[shape, shape],
        in_specs=[vmem()] * 4,
        out_specs=[vector, vector],
        scratch_shapes=[pltpu.VMEM((8, lanes), jnp.float32)],
        compiler_params=pltpu.CompilerParams(vmem_limit_bytes=12 * MIB),
        name="final",
    )(right_side, image, later, gathered)


def body(right_side, onsite, energies, ks_tiles, correlation_tiles, tile_slot, readers):
    span, served = readers.shape[1:]
    clusters, _, width, _ = ks_tiles.shape
    rows = lax.axis_size("row")
    devices = rows * lax.axis_size("col")
    onsite = onsite.reshape(-1, width)
    energies = energies.reshape(1, -1)
    plan = Plan(rows, span, rows == 8 and span == 7)

    def partial(items):
        sums = []
        for group in (items[:1], items[1:3], items[3:-2]):
            sums = couple(dense, Vectors(plan, group), energies, sums)
        return dense, Vectors(plan, items[-2:]), energies, sums

    direct, own, full = pack(plan, readers, right_side, onsite)
    items, chosen = exchange(plan, direct, own, full, None, served, width)
    level = levels(onsite)
    dense = spread(tile_slot, ks_tiles, correlation_tiles, span, served)
    image, weighted, lines, direct, out, full = finish_first(
        plan, *partial(items), right_side, level, own, readers
    )
    items, _ = exchange(plan, direct, out, full, chosen, served, width)
    later, gathered = finish_second(
        *partial(items), right_side, level, image, weighted, lines, devices
    )
    return tuple(final(right_side, image, later, summed(gathered)))


def solution(mesh):
    placed = (
        P(None, "row", "col"),
        P("row"),
        P("col"),
        P("row", None, None, None),
        P("row", None, None, None),
        P("row", None),
        P("row", None, None),
    )
    return jax.shard_map(
        body,
        mesh=mesh,
        in_specs=placed,
        out_specs=(P(None, "row", "col"), P(None, "row", "col")),
        check_vma=False,
    )
```

```python
import functools

import jax
import jax.numpy as jnp
from jax import lax
from jax.experimental import pallas as pl
from jax.experimental.pallas import tpu as pltpu
from jax.sharding import PartitionSpec as P

MIB = 2**20
EXTRA = 16
BATCH = 2


def shifted(array, axis, by):
    count = lax.axis_size(axis)
    return lax.ppermute(array, axis, [(i, (i + by) % count) for i in range(count)])


def vmem():
    return pl.BlockSpec(memory_space=pltpu.VMEM)


def smem():
    return pl.BlockSpec(memory_space=pltpu.SMEM)


def call(kernel, name, out_shape, specs, scratch=(), flops=0, moved=MIB, limit=12):
    return pl.pallas_call(
        kernel,
        out_shape=out_shape,
        in_specs=specs,
        out_specs=jax.tree.map(lambda _: vmem(), out_shape),
        scratch_shapes=list(scratch),
        compiler_params=pltpu.CompilerParams(vmem_limit_bytes=limit * MIB),
        cost_estimate=pl.CostEstimate(flops=flops, bytes_accessed=moved, transcendentals=0),
        name=name,
    )


def wide(parts):
    return jnp.concatenate(parts, axis=1)


def folded(term):
    return jnp.sum(term.reshape(-1, 8, term.shape[-1]), axis=0)


def lined(parts, lines):
    parts = [jnp.sum(p, axis=0, keepdims=True) for p in parts]
    parts.append(jnp.zeros((lines - len(parts), parts[0].shape[1]), jnp.float32))
    return jnp.concatenate(parts, axis=0)


def per_field(values, orbitals):
    return wide([jnp.broadcast_to(v, (1, orbitals)) for v in values])


def field_sums(lines, fields):
    orbitals = lines.shape[1] // fields
    return [
        jnp.sum(lines[:, f * orbitals : (f + 1) * orbitals], axis=1, keepdims=True)
        for f in range(fields)
    ]


class Plan:
    def __init__(self, count, span, relayed):
        self.count, self.span, self.middle, self.relayed = count, span, (span - 1) // 2, relayed

    def offset(self, source, reader):
        value = lax.rem(source - reader + (self.middle + self.count), self.count)
        return jnp.minimum(value, self.span - 1) if self.relayed else value

    def direct(self):
        if self.relayed:
            return [1, 2, 3, 7, 6, 5]
        far = range(self.middle, 0, -1)
        return [by for f in far for by in (f, -f)]

    def reader(self, key, me):
        return me ^ key if self.relayed else lax.rem(me + key + self.count, self.count)

    def source(self, key, me):
        return me ^ key if self.relayed else lax.rem(me - key + self.count, self.count)

    def pairs(self, key):
        if not self.relayed:
            return [(i, (i + key) % self.count) for i in range(self.count)]
        return [(i, i ^ key) for i in range(self.count) if key < 4 or i not in INNER]


INNER = (2, 3, 4, 5)


def is_inner(me):
    return (me >= INNER[0]) & (me <= INNER[-1])


def pack(plan, readers, right_side, onsite):
    fields, rows, orbitals = right_side.shape
    served = readers.shape[2]
    clusters, width = onsite.shape
    lanes = fields * orbitals
    keys = plan.direct()

    def kernel(readers_ref, right_ref, onsite_ref, *refs):
        messages, rounded = refs[:-1], refs[-1]
        norm = [jnp.zeros((8, orbitals), jnp.float32)] * fields
        heavy = [jnp.zeros((8, orbitals), jnp.float32)] * fields
        for cluster in range(clusters):
            weight = jnp.broadcast_to(onsite_ref[cluster : cluster + 1, :], (8, width))
            here = slice(cluster * width, (cluster + 1) * width)
            for field in range(fields):
                right = right_ref[field, here, :]
                rounded[here, field * orbitals : (field + 1) * orbitals] = right.astype(jnp.bfloat16)
                square = right * right
                norm[field] += folded(square)
                heavy[field] += jnp.dot(weight, square, preferred_element_type=jnp.float32)
        centers = [
            jnp.sum(h[:1], axis=1, keepdims=True)
            / jnp.maximum(jnp.sum(jnp.sum(n, axis=0, keepdims=True), axis=1, keepdims=True), 1e-30)
            for h, n in zip(heavy, norm)
        ]
        rest = jnp.broadcast_to(per_field(centers, orbitals), (EXTRA, lanes))
        line, lane = (lax.broadcasted_iota(jnp.int32, (EXTRA, lanes), d) for d in (0, 1))
        for offset in range(readers_ref.shape[1]):
            for slot in range(served):
                here = (line == offset + 1) & (lane == slot)
                rest = jnp.where(here, readers_ref[0, offset, slot].astype(jnp.float32), rest)
        rounded[clusters * width :, :] = rest.astype(jnp.bfloat16)
        fill(plan, keys, readers_ref, rounded, messages, width)

    message = jax.ShapeDtypeStruct((served * width + EXTRA, lanes), jnp.bfloat16)
    full = jax.ShapeDtypeStruct((clusters * width + EXTRA, lanes), jnp.bfloat16)
    *messages, own, full = call(
        kernel, "pack", [message] * (len(keys) + 1) + [full], [smem(), vmem(), vmem()]
    )(readers, right_side, onsite)
    return dict(zip(keys, messages)), own, full


def fill(plan, keys, readers_ref, rounded, messages, width):
    me = lax.axis_index("row")
    offsets = [plan.offset(me, plan.reader(key, me)) for key in keys] + [plan.middle]
    for offset, message in zip(offsets, messages):
        served = readers_ref.shape[2]
        gather([readers_ref[0, offset, slot] for slot in range(served)], rounded, message, width)


def gather(clusters, rounded, message, width):
    for slot, cluster in enumerate(clusters):
        start = pl.multiple_of(cluster * width, width)
        message[slot * width : (slot + 1) * width, :] = rounded[pl.ds(start, width), :]
    used = len(clusters) * width
    if message.shape[0] > used:
        message[used:, :] = rounded[rounded.shape[0] - EXTRA :, :]


def relay(plan, full, chosen, served, width):
    lanes = full.shape[1]
    extra = EXTRA if chosen is None else 0
    message = jax.ShapeDtypeStruct((served * width + extra, lanes), jnp.bfloat16)

    def kernel(*refs):
        if chosen is None:
            full_ref, *messages, chosen_ref = refs
            me = lax.axis_index("row")
            base = full_ref.shape[0] - EXTRA
            table = full_ref[base : base + EXTRA, 0:width].astype(jnp.float32)
            line, lane = (lax.broadcasted_iota(jnp.int32, table.shape, d) for d in (0, 1))
            for index, reader in enumerate((me, me ^ 1, me ^ 3)):
                offset = plan.offset(me ^ 6, reader)
                for slot in range(served):
                    here = (line == offset + 1) & (lane == slot)
                    chosen_ref[index, slot] = jnp.sum(jnp.where(here, table, 0.0)).astype(jnp.int32)
        else:
            chosen_ref, full_ref, *messages = refs
        for index, out in enumerate(messages):
            gather([chosen_ref[index, slot] for slot in range(served)], full_ref, out, width)

    if chosen is not None:
        return call(kernel, "relay", [message] * 3, [smem(), vmem()])(chosen, full), chosen
    *messages, chosen = pl.pallas_call(
        kernel,
        out_shape=[message] * 3 + [jax.ShapeDtypeStruct((3, served), jnp.int32)],
        in_specs=[vmem()],
        out_specs=[vmem()] * 3 + [smem()],
        compiler_params=pltpu.CompilerParams(vmem_limit_bytes=12 * MIB),
        cost_estimate=pl.CostEstimate(flops=0, bytes_accessed=MIB, transcendentals=0),
        name="relay",
    )(full)
    return messages, chosen


def exchange(plan, direct, own, full, chosen, served, width):
    if plan.relayed:
        full = lax.ppermute(full, "row", [(i, i ^ 6) for i in INNER])
    sent = {k: lax.ppermute(m, "row", plan.pairs(k)) for k, m in direct.items()}
    if not plan.relayed:
        return [(own, 0)] + [(sent[k], k) for k in plan.direct()], None
    (mine, beside, beyond), chosen = relay(plan, full, chosen, served, width)
    beside = lax.ppermute(beside, "row", [(i, i ^ 1) for i in INNER])
    beyond = lax.ppermute(beyond, "row", [(i, i ^ 3) for i in INNER])
    items = [
        (own, 0),
        (sent[1], 1),
        (sent[2], 2),
        (sent[3], 3),
        ((mine, sent[7]), (6, 7)),
        ((beside, sent[6]), (7, 6)),
        ((sent[5], beyond), (5, 5)),
    ]
    return items, chosen


class Vectors:
    def __init__(self, plan, items):
        self.plan, self.items = plan, items
        self.arrays, self.scratch = [], []
        for value, _ in items:
            many = isinstance(value, tuple)
            self.arrays += list(value) if many else [value]
            if many:
                self.scratch.append(pltpu.VMEM(value[0].shape, value[0].dtype))
        self.lanes = self.arrays[0].shape[1]
        self.rows = self.arrays[0].shape[0]

    def open(self, refs, scratch):
        refs, scratch = list(refs), list(scratch)
        me = lax.axis_index("row")
        opened = []
        for value, key in self.items:
            if isinstance(value, tuple):
                inner, outer, held = refs.pop(0), refs.pop(0), scratch.pop(0)

                @pl.when(is_inner(me))
                def _():
                    held[...] = inner[...]

                @pl.when(jnp.logical_not(is_inner(me)))
                def _():
                    held[...] = outer[...]

                source = jnp.where(is_inner(me), me ^ key[0], me ^ key[1])
                opened.append((self.plan.offset(source, me), held))
            elif self.plan.relayed:
                opened.append((self.plan.offset(me ^ key, me), refs.pop(0)))
            else:
                opened.append((self.plan.middle - key, refs.pop(0)))
        return opened


def levels(onsite):
    clusters, width = onsite.shape

    def kernel(onsite_ref, level_ref):
        for cluster in range(clusters):
            level_ref[cluster] = jnp.transpose(
                jnp.broadcast_to(onsite_ref[cluster : cluster + 1, :], (width, width))
            )

    shape = jax.ShapeDtypeStruct((clusters, width, width), jnp.float32)
    return call(kernel, "levels", shape, [vmem()])(onsite)


def spread(tile_slot, ks_tiles, correlation_tiles, span, served):
    clusters, _, width, _ = ks_tiles.shape
    slots = span * served

    def kernel(slot_ref, ks_ref, correlation_ref, out_ref, where):
        @pl.loop(0, clusters)
        def _(cluster):
            for kind, ref in enumerate((ks_ref, correlation_ref)):
                count = ref.shape[1]
                for slot in range(slots):
                    where[slot] = count
                for tile in range(count):
                    where[slot_ref[cluster, tile]] = tile
                for slot in range(slots):
                    tile = where[slot]
                    block = ref[cluster, jnp.minimum(tile, count - 1)]
                    block = jnp.where(tile < count, block, jnp.zeros_like(block))
                    lane = slot % served * width
                    out_ref[
                        slot // served, cluster, kind * width : (kind + 1) * width, lane : lane + width
                    ] = block

    return call(
        kernel,
        "spread",
        jax.ShapeDtypeStruct((span, clusters, 2 * width, served * width), jnp.bfloat16),
        [smem(), vmem(), vmem()],
        [pltpu.SMEM((slots,), jnp.int32)],
        moved=16 * MIB,
    )(tile_slot, ks_tiles, correlation_tiles)


def products(dense_ref, opened, clusters, energy):
    depth = dense_ref.shape[-1]
    for offset, vector in opened:
        left = dense_ref[offset, clusters]
        count, height, _ = left.shape
        value = jnp.dot(
            left.reshape(count * height, depth), vector[0:depth, :], preferred_element_type=jnp.float32
        )
        value = value.reshape(count, 2, height // 2, value.shape[1])
        yield value[:, 0] - energy * value[:, 1]


def centers(opened, depth):
    return [vector[depth : depth + EXTRA, :].astype(jnp.float32)[:1] for _, vector in opened]


def work(dense, items, lanes):
    return 2 * len(items) * dense.shape[1] * dense.shape[2] * dense.shape[3] * lanes


def couple(dense, vectors, energies, sums):
    _, clusters, height, depth = dense.shape
    lanes = vectors.lanes
    count = len(vectors.arrays)
    outs = 2 if vectors.rows > depth else 1
    had = len(sums)

    def kernel(dense_ref, energies_ref, *refs):
        refs = list(refs)
        vector_refs, sum_refs = refs[:count], refs[count : count + had]
        out_refs, scratch = refs[count + had : count + had + outs], refs[count + had + outs :]
        energy = wide([energies_ref[...]] * (lanes // energies_ref.shape[1]))
        opened = vectors.open(vector_refs, scratch)
        weights = centers(opened, depth) if outs == 2 else [None] * len(opened)

        @pl.loop(0, clusters // BATCH)
        def _(batch):
            here = pl.ds(batch * BATCH, BATCH)
            values = [ref[here] for ref in sum_refs]
            for weight, part in zip(weights, products(dense_ref, opened, here, energy)):
                terms = [part] if weight is None else [part, weight * part]
                values = [v + t for v, t in zip(values, terms)] if values else terms
            for ref, value in zip(out_refs, values):
                ref[here] = value

    inputs = [dense, energies, *vectors.arrays, *sums]
    shape = jax.ShapeDtypeStruct((clusters, height // 2, lanes), jnp.float32)
    return call(
        kernel,
        "couple",
        [shape] * outs,
        [vmem()] * len(inputs),
        vectors.scratch,
        flops=work(dense, vectors.items, lanes),
        moved=4 * MIB,
    )(*inputs)


def finish_first(plan, dense, vectors, energies, sums, right_side, level, own, readers):
    _, clusters, height, depth = dense.shape
    lanes = vectors.lanes
    fields = right_side.shape[0]
    width = height // 2
    count = len(vectors.arrays)
    keys = plan.direct()

    def kernel(dense_ref, energies_ref, *refs):
        vector_refs, refs = refs[:count], refs[count:]
        sum_ref, weighted_ref, right_ref, level_ref, own_ref, readers_ref = refs[:6]
        image_ref, shifted_ref, lines_ref = refs[6:9]
        messages, outgoing = refs[9 : 10 + len(keys)], refs[10 + len(keys)]
        norm, bend, square, *scratch = refs[11 + len(keys) :]
        energy = wide([energies_ref[...]] * fields)
        opened = vectors.open(vector_refs, scratch)
        weights = centers(opened, depth)
        (center,) = centers([(0, own_ref)], depth)
        for ref in (norm, bend, square):
            ref[...] = jnp.zeros_like(ref)

        @pl.loop(0, clusters // BATCH)
        def _(batch):
            here = pl.ds(batch * BATCH, BATCH)
            value, weighted = sum_ref[here], weighted_ref[here]
            for weight, part in zip(weights, products(dense_ref, opened, here, energy)):
                value, weighted = value + part, weighted + weight * part
            shifted_ref[here] = weighted
            for local in range(BATCH):
                cluster = batch * BATCH + local
                rows = pl.ds(pl.multiple_of(cluster * width, width), width)
                right = wide([right_ref[f, rows, :] for f in range(fields)])
                image = wide([level_ref[cluster]] * fields) * right + value[local]
                image_ref[cluster] = image
                outgoing[rows, :] = (image - center * right).astype(jnp.bfloat16)
                norm[...] += folded(right * right)
                bend[...] += folded(right * image)
                square[...] += folded(image * image)

        fill(plan, keys, readers_ref, outgoing, messages, width)
        lines_ref[...] = lined([norm[...], bend[...], square[...]], 8)

    message = jax.ShapeDtypeStruct((depth, lanes), jnp.bfloat16)
    full = jax.ShapeDtypeStruct((clusters * width, lanes), jnp.bfloat16)
    vector = jax.ShapeDtypeStruct((clusters, width, lanes), jnp.float32)
    image, weighted, lines, *messages, own, full = call(
        kernel,
        "finish_first",
        [vector, vector, jax.ShapeDtypeStruct((8, lanes), jnp.float32)]
        + [message] * (len(keys) + 1)
        + [full],
        [vmem()] * (2 + count + 5) + [smem()],
        [pltpu.VMEM((8, lanes), jnp.float32)] * 3 + vectors.scratch,
        flops=work(dense, vectors.items, lanes),
        moved=8 * MIB,
    )(dense, energies, *vectors.arrays, *sums, right_side, level, own, readers)
    return image, weighted, lines, dict(zip(keys, messages)), own, full


def guesses(lines, fields):
    orbitals = lines.shape[1] // fields
    alphas, growths = [], []
    for column in field_sums(lines, fields):
        norm, bend, square = column[0:1], column[1:2], column[2:3]
        norm = jnp.maximum(norm, 1e-30)
        alpha = norm / jnp.maximum(bend, 4.0 * norm)
        alphas.append(alpha)
        growths.append(jnp.clip(alpha * alpha * square / norm, 1.0, 2.0))
    return per_field(alphas, orbitals), per_field(growths, orbitals)


def finish_second(dense, vectors, energies, sums, right_side, level, image, weighted, lines, devices):
    _, clusters, height, _ = dense.shape
    lanes = vectors.lanes
    fields = right_side.shape[0]
    width = height // 2
    count = len(vectors.arrays)

    def kernel(dense_ref, energies_ref, *refs):
        vector_refs, refs = refs[:count], refs[count:]
        sum_ref, right_ref, level_ref, image_ref, weighted_ref, lines_ref = refs[:6]
        later_ref, out_ref, kept, *scratch = refs[6:]
        energy = wide([energies_ref[...]] * fields)
        alpha, growth = guesses(lines_ref[...], fields)
        kept[...] = jnp.zeros_like(kept)

        opened = vectors.open(vector_refs, scratch)

        @pl.loop(0, clusters // BATCH)
        def _(batch):
            here = pl.ds(batch * BATCH, BATCH)
            value = sum_ref[here] + weighted_ref[here]
            for part in products(dense_ref, opened, here, energy):
                value = value + part
            for local in range(BATCH):
                cluster = batch * BATCH + local
                rows = pl.ds(pl.multiple_of(cluster * width, width), width)
                right = wide([right_ref[f, rows, :] for f in range(fields)])
                first = image_ref[cluster]
                later = wide([level_ref[cluster]] * fields) * first + value[local]
                later_ref[cluster] = later
                step = alpha * first
                residual = right - step
                direction = growth * right - step
                bent = growth * first - alpha * later
                terms = (
                    residual * residual,
                    residual * first,
                    direction * bent,
                    direction * first + right * bent,
                    direction * later + first * bent,
                    right * later + first * first,
                    first * later,
                )
                for index, term in enumerate(terms):
                    kept[index] += folded(term)

        count_terms = kept.shape[0]
        block = jnp.concatenate(
            [
                lines_ref[0:3, :],
                lined([kept[i] for i in range(count_terms)], count_terms + 1)[:count_terms],
            ],
            axis=0,
        )
        block = jnp.concatenate([block, jnp.zeros((16 - 3 - count_terms, lanes), jnp.float32)], axis=0)
        orbitals = lanes // fields
        line, lane = (lax.broadcasted_iota(jnp.int32, (16, 128), d) for d in (0, 1))
        rows = []
        for f, column in enumerate(field_sums(block, fields)):
            first_lane = slice(f * orbitals, f * orbitals + 1)
            filled = jnp.broadcast_to(column, (16, 128))
            filled = jnp.where(line == 10, jnp.broadcast_to(alpha[:, first_lane], (16, 128)), filled)
            filled = jnp.where(line == 11, jnp.broadcast_to(growth[:, first_lane], (16, 128)), filled)
            rows.append(jnp.sum(jnp.where(line == lane, filled, 0.0), axis=0, keepdims=True))
        rows.append(jnp.zeros((8 - fields, 128), jnp.float32))
        out_ref[...] = jnp.broadcast_to(jnp.concatenate(rows, axis=0)[None], out_ref.shape)

    return call(
        kernel,
        "finish_second",
        [
            jax.ShapeDtypeStruct((clusters, width, lanes), jnp.float32),
            jax.ShapeDtypeStruct((devices, 8, 128), jnp.float32),
        ],
        [vmem()] * (2 + count + 6),
        [pltpu.VMEM((7, 8, lanes), jnp.float32)] + vectors.scratch,
        flops=work(dense, vectors.items, lanes),
        moved=8 * MIB,
    )(dense, energies, *vectors.arrays, *sums, right_side, level, image, weighted, lines)


def step_sizes(gathered, fields, orbitals):
    rows = gathered.reshape(-1, 128)
    flat = wide([jnp.transpose(rows[i : i + 128]) for i in range(0, rows.shape[0], 128)])
    line = [flat[i : i + 1, :] for i in range(12)]
    place = lax.broadcasted_iota(jnp.int32, line[0].shape, 1) & 7
    whole = lambda v: [
        jnp.sum(jnp.where(place == f, v, 0.0), axis=1, keepdims=True) for f in range(fields)
    ]

    def back(values):
        row = jnp.zeros_like(line[0])
        for f, value in enumerate(values):
            row = jnp.where(place == f, jnp.broadcast_to(value, row.shape), row)
        return row

    norm = whole(line[0])
    alpha = [n / b for n, b in zip(norm, whole(line[1]))]
    growth = [a * a * s / n for a, s, n in zip(alpha, whole(line[2]), norm)]
    off, more = back(alpha) - line[10], back(growth) - line[11]
    after = whole(line[3] - 2.0 * off * line[4] + off * off * line[2])
    bend = whole(
        line[5]
        + more * line[6]
        - off * line[7]
        + more * more * line[1]
        - more * off * line[8]
        + off * off * line[9]
    )
    gain = [a / b for a, b in zip(after, bend)]
    return [per_field(v, orbitals) for v in (alpha, growth, gain)]


def final(right_side, image, later, gathered):
    fields, rows, orbitals = right_side.shape
    clusters, width, lanes = image.shape
    blocks = 4
    each = clusters // blocks

    def kernel(right_ref, image_ref, later_ref, gathered_ref, solution_ref, residual_ref, steps):
        step = pl.program_id(0)

        @pl.when(step == 0)
        def _():
            alpha, growth, gain = step_sizes(gathered_ref[...], fields, orbitals)
            steps[0:1, :] = alpha + gain * growth
            steps[1:2, :] = gain * alpha

        for local in range(each):
            cluster = step * each + local
            rows = pl.ds(pl.multiple_of(cluster * width, width), width)
            here = slice(local * width, (local + 1) * width)
            for field in range(fields):
                part = slice(field * orbitals, (field + 1) * orbitals)
                one, two = steps[0:1, part], steps[1:2, part]
                right = right_ref[field, rows, :]
                first = image_ref[cluster, :, part]
                later = later_ref[cluster, :, part]
                solution_ref[field, here, :] = one * right - two * first
                residual_ref[field, here, :] = (right - one * first) + two * later

    vector = pl.BlockSpec((fields, each * width, orbitals), lambda i: (0, i, 0))
    shape = jax.ShapeDtypeStruct(right_side.shape, jnp.float32)
    return pl.pallas_call(
        kernel,
        grid=(blocks,),
        out_shape=[shape, shape],
        in_specs=[vmem()] * 4,
        out_specs=[vector, vector],
        scratch_shapes=[pltpu.VMEM((8, lanes), jnp.float32)],
        compiler_params=pltpu.CompilerParams(vmem_limit_bytes=12 * MIB),
        name="final",
    )(right_side, image, later, gathered)


def body(right_side, onsite, energies, ks_tiles, correlation_tiles, tile_slot, readers):
    span, served = readers.shape[1:]
    clusters, _, width, _ = ks_tiles.shape
    rows = lax.axis_size("row")
    devices = rows * lax.axis_size("col")
    onsite = onsite.reshape(-1, width)
    energies = energies.reshape(1, -1)
    plan = Plan(rows, span, rows == 8 and span == 7)

    def partial(items):
        sums = []
        for group in (items[:1], items[1:3], items[3:-2]):
            sums = couple(dense, Vectors(plan, group), energies, sums)
        return dense, Vectors(plan, items[-2:]), energies, sums

    direct, own, full = pack(plan, readers, right_side, onsite)
    items, chosen = exchange(plan, direct, own, full, None, served, width)
    level = levels(onsite)
    dense = spread(tile_slot, ks_tiles, correlation_tiles, span, served)
    image, weighted, lines, direct, out, full = finish_first(
        plan, *partial(items), right_side, level, own, readers
    )
    items, _ = exchange(plan, direct, out, full, chosen, served, width)
    later, gathered = finish_second(
        *partial(items), right_side, level, image, weighted, lines, devices
    )
    gathered = lax.all_to_all(gathered, ("row", "col"), 0, 0)
    return tuple(final(right_side, image, later, gathered))


def solution(mesh):
    placed = (
        P(None, "row", "col"),
        P("row"),
        P("col"),
        P("row", None, None, None),
        P("row", None, None, None),
        P("row", None),
        P("row", None, None),
    )
    return jax.shard_map(
        body,
        mesh=mesh,
        in_specs=placed,
        out_specs=(P(None, "row", "col"), P(None, "row", "col")),
        check_vma=False,
    )
```

```python
import functools

import jax
import jax.numpy as jnp
from jax import lax
from jax.experimental import pallas as pl
from jax.experimental.pallas import tpu as pltpu
from jax.sharding import PartitionSpec as P

MIB = 2**20
EXTRA = 16
BATCH = 2


def shifted(array, axis, by):
    count = lax.axis_size(axis)
    return lax.ppermute(array, axis, [(i, (i + by) % count) for i in range(count)])


def vmem():
    return pl.BlockSpec(memory_space=pltpu.VMEM)


def smem():
    return pl.BlockSpec(memory_space=pltpu.SMEM)


def call(kernel, name, out_shape, specs, scratch=(), flops=0, moved=MIB, limit=12):
    return pl.pallas_call(
        kernel,
        out_shape=out_shape,
        in_specs=specs,
        out_specs=jax.tree.map(lambda _: vmem(), out_shape),
        scratch_shapes=list(scratch),
        compiler_params=pltpu.CompilerParams(vmem_limit_bytes=limit * MIB),
        cost_estimate=pl.CostEstimate(flops=flops, bytes_accessed=moved, transcendentals=0),
        name=name,
    )


def wide(parts):
    return jnp.concatenate(parts, axis=1)


def folded(term):
    return jnp.sum(term.reshape(-1, 8, term.shape[-1]), axis=0)


def lined(parts, lines):
    parts = [jnp.sum(p, axis=0, keepdims=True) for p in parts]
    parts.append(jnp.zeros((lines - len(parts), parts[0].shape[1]), jnp.float32))
    return jnp.concatenate(parts, axis=0)


def per_field(values, orbitals):
    return wide([jnp.broadcast_to(v, (1, orbitals)) for v in values])


def field_sums(lines, fields):
    orbitals = lines.shape[1] // fields
    return [
        jnp.sum(lines[:, f * orbitals : (f + 1) * orbitals], axis=1, keepdims=True)
        for f in range(fields)
    ]


class Plan:
    def __init__(self, count, span, relayed):
        self.count, self.span, self.middle, self.relayed = count, span, (span - 1) // 2, relayed

    def offset(self, source, reader):
        value = lax.rem(source - reader + (self.middle + self.count), self.count)
        return jnp.minimum(value, self.span - 1) if self.relayed else value

    def direct(self):
        if self.relayed:
            return [1, 2, 3, 7]
        far = range(self.middle, 0, -1)
        return [by for f in far for by in (f, -f)]

    def reader(self, key, me):
        return me ^ key if self.relayed else lax.rem(me + key + self.count, self.count)

    def source(self, key, me):
        return me ^ key if self.relayed else lax.rem(me - key + self.count, self.count)

    def pairs(self, key):
        if not self.relayed:
            return [(i, (i + key) % self.count) for i in range(self.count)]
        return [(i, i ^ key) for i in range(self.count) if key < 4 or i not in INNER]


INNER = (2, 3, 4, 5)


def is_inner(me):
    return (me >= INNER[0]) & (me <= INNER[-1])


def pack(plan, readers, right_side, onsite):
    fields, rows, orbitals = right_side.shape
    served = readers.shape[1]
    clusters, width = onsite.shape
    lanes = fields * orbitals
    keys = plan.direct()

    def kernel(readers_hbm, right_hbm, onsite_hbm, *refs):
        messages, rounded = refs[: len(keys) + 1], refs[len(keys) + 1]
        readers_ref, right_ref, onsite_ref, sems, more = refs[len(keys) + 2 :]
        copies = []
        for cluster in range(clusters):
            here = pl.ds(cluster * width, width)
            copies.append(
                pltpu.make_async_copy(
                    right_hbm.at[:, here, :], right_ref.at[:, here, :], sems.at[cluster]
                )
            )
        others = [
            pltpu.make_async_copy(onsite_hbm, onsite_ref, more.at[0]),
            pltpu.make_async_copy(readers_hbm, readers_ref, more.at[1]),
        ]
        for copy in copies[:1] + others + copies[1:]:
            copy.start()
        others[0].wait()
        norm = [jnp.zeros((8, orbitals), jnp.float32)] * fields
        heavy = [jnp.zeros((8, orbitals), jnp.float32)] * fields
        for cluster in range(clusters):
            copies[cluster].wait()
            weight = jnp.broadcast_to(onsite_ref[cluster : cluster + 1, :], (8, width))
            here = slice(cluster * width, (cluster + 1) * width)
            for field in range(fields):
                right = right_ref[field, here, :]
                rounded[here, field * orbitals : (field + 1) * orbitals] = right.astype(jnp.bfloat16)
                square = right * right
                norm[field] += folded(square)
                heavy[field] += jnp.dot(weight, square, preferred_element_type=jnp.float32)
        centers = [
            jnp.sum(h[:1], axis=1, keepdims=True)
            / jnp.maximum(jnp.sum(jnp.sum(n, axis=0, keepdims=True), axis=1, keepdims=True), 1e-30)
            for h, n in zip(heavy, norm)
        ]
        others[1].wait()
        rest = jnp.broadcast_to(per_field(centers, orbitals), (EXTRA, lanes))
        line, lane = (lax.broadcasted_iota(jnp.int32, (EXTRA, lanes), d) for d in (0, 1))
        for offset in range(readers_ref.shape[2]):
            for slot in range(served):
                here = (line == offset + 1) & (lane == slot)
                rest = jnp.where(here, readers_ref[0, slot, offset].astype(jnp.float32), rest)
        rounded[clusters * width :, :] = rest.astype(jnp.bfloat16)
        fill(plan, keys, readers_ref, rounded, messages, width)

    message = jax.ShapeDtypeStruct((served * width + EXTRA, lanes), jnp.bfloat16)
    full = jax.ShapeDtypeStruct((clusters * width + EXTRA, lanes), jnp.bfloat16)
    *messages, own, full = call(
        kernel,
        "pack",
        [message] * (len(keys) + 1) + [full],
        [pl.BlockSpec(memory_space=pltpu.HBM)] * 3,
        [
            pltpu.SMEM(readers.shape, readers.dtype),
            pltpu.VMEM(right_side.shape, jnp.float32),
            pltpu.VMEM(onsite.shape, jnp.float32),
            pltpu.SemaphoreType.DMA((clusters,)),
            pltpu.SemaphoreType.DMA((2,)),
        ],
        limit=51,
    )(readers, right_side, onsite)
    return dict(zip(keys, messages)), own, full


def deal(plan, readers, full, served, width):
    keys = plan.direct()

    def kernel(readers_ref, full_ref, *messages):
        fill(plan, keys, readers_ref, full_ref, messages, width)

    message = jax.ShapeDtypeStruct((served * width, full.shape[1]), jnp.bfloat16)
    *messages, own = call(kernel, "deal", [message] * (len(keys) + 1), [smem(), vmem()])(
        readers, full
    )
    return dict(zip(keys, messages)), own


def fill(plan, keys, readers_ref, rounded, messages, width):
    me = lax.axis_index("row")
    offsets = [plan.offset(me, plan.reader(key, me)) for key in keys] + [plan.middle]
    for offset, message in zip(offsets, messages):
        served = readers_ref.shape[1]
        gather([readers_ref[0, slot, offset] for slot in range(served)], rounded, message, width)


def gather(clusters, rounded, message, width):
    for slot, cluster in enumerate(clusters):
        start = pl.multiple_of(cluster * width, width)
        message[slot * width : (slot + 1) * width, :] = rounded[pl.ds(start, width), :]
    used = len(clusters) * width
    if message.shape[0] > used:
        message[used:, :] = rounded[rounded.shape[0] - EXTRA :, :]


def relay(plan, readers, mine, full, chosen, after, served, width):
    lanes = full.shape[1]
    extra = EXTRA if chosen is None else 0
    message = jax.ShapeDtypeStruct((served * width + extra, lanes), jnp.bfloat16)

    def kernel(*refs):
        readers_ref, mine_ref, full_ref, given_ref, *messages = refs[:7]
        me = lax.axis_index("row")
        chosen_ref = given_ref if chosen is not None else refs[7]
        if chosen is None:
            base = full_ref.shape[0] - EXTRA
            table = full_ref[base : base + EXTRA, 0:width].astype(jnp.float32)
            line, lane = (lax.broadcasted_iota(jnp.int32, table.shape, d) for d in (0, 1))
            for index, reader in enumerate((me, me ^ 1, me ^ 3)):
                offset = plan.offset(me ^ 6, reader)
                for slot in range(served):
                    here = (line == offset + 1) & (lane == slot)
                    chosen_ref[index, slot] = jnp.sum(jnp.where(here, table, 0.0)).astype(jnp.int32)

        @pl.when(is_inner(me))
        def _():
            for index, out in enumerate(messages):
                gather([chosen_ref[index, slot] for slot in range(served)], full_ref, out, width)

        @pl.when(jnp.logical_not(is_inner(me)))
        def _():
            for key, out in zip((6, 5), messages[1:]):
                offset = plan.offset(me, me ^ key)
                clusters = [readers_ref[0, slot, offset] for slot in range(served)]
                gather(clusters, mine_ref, out, width)

    inputs = [readers, mine, full, after if chosen is None else chosen]
    specs = [smem(), vmem(), vmem(), pl.BlockSpec(memory_space=pl.ANY) if chosen is None else smem()]
    shapes, outs = [message] * 3, [vmem()] * 3
    if chosen is None:
        shapes.append(jax.ShapeDtypeStruct((3, served), jnp.int32))
        outs.append(smem())
    *messages, last = pl.pallas_call(
        kernel,
        out_shape=shapes,
        in_specs=specs,
        out_specs=outs,
        compiler_params=pltpu.CompilerParams(vmem_limit_bytes=12 * MIB),
        cost_estimate=pl.CostEstimate(flops=0, bytes_accessed=MIB, transcendentals=0),
        name="relay",
    )(*inputs)
    return (messages, last) if chosen is None else (messages + [last], chosen)


def exchange(plan, readers, direct, own, full, chosen, after, served, width):
    sent = {k: lax.ppermute(m, "row", plan.pairs(k)) for k, m in direct.items()}
    if not plan.relayed:
        return [(own, 0)] + [(sent[k], k) for k in plan.direct()], None
    theirs = lax.ppermute(full, "row", [(i, i ^ 6) for i in INNER])
    (mine, near, far), chosen = relay(plan, readers, full, theirs, chosen, after, served, width)
    near = lax.ppermute(near, "row", [(i, i ^ (1 if i in INNER else 6)) for i in range(plan.count)])
    far = lax.ppermute(far, "row", [(i, i ^ (3 if i in INNER else 5)) for i in range(plan.count)])
    items = [
        (own, 0),
        (sent[1], 1),
        (sent[2], 2),
        (sent[3], 3),
        ((mine, sent[7]), (6, 7)),
        (near, (7, 6)),
        (far, 5),
    ]
    return items, chosen


class Vectors:
    def __init__(self, plan, items):
        self.plan, self.items = plan, items
        self.arrays, self.scratch = [], []
        for value, _ in items:
            many = isinstance(value, tuple)
            self.arrays += list(value) if many else [value]
            if many:
                self.scratch.append(pltpu.VMEM(value[0].shape, value[0].dtype))
        self.lanes = self.arrays[0].shape[1]
        self.rows = self.arrays[0].shape[0]

    def open(self, refs, scratch):
        refs, scratch = list(refs), list(scratch)
        me = lax.axis_index("row")
        opened = []
        for value, key in self.items:
            if not self.plan.relayed:
                opened.append((self.plan.middle - key, refs.pop(0)))
                continue
            inner, outer = key if isinstance(key, tuple) else (key, key)
            held = refs.pop(0)
            if isinstance(value, tuple):
                kept, held, other = held, scratch.pop(0), refs.pop(0)

                @pl.when(is_inner(me))
                def _():
                    held[...] = kept[...]

                @pl.when(jnp.logical_not(is_inner(me)))
                def _():
                    held[...] = other[...]

            source = jnp.where(is_inner(me), me ^ inner, me ^ outer)
            opened.append((self.plan.offset(source, me), held))
        return opened


def levels(onsite):
    clusters, width = onsite.shape

    def kernel(onsite_ref, level_ref):
        for cluster in range(clusters):
            level_ref[cluster] = jnp.transpose(
                jnp.broadcast_to(onsite_ref[cluster : cluster + 1, :], (width, width))
            )

    shape = jax.ShapeDtypeStruct((clusters, width, width), jnp.float32)
    return call(kernel, "levels", shape, [vmem()])(onsite)


def spread(tile_slot, ks_tiles, correlation_tiles, span, served):
    clusters, _, width, _ = ks_tiles.shape
    slots = span * served

    def kernel(slot_ref, ks_ref, correlation_ref, out_ref, where):
        @pl.loop(0, clusters)
        def _(cluster):
            for kind, ref in enumerate((ks_ref, correlation_ref)):
                count = ref.shape[1]
                for slot in range(slots):
                    where[slot] = count
                for tile in range(count):
                    where[slot_ref[cluster, tile]] = tile
                for slot in range(slots):
                    tile = where[slot]
                    block = ref[cluster, jnp.minimum(tile, count - 1)]
                    block = jnp.where(tile < count, block, jnp.zeros_like(block))
                    lane = slot % served * width
                    out_ref[
                        slot // served, cluster, kind * width : (kind + 1) * width, lane : lane + width
                    ] = block

    return call(
        kernel,
        "spread",
        jax.ShapeDtypeStruct((span, clusters, 2 * width, served * width), jnp.bfloat16),
        [smem(), vmem(), vmem()],
        [pltpu.SMEM((slots,), jnp.int32)],
        moved=16 * MIB,
    )(tile_slot, ks_tiles, correlation_tiles)


def products(dense_ref, opened, clusters, energy):
    depth = dense_ref.shape[-1]
    for offset, vector in opened:
        left = dense_ref[offset, clusters]
        count, height, _ = left.shape
        value = jnp.dot(
            left.reshape(count * height, depth), vector[0:depth, :], preferred_element_type=jnp.float32
        )
        value = value.reshape(count, 2, height // 2, value.shape[1])
        yield value[:, 0] - energy * value[:, 1]


def centers(opened, depth):
    return [vector[depth : depth + EXTRA, :].astype(jnp.float32)[:1] for _, vector in opened]


def work(dense, items, lanes):
    return 2 * len(items) * dense.shape[1] * dense.shape[2] * dense.shape[3] * lanes


def couple(dense, vectors, energies, sums, after=None):
    _, clusters, height, depth = dense.shape
    lanes = vectors.lanes
    count = len(vectors.arrays)
    outs = 2 if vectors.rows > depth else 1
    had = len(sums)

    def kernel(dense_ref, energies_ref, *refs):
        refs = list(refs[1:] if after is not None else refs)
        vector_refs, sum_refs = refs[:count], refs[count : count + had]
        out_refs, scratch = refs[count + had : count + had + outs], refs[count + had + outs :]
        energy = wide([energies_ref[...]] * (lanes // energies_ref.shape[1]))
        opened = vectors.open(vector_refs, scratch)
        weights = centers(opened, depth) if outs == 2 else [None] * len(opened)

        @pl.loop(0, clusters // BATCH)
        def _(batch):
            here = pl.ds(batch * BATCH, BATCH)
            values = [ref[here] for ref in sum_refs]
            for weight, part in zip(weights, products(dense_ref, opened, here, energy)):
                terms = [part] if weight is None else [part, weight * part]
                values = [v + t for v, t in zip(values, terms)] if values else terms
            for ref, value in zip(out_refs, values):
                ref[here] = value

    order = [] if after is None else [after]
    inputs = [dense, energies, *order, *vectors.arrays, *sums]
    shape = jax.ShapeDtypeStruct((clusters, height // 2, lanes), jnp.float32)
    return call(
        kernel,
        "couple",
        [shape] * outs,
        [vmem()] * 2
        + [pl.BlockSpec(memory_space=pl.ANY)] * len(order)
        + [vmem()] * (len(vectors.arrays) + had),
        vectors.scratch,
        flops=work(dense, vectors.items, lanes),
        moved=4 * MIB,
    )(*inputs)


def finish_first(dense, vectors, energies, value_sum, right_side, level, own):
    _, clusters, height, depth = dense.shape
    lanes = vectors.lanes
    fields = right_side.shape[0]
    width = height // 2
    count = len(vectors.arrays)

    def kernel(dense_ref, energies_ref, *refs):
        vector_refs, refs = refs[:count], refs[count:]
        sum_ref, right_ref, level_ref, own_ref, image_ref, outgoing, *scratch = refs
        energy = wide([energies_ref[...]] * fields)
        opened = vectors.open(vector_refs, scratch)
        (center,) = centers([(0, own_ref)], depth)

        @pl.loop(0, clusters // BATCH)
        def _(batch):
            here = pl.ds(batch * BATCH, BATCH)
            value = sum_ref[here]
            for part in products(dense_ref, opened, here, energy):
                value = value + part
            for local in range(BATCH):
                cluster = batch * BATCH + local
                rows = pl.ds(pl.multiple_of(cluster * width, width), width)
                right = wide([right_ref[f, rows, :] for f in range(fields)])
                image = wide([level_ref[cluster]] * fields) * right + value[local]
                image_ref[cluster] = image
                outgoing[rows, :] = (image - center * right).astype(jnp.bfloat16)

    return call(
        kernel,
        "finish_first",
        [
            jax.ShapeDtypeStruct((clusters, width, lanes), jnp.float32),
            jax.ShapeDtypeStruct((clusters * width, lanes), jnp.bfloat16),
        ],
        [vmem()] * (2 + count + 4),
        vectors.scratch,
        flops=work(dense, vectors.items, lanes),
        moved=8 * MIB,
    )(dense, energies, *vectors.arrays, value_sum, right_side, level, own)


def guesses(lines, fields):
    orbitals = lines.shape[1] // fields
    alphas, growths = [], []
    for column in field_sums(lines, fields):
        norm, bend, square = column[0:1], column[1:2], column[2:3]
        norm = jnp.maximum(norm, 1e-30)
        alpha = norm / jnp.maximum(bend, 4.0 * norm)
        alphas.append(alpha)
        growths.append(jnp.clip(alpha * alpha * square / norm, 1.0, 2.0))
    return per_field(alphas, orbitals), per_field(growths, orbitals)


def prepare(right_side, image, after):
    fields, rows, orbitals = right_side.shape
    clusters, width, lanes = image.shape

    def kernel(right_ref, image_ref, _, lines_ref, kept):
        kept[...] = jnp.zeros_like(kept)

        def sweep(base, terms):
            @pl.loop(0, clusters)
            def _(cluster):
                here = pl.ds(pl.multiple_of(cluster * width, width), width)
                right = wide([right_ref[f, here, :] for f in range(fields)])
                for index, term in enumerate(terms(right, image_ref[cluster])):
                    kept[base + index] += folded(term)

        sweep(0, lambda right, first: (right * right, right * first, first * first))
        alpha, growth = guesses(lined([kept[i] for i in range(3)], 8), fields)

        def later_terms(right, first):
            step = alpha * first
            residual = right - step
            return residual * residual, residual * first, (growth * right - step) * first

        sweep(3, later_terms)
        lines_ref[...] = lined([kept[i] for i in range(6)], 8)
        lines_ref[6:7, :] = alpha
        lines_ref[7:8, :] = growth

    return call(
        kernel,
        "prepare",
        jax.ShapeDtypeStruct((8, lanes), jnp.float32),
        [vmem(), vmem(), pl.BlockSpec(memory_space=pl.ANY)],
        [pltpu.VMEM((6, 8, lanes), jnp.float32)],
        flops=8 * MIB,
        moved=4 * MIB,
    )(right_side, image, after)


def finish_second(dense, vectors, energies, value_sum, right_side, level, image, weighted, lines, devices):
    _, clusters, height, _ = dense.shape
    lanes = vectors.lanes
    fields = right_side.shape[0]
    width = height // 2
    count = len(vectors.arrays)

    def kernel(dense_ref, energies_ref, *refs):
        vector_refs, refs = refs[:count], refs[count:]
        sum_ref, right_ref, level_ref, image_ref, weighted_ref, lines_ref = refs[:6]
        later_ref, out_ref, kept, *scratch = refs[6:]
        energy = wide([energies_ref[...]] * fields)
        alpha, growth = lines_ref[6:7, :], lines_ref[7:8, :]
        kept[...] = jnp.zeros_like(kept)
        opened = vectors.open(vector_refs, scratch)

        @pl.loop(0, clusters // BATCH)
        def _(batch):
            here = pl.ds(batch * BATCH, BATCH)
            value = sum_ref[here] + weighted_ref[here]
            for part in products(dense_ref, opened, here, energy):
                value = value + part
            for local in range(BATCH):
                cluster = batch * BATCH + local
                rows = pl.ds(pl.multiple_of(cluster * width, width), width)
                right = wide([right_ref[f, rows, :] for f in range(fields)])
                first = image_ref[cluster]
                later = wide([level_ref[cluster]] * fields) * first + value[local]
                later_ref[cluster] = later
                direction = growth * right - alpha * first
                for index, left in enumerate((direction, right, first)):
                    kept[index] += folded(left * later)

        block = jnp.concatenate([lines_ref[0:6, :], lined([kept[i] for i in range(3)], 10)], axis=0)
        orbitals = lanes // fields
        line, lane = (lax.broadcasted_iota(jnp.int32, (16, 128), d) for d in (0, 1))
        rows = []
        for f, column in enumerate(field_sums(block, fields)):
            first_lane = slice(f * orbitals, f * orbitals + 1)
            filled = jnp.broadcast_to(column, (16, 128))
            filled = jnp.where(line == 9, jnp.broadcast_to(alpha[:, first_lane], (16, 128)), filled)
            filled = jnp.where(line == 10, jnp.broadcast_to(growth[:, first_lane], (16, 128)), filled)
            rows.append(jnp.sum(jnp.where(line == lane, filled, 0.0), axis=0, keepdims=True))
        rows.append(jnp.zeros((8 - fields, 128), jnp.float32))
        out_ref[...] = jnp.broadcast_to(jnp.concatenate(rows, axis=0)[None], out_ref.shape)

    return call(
        kernel,
        "finish_second",
        [
            jax.ShapeDtypeStruct((clusters, width, lanes), jnp.float32),
            jax.ShapeDtypeStruct((devices, 8, 128), jnp.float32),
        ],
        [vmem()] * (2 + count + 6),
        [pltpu.VMEM((3, 8, lanes), jnp.float32)] + vectors.scratch,
        flops=work(dense, vectors.items, lanes),
        moved=8 * MIB,
    )(dense, energies, *vectors.arrays, value_sum, right_side, level, image, weighted, lines)


def step_sizes(gathered, fields, orbitals):
    rows = gathered.reshape(-1, 128)
    flat = wide([jnp.transpose(rows[i : i + 128]) for i in range(0, rows.shape[0], 128)])
    line = [flat[i : i + 1, :] for i in range(11)]
    place = lax.broadcasted_iota(jnp.int32, line[0].shape, 1) & 7
    whole = lambda v: [
        jnp.sum(jnp.where(place == f, v, 0.0), axis=1, keepdims=True) for f in range(fields)
    ]

    def back(values):
        row = jnp.zeros_like(line[0])
        for f, value in enumerate(values):
            row = jnp.where(place == f, jnp.broadcast_to(value, row.shape), row)
        return row

    norm = whole(line[0])
    alpha = [n / b for n, b in zip(norm, whole(line[1]))]
    growth = [a * a * s / n for a, s, n in zip(alpha, whole(line[2]), norm)]
    off, more = back(alpha) - line[9], back(growth) - line[10]
    after = whole(line[3] - 2.0 * off * line[4] + off * off * line[2])
    bend = whole(
        (line[10] * line[5] - line[9] * line[6])
        + more * (line[5] + line[10] * line[1] - line[9] * line[7])
        - off * (line[6] + line[10] * line[2] - line[9] * line[8])
        + more * more * line[1]
        - more * off * (line[7] + line[2])
        + off * off * line[8]
    )
    gain = [a / b for a, b in zip(after, bend)]
    return [per_field(v, orbitals) for v in (alpha, growth, gain)]


def final(right_side, image, later, gathered):
    fields, rows, orbitals = right_side.shape
    clusters, width, lanes = image.shape
    blocks = 8
    each = clusters // blocks

    def kernel(right_ref, image_ref, later_ref, gathered_ref, solution_ref, residual_ref, steps):
        step = pl.program_id(0)

        @pl.when(step == 0)
        def _():
            alpha, growth, gain = step_sizes(gathered_ref[...], fields, orbitals)
            steps[0:1, :] = alpha + gain * growth
            steps[1:2, :] = gain * alpha

        for local in range(each):
            cluster = step * each + local
            rows = pl.ds(pl.multiple_of(cluster * width, width), width)
            here = slice(local * width, (local + 1) * width)
            for field in range(fields):
                part = slice(field * orbitals, (field + 1) * orbitals)
                one, two = steps[0:1, part], steps[1:2, part]
                right = right_ref[field, rows, :]
                first = image_ref[cluster, :, part]
                later = later_ref[cluster, :, part]
                solution_ref[field, here, :] = one * right - two * first
                residual_ref[field, here, :] = (right - one * first) + two * later

    vector = pl.BlockSpec((fields, each * width, orbitals), lambda i: (0, i, 0))
    shape = jax.ShapeDtypeStruct(right_side.shape, jnp.float32)
    return pl.pallas_call(
        kernel,
        grid=(blocks,),
        out_shape=[shape, shape],
        in_specs=[vmem()] * 4,
        out_specs=[vector, vector],
        scratch_shapes=[pltpu.VMEM((8, lanes), jnp.float32)],
        compiler_params=pltpu.CompilerParams(vmem_limit_bytes=12 * MIB),
        name="final",
    )(right_side, image, later, gathered)


def body(right_side, onsite, energies, ks_tiles, correlation_tiles, tile_slot, readers):
    span, served = readers.shape[1:]
    clusters, _, width, _ = ks_tiles.shape
    rows = lax.axis_size("row")
    devices = rows * lax.axis_size("col")
    onsite = onsite.reshape(-1, width)
    energies = energies.reshape(1, -1)
    plan = Plan(rows, span, rows == 8 and span == 7)
    readers = jnp.swapaxes(readers, 1, 2)

    def partial(items):
        sums = [[]]
        for group in (items[:3], items[3:-2], items[-2:-1]):
            sums.append(couple(dense, Vectors(plan, group), energies, sums[-1]))
        return sums[-1], sums[1][0]

    direct, own, full = pack(plan, readers, right_side, onsite)
    dense = spread(tile_slot, ks_tiles, correlation_tiles, span, served)
    items, chosen = exchange(plan, readers, direct, own, full, None, dense, served, width)
    level = levels(onsite)
    sums, _ = partial(items)
    last = Vectors(plan, items[-1:])
    image, full = finish_first(dense, last, energies, sums[0], right_side, level, own)

    direct, out = deal(plan, readers, full, served, width)
    items, _ = exchange(plan, readers, direct, out, full, chosen, None, served, width)
    (value,), begun = partial(items)
    lines = prepare(right_side, image, begun)
    _, weighted = couple(dense, last, energies, sums, begun)
    last = Vectors(plan, items[-1:])
    later, gathered = finish_second(
        dense, last, energies, value, right_side, level, image, weighted, lines, devices
    )
    gathered = lax.all_to_all(gathered, ("row", "col"), 0, 0)
    return tuple(final(right_side, image, later, gathered))


def solution(mesh):
    placed = (
        P(None, "row", "col"),
        P("row"),
        P("col"),
        P("row", None, None, None),
        P("row", None, None, None),
        P("row", None),
        P("row", None, None),
    )
    return jax.shard_map(
        body,
        mesh=mesh,
        in_specs=placed,
        out_specs=(P(None, "row", "col"), P(None, "row", "col")),
        check_vma=False,
    )
```

```python
import functools

import jax
import jax.numpy as jnp
from jax import lax
from jax.experimental import pallas as pl
from jax.experimental.pallas import tpu as pltpu
from jax.sharding import PartitionSpec as P

MIB = 2**20
EXTRA = 16
BATCH = 2


def shifted(array, axis, by):
    count = lax.axis_size(axis)
    return lax.ppermute(array, axis, [(i, (i + by) % count) for i in range(count)])


def vmem():
    return pl.BlockSpec(memory_space=pltpu.VMEM)


def smem():
    return pl.BlockSpec(memory_space=pltpu.SMEM)


def call(kernel, name, out_shape, specs, scratch=(), flops=0, moved=MIB, limit=12):
    return pl.pallas_call(
        kernel,
        out_shape=out_shape,
        in_specs=specs,
        out_specs=jax.tree.map(lambda _: vmem(), out_shape),
        scratch_shapes=list(scratch),
        compiler_params=pltpu.CompilerParams(vmem_limit_bytes=limit * MIB),
        cost_estimate=pl.CostEstimate(flops=flops, bytes_accessed=moved, transcendentals=0),
        name=name,
    )


def wide(parts):
    return jnp.concatenate(parts, axis=1)


def folded(term):
    return jnp.sum(term.reshape(-1, 8, term.shape[-1]), axis=0)


def lined(parts, lines):
    parts = [jnp.sum(p, axis=0, keepdims=True) for p in parts]
    parts.append(jnp.zeros((lines - len(parts), parts[0].shape[1]), jnp.float32))
    return jnp.concatenate(parts, axis=0)


def per_field(values, orbitals):
    return wide([jnp.broadcast_to(v, (1, orbitals)) for v in values])


def field_sums(lines, fields):
    orbitals = lines.shape[1] // fields
    return [
        jnp.sum(lines[:, f * orbitals : (f + 1) * orbitals], axis=1, keepdims=True)
        for f in range(fields)
    ]


class Plan:
    def __init__(self, count, span, relayed):
        self.count, self.span, self.middle, self.relayed = count, span, (span - 1) // 2, relayed

    def offset(self, source, reader):
        value = lax.rem(source - reader + (self.middle + self.count), self.count)
        return jnp.minimum(value, self.span - 1) if self.relayed else value

    def direct(self):
        if self.relayed:
            return [1, 2, 3, 7]
        far = range(self.middle, 0, -1)
        return [by for f in far for by in (f, -f)]

    def reader(self, key, me):
        return me ^ key if self.relayed else lax.rem(me + key + self.count, self.count)

    def source(self, key, me):
        return me ^ key if self.relayed else lax.rem(me - key + self.count, self.count)

    def pairs(self, key):
        if not self.relayed:
            return [(i, (i + key) % self.count) for i in range(self.count)]
        return [(i, i ^ key) for i in range(self.count) if key < 4 or i not in INNER]


INNER = (2, 3, 4, 5)


def is_inner(me):
    return (me >= INNER[0]) & (me <= INNER[-1])


def pack(plan, readers, right_side, onsite):
    fields, rows, orbitals = right_side.shape
    served = readers.shape[1]
    clusters, width = onsite.shape
    lanes = fields * orbitals
    keys = plan.direct()

    def kernel(readers_hbm, right_hbm, onsite_hbm, *refs):
        messages, rounded = refs[: len(keys) + 1], refs[len(keys) + 1]
        readers_ref, right_ref, onsite_ref, sems, more = refs[len(keys) + 2 :]
        copies = []
        for cluster in range(clusters):
            here = pl.ds(cluster * width, width)
            copies.append(
                pltpu.make_async_copy(
                    right_hbm.at[:, here, :], right_ref.at[:, here, :], sems.at[cluster]
                )
            )
        others = [
            pltpu.make_async_copy(onsite_hbm, onsite_ref, more.at[0]),
            pltpu.make_async_copy(readers_hbm, readers_ref, more.at[1]),
        ]
        for copy in copies[:1] + others + copies[1:]:
            copy.start()
        others[0].wait()
        norm = [jnp.zeros((8, orbitals), jnp.float32)] * fields
        heavy = [jnp.zeros((8, orbitals), jnp.float32)] * fields
        for cluster in range(clusters):
            copies[cluster].wait()
            weight = jnp.broadcast_to(onsite_ref[cluster : cluster + 1, :], (8, width))
            here = slice(cluster * width, (cluster + 1) * width)
            for field in range(fields):
                right = right_ref[field, here, :]
                rounded[here, field * orbitals : (field + 1) * orbitals] = right.astype(jnp.bfloat16)
                square = right * right
                norm[field] += folded(square)
                heavy[field] += jnp.dot(weight, square, preferred_element_type=jnp.float32)
        centers = [
            jnp.sum(h[:1], axis=1, keepdims=True)
            / jnp.maximum(jnp.sum(jnp.sum(n, axis=0, keepdims=True), axis=1, keepdims=True), 1e-30)
            for h, n in zip(heavy, norm)
        ]
        others[1].wait()
        rest = jnp.broadcast_to(per_field(centers, orbitals), (EXTRA, lanes))
        line, lane = (lax.broadcasted_iota(jnp.int32, (EXTRA, lanes), d) for d in (0, 1))
        for offset in range(readers_ref.shape[2]):
            for slot in range(served):
                here = (line == offset + 1) & (lane == slot)
                rest = jnp.where(here, readers_ref[0, slot, offset].astype(jnp.float32), rest)
        rounded[clusters * width :, :] = rest.astype(jnp.bfloat16)
        fill(plan, keys, readers_ref, rounded, messages, width)

    message = jax.ShapeDtypeStruct((served * width + EXTRA, lanes), jnp.bfloat16)
    full = jax.ShapeDtypeStruct((clusters * width + EXTRA, lanes), jnp.bfloat16)
    *messages, own, full = call(
        kernel,
        "pack",
        [message] * (len(keys) + 1) + [full],
        [pl.BlockSpec(memory_space=pltpu.HBM)] * 3,
        [
            pltpu.SMEM(readers.shape, readers.dtype),
            pltpu.VMEM(right_side.shape, jnp.float32),
            pltpu.VMEM(onsite.shape, jnp.float32),
            pltpu.SemaphoreType.DMA((clusters,)),
            pltpu.SemaphoreType.DMA((2,)),
        ],
        limit=51,
    )(readers, right_side, onsite)
    return dict(zip(keys, messages)), own, full


def fill(plan, keys, readers_ref, rounded, messages, width):
    me = lax.axis_index("row")
    offsets = [plan.offset(me, plan.reader(key, me)) for key in keys] + [plan.middle]
    for offset, message in zip(offsets, messages):
        served = readers_ref.shape[1]
        gather([readers_ref[0, slot, offset] for slot in range(served)], rounded, message, width)


def gather(clusters, rounded, message, width):
    for slot, cluster in enumerate(clusters):
        start = pl.multiple_of(cluster * width, width)
        message[slot * width : (slot + 1) * width, :] = rounded[pl.ds(start, width), :]
    used = len(clusters) * width
    if message.shape[0] > used:
        message[used:, :] = rounded[rounded.shape[0] - EXTRA :, :]


def relay(plan, readers, mine, full, chosen, after, served, width):
    lanes = full.shape[1]
    extra = EXTRA if chosen is None else 0
    message = jax.ShapeDtypeStruct((served * width + extra, lanes), jnp.bfloat16)

    def kernel(*refs):
        readers_ref, mine_ref, full_ref, given_ref, *messages = refs[:7]
        me = lax.axis_index("row")
        chosen_ref = given_ref if chosen is not None else refs[7]
        if chosen is None:
            base = full_ref.shape[0] - EXTRA
            table = full_ref[base : base + EXTRA, 0:width].astype(jnp.float32)
            line, lane = (lax.broadcasted_iota(jnp.int32, table.shape, d) for d in (0, 1))
            for index, reader in enumerate((me, me ^ 1, me ^ 3)):
                offset = plan.offset(me ^ 6, reader)
                for slot in range(served):
                    here = (line == offset + 1) & (lane == slot)
                    chosen_ref[index, slot] = jnp.sum(jnp.where(here, table, 0.0)).astype(jnp.int32)

        @pl.when(is_inner(me))
        def _():
            for index, out in enumerate(messages):
                gather([chosen_ref[index, slot] for slot in range(served)], full_ref, out, width)

        @pl.when(jnp.logical_not(is_inner(me)))
        def _():
            for key, out in zip((6, 5), messages[1:]):
                offset = plan.offset(me, me ^ key)
                clusters = [readers_ref[0, slot, offset] for slot in range(served)]
                gather(clusters, mine_ref, out, width)

    inputs = [readers, mine, full, after if chosen is None else chosen]
    specs = [smem(), vmem(), vmem(), pl.BlockSpec(memory_space=pl.ANY) if chosen is None else smem()]
    shapes, outs = [message] * 3, [vmem()] * 3
    if chosen is None:
        shapes.append(jax.ShapeDtypeStruct((3, served), jnp.int32))
        outs.append(smem())
    *messages, last = pl.pallas_call(
        kernel,
        out_shape=shapes,
        in_specs=specs,
        out_specs=outs,
        compiler_params=pltpu.CompilerParams(vmem_limit_bytes=12 * MIB),
        cost_estimate=pl.CostEstimate(flops=0, bytes_accessed=MIB, transcendentals=0),
        name="relay",
    )(*inputs)
    return (messages, last) if chosen is None else (messages + [last], chosen)


def exchange(plan, readers, direct, own, full, chosen, after, served, width):
    sent = {k: lax.ppermute(m, "row", plan.pairs(k)) for k, m in direct.items()}
    if not plan.relayed:
        return [(own, 0)] + [(sent[k], k) for k in plan.direct()], None
    theirs = lax.ppermute(full, "row", [(i, i ^ 6) for i in INNER])
    (mine, near, far), chosen = relay(plan, readers, full, theirs, chosen, after, served, width)
    near = lax.ppermute(near, "row", [(i, i ^ (1 if i in INNER else 6)) for i in range(plan.count)])
    far = lax.ppermute(far, "row", [(i, i ^ (3 if i in INNER else 5)) for i in range(plan.count)])
    items = [
        (own, 0),
        ((mine, sent[7]), (6, 7)),
        (sent[1], 1),
        (sent[2], 2),
        (sent[3], 3),
        (far, 5),
        (near, (7, 6)),
    ]
    return items, chosen


class Vectors:
    def __init__(self, plan, items):
        self.plan, self.items = plan, items
        self.arrays, self.scratch = [], []
        for value, _ in items:
            many = isinstance(value, tuple)
            self.arrays += list(value) if many else [value]
            if many:
                self.scratch.append(pltpu.VMEM(value[0].shape, value[0].dtype))
        self.lanes = self.arrays[0].shape[1]
        self.rows = self.arrays[0].shape[0]

    def open(self, refs, scratch):
        refs, scratch = list(refs), list(scratch)
        me = lax.axis_index("row")
        opened = []
        for value, key in self.items:
            if not self.plan.relayed:
                opened.append((self.plan.middle - key, refs.pop(0)))
                continue
            inner, outer = key if isinstance(key, tuple) else (key, key)
            held = refs.pop(0)
            if isinstance(value, tuple):
                kept, held, other = held, scratch.pop(0), refs.pop(0)

                @pl.when(is_inner(me))
                def _():
                    held[...] = kept[...]

                @pl.when(jnp.logical_not(is_inner(me)))
                def _():
                    held[...] = other[...]

            source = jnp.where(is_inner(me), me ^ inner, me ^ outer)
            opened.append((self.plan.offset(source, me), held))
        return opened


def levels(onsite):
    clusters, width = onsite.shape

    def kernel(onsite_ref, level_ref):
        for cluster in range(clusters):
            level_ref[cluster] = jnp.transpose(
                jnp.broadcast_to(onsite_ref[cluster : cluster + 1, :], (width, width))
            )

    shape = jax.ShapeDtypeStruct((clusters, width, width), jnp.float32)
    return call(kernel, "levels", shape, [vmem()])(onsite)


def spread(tile_slot, ks_tiles, correlation_tiles, span, served):
    clusters, _, width, _ = ks_tiles.shape
    slots = span * served

    def kernel(slot_ref, ks_ref, correlation_ref, out_ref, where):
        @pl.loop(0, clusters)
        def _(cluster):
            for kind, ref in enumerate((ks_ref, correlation_ref)):
                count = ref.shape[1]
                for slot in range(slots):
                    where[slot] = count
                for tile in range(count):
                    where[slot_ref[cluster, tile]] = tile
                for slot in range(slots):
                    tile = where[slot]
                    block = ref[cluster, jnp.minimum(tile, count - 1)]
                    block = jnp.where(tile < count, block, jnp.zeros_like(block))
                    lane = slot % served * width
                    out_ref[
                        slot // served, cluster, kind * width : (kind + 1) * width, lane : lane + width
                    ] = block

    return call(
        kernel,
        "spread",
        jax.ShapeDtypeStruct((span, clusters, 2 * width, served * width), jnp.bfloat16),
        [smem(), vmem(), vmem()],
        [pltpu.SMEM((slots,), jnp.int32)],
        moved=16 * MIB,
    )(tile_slot, ks_tiles, correlation_tiles)


def products(dense_ref, opened, clusters, energy):
    depth = dense_ref.shape[-1]
    for offset, vector in opened:
        left = dense_ref[offset, clusters]
        count, height, _ = left.shape
        value = jnp.dot(
            left.reshape(count * height, depth), vector[0:depth, :], preferred_element_type=jnp.float32
        )
        value = value.reshape(count, 2, height // 2, value.shape[1])
        yield value[:, 0] - energy * value[:, 1]


def centers(opened, depth):
    return [vector[depth : depth + EXTRA, :].astype(jnp.float32)[:1] for _, vector in opened]


def work(dense, items, lanes):
    return 2 * len(items) * dense.shape[1] * dense.shape[2] * dense.shape[3] * lanes


def couple(dense, vectors, energies, sums, after=None):
    _, clusters, height, depth = dense.shape
    lanes = vectors.lanes
    count = len(vectors.arrays)
    outs = 2 if vectors.rows > depth else 1
    had = len(sums)

    def kernel(dense_ref, energies_ref, *refs):
        refs = list(refs[1:] if after is not None else refs)
        vector_refs, sum_refs = refs[:count], refs[count : count + had]
        out_refs, scratch = refs[count + had : count + had + outs], refs[count + had + outs :]
        energy = wide([energies_ref[...]] * (lanes // energies_ref.shape[1]))
        opened = vectors.open(vector_refs, scratch)
        weights = centers(opened, depth) if outs == 2 else [None] * len(opened)

        @pl.loop(0, clusters // BATCH)
        def _(batch):
            here = pl.ds(batch * BATCH, BATCH)
            values = [ref[here] for ref in sum_refs]
            for weight, part in zip(weights, products(dense_ref, opened, here, energy)):
                terms = [part] if weight is None else [part, weight * part]
                values = [v + t for v, t in zip(values, terms)] if values else terms
            for ref, value in zip(out_refs, values):
                ref[here] = value

    order = [] if after is None else [after]
    inputs = [dense, energies, *order, *vectors.arrays, *sums]
    shape = jax.ShapeDtypeStruct((clusters, height // 2, lanes), jnp.float32)
    return call(
        kernel,
        "couple",
        [shape] * outs,
        [vmem()] * 2
        + [pl.BlockSpec(memory_space=pl.ANY)] * len(order)
        + [vmem()] * (len(vectors.arrays) + had),
        vectors.scratch,
        flops=work(dense, vectors.items, lanes),
        moved=4 * MIB,
    )(*inputs)


def finish_first(plan, dense, vectors, energies, value_sum, right_side, level, own, readers):
    _, clusters, height, depth = dense.shape
    lanes = vectors.lanes
    fields = right_side.shape[0]
    width = height // 2
    count = len(vectors.arrays)
    keys = plan.direct()
    outs = len(keys) + 1

    def kernel(dense_ref, energies_ref, *refs):
        vector_refs, refs = refs[:count], refs[count:]
        sum_ref, right_ref, level_ref, own_ref, readers_ref, image_ref, outgoing = refs[:7]
        messages, scratch = refs[7 : 7 + outs], refs[7 + outs :]
        energy = wide([energies_ref[...]] * fields)
        opened = vectors.open(vector_refs, scratch)
        (center,) = centers([(0, own_ref)], depth)

        @pl.loop(0, clusters // BATCH)
        def _(batch):
            here = pl.ds(batch * BATCH, BATCH)
            value = sum_ref[here]
            for part in products(dense_ref, opened, here, energy):
                value = value + part
            for local in range(BATCH):
                cluster = batch * BATCH + local
                rows = pl.ds(pl.multiple_of(cluster * width, width), width)
                right = wide([right_ref[f, rows, :] for f in range(fields)])
                image = wide([level_ref[cluster]] * fields) * right + value[local]
                image_ref[cluster] = image
                outgoing[rows, :] = (image - center * right).astype(jnp.bfloat16)

        fill(plan, keys, readers_ref, outgoing, messages, width)

    image, full, *messages, out = call(
        kernel,
        "finish_first",
        [
            jax.ShapeDtypeStruct((clusters, width, lanes), jnp.float32),
            jax.ShapeDtypeStruct((clusters * width, lanes), jnp.bfloat16),
        ]
        + [jax.ShapeDtypeStruct((depth, lanes), jnp.bfloat16)] * outs,
        [vmem()] * (2 + count + 4) + [smem()],
        vectors.scratch,
        flops=work(dense, vectors.items, lanes),
        moved=8 * MIB,
    )(dense, energies, *vectors.arrays, value_sum, right_side, level, own, readers)
    return image, full, dict(zip(keys, messages)), out


def guesses(lines, fields):
    orbitals = lines.shape[1] // fields
    alphas, growths = [], []
    for column in field_sums(lines, fields):
        norm, bend, square = column[0:1], column[1:2], column[2:3]
        norm = jnp.maximum(norm, 1e-30)
        alpha = norm / jnp.maximum(bend, 4.0 * norm)
        alphas.append(alpha)
        growths.append(jnp.clip(alpha * alpha * square / norm, 1.0, 2.0))
    return per_field(alphas, orbitals), per_field(growths, orbitals)


def prepare(right_side, image, after):
    fields, rows, orbitals = right_side.shape
    clusters, width, lanes = image.shape

    def kernel(right_ref, image_ref, _, lines_ref, kept):
        kept[...] = jnp.zeros_like(kept)

        def sweep(base, terms):
            @pl.loop(0, clusters)
            def _(cluster):
                here = pl.ds(pl.multiple_of(cluster * width, width), width)
                right = wide([right_ref[f, here, :] for f in range(fields)])
                for index, term in enumerate(terms(right, image_ref[cluster])):
                    kept[base + index] += folded(term)

        sweep(0, lambda right, first: (right * right, right * first, first * first))
        alpha, growth = guesses(lined([kept[i] for i in range(3)], 8), fields)

        def later_terms(right, first):
            step = alpha * first
            residual = right - step
            return residual * residual, residual * first, (growth * right - step) * first

        sweep(3, later_terms)
        lines_ref[...] = lined([kept[i] for i in range(6)], 8)
        lines_ref[6:7, :] = alpha
        lines_ref[7:8, :] = growth

    return call(
        kernel,
        "prepare",
        jax.ShapeDtypeStruct((8, lanes), jnp.float32),
        [vmem(), vmem(), pl.BlockSpec(memory_space=pl.ANY)],
        [pltpu.VMEM((6, 8, lanes), jnp.float32)],
        flops=8 * MIB,
        moved=4 * MIB,
    )(right_side, image, after)


def finish_second(dense, vectors, energies, value_sum, right_side, level, image, weighted, lines, devices):
    _, clusters, height, _ = dense.shape
    lanes = vectors.lanes
    fields = right_side.shape[0]
    width = height // 2
    count = len(vectors.arrays)

    def kernel(dense_ref, energies_ref, *refs):
        vector_refs, refs = refs[:count], refs[count:]
        sum_ref, right_ref, level_ref, image_ref, weighted_ref, lines_ref = refs[:6]
        later_ref, out_ref, kept, *scratch = refs[6:]
        energy = wide([energies_ref[...]] * fields)
        alpha, growth = lines_ref[6:7, :], lines_ref[7:8, :]
        kept[...] = jnp.zeros_like(kept)
        opened = vectors.open(vector_refs, scratch)

        @pl.loop(0, clusters // BATCH)
        def _(batch):
            here = pl.ds(batch * BATCH, BATCH)
            value = sum_ref[here] + weighted_ref[here]
            for part in products(dense_ref, opened, here, energy):
                value = value + part
            for local in range(BATCH):
                cluster = batch * BATCH + local
                rows = pl.ds(pl.multiple_of(cluster * width, width), width)
                right = wide([right_ref[f, rows, :] for f in range(fields)])
                first = image_ref[cluster]
                later = wide([level_ref[cluster]] * fields) * first + value[local]
                later_ref[cluster] = later
                direction = growth * right - alpha * first
                for index, left in enumerate((direction, right, first)):
                    kept[index] += folded(left * later)

        block = jnp.concatenate([lines_ref[0:6, :], lined([kept[i] for i in range(3)], 10)], axis=0)
        orbitals = lanes // fields
        line, lane = (lax.broadcasted_iota(jnp.int32, (16, 128), d) for d in (0, 1))
        rows = []
        for f, column in enumerate(field_sums(block, fields)):
            first_lane = slice(f * orbitals, f * orbitals + 1)
            filled = jnp.broadcast_to(column, (16, 128))
            filled = jnp.where(line == 9, jnp.broadcast_to(alpha[:, first_lane], (16, 128)), filled)
            filled = jnp.where(line == 10, jnp.broadcast_to(growth[:, first_lane], (16, 128)), filled)
            rows.append(jnp.sum(jnp.where(line == lane, filled, 0.0), axis=0, keepdims=True))
        rows.append(jnp.zeros((8 - fields, 128), jnp.float32))
        out_ref[...] = jnp.broadcast_to(jnp.concatenate(rows, axis=0)[None], out_ref.shape)

    return call(
        kernel,
        "finish_second",
        [
            jax.ShapeDtypeStruct((clusters, width, lanes), jnp.float32),
            jax.ShapeDtypeStruct((devices, 8, 128), jnp.float32),
        ],
        [vmem()] * (2 + count + 6),
        [pltpu.VMEM((3, 8, lanes), jnp.float32)] + vectors.scratch,
        flops=work(dense, vectors.items, lanes),
        moved=8 * MIB,
    )(dense, energies, *vectors.arrays, value_sum, right_side, level, image, weighted, lines)


def step_sizes(gathered, fields, orbitals):
    rows = gathered.reshape(-1, 128)
    flat = wide([jnp.transpose(rows[i : i + 128]) for i in range(0, rows.shape[0], 128)])
    line = [flat[i : i + 1, :] for i in range(11)]
    place = lax.broadcasted_iota(jnp.int32, line[0].shape, 1) & 7
    whole = lambda v: [
        jnp.sum(jnp.where(place == f, v, 0.0), axis=1, keepdims=True) for f in range(fields)
    ]

    def back(values):
        row = jnp.zeros_like(line[0])
        for f, value in enumerate(values):
            row = jnp.where(place == f, jnp.broadcast_to(value, row.shape), row)
        return row

    norm = whole(line[0])
    alpha = [n / b for n, b in zip(norm, whole(line[1]))]
    growth = [a * a * s / n for a, s, n in zip(alpha, whole(line[2]), norm)]
    off, more = back(alpha) - line[9], back(growth) - line[10]
    after = whole(line[3] - 2.0 * off * line[4] + off * off * line[2])
    bend = whole(
        (line[10] * line[5] - line[9] * line[6])
        + more * (line[5] + line[10] * line[1] - line[9] * line[7])
        - off * (line[6] + line[10] * line[2] - line[9] * line[8])
        + more * more * line[1]
        - more * off * (line[7] + line[2])
        + off * off * line[8]
    )
    gain = [a / b for a, b in zip(after, bend)]
    return [per_field(v, orbitals) for v in (alpha, growth, gain)]


def final(right_side, image, later, gathered):
    fields, rows, orbitals = right_side.shape
    clusters, width, lanes = image.shape
    blocks = 4
    each = clusters // blocks

    def kernel(right_ref, image_ref, later_ref, gathered_ref, solution_ref, residual_ref, steps):
        step = pl.program_id(0)

        @pl.when(step == 0)
        def _():
            alpha, growth, gain = step_sizes(gathered_ref[...], fields, orbitals)
            steps[0:1, :] = alpha + gain * growth
            steps[1:2, :] = gain * alpha

        for local in range(each):
            cluster = step * each + local
            rows = pl.ds(pl.multiple_of(cluster * width, width), width)
            here = slice(local * width, (local + 1) * width)
            for field in range(fields):
                part = slice(field * orbitals, (field + 1) * orbitals)
                one, two = steps[0:1, part], steps[1:2, part]
                right = right_ref[field, rows, :]
                first = image_ref[cluster, :, part]
                later = later_ref[cluster, :, part]
                solution_ref[field, here, :] = one * right - two * first
                residual_ref[field, here, :] = (right - one * first) + two * later

    vector = pl.BlockSpec((fields, each * width, orbitals), lambda i: (0, i, 0))
    shape = jax.ShapeDtypeStruct(right_side.shape, jnp.float32)
    return pl.pallas_call(
        kernel,
        grid=(blocks,),
        out_shape=[shape, shape],
        in_specs=[vmem()] * 4,
        out_specs=[vector, vector],
        scratch_shapes=[pltpu.VMEM((8, lanes), jnp.float32)],
        compiler_params=pltpu.CompilerParams(vmem_limit_bytes=12 * MIB),
        name="final",
    )(right_side, image, later, gathered)


def body(right_side, onsite, energies, ks_tiles, correlation_tiles, tile_slot, readers):
    span, served = readers.shape[1:]
    clusters, _, width, _ = ks_tiles.shape
    rows = lax.axis_size("row")
    devices = rows * lax.axis_size("col")
    onsite = onsite.reshape(-1, width)
    energies = energies.reshape(1, -1)
    plan = Plan(rows, span, rows == 8 and span == 7)
    readers = jnp.swapaxes(readers, 1, 2)

    def partial(items):
        sums = [[]]
        for group in (items[:2], items[2:-2], items[-2:-1]):
            sums.append(couple(dense, Vectors(plan, group), energies, sums[-1]))
        return sums[-1], sums[1][0]

    direct, own, full = pack(plan, readers, right_side, onsite)
    dense = spread(tile_slot, ks_tiles, correlation_tiles, span, served)
    items, chosen = exchange(plan, readers, direct, own, full, None, dense, served, width)
    level = levels(onsite)
    sums, _ = partial(items)
    last = Vectors(plan, items[-1:])
    image, full, direct, out = finish_first(
        plan, dense, last, energies, sums[0], right_side, level, own, readers
    )

    items, _ = exchange(plan, readers, direct, out, full, chosen, None, served, width)
    (value,), begun = partial(items)
    lines = prepare(right_side, image, begun)
    _, weighted = couple(dense, last, energies, sums, begun)
    last = Vectors(plan, items[-1:])
    later, gathered = finish_second(
        dense, last, energies, value, right_side, level, image, weighted, lines, devices
    )
    gathered = lax.all_to_all(gathered, ("row", "col"), 0, 0)
    return tuple(final(right_side, image, later, gathered))


def solution(mesh):
    placed = (
        P(None, "row", "col"),
        P("row"),
        P("col"),
        P("row", None, None, None),
        P("row", None, None, None),
        P("row", None),
        P("row", None, None),
    )
    return jax.shard_map(
        body,
        mesh=mesh,
        in_specs=placed,
        out_specs=(P(None, "row", "col"), P(None, "row", "col")),
        check_vma=False,
    )
```

```python
import functools

import jax
import jax.numpy as jnp
from jax import lax
from jax.experimental import pallas as pl
from jax.experimental.pallas import tpu as pltpu
from jax.sharding import PartitionSpec as P

MIB = 2**20
EXTRA = 16
BATCH = 2


def shifted(array, axis, by):
    count = lax.axis_size(axis)
    return lax.ppermute(array, axis, [(i, (i + by) % count) for i in range(count)])


def vmem():
    return pl.BlockSpec(memory_space=pltpu.VMEM)


def smem():
    return pl.BlockSpec(memory_space=pltpu.SMEM)


def call(kernel, name, out_shape, specs, scratch=(), flops=0, moved=MIB, limit=12):
    return pl.pallas_call(
        kernel,
        out_shape=out_shape,
        in_specs=specs,
        out_specs=jax.tree.map(lambda _: vmem(), out_shape),
        scratch_shapes=list(scratch),
        compiler_params=pltpu.CompilerParams(vmem_limit_bytes=limit * MIB),
        cost_estimate=pl.CostEstimate(flops=flops, bytes_accessed=moved, transcendentals=0),
        name=name,
    )


def wide(parts):
    return jnp.concatenate(parts, axis=1)


def folded(term):
    return jnp.sum(term.reshape(-1, 8, term.shape[-1]), axis=0)


def lined(parts, lines):
    parts = [jnp.sum(p, axis=0, keepdims=True) for p in parts]
    parts.append(jnp.zeros((lines - len(parts), parts[0].shape[1]), jnp.float32))
    return jnp.concatenate(parts, axis=0)


def per_field(values, orbitals):
    return wide([jnp.broadcast_to(v, (1, orbitals)) for v in values])


def field_sums(lines, fields):
    orbitals = lines.shape[1] // fields
    return [
        jnp.sum(lines[:, f * orbitals : (f + 1) * orbitals], axis=1, keepdims=True)
        for f in range(fields)
    ]


class Plan:
    def __init__(self, count, span, relayed):
        self.count, self.span, self.middle, self.relayed = count, span, (span - 1) // 2, relayed

    def offset(self, source, reader):
        value = lax.rem(source - reader + (self.middle + self.count), self.count)
        return jnp.minimum(value, self.span - 1) if self.relayed else value

    def direct(self):
        if self.relayed:
            return [1, 2, 3, 7]
        far = range(self.middle, 0, -1)
        return [by for f in far for by in (f, -f)]

    def reader(self, key, me):
        return me ^ key if self.relayed else lax.rem(me + key + self.count, self.count)

    def source(self, key, me):
        return me ^ key if self.relayed else lax.rem(me - key + self.count, self.count)

    def pairs(self, key):
        if not self.relayed:
            return [(i, (i + key) % self.count) for i in range(self.count)]
        return [(i, i ^ key) for i in range(self.count) if key < 4 or i not in INNER]


INNER = (2, 3, 4, 5)


def is_inner(me):
    return (me >= INNER[0]) & (me <= INNER[-1])


def pack(plan, readers, right_side, onsite):
    fields, rows, orbitals = right_side.shape
    served = readers.shape[1]
    clusters, width = onsite.shape
    lanes = fields * orbitals
    keys = plan.direct()

    def kernel(readers_hbm, right_hbm, onsite_hbm, *refs):
        messages, rounded = refs[: len(keys) + 1], refs[len(keys) + 1]
        readers_ref, right_ref, onsite_ref, sems, more = refs[len(keys) + 2 :]
        copies = []
        for cluster in range(clusters):
            here = pl.ds(cluster * width, width)
            copies.append(
                pltpu.make_async_copy(
                    right_hbm.at[:, here, :], right_ref.at[:, here, :], sems.at[cluster]
                )
            )
        others = [
            pltpu.make_async_copy(onsite_hbm, onsite_ref, more.at[0]),
            pltpu.make_async_copy(readers_hbm, readers_ref, more.at[1]),
        ]
        for copy in copies[:1] + others + copies[1:]:
            copy.start()
        others[0].wait()
        norm = [jnp.zeros((8, orbitals), jnp.float32)] * fields
        heavy = [jnp.zeros((8, orbitals), jnp.float32)] * fields
        for cluster in range(clusters):
            copies[cluster].wait()
            weight = jnp.broadcast_to(onsite_ref[cluster : cluster + 1, :], (8, width))
            here = slice(cluster * width, (cluster + 1) * width)
            for field in range(fields):
                right = right_ref[field, here, :]
                rounded[here, field * orbitals : (field + 1) * orbitals] = right.astype(jnp.bfloat16)
                square = right * right
                norm[field] += folded(square)
                heavy[field] += jnp.dot(weight, square, preferred_element_type=jnp.float32)
        centers = [
            jnp.sum(h[:1], axis=1, keepdims=True)
            / jnp.maximum(jnp.sum(jnp.sum(n, axis=0, keepdims=True), axis=1, keepdims=True), 1e-30)
            for h, n in zip(heavy, norm)
        ]
        others[1].wait()
        rest = jnp.broadcast_to(per_field(centers, orbitals), (EXTRA, lanes))
        line, lane = (lax.broadcasted_iota(jnp.int32, (EXTRA, lanes), d) for d in (0, 1))
        for offset in range(readers_ref.shape[2]):
            for slot in range(served):
                here = (line == offset + 1) & (lane == slot)
                rest = jnp.where(here, readers_ref[0, slot, offset].astype(jnp.float32), rest)
        rounded[clusters * width :, :] = rest.astype(jnp.bfloat16)
        fill(plan, keys, readers_ref, rounded, messages, width)

    message = jax.ShapeDtypeStruct((served * width + EXTRA, lanes), jnp.bfloat16)
    full = jax.ShapeDtypeStruct((clusters * width + EXTRA, lanes), jnp.bfloat16)
    *messages, own, full = call(
        kernel,
        "pack",
        [message] * (len(keys) + 1) + [full],
        [pl.BlockSpec(memory_space=pltpu.HBM)] * 3,
        [
            pltpu.SMEM(readers.shape, readers.dtype),
            pltpu.VMEM(right_side.shape, jnp.float32),
            pltpu.VMEM(onsite.shape, jnp.float32),
            pltpu.SemaphoreType.DMA((clusters,)),
            pltpu.SemaphoreType.DMA((2,)),
        ],
        limit=51,
    )(readers, right_side, onsite)
    return dict(zip(keys, messages)), own, full


def fill(plan, keys, readers_ref, rounded, messages, width):
    me = lax.axis_index("row")
    offsets = [plan.offset(me, plan.reader(key, me)) for key in keys] + [plan.middle]
    for offset, message in zip(offsets, messages):
        served = readers_ref.shape[1]
        gather([readers_ref[0, slot, offset] for slot in range(served)], rounded, message, width)


def gather(clusters, rounded, message, width):
    for slot, cluster in enumerate(clusters):
        start = pl.multiple_of(cluster * width, width)
        message[slot * width : (slot + 1) * width, :] = rounded[pl.ds(start, width), :]
    used = len(clusters) * width
    if message.shape[0] > used:
        message[used:, :] = rounded[rounded.shape[0] - EXTRA :, :]


def relay(plan, readers, mine, full, chosen, after, served, width):
    lanes = full.shape[1]
    extra = EXTRA if chosen is None else 0
    message = jax.ShapeDtypeStruct((served * width + extra, lanes), jnp.bfloat16)

    def kernel(*refs):
        readers_ref, mine_ref, full_ref, _, *refs = refs
        me = lax.axis_index("row")
        *messages, chosen_ref = refs if chosen is None else [*refs[1:], refs[0]]
        if chosen is None:
            base = full_ref.shape[0] - EXTRA
            table = full_ref[base : base + EXTRA, 0:width].astype(jnp.float32)
            line, lane = (lax.broadcasted_iota(jnp.int32, table.shape, d) for d in (0, 1))
            for index, reader in enumerate((me, me ^ 1, me ^ 3)):
                offset = plan.offset(me ^ 6, reader)
                for slot in range(served):
                    here = (line == offset + 1) & (lane == slot)
                    chosen_ref[index, slot] = jnp.sum(jnp.where(here, table, 0.0)).astype(jnp.int32)

        @pl.when(is_inner(me))
        def _():
            for index, out in enumerate(messages):
                gather([chosen_ref[index, slot] for slot in range(served)], full_ref, out, width)

        @pl.when(jnp.logical_not(is_inner(me)))
        def _():
            for key, out in zip((6, 5), messages[1:]):
                offset = plan.offset(me, me ^ key)
                clusters = [readers_ref[0, slot, offset] for slot in range(served)]
                gather(clusters, mine_ref, out, width)

    inputs = [readers, mine, full, after] + ([] if chosen is None else [chosen])
    specs = [smem(), vmem(), vmem(), pl.BlockSpec(memory_space=pl.ANY)]
    specs += [] if chosen is None else [smem()]
    shapes, outs = [message] * 3, [vmem()] * 3
    if chosen is None:
        shapes.append(jax.ShapeDtypeStruct((3, served), jnp.int32))
        outs.append(smem())
    *messages, last = pl.pallas_call(
        kernel,
        out_shape=shapes,
        in_specs=specs,
        out_specs=outs,
        compiler_params=pltpu.CompilerParams(vmem_limit_bytes=12 * MIB),
        cost_estimate=pl.CostEstimate(flops=0, bytes_accessed=MIB, transcendentals=0),
        name="relay",
    )(*inputs)
    return (messages, last) if chosen is None else (messages + [last], chosen)


def exchange(plan, readers, direct, own, full, chosen, begin, served, width):
    sent = {k: lax.ppermute(m, "row", plan.pairs(k)) for k, m in direct.items()}
    if not plan.relayed:
        items = [(own, 0)] + [(sent[k], k) for k in plan.direct()]
        sums = begin(items[:3], None)
        return items, sums, None, sums[0]
    theirs = lax.ppermute(full, "row", [(i, i ^ 6) for i in INNER])
    items = [(own, 0), (sent[1], 1), (sent[2], 2), (sent[3], 3)]
    sums = begin(items[:3], theirs)
    (mine, near, far), chosen = relay(
        plan, readers, full, theirs, chosen, sums[0], served, width
    )
    near = lax.ppermute(near, "row", [(i, i ^ (1 if i in INNER else 6)) for i in range(plan.count)])
    far = lax.ppermute(far, "row", [(i, i ^ (3 if i in INNER else 5)) for i in range(plan.count)])
    items += [((mine, sent[7]), (6, 7)), (far, 5), (near, (7, 6))]
    return items, sums, chosen, mine


class Vectors:
    def __init__(self, plan, items):
        self.plan, self.items = plan, items
        self.arrays, self.scratch = [], []
        for value, _ in items:
            many = isinstance(value, tuple)
            self.arrays += list(value) if many else [value]
            if many:
                self.scratch.append(pltpu.VMEM(value[0].shape, value[0].dtype))
        self.lanes = self.arrays[0].shape[1]
        self.rows = self.arrays[0].shape[0]

    def open(self, refs, scratch):
        refs, scratch = list(refs), list(scratch)
        me = lax.axis_index("row")
        opened = []
        for value, key in self.items:
            if not self.plan.relayed:
                opened.append((self.plan.middle - key, refs.pop(0)))
                continue
            inner, outer = key if isinstance(key, tuple) else (key, key)
            held = refs.pop(0)
            if isinstance(value, tuple):
                kept, held, other = held, scratch.pop(0), refs.pop(0)

                @pl.when(is_inner(me))
                def _():
                    held[...] = kept[...]

                @pl.when(jnp.logical_not(is_inner(me)))
                def _():
                    held[...] = other[...]

            source = jnp.where(is_inner(me), me ^ inner, me ^ outer)
            opened.append((self.plan.offset(source, me), held))
        return opened


def levels(onsite):
    clusters, width = onsite.shape

    def kernel(onsite_ref, level_ref):
        for cluster in range(clusters):
            level_ref[cluster] = jnp.transpose(
                jnp.broadcast_to(onsite_ref[cluster : cluster + 1, :], (width, width))
            )

    shape = jax.ShapeDtypeStruct((clusters, width, width), jnp.float32)
    return call(kernel, "levels", shape, [vmem()])(onsite)


def spread(tile_slot, ks_tiles, correlation_tiles, span, served):
    clusters, _, width, _ = ks_tiles.shape
    slots = span * served

    def kernel(slot_ref, ks_ref, correlation_ref, out_ref, where):
        @pl.loop(0, clusters)
        def _(cluster):
            for kind, ref in enumerate((ks_ref, correlation_ref)):
                count = ref.shape[1]
                for slot in range(slots):
                    where[slot] = count
                for tile in range(count):
                    where[slot_ref[cluster, tile]] = tile
                for slot in range(slots):
                    tile = where[slot]
                    block = ref[cluster, jnp.minimum(tile, count - 1)]
                    block = jnp.where(tile < count, block, jnp.zeros_like(block))
                    lane = slot % served * width
                    out_ref[
                        slot // served, cluster, kind * width : (kind + 1) * width, lane : lane + width
                    ] = block

    return call(
        kernel,
        "spread",
        jax.ShapeDtypeStruct((span, clusters, 2 * width, served * width), jnp.bfloat16),
        [smem(), vmem(), vmem()],
        [pltpu.SMEM((slots,), jnp.int32)],
        moved=16 * MIB,
    )(tile_slot, ks_tiles, correlation_tiles)


def products(dense_ref, opened, clusters, energy):
    depth = dense_ref.shape[-1]
    for offset, vector in opened:
        left = dense_ref[offset, clusters]
        count, height, _ = left.shape
        value = jnp.dot(
            left.reshape(count * height, depth), vector[0:depth, :], preferred_element_type=jnp.float32
        )
        value = value.reshape(count, 2, height // 2, value.shape[1])
        yield value[:, 0] - energy * value[:, 1]


def centers(opened, depth):
    return [vector[depth : depth + EXTRA, :].astype(jnp.float32)[:1] for _, vector in opened]


def work(dense, items, lanes):
    return 2 * len(items) * dense.shape[1] * dense.shape[2] * dense.shape[3] * lanes


def couple(dense, vectors, energies, sums, after=None):
    _, clusters, height, depth = dense.shape
    lanes = vectors.lanes
    count = len(vectors.arrays)
    outs = 2 if vectors.rows > depth else 1
    had = len(sums)

    def kernel(dense_ref, energies_ref, *refs):
        refs = list(refs[1:] if after is not None else refs)
        vector_refs, sum_refs = refs[:count], refs[count : count + had]
        out_refs, scratch = refs[count + had : count + had + outs], refs[count + had + outs :]
        energy = wide([energies_ref[...]] * (lanes // energies_ref.shape[1]))
        opened = vectors.open(vector_refs, scratch)
        weights = centers(opened, depth) if outs == 2 else [None] * len(opened)

        @pl.loop(0, clusters // BATCH)
        def _(batch):
            here = pl.ds(batch * BATCH, BATCH)
            values = [ref[here] for ref in sum_refs]
            for weight, part in zip(weights, products(dense_ref, opened, here, energy)):
                terms = [part] if weight is None else [part, weight * part]
                values = [v + t for v, t in zip(values, terms)] if values else terms
            for ref, value in zip(out_refs, values):
                ref[here] = value

    order = [] if after is None else [after]
    inputs = [dense, energies, *order, *vectors.arrays, *sums]
    shape = jax.ShapeDtypeStruct((clusters, height // 2, lanes), jnp.float32)
    return call(
        kernel,
        "couple",
        [shape] * outs,
        [vmem()] * 2
        + [pl.BlockSpec(memory_space=pl.ANY)] * len(order)
        + [vmem()] * (len(vectors.arrays) + had),
        vectors.scratch,
        flops=work(dense, vectors.items, lanes),
        moved=4 * MIB,
    )(*inputs)


def finish_first(plan, dense, vectors, energies, value_sum, right_side, level, own, readers):
    _, clusters, height, depth = dense.shape
    lanes = vectors.lanes
    fields = right_side.shape[0]
    width = height // 2
    count = len(vectors.arrays)
    keys = plan.direct()
    outs = len(keys) + 1

    def kernel(dense_ref, energies_ref, *refs):
        vector_refs, refs = refs[:count], refs[count:]
        sum_ref, right_ref, level_ref, own_ref, readers_ref, image_ref, outgoing = refs[:7]
        messages, scratch = refs[7 : 7 + outs], refs[7 + outs :]
        energy = wide([energies_ref[...]] * fields)
        opened = vectors.open(vector_refs, scratch)
        (center,) = centers([(0, own_ref)], depth)

        @pl.loop(0, clusters // BATCH)
        def _(batch):
            here = pl.ds(batch * BATCH, BATCH)
            value = sum_ref[here]
            for part in products(dense_ref, opened, here, energy):
                value = value + part
            for local in range(BATCH):
                cluster = batch * BATCH + local
                rows = pl.ds(pl.multiple_of(cluster * width, width), width)
                right = wide([right_ref[f, rows, :] for f in range(fields)])
                image = wide([level_ref[cluster]] * fields) * right + value[local]
                image_ref[cluster] = image
                outgoing[rows, :] = (image - center * right).astype(jnp.bfloat16)

        fill(plan, keys, readers_ref, outgoing, messages, width)

    image, full, *messages, out = call(
        kernel,
        "finish_first",
        [
            jax.ShapeDtypeStruct((clusters, width, lanes), jnp.float32),
            jax.ShapeDtypeStruct((clusters * width, lanes), jnp.bfloat16),
        ]
        + [jax.ShapeDtypeStruct((depth, lanes), jnp.bfloat16)] * outs,
        [vmem()] * (2 + count + 4) + [smem()],
        vectors.scratch,
        flops=work(dense, vectors.items, lanes),
        moved=8 * MIB,
    )(dense, energies, *vectors.arrays, value_sum, right_side, level, own, readers)
    return image, full, dict(zip(keys, messages)), out


def guesses(lines, fields):
    orbitals = lines.shape[1] // fields
    alphas, growths = [], []
    for column in field_sums(lines, fields):
        norm, bend, square = column[0:1], column[1:2], column[2:3]
        norm = jnp.maximum(norm, 1e-30)
        alpha = norm / jnp.maximum(bend, 4.0 * norm)
        alphas.append(alpha)
        growths.append(jnp.clip(alpha * alpha * square / norm, 1.0, 2.0))
    return per_field(alphas, orbitals), per_field(growths, orbitals)


def prepare(right_side, image, after):
    fields, rows, orbitals = right_side.shape
    clusters, width, lanes = image.shape

    def kernel(right_ref, image_ref, _, lines_ref, kept):
        kept[...] = jnp.zeros_like(kept)

        def sweep(base, terms):
            @pl.loop(0, clusters)
            def _(cluster):
                here = pl.ds(pl.multiple_of(cluster * width, width), width)
                right = wide([right_ref[f, here, :] for f in range(fields)])
                for index, term in enumerate(terms(right, image_ref[cluster])):
                    kept[base + index] += folded(term)

        sweep(0, lambda right, first: (right * right, right * first, first * first))
        alpha, growth = guesses(lined([kept[i] for i in range(3)], 8), fields)

        def later_terms(right, first):
            step = alpha * first
            residual = right - step
            return residual * residual, residual * first, (growth * right - step) * first

        sweep(3, later_terms)
        lines_ref[...] = lined([kept[i] for i in range(6)], 8)
        lines_ref[6:7, :] = alpha
        lines_ref[7:8, :] = growth

    return call(
        kernel,
        "prepare",
        jax.ShapeDtypeStruct((8, lanes), jnp.float32),
        [vmem(), vmem(), pl.BlockSpec(memory_space=pl.ANY)],
        [pltpu.VMEM((6, 8, lanes), jnp.float32)],
        flops=8 * MIB,
        moved=4 * MIB,
    )(right_side, image, after)


def finish_second(dense, vectors, energies, value_sum, right_side, level, image, weighted, lines, devices):
    _, clusters, height, _ = dense.shape
    lanes = vectors.lanes
    fields = right_side.shape[0]
    width = height // 2
    count = len(vectors.arrays)

    def kernel(dense_ref, energies_ref, *refs):
        vector_refs, refs = refs[:count], refs[count:]
        sum_ref, right_ref, level_ref, image_ref, weighted_ref, lines_ref = refs[:6]
        later_ref, out_ref, kept, *scratch = refs[6:]
        energy = wide([energies_ref[...]] * fields)
        alpha, growth = lines_ref[6:7, :], lines_ref[7:8, :]
        kept[...] = jnp.zeros_like(kept)
        opened = vectors.open(vector_refs, scratch)

        @pl.loop(0, clusters // BATCH)
        def _(batch):
            here = pl.ds(batch * BATCH, BATCH)
            value = sum_ref[here] + weighted_ref[here]
            for part in products(dense_ref, opened, here, energy):
                value = value + part
            for local in range(BATCH):
                cluster = batch * BATCH + local
                rows = pl.ds(pl.multiple_of(cluster * width, width), width)
                right = wide([right_ref[f, rows, :] for f in range(fields)])
                first = image_ref[cluster]
                later = wide([level_ref[cluster]] * fields) * first + value[local]
                later_ref[cluster] = later
                direction = growth * right - alpha * first
                for index, left in enumerate((direction, right, first)):
                    kept[index] += folded(left * later)

        block = jnp.concatenate([lines_ref[0:6, :], lined([kept[i] for i in range(3)], 10)], axis=0)
        orbitals = lanes // fields
        line, lane = (lax.broadcasted_iota(jnp.int32, (16, 128), d) for d in (0, 1))
        rows = []
        for f, column in enumerate(field_sums(block, fields)):
            first_lane = slice(f * orbitals, f * orbitals + 1)
            filled = jnp.broadcast_to(column, (16, 128))
            filled = jnp.where(line == 9, jnp.broadcast_to(alpha[:, first_lane], (16, 128)), filled)
            filled = jnp.where(line == 10, jnp.broadcast_to(growth[:, first_lane], (16, 128)), filled)
            rows.append(jnp.sum(jnp.where(line == lane, filled, 0.0), axis=0, keepdims=True))
        rows.append(jnp.zeros((8 - fields, 128), jnp.float32))
        out_ref[...] = jnp.broadcast_to(jnp.concatenate(rows, axis=0)[None], out_ref.shape)

    return call(
        kernel,
        "finish_second",
        [
            jax.ShapeDtypeStruct((clusters, width, lanes), jnp.float32),
            jax.ShapeDtypeStruct((devices, 8, 128), jnp.float32),
        ],
        [vmem()] * (2 + count + 6),
        [pltpu.VMEM((3, 8, lanes), jnp.float32)] + vectors.scratch,
        flops=work(dense, vectors.items, lanes),
        moved=8 * MIB,
    )(dense, energies, *vectors.arrays, value_sum, right_side, level, image, weighted, lines)


def step_sizes(gathered, fields, orbitals):
    rows = gathered.reshape(-1, 128)
    flat = wide([jnp.transpose(rows[i : i + 128]) for i in range(0, rows.shape[0], 128)])
    line = [flat[i : i + 1, :] for i in range(11)]
    place = lax.broadcasted_iota(jnp.int32, line[0].shape, 1) & 7
    whole = lambda v: [
        jnp.sum(jnp.where(place == f, v, 0.0), axis=1, keepdims=True) for f in range(fields)
    ]

    def back(values):
        row = jnp.zeros_like(line[0])
        for f, value in enumerate(values):
            row = jnp.where(place == f, jnp.broadcast_to(value, row.shape), row)
        return row

    norm = whole(line[0])
    alpha = [n / b for n, b in zip(norm, whole(line[1]))]
    growth = [a * a * s / n for a, s, n in zip(alpha, whole(line[2]), norm)]
    off, more = back(alpha) - line[9], back(growth) - line[10]
    after = whole(line[3] - 2.0 * off * line[4] + off * off * line[2])
    bend = whole(
        (line[10] * line[5] - line[9] * line[6])
        + more * (line[5] + line[10] * line[1] - line[9] * line[7])
        - off * (line[6] + line[10] * line[2] - line[9] * line[8])
        + more * more * line[1]
        - more * off * (line[7] + line[2])
        + off * off * line[8]
    )
    gain = [a / b for a, b in zip(after, bend)]
    return [per_field(v, orbitals) for v in (alpha, growth, gain)]


def final(right_side, image, later, gathered):
    fields, rows, orbitals = right_side.shape
    clusters, width, lanes = image.shape
    blocks = 4
    each = clusters // blocks

    def kernel(right_ref, image_ref, later_ref, gathered_ref, solution_ref, residual_ref, steps):
        step = pl.program_id(0)

        @pl.when(step == 0)
        def _():
            alpha, growth, gain = step_sizes(gathered_ref[...], fields, orbitals)
            steps[0:1, :] = alpha + gain * growth
            steps[1:2, :] = gain * alpha

        for local in range(each):
            cluster = step * each + local
            rows = pl.ds(pl.multiple_of(cluster * width, width), width)
            here = slice(local * width, (local + 1) * width)
            for field in range(fields):
                part = slice(field * orbitals, (field + 1) * orbitals)
                one, two = steps[0:1, part], steps[1:2, part]
                right = right_ref[field, rows, :]
                first = image_ref[cluster, :, part]
                later = later_ref[cluster, :, part]
                solution_ref[field, here, :] = one * right - two * first
                residual_ref[field, here, :] = (right - one * first) + two * later

    vector = pl.BlockSpec((fields, each * width, orbitals), lambda i: (0, i, 0))
    shape = jax.ShapeDtypeStruct(right_side.shape, jnp.float32)
    return pl.pallas_call(
        kernel,
        grid=(blocks,),
        out_shape=[shape, shape],
        in_specs=[vmem()] * 4,
        out_specs=[vector, vector],
        scratch_shapes=[pltpu.VMEM((8, lanes), jnp.float32)],
        compiler_params=pltpu.CompilerParams(vmem_limit_bytes=12 * MIB),
        name="final",
    )(right_side, image, later, gathered)


def body(right_side, onsite, energies, ks_tiles, correlation_tiles, tile_slot, readers):
    span, served = readers.shape[1:]
    clusters, _, width, _ = ks_tiles.shape
    rows = lax.axis_size("row")
    devices = rows * lax.axis_size("col")
    onsite = onsite.reshape(-1, width)
    energies = energies.reshape(1, -1)
    plan = Plan(rows, span, rows == 8 and span == 7)
    readers = jnp.swapaxes(readers, 1, 2)

    def begin(items, after):
        return couple(dense, Vectors(plan, items), energies, [], after)

    def partial(items, sums):
        for group in (items[3:-2], items[-2:-1]):
            sums = couple(dense, Vectors(plan, group), energies, sums)
        return sums, Vectors(plan, items[-1:])

    direct, own, full = pack(plan, readers, right_side, onsite)
    dense = spread(tile_slot, ks_tiles, correlation_tiles, span, served)
    items, sums, chosen, _ = exchange(plan, readers, direct, own, full, None, begin, served, width)
    level = levels(onsite)
    sums, last = partial(items, sums)
    image, full, direct, out = finish_first(
        plan, dense, last, energies, sums[0], right_side, level, own, readers
    )

    items, begun, _, mark = exchange(plan, readers, direct, out, full, chosen, begin, served, width)
    lines = prepare(right_side, image, mark)
    _, weighted = couple(dense, last, energies, sums, mark)
    (value,), last = partial(items, begun)
    later, gathered = finish_second(
        dense, last, energies, value, right_side, level, image, weighted, lines, devices
    )
    gathered = lax.all_to_all(gathered, ("row", "col"), 0, 0)
    return tuple(final(right_side, image, later, gathered))


def solution(mesh):
    placed = (
        P(None, "row", "col"),
        P("row"),
        P("col"),
        P("row", None, None, None),
        P("row", None, None, None),
        P("row", None),
        P("row", None, None),
    )
    return jax.shard_map(
        body,
        mesh=mesh,
        in_specs=placed,
        out_specs=(P(None, "row", "col"), P(None, "row", "col")),
        check_vma=False,
    )
```

```python
import functools

import jax
import jax.numpy as jnp
from jax import lax
from jax.experimental import pallas as pl
from jax.experimental.pallas import tpu as pltpu
from jax.sharding import PartitionSpec as P

MIB = 2**20
EXTRA = 16
BATCH = 2


def shifted(array, axis, by):
    count = lax.axis_size(axis)
    return lax.ppermute(array, axis, [(i, (i + by) % count) for i in range(count)])


def vmem():
    return pl.BlockSpec(memory_space=pltpu.VMEM)


def smem():
    return pl.BlockSpec(memory_space=pltpu.SMEM)


def call(kernel, name, out_shape, specs, scratch=(), flops=0, moved=MIB, limit=12):
    return pl.pallas_call(
        kernel,
        out_shape=out_shape,
        in_specs=specs,
        out_specs=jax.tree.map(lambda _: vmem(), out_shape),
        scratch_shapes=list(scratch),
        compiler_params=pltpu.CompilerParams(vmem_limit_bytes=limit * MIB),
        cost_estimate=pl.CostEstimate(flops=flops, bytes_accessed=moved, transcendentals=0),
        name=name,
    )


def wide(parts):
    return jnp.concatenate(parts, axis=1)


def folded(term):
    return jnp.sum(term.reshape(-1, 8, term.shape[-1]), axis=0)


def lined(parts, lines):
    parts = [jnp.sum(p, axis=0, keepdims=True) for p in parts]
    parts.append(jnp.zeros((lines - len(parts), parts[0].shape[1]), jnp.float32))
    return jnp.concatenate(parts, axis=0)


def per_field(values, orbitals):
    return wide([jnp.broadcast_to(v, (1, orbitals)) for v in values])


def field_sums(lines, fields):
    orbitals = lines.shape[1] // fields
    return [
        jnp.sum(lines[:, f * orbitals : (f + 1) * orbitals], axis=1, keepdims=True)
        for f in range(fields)
    ]


class Plan:
    def __init__(self, count, span, relayed):
        self.count, self.span, self.middle, self.relayed = count, span, (span - 1) // 2, relayed

    def offset(self, source, reader):
        value = lax.rem(source - reader + (self.middle + self.count), self.count)
        return jnp.minimum(value, self.span - 1) if self.relayed else value

    def early(self):
        return [2, 3] if self.relayed else self.direct()

    def direct(self):
        if self.relayed:
            return [2, 3, 1, 7]
        far = range(self.middle, 0, -1)
        return [by for f in far for by in (f, -f)]

    def reader(self, key, me):
        return me ^ key if self.relayed else lax.rem(me + key + self.count, self.count)

    def source(self, key, me):
        return me ^ key if self.relayed else lax.rem(me - key + self.count, self.count)

    def pairs(self, key):
        if not self.relayed:
            return [(i, (i + key) % self.count) for i in range(self.count)]
        return [(i, i ^ key) for i in range(self.count) if key < 4 or i not in INNER]


INNER = (2, 3, 4, 5)


def is_inner(me):
    return (me >= INNER[0]) & (me <= INNER[-1])


def pack(plan, readers, right_side, onsite):
    fields, rows, orbitals = right_side.shape
    served = readers.shape[1]
    clusters, width = onsite.shape
    lanes = fields * orbitals
    keys = plan.early()

    def kernel(readers_hbm, right_hbm, onsite_hbm, *refs):
        messages, rounded = refs[: len(keys)], refs[len(keys)]
        readers_ref, right_ref, onsite_ref, sems, more = refs[len(keys) + 1 :]
        copies = []
        for cluster in range(clusters):
            here = pl.ds(cluster * width, width)
            copies.append(
                pltpu.make_async_copy(
                    right_hbm.at[:, here, :], right_ref.at[:, here, :], sems.at[cluster]
                )
            )
        others = [
            pltpu.make_async_copy(onsite_hbm, onsite_ref, more.at[0]),
            pltpu.make_async_copy(readers_hbm, readers_ref, more.at[1]),
        ]
        for copy in copies[:1] + others + copies[1:]:
            copy.start()
        others[0].wait()
        norm = [jnp.zeros((8, orbitals), jnp.float32)] * fields
        heavy = [jnp.zeros((8, orbitals), jnp.float32)] * fields
        for cluster in range(clusters):
            copies[cluster].wait()
            weight = jnp.broadcast_to(onsite_ref[cluster : cluster + 1, :], (8, width))
            here = slice(cluster * width, (cluster + 1) * width)
            for field in range(fields):
                right = right_ref[field, here, :]
                rounded[here, field * orbitals : (field + 1) * orbitals] = right.astype(jnp.bfloat16)
                square = right * right
                norm[field] += folded(square)
                heavy[field] += jnp.dot(weight, square, preferred_element_type=jnp.float32)
        centers = [
            jnp.sum(h[:1], axis=1, keepdims=True)
            / jnp.maximum(jnp.sum(jnp.sum(n, axis=0, keepdims=True), axis=1, keepdims=True), 1e-30)
            for h, n in zip(heavy, norm)
        ]
        others[1].wait()
        rest = jnp.broadcast_to(per_field(centers, orbitals), (EXTRA, lanes))
        line, lane = (lax.broadcasted_iota(jnp.int32, (EXTRA, lanes), d) for d in (0, 1))
        for offset in range(readers_ref.shape[2]):
            for slot in range(served):
                here = (line == offset + 1) & (lane == slot)
                rest = jnp.where(here, readers_ref[0, slot, offset].astype(jnp.float32), rest)
        rounded[clusters * width :, :] = rest.astype(jnp.bfloat16)
        fill(plan, keys, readers_ref, rounded, messages, width)

    message = jax.ShapeDtypeStruct((served * width + EXTRA, lanes), jnp.bfloat16)
    full = jax.ShapeDtypeStruct((clusters * width + EXTRA, lanes), jnp.bfloat16)
    *messages, full = call(
        kernel,
        "pack",
        [message] * len(keys) + [full],
        [pl.BlockSpec(memory_space=pltpu.HBM)] * 3,
        [
            pltpu.SMEM(readers.shape, readers.dtype),
            pltpu.VMEM(right_side.shape, jnp.float32),
            pltpu.VMEM(onsite.shape, jnp.float32),
            pltpu.SemaphoreType.DMA((clusters,)),
            pltpu.SemaphoreType.DMA((2,)),
        ],
        limit=52,
    )(readers, right_side, onsite)
    return dict(zip(keys, messages)), full


def deal(plan, readers, full, served, width):
    keys = [key for key in plan.direct() if key not in plan.early()]
    lanes = full.shape[1]

    def kernel(readers_ref, full_ref, same_ref, *messages):
        fill(plan, keys, readers_ref, full_ref, messages, width)

    message = jax.ShapeDtypeStruct((served * width + EXTRA, lanes), jnp.bfloat16)
    full, *messages, own = pl.pallas_call(
        kernel,
        out_shape=[jax.ShapeDtypeStruct(full.shape, full.dtype)] + [message] * (len(keys) + 1),
        in_specs=[smem(), vmem()],
        out_specs=[vmem()] * (len(keys) + 2),
        input_output_aliases={1: 0},
        compiler_params=pltpu.CompilerParams(vmem_limit_bytes=12 * MIB),
        cost_estimate=pl.CostEstimate(flops=0, bytes_accessed=MIB, transcendentals=0),
        name="deal",
    )(readers, full)
    return dict(zip(keys, messages)), own, full


def fill(plan, keys, readers_ref, rounded, messages, width):
    me = lax.axis_index("row")
    offsets = [plan.offset(me, plan.reader(key, me)) for key in keys] + [plan.middle]
    for offset, message in zip(offsets, messages):
        served = readers_ref.shape[1]
        gather([readers_ref[0, slot, offset] for slot in range(served)], rounded, message, width)


def gather(clusters, rounded, message, width):
    for slot, cluster in enumerate(clusters):
        start = pl.multiple_of(cluster * width, width)
        message[slot * width : (slot + 1) * width, :] = rounded[pl.ds(start, width), :]
    used = len(clusters) * width
    if message.shape[0] > used:
        message[used:, :] = rounded[rounded.shape[0] - EXTRA :, :]


def relay(plan, readers, mine, full, chosen, after, served, width):
    lanes = full.shape[1]
    extra = EXTRA if chosen is None else 0
    message = jax.ShapeDtypeStruct((served * width + extra, lanes), jnp.bfloat16)

    def kernel(*refs):
        readers_ref, mine_ref, full_ref, _, *refs = refs
        me = lax.axis_index("row")
        *messages, chosen_ref = refs if chosen is None else [*refs[1:], refs[0]]
        if chosen is None:
            base = full_ref.shape[0] - EXTRA
            table = full_ref[base : base + EXTRA, 0:width].astype(jnp.float32)
            line, lane = (lax.broadcasted_iota(jnp.int32, table.shape, d) for d in (0, 1))
            for index, reader in enumerate((me, me ^ 1, me ^ 3)):
                offset = plan.offset(me ^ 6, reader)
                for slot in range(served):
                    here = (line == offset + 1) & (lane == slot)
                    chosen_ref[index, slot] = jnp.sum(jnp.where(here, table, 0.0)).astype(jnp.int32)

        @pl.when(is_inner(me))
        def _():
            for index, out in enumerate(messages):
                gather([chosen_ref[index, slot] for slot in range(served)], full_ref, out, width)

        @pl.when(jnp.logical_not(is_inner(me)))
        def _():
            for key, out in zip((6, 5), messages[1:]):
                offset = plan.offset(me, me ^ key)
                clusters = [readers_ref[0, slot, offset] for slot in range(served)]
                gather(clusters, mine_ref, out, width)

    inputs = [readers, mine, full, after] + ([] if chosen is None else [chosen])
    specs = [smem(), vmem(), vmem(), pl.BlockSpec(memory_space=pl.ANY)]
    specs += [] if chosen is None else [smem()]
    shapes, outs = [message] * 3, [vmem()] * 3
    if chosen is None:
        shapes.append(jax.ShapeDtypeStruct((3, served), jnp.int32))
        outs.append(smem())
    *messages, last = pl.pallas_call(
        kernel,
        out_shape=shapes,
        in_specs=specs,
        out_specs=outs,
        compiler_params=pltpu.CompilerParams(vmem_limit_bytes=12 * MIB),
        cost_estimate=pl.CostEstimate(flops=0, bytes_accessed=MIB, transcendentals=0),
        name="relay",
    )(*inputs)
    return (messages, last) if chosen is None else (messages + [last], chosen)


def exchange(plan, readers, direct, own, full, chosen, begin, served, width):
    sent = {k: lax.ppermute(m, "row", plan.pairs(k)) for k, m in direct.items()}
    if not plan.relayed:
        items = [(own, 0)] + [(sent[k], k) for k in plan.direct()]
        sums = begin(items[:3])
        return items, sums, None, sums[0]
    theirs = lax.ppermute(full, "row", [(i, i ^ 6) for i in INNER])
    items = [(own, 0), (sent[2], 2), (sent[3], 3), (sent[1], 1)]
    sums = begin(items[:3])
    (mine, near, far), chosen = relay(
        plan, readers, full, theirs, chosen, sums[0], served, width
    )
    near = lax.ppermute(near, "row", [(i, i ^ (1 if i in INNER else 6)) for i in range(plan.count)])
    far = lax.ppermute(far, "row", [(i, i ^ (3 if i in INNER else 5)) for i in range(plan.count)])
    items += [((mine, sent[7]), (6, 7)), (far, 5), (near, (7, 6))]
    return items, sums, chosen, mine


class Vectors:
    def __init__(self, plan, items):
        self.plan, self.items = plan, items
        self.arrays, self.scratch = [], []
        for value, _ in items:
            many = isinstance(value, tuple)
            self.arrays += list(value) if many else [value]
            if many:
                self.scratch.append(pltpu.VMEM(value[0].shape, value[0].dtype))
        self.lanes = self.arrays[0].shape[1]
        self.rows = self.arrays[0].shape[0]

    def open(self, refs, scratch):
        refs, scratch = list(refs), list(scratch)
        me = lax.axis_index("row")
        opened = []
        for value, key in self.items:
            if not self.plan.relayed:
                opened.append((self.plan.middle - key, refs.pop(0)))
                continue
            inner, outer = key if isinstance(key, tuple) else (key, key)
            held = refs.pop(0)
            if isinstance(value, tuple):
                kept, held, other = held, scratch.pop(0), refs.pop(0)

                @pl.when(is_inner(me))
                def _():
                    held[...] = kept[...]

                @pl.when(jnp.logical_not(is_inner(me)))
                def _():
                    held[...] = other[...]

            source = jnp.where(is_inner(me), me ^ inner, me ^ outer)
            opened.append((self.plan.offset(source, me), held))
        return opened


def levels(onsite):
    clusters, width = onsite.shape

    def kernel(onsite_ref, level_ref):
        for cluster in range(clusters):
            level_ref[cluster] = jnp.transpose(
                jnp.broadcast_to(onsite_ref[cluster : cluster + 1, :], (width, width))
            )

    shape = jax.ShapeDtypeStruct((clusters, width, width), jnp.float32)
    return call(kernel, "levels", shape, [vmem()])(onsite)


def spread(tile_slot, ks_tiles, correlation_tiles, span, served):
    clusters, _, width, _ = ks_tiles.shape
    slots = span * served

    def kernel(slot_ref, ks_ref, correlation_ref, out_ref, where):
        @pl.loop(0, clusters)
        def _(cluster):
            for kind, ref in enumerate((ks_ref, correlation_ref)):
                count = ref.shape[1]
                for slot in range(slots):
                    where[slot] = count
                for tile in range(count):
                    where[slot_ref[cluster, tile]] = tile
                for slot in range(slots):
                    tile = where[slot]
                    block = ref[cluster, jnp.minimum(tile, count - 1)]
                    block = jnp.where(tile < count, block, jnp.zeros_like(block))
                    lane = slot % served * width
                    out_ref[
                        slot // served, cluster, kind * width : (kind + 1) * width, lane : lane + width
                    ] = block

    return call(
        kernel,
        "spread",
        jax.ShapeDtypeStruct((span, clusters, 2 * width, served * width), jnp.bfloat16),
        [smem(), vmem(), vmem()],
        [pltpu.SMEM((slots,), jnp.int32)],
        moved=16 * MIB,
    )(tile_slot, ks_tiles, correlation_tiles)


def products(dense_ref, opened, clusters, energy):
    depth = dense_ref.shape[-1]
    for offset, vector in opened:
        left = dense_ref[offset, clusters]
        count, height, _ = left.shape
        value = jnp.dot(
            left.reshape(count * height, depth), vector[0:depth, :], preferred_element_type=jnp.float32
        )
        value = value.reshape(count, 2, height // 2, value.shape[1])
        yield value[:, 0] - energy * value[:, 1]


def centers(opened, depth):
    return [vector[depth : depth + EXTRA, :].astype(jnp.float32)[:1] for _, vector in opened]


def work(dense, items, lanes):
    return 2 * len(items) * dense.shape[1] * dense.shape[2] * dense.shape[3] * lanes


def couple(dense, vectors, energies, sums, after=None, weight=1):
    _, clusters, height, depth = dense.shape
    lanes = vectors.lanes
    count = len(vectors.arrays)
    outs = 2 if vectors.rows > depth else 1
    had = len(sums)

    def kernel(dense_ref, energies_ref, *refs):
        refs = list(refs[1:] if after is not None else refs)
        vector_refs, sum_refs = refs[:count], refs[count : count + had]
        out_refs, scratch = refs[count + had : count + had + outs], refs[count + had + outs :]
        energy = wide([energies_ref[...]] * (lanes // energies_ref.shape[1]))
        opened = vectors.open(vector_refs, scratch)
        weights = centers(opened, depth) if outs == 2 else [None] * len(opened)

        @pl.loop(0, clusters // BATCH)
        def _(batch):
            here = pl.ds(batch * BATCH, BATCH)
            values = [ref[here] for ref in sum_refs]
            for weight, part in zip(weights, products(dense_ref, opened, here, energy)):
                terms = [part] if weight is None else [part, weight * part]
                values = [v + t for v, t in zip(values, terms)] if values else terms
            for ref, value in zip(out_refs, values):
                ref[here] = value

    order = [] if after is None else [after]
    inputs = [dense, energies, *order, *vectors.arrays, *sums]
    shape = jax.ShapeDtypeStruct((clusters, height // 2, lanes), jnp.float32)
    return call(
        kernel,
        "couple",
        [shape] * outs,
        [vmem()] * 2
        + [pl.BlockSpec(memory_space=pl.ANY)] * len(order)
        + [vmem()] * (len(vectors.arrays) + had),
        vectors.scratch,
        flops=weight * work(dense, vectors.items, lanes),
        moved=4 * MIB,
    )(*inputs)


def finish_first(plan, dense, vectors, energies, value_sum, right_side, level, own, readers):
    _, clusters, height, depth = dense.shape
    lanes = vectors.lanes
    fields = right_side.shape[0]
    width = height // 2
    count = len(vectors.arrays)
    keys = plan.direct()
    outs = len(keys) + 1

    def kernel(dense_ref, energies_ref, *refs):
        vector_refs, refs = refs[:count], refs[count:]
        sum_ref, right_ref, level_ref, own_ref, readers_ref, image_ref, outgoing = refs[:7]
        messages, scratch = refs[7 : 7 + outs], refs[7 + outs :]
        energy = wide([energies_ref[...]] * fields)
        opened = vectors.open(vector_refs, scratch)
        (center,) = centers([(0, own_ref)], depth)

        @pl.loop(0, clusters // BATCH)
        def _(batch):
            here = pl.ds(batch * BATCH, BATCH)
            value = sum_ref[here]
            for part in products(dense_ref, opened, here, energy):
                value = value + part
            for local in range(BATCH):
                cluster = batch * BATCH + local
                rows = pl.ds(pl.multiple_of(cluster * width, width), width)
                right = wide([right_ref[f, rows, :] for f in range(fields)])
                image = wide([level_ref[cluster]] * fields) * right + value[local]
                image_ref[cluster] = image
                outgoing[rows, :] = (image - center * right).astype(jnp.bfloat16)

        fill(plan, keys, readers_ref, outgoing, messages, width)

    image, full, *messages, out = call(
        kernel,
        "finish_first",
        [
            jax.ShapeDtypeStruct((clusters, width, lanes), jnp.float32),
            jax.ShapeDtypeStruct((clusters * width, lanes), jnp.bfloat16),
        ]
        + [jax.ShapeDtypeStruct((depth, lanes), jnp.bfloat16)] * outs,
        [vmem()] * (2 + count + 4) + [smem()],
        vectors.scratch,
        flops=work(dense, vectors.items, lanes),
        moved=8 * MIB,
    )(dense, energies, *vectors.arrays, value_sum, right_side, level, own, readers)
    return image, full, dict(zip(keys, messages)), out


def guesses(lines, fields):
    orbitals = lines.shape[1] // fields
    alphas, growths = [], []
    for column in field_sums(lines, fields):
        norm, bend, square = column[0:1], column[1:2], column[2:3]
        norm = jnp.maximum(norm, 1e-30)
        alpha = norm / jnp.maximum(bend, 4.0 * norm)
        alphas.append(alpha)
        growths.append(jnp.clip(alpha * alpha * square / norm, 1.0, 2.0))
    return per_field(alphas, orbitals), per_field(growths, orbitals)


def prepare(right_side, image, after):
    fields, rows, orbitals = right_side.shape
    clusters, width, lanes = image.shape

    def kernel(right_ref, image_ref, _, lines_ref, kept):
        kept[...] = jnp.zeros_like(kept)

        def sweep(base, terms):
            @pl.loop(0, clusters)
            def _(cluster):
                here = pl.ds(pl.multiple_of(cluster * width, width), width)
                right = wide([right_ref[f, here, :] for f in range(fields)])
                for index, term in enumerate(terms(right, image_ref[cluster])):
                    kept[base + index] += folded(term)

        sweep(0, lambda right, first: (right * right, right * first, first * first))
        alpha, growth = guesses(lined([kept[i] for i in range(3)], 8), fields)

        def later_terms(right, first):
            step = alpha * first
            residual = right - step
            return residual * residual, residual * first, (growth * right - step) * first

        sweep(3, later_terms)
        lines_ref[...] = lined([kept[i] for i in range(6)], 8)
        lines_ref[6:7, :] = alpha
        lines_ref[7:8, :] = growth

    return call(
        kernel,
        "prepare",
        jax.ShapeDtypeStruct((8, lanes), jnp.float32),
        [vmem(), vmem(), pl.BlockSpec(memory_space=pl.ANY)],
        [pltpu.VMEM((6, 8, lanes), jnp.float32)],
        flops=8 * MIB,
        moved=4 * MIB,
    )(right_side, image, after)


def finish_second(dense, vectors, energies, value_sum, right_side, level, image, weighted, lines, devices):
    _, clusters, height, _ = dense.shape
    lanes = vectors.lanes
    fields = right_side.shape[0]
    width = height // 2
    count = len(vectors.arrays)

    def kernel(dense_ref, energies_ref, *refs):
        vector_refs, refs = refs[:count], refs[count:]
        sum_ref, right_ref, level_ref, image_ref, weighted_ref, lines_ref = refs[:6]
        later_ref, out_ref, kept, *scratch = refs[6:]
        energy = wide([energies_ref[...]] * fields)
        alpha, growth = lines_ref[6:7, :], lines_ref[7:8, :]
        kept[...] = jnp.zeros_like(kept)
        opened = vectors.open(vector_refs, scratch)

        @pl.loop(0, clusters // BATCH)
        def _(batch):
            here = pl.ds(batch * BATCH, BATCH)
            value = sum_ref[here] + weighted_ref[here]
            for part in products(dense_ref, opened, here, energy):
                value = value + part
            for local in range(BATCH):
                cluster = batch * BATCH + local
                rows = pl.ds(pl.multiple_of(cluster * width, width), width)
                right = wide([right_ref[f, rows, :] for f in range(fields)])
                first = image_ref[cluster]
                later = wide([level_ref[cluster]] * fields) * first + value[local]
                later_ref[cluster] = later
                direction = growth * right - alpha * first
                for index, left in enumerate((direction, right, first)):
                    kept[index] += folded(left * later)

        block = jnp.concatenate([lines_ref[0:6, :], lined([kept[i] for i in range(3)], 10)], axis=0)
        orbitals = lanes // fields
        line, lane = (lax.broadcasted_iota(jnp.int32, (16, 128), d) for d in (0, 1))
        rows = []
        for f, column in enumerate(field_sums(block, fields)):
            first_lane = slice(f * orbitals, f * orbitals + 1)
            filled = jnp.broadcast_to(column, (16, 128))
            filled = jnp.where(line == 9, jnp.broadcast_to(alpha[:, first_lane], (16, 128)), filled)
            filled = jnp.where(line == 10, jnp.broadcast_to(growth[:, first_lane], (16, 128)), filled)
            rows.append(jnp.sum(jnp.where(line == lane, filled, 0.0), axis=0, keepdims=True))
        rows.append(jnp.zeros((8 - fields, 128), jnp.float32))
        out_ref[...] = jnp.broadcast_to(jnp.concatenate(rows, axis=0)[None], out_ref.shape)

    return call(
        kernel,
        "finish_second",
        [
            jax.ShapeDtypeStruct((clusters, width, lanes), jnp.float32),
            jax.ShapeDtypeStruct((devices, 8, 128), jnp.float32),
        ],
        [vmem()] * (2 + count + 6),
        [pltpu.VMEM((3, 8, lanes), jnp.float32)] + vectors.scratch,
        flops=work(dense, vectors.items, lanes),
        moved=8 * MIB,
    )(dense, energies, *vectors.arrays, value_sum, right_side, level, image, weighted, lines)


def step_sizes(gathered, fields, orbitals):
    rows = gathered.reshape(-1, 128)
    flat = wide([jnp.transpose(rows[i : i + 128]) for i in range(0, rows.shape[0], 128)])
    line = [flat[i : i + 1, :] for i in range(11)]
    place = lax.broadcasted_iota(jnp.int32, line[0].shape, 1) & 7
    whole = lambda v: [
        jnp.sum(jnp.where(place == f, v, 0.0), axis=1, keepdims=True) for f in range(fields)
    ]

    def back(values):
        row = jnp.zeros_like(line[0])
        for f, value in enumerate(values):
            row = jnp.where(place == f, jnp.broadcast_to(value, row.shape), row)
        return row

    norm = whole(line[0])
    alpha = [n / b for n, b in zip(norm, whole(line[1]))]
    growth = [a * a * s / n for a, s, n in zip(alpha, whole(line[2]), norm)]
    off, more = back(alpha) - line[9], back(growth) - line[10]
    after = whole(line[3] - 2.0 * off * line[4] + off * off * line[2])
    bend = whole(
        (line[10] * line[5] - line[9] * line[6])
        + more * (line[5] + line[10] * line[1] - line[9] * line[7])
        - off * (line[6] + line[10] * line[2] - line[9] * line[8])
        + more * more * line[1]
        - more * off * (line[7] + line[2])
        + off * off * line[8]
    )
    gain = [a / b for a, b in zip(after, bend)]
    return [per_field(v, orbitals) for v in (alpha, growth, gain)]


def final(right_side, image, later, gathered):
    fields, rows, orbitals = right_side.shape
    clusters, width, lanes = image.shape
    blocks = 4
    each = clusters // blocks

    def kernel(right_ref, image_ref, later_ref, gathered_ref, solution_ref, residual_ref, steps):
        step = pl.program_id(0)

        @pl.when(step == 0)
        def _():
            alpha, growth, gain = step_sizes(gathered_ref[...], fields, orbitals)
            steps[0:1, :] = alpha + gain * growth
            steps[1:2, :] = gain * alpha

        for local in range(each):
            cluster = step * each + local
            rows = pl.ds(pl.multiple_of(cluster * width, width), width)
            here = slice(local * width, (local + 1) * width)
            for field in range(fields):
                part = slice(field * orbitals, (field + 1) * orbitals)
                one, two = steps[0:1, part], steps[1:2, part]
                right = right_ref[field, rows, :]
                first = image_ref[cluster, :, part]
                later = later_ref[cluster, :, part]
                solution_ref[field, here, :] = one * right - two * first
                residual_ref[field, here, :] = (right - one * first) + two * later

    vector = pl.BlockSpec((fields, each * width, orbitals), lambda i: (0, i, 0))
    shape = jax.ShapeDtypeStruct(right_side.shape, jnp.float32)
    return pl.pallas_call(
        kernel,
        grid=(blocks,),
        out_shape=[shape, shape],
        in_specs=[vmem()] * 4,
        out_specs=[vector, vector],
        scratch_shapes=[pltpu.VMEM((8, lanes), jnp.float32)],
        compiler_params=pltpu.CompilerParams(vmem_limit_bytes=12 * MIB),
        name="final",
    )(right_side, image, later, gathered)


def body(right_side, onsite, energies, ks_tiles, correlation_tiles, tile_slot, readers):
    span, served = readers.shape[1:]
    clusters, _, width, _ = ks_tiles.shape
    rows = lax.axis_size("row")
    devices = rows * lax.axis_size("col")
    onsite = onsite.reshape(-1, width)
    energies = energies.reshape(1, -1)
    plan = Plan(rows, span, rows == 8 and span == 7)
    readers = jnp.swapaxes(readers, 1, 2)

    def begin(weight):
        return lambda items: couple(dense, Vectors(plan, items), energies, [], weight=weight)

    def partial(items, sums):
        for group in (items[3:-2], items[-2:-1]):
            sums = couple(dense, Vectors(plan, group), energies, sums)
        return sums, Vectors(plan, items[-1:])

    early, full = pack(plan, readers, right_side, onsite)
    direct, own, full = deal(plan, readers, full, served, width)
    direct = early | direct
    dense = spread(tile_slot, ks_tiles, correlation_tiles, span, served)
    items, sums, chosen, _ = exchange(plan, readers, direct, own, full, None, begin(8), served, width)
    level = levels(onsite)
    sums, last = partial(items, sums)
    image, full, direct, out = finish_first(
        plan, dense, last, energies, sums[0], right_side, level, own, readers
    )

    items, begun, _, mark = exchange(plan, readers, direct, out, full, chosen, begin(1), served, width)
    lines = prepare(right_side, image, mark)
    _, weighted = couple(dense, last, energies, sums, mark)
    (value,), last = partial(items, begun)
    later, gathered = finish_second(
        dense, last, energies, value, right_side, level, image, weighted, lines, devices
    )
    gathered = lax.all_to_all(gathered, ("row", "col"), 0, 0)
    return tuple(final(right_side, image, later, gathered))


def solution(mesh):
    placed = (
        P(None, "row", "col"),
        P("row"),
        P("col"),
        P("row", None, None, None),
        P("row", None, None, None),
        P("row", None),
        P("row", None, None),
    )
    return jax.shard_map(
        body,
        mesh=mesh,
        in_specs=placed,
        out_specs=(P(None, "row", "col"), P(None, "row", "col")),
        check_vma=False,
    )
```

```python
import functools

import jax
import jax.numpy as jnp
from jax import lax
from jax.experimental import pallas as pl
from jax.experimental.pallas import tpu as pltpu
from jax.sharding import PartitionSpec as P

MIB = 2**20
EXTRA = 16
BATCH = 2


def shifted(array, axis, by):
    count = lax.axis_size(axis)
    return lax.ppermute(array, axis, [(i, (i + by) % count) for i in range(count)])


def vmem():
    return pl.BlockSpec(memory_space=pltpu.VMEM)


def smem():
    return pl.BlockSpec(memory_space=pltpu.SMEM)


def call(kernel, name, out_shape, specs, scratch=(), flops=0, moved=MIB, limit=12):
    return pl.pallas_call(
        kernel,
        out_shape=out_shape,
        in_specs=specs,
        out_specs=jax.tree.map(lambda _: vmem(), out_shape),
        scratch_shapes=list(scratch),
        compiler_params=pltpu.CompilerParams(vmem_limit_bytes=limit * MIB),
        cost_estimate=pl.CostEstimate(flops=flops, bytes_accessed=moved, transcendentals=0),
        name=name,
    )


def wide(parts):
    return jnp.concatenate(parts, axis=1)


def folded(term):
    return jnp.sum(term.reshape(-1, 8, term.shape[-1]), axis=0)


def lined(parts, lines):
    parts = [jnp.sum(p, axis=0, keepdims=True) for p in parts]
    parts.append(jnp.zeros((lines - len(parts), parts[0].shape[1]), jnp.float32))
    return jnp.concatenate(parts, axis=0)


def per_field(values, orbitals):
    return wide([jnp.broadcast_to(v, (1, orbitals)) for v in values])


def field_sums(lines, fields):
    orbitals = lines.shape[1] // fields
    return [
        jnp.sum(lines[:, f * orbitals : (f + 1) * orbitals], axis=1, keepdims=True)
        for f in range(fields)
    ]


class Plan:
    def __init__(self, count, span, relayed):
        self.count, self.span, self.middle, self.relayed = count, span, (span - 1) // 2, relayed

    def offset(self, source, reader):
        value = lax.rem(source - reader + (self.middle + self.count), self.count)
        return jnp.minimum(value, self.span - 1) if self.relayed else value

    def early(self):
        return [2] if self.relayed else self.direct()

    def direct(self):
        if self.relayed:
            return [2, 3, 1, 7]
        far = range(self.middle, 0, -1)
        return [by for f in far for by in (f, -f)]

    def reader(self, key, me):
        return me ^ key if self.relayed else lax.rem(me + key + self.count, self.count)

    def source(self, key, me):
        return me ^ key if self.relayed else lax.rem(me - key + self.count, self.count)

    def pairs(self, key):
        if not self.relayed:
            return [(i, (i + key) % self.count) for i in range(self.count)]
        return [(i, i ^ key) for i in range(self.count) if key < 4 or i not in INNER]


INNER = (2, 3, 4, 5)


def is_inner(me):
    return (me >= INNER[0]) & (me <= INNER[-1])


def pack(plan, readers, right_side, onsite):
    fields, rows, orbitals = right_side.shape
    served = readers.shape[1]
    clusters, width = onsite.shape
    lanes = fields * orbitals
    keys = plan.early()

    def kernel(readers_hbm, right_hbm, onsite_hbm, *refs):
        messages, rounded = refs[: len(keys)], refs[len(keys)]
        readers_ref, right_ref, onsite_ref, sems, more = refs[len(keys) + 1 :]
        copies = []
        for cluster in range(clusters):
            here = pl.ds(cluster * width, width)
            copies.append(
                pltpu.make_async_copy(
                    right_hbm.at[:, here, :], right_ref.at[:, here, :], sems.at[cluster]
                )
            )
        others = [
            pltpu.make_async_copy(onsite_hbm, onsite_ref, more.at[0]),
            pltpu.make_async_copy(readers_hbm, readers_ref, more.at[1]),
        ]
        for copy in copies[:1] + others + copies[1:]:
            copy.start()
        others[0].wait()
        norm = [jnp.zeros((8, orbitals), jnp.float32)] * fields
        heavy = [jnp.zeros((8, orbitals), jnp.float32)] * fields
        for cluster in range(clusters):
            copies[cluster].wait()
            weight = jnp.broadcast_to(onsite_ref[cluster : cluster + 1, :], (8, width))
            here = slice(cluster * width, (cluster + 1) * width)
            for field in range(fields):
                right = right_ref[field, here, :]
                rounded[here, field * orbitals : (field + 1) * orbitals] = right.astype(jnp.bfloat16)
                square = right * right
                norm[field] += folded(square)
                heavy[field] += jnp.dot(weight, square, preferred_element_type=jnp.float32)
        centers = [
            jnp.sum(h[:1], axis=1, keepdims=True)
            / jnp.maximum(jnp.sum(jnp.sum(n, axis=0, keepdims=True), axis=1, keepdims=True), 1e-30)
            for h, n in zip(heavy, norm)
        ]
        others[1].wait()
        rest = jnp.broadcast_to(per_field(centers, orbitals), (EXTRA, lanes))
        line, lane = (lax.broadcasted_iota(jnp.int32, (EXTRA, lanes), d) for d in (0, 1))
        for offset in range(readers_ref.shape[2]):
            for slot in range(served):
                here = (line == offset + 1) & (lane == slot)
                rest = jnp.where(here, readers_ref[0, slot, offset].astype(jnp.float32), rest)
        rounded[clusters * width :, :] = rest.astype(jnp.bfloat16)
        fill(plan, keys, readers_ref, rounded, messages, width)

    message = jax.ShapeDtypeStruct((served * width + EXTRA, lanes), jnp.bfloat16)
    full = jax.ShapeDtypeStruct((clusters * width + EXTRA, lanes), jnp.bfloat16)
    *messages, full = call(
        kernel,
        "pack",
        [message] * len(keys) + [full],
        [pl.BlockSpec(memory_space=pltpu.HBM)] * 3,
        [
            pltpu.SMEM(readers.shape, readers.dtype),
            pltpu.VMEM(right_side.shape, jnp.float32),
            pltpu.VMEM(onsite.shape, jnp.float32),
            pltpu.SemaphoreType.DMA((clusters,)),
            pltpu.SemaphoreType.DMA((2,)),
        ],
        limit=52,
    )(readers, right_side, onsite)
    return dict(zip(keys, messages)), full


def deal(plan, readers, full, served, width):
    keys = [key for key in plan.direct() if key not in plan.early()]
    lanes = full.shape[1]

    def kernel(readers_ref, full_ref, same_ref, *messages):
        fill(plan, keys, readers_ref, full_ref, messages, width)

    message = jax.ShapeDtypeStruct((served * width + EXTRA, lanes), jnp.bfloat16)
    full, *messages, own = pl.pallas_call(
        kernel,
        out_shape=[jax.ShapeDtypeStruct(full.shape, full.dtype)] + [message] * (len(keys) + 1),
        in_specs=[smem(), vmem()],
        out_specs=[vmem()] * (len(keys) + 2),
        input_output_aliases={1: 0},
        compiler_params=pltpu.CompilerParams(vmem_limit_bytes=12 * MIB),
        cost_estimate=pl.CostEstimate(flops=0, bytes_accessed=MIB, transcendentals=0),
        name="deal",
    )(readers, full)
    return dict(zip(keys, messages)), own, full


def fill(plan, keys, readers_ref, rounded, messages, width):
    me = lax.axis_index("row")
    offsets = [plan.offset(me, plan.reader(key, me)) for key in keys] + [plan.middle]
    for offset, message in zip(offsets, messages):
        served = readers_ref.shape[1]
        gather([readers_ref[0, slot, offset] for slot in range(served)], rounded, message, width)


def gather(clusters, rounded, message, width):
    for slot, cluster in enumerate(clusters):
        start = pl.multiple_of(cluster * width, width)
        message[slot * width : (slot + 1) * width, :] = rounded[pl.ds(start, width), :]
    used = len(clusters) * width
    if message.shape[0] > used:
        message[used:, :] = rounded[rounded.shape[0] - EXTRA :, :]


def relay(plan, readers, mine, full, chosen, after, served, width):
    lanes = full.shape[1]
    extra = EXTRA if chosen is None else 0
    message = jax.ShapeDtypeStruct((served * width + extra, lanes), jnp.bfloat16)

    def kernel(*refs):
        readers_ref, mine_ref, full_ref, _, *refs = refs
        me = lax.axis_index("row")
        *messages, chosen_ref = refs if chosen is None else [*refs[1:], refs[0]]
        if chosen is None:
            base = full_ref.shape[0] - EXTRA
            table = full_ref[base : base + EXTRA, 0:width].astype(jnp.float32)
            line, lane = (lax.broadcasted_iota(jnp.int32, table.shape, d) for d in (0, 1))
            for index, reader in enumerate((me, me ^ 1, me ^ 3)):
                offset = plan.offset(me ^ 6, reader)
                for slot in range(served):
                    here = (line == offset + 1) & (lane == slot)
                    chosen_ref[index, slot] = jnp.sum(jnp.where(here, table, 0.0)).astype(jnp.int32)

        @pl.when(is_inner(me))
        def _():
            for index, out in enumerate(messages):
                gather([chosen_ref[index, slot] for slot in range(served)], full_ref, out, width)

        @pl.when(jnp.logical_not(is_inner(me)))
        def _():
            for key, out in zip((6, 5), messages[1:]):
                offset = plan.offset(me, me ^ key)
                clusters = [readers_ref[0, slot, offset] for slot in range(served)]
                gather(clusters, mine_ref, out, width)

    inputs = [readers, mine, full, after] + ([] if chosen is None else [chosen])
    specs = [smem(), vmem(), vmem(), pl.BlockSpec(memory_space=pl.ANY)]
    specs += [] if chosen is None else [smem()]
    shapes, outs = [message] * 3, [vmem()] * 3
    if chosen is None:
        shapes.append(jax.ShapeDtypeStruct((3, served), jnp.int32))
        outs.append(smem())
    *messages, last = pl.pallas_call(
        kernel,
        out_shape=shapes,
        in_specs=specs,
        out_specs=outs,
        compiler_params=pltpu.CompilerParams(vmem_limit_bytes=12 * MIB),
        cost_estimate=pl.CostEstimate(flops=0, bytes_accessed=MIB, transcendentals=0),
        name="relay",
    )(*inputs)
    return (messages, last) if chosen is None else (messages + [last], chosen)


def exchange(plan, readers, direct, own, full, chosen, begin, served, width):
    sent = {k: lax.ppermute(m, "row", plan.pairs(k)) for k, m in direct.items()}
    if not plan.relayed:
        items = [(own, 0)] + [(sent[k], k) for k in plan.direct()]
        sums = begin(items[:2])
        return items, sums, None, sums[0]
    theirs = lax.ppermute(full, "row", [(i, i ^ 6) for i in INNER])
    items = [(own, 0), (sent[2], 2), (sent[3], 3), (sent[1], 1)]
    sums = begin(items[:2])
    (mine, near, far), chosen = relay(
        plan, readers, full, theirs, chosen, sums[0], served, width
    )
    near = lax.ppermute(near, "row", [(i, i ^ (1 if i in INNER else 6)) for i in range(plan.count)])
    far = lax.ppermute(far, "row", [(i, i ^ (3 if i in INNER else 5)) for i in range(plan.count)])
    items += [((mine, sent[7]), (6, 7)), (far, 5), (near, (7, 6))]
    return items, sums, chosen, mine


class Vectors:
    def __init__(self, plan, items):
        self.plan, self.items = plan, items
        self.arrays, self.scratch = [], []
        for value, _ in items:
            many = isinstance(value, tuple)
            self.arrays += list(value) if many else [value]
            if many:
                self.scratch.append(pltpu.VMEM(value[0].shape, value[0].dtype))
        self.lanes = self.arrays[0].shape[1]
        self.rows = self.arrays[0].shape[0]

    def open(self, refs, scratch):
        refs, scratch = list(refs), list(scratch)
        me = lax.axis_index("row")
        opened = []
        for value, key in self.items:
            if not self.plan.relayed:
                opened.append((self.plan.middle - key, refs.pop(0)))
                continue
            inner, outer = key if isinstance(key, tuple) else (key, key)
            held = refs.pop(0)
            if isinstance(value, tuple):
                kept, held, other = held, scratch.pop(0), refs.pop(0)

                @pl.when(is_inner(me))
                def _():
                    held[...] = kept[...]

                @pl.when(jnp.logical_not(is_inner(me)))
                def _():
                    held[...] = other[...]

            source = jnp.where(is_inner(me), me ^ inner, me ^ outer)
            opened.append((self.plan.offset(source, me), held))
        return opened


def levels(onsite):
    clusters, width = onsite.shape

    def kernel(onsite_ref, level_ref):
        for cluster in range(clusters):
            level_ref[cluster] = jnp.transpose(
                jnp.broadcast_to(onsite_ref[cluster : cluster + 1, :], (width, width))
            )

    shape = jax.ShapeDtypeStruct((clusters, width, width), jnp.float32)
    return call(kernel, "levels", shape, [vmem()])(onsite)


def spread(tile_slot, ks_tiles, correlation_tiles, span, served):
    clusters, _, width, _ = ks_tiles.shape
    slots = span * served

    def kernel(slot_ref, ks_ref, correlation_ref, out_ref, where):
        @pl.loop(0, clusters)
        def _(cluster):
            for kind, ref in enumerate((ks_ref, correlation_ref)):
                count = ref.shape[1]
                for slot in range(slots):
                    where[slot] = count
                for tile in range(count):
                    where[slot_ref[cluster, tile]] = tile
                for slot in range(slots):
                    tile = where[slot]
                    block = ref[cluster, jnp.minimum(tile, count - 1)]
                    block = jnp.where(tile < count, block, jnp.zeros_like(block))
                    lane = slot % served * width
                    out_ref[
                        slot // served, cluster, kind * width : (kind + 1) * width, lane : lane + width
                    ] = block

    return call(
        kernel,
        "spread",
        jax.ShapeDtypeStruct((span, clusters, 2 * width, served * width), jnp.bfloat16),
        [smem(), vmem(), vmem()],
        [pltpu.SMEM((slots,), jnp.int32)],
        moved=16 * MIB,
    )(tile_slot, ks_tiles, correlation_tiles)


def products(dense_ref, opened, clusters, energy):
    depth = dense_ref.shape[-1]
    for offset, vector in opened:
        left = dense_ref[offset, clusters]
        count, height, _ = left.shape
        value = jnp.dot(
            left.reshape(count * height, depth), vector[0:depth, :], preferred_element_type=jnp.float32
        )
        value = value.reshape(count, 2, height // 2, value.shape[1])
        yield value[:, 0] - energy * value[:, 1]


def centers(opened, depth):
    return [vector[depth : depth + EXTRA, :].astype(jnp.float32)[:1] for _, vector in opened]


def work(dense, items, lanes):
    return 2 * len(items) * dense.shape[1] * dense.shape[2] * dense.shape[3] * lanes


def couple(dense, vectors, energies, sums, after=None, weight=1):
    _, clusters, height, depth = dense.shape
    lanes = vectors.lanes
    count = len(vectors.arrays)
    outs = 2 if vectors.rows > depth else 1
    had = len(sums)

    def kernel(dense_ref, energies_ref, *refs):
        refs = list(refs[1:] if after is not None else refs)
        vector_refs, sum_refs = refs[:count], refs[count : count + had]
        out_refs, scratch = refs[count + had : count + had + outs], refs[count + had + outs :]
        energy = wide([energies_ref[...]] * (lanes // energies_ref.shape[1]))
        opened = vectors.open(vector_refs, scratch)
        weights = centers(opened, depth) if outs == 2 else [None] * len(opened)

        @pl.loop(0, clusters // BATCH)
        def _(batch):
            here = pl.ds(batch * BATCH, BATCH)
            values = [ref[here] for ref in sum_refs]
            for weight, part in zip(weights, products(dense_ref, opened, here, energy)):
                terms = [part] if weight is None else [part, weight * part]
                values = [v + t for v, t in zip(values, terms)] if values else terms
            for ref, value in zip(out_refs, values):
                ref[here] = value

    order = [] if after is None else [after]
    inputs = [dense, energies, *order, *vectors.arrays, *sums]
    shape = jax.ShapeDtypeStruct((clusters, height // 2, lanes), jnp.float32)
    return call(
        kernel,
        "couple",
        [shape] * outs,
        [vmem()] * 2
        + [pl.BlockSpec(memory_space=pl.ANY)] * len(order)
        + [vmem()] * (len(vectors.arrays) + had),
        vectors.scratch,
        flops=weight * work(dense, vectors.items, lanes),
        moved=4 * MIB,
    )(*inputs)


def finish_first(plan, dense, vectors, energies, value_sum, right_side, level, own, readers):
    _, clusters, height, depth = dense.shape
    lanes = vectors.lanes
    fields = right_side.shape[0]
    width = height // 2
    count = len(vectors.arrays)
    keys = plan.direct()
    outs = len(keys) + 1

    def kernel(dense_ref, energies_ref, *refs):
        vector_refs, refs = refs[:count], refs[count:]
        sum_ref, right_ref, level_ref, own_ref, readers_ref, image_ref, outgoing = refs[:7]
        messages, scratch = refs[7 : 7 + outs], refs[7 + outs :]
        energy = wide([energies_ref[...]] * fields)
        opened = vectors.open(vector_refs, scratch)
        (center,) = centers([(0, own_ref)], depth)

        @pl.loop(0, clusters // BATCH)
        def _(batch):
            here = pl.ds(batch * BATCH, BATCH)
            value = sum_ref[here]
            for part in products(dense_ref, opened, here, energy):
                value = value + part
            for local in range(BATCH):
                cluster = batch * BATCH + local
                rows = pl.ds(pl.multiple_of(cluster * width, width), width)
                right = wide([right_ref[f, rows, :] for f in range(fields)])
                image = wide([level_ref[cluster]] * fields) * right + value[local]
                image_ref[cluster] = image
                outgoing[rows, :] = (image - center * right).astype(jnp.bfloat16)

        fill(plan, keys, readers_ref, outgoing, messages, width)

    image, full, *messages, out = call(
        kernel,
        "finish_first",
        [
            jax.ShapeDtypeStruct((clusters, width, lanes), jnp.float32),
            jax.ShapeDtypeStruct((clusters * width, lanes), jnp.bfloat16),
        ]
        + [jax.ShapeDtypeStruct((depth, lanes), jnp.bfloat16)] * outs,
        [vmem()] * (2 + count + 4) + [smem()],
        vectors.scratch,
        flops=work(dense, vectors.items, lanes),
        moved=8 * MIB,
    )(dense, energies, *vectors.arrays, value_sum, right_side, level, own, readers)
    return image, full, dict(zip(keys, messages)), out


def guesses(lines, fields):
    orbitals = lines.shape[1] // fields
    alphas, growths = [], []
    for column in field_sums(lines, fields):
        norm, bend, square = column[0:1], column[1:2], column[2:3]
        norm = jnp.maximum(norm, 1e-30)
        alpha = norm / jnp.maximum(bend, 4.0 * norm)
        alphas.append(alpha)
        growths.append(jnp.clip(alpha * alpha * square / norm, 1.0, 2.0))
    return per_field(alphas, orbitals), per_field(growths, orbitals)


def prepare(right_side, image, after):
    fields, rows, orbitals = right_side.shape
    clusters, width, lanes = image.shape

    def kernel(right_ref, image_ref, _, lines_ref, kept):
        kept[...] = jnp.zeros_like(kept)

        def sweep(base, terms):
            @pl.loop(0, clusters)
            def _(cluster):
                here = pl.ds(pl.multiple_of(cluster * width, width), width)
                right = wide([right_ref[f, here, :] for f in range(fields)])
                for index, term in enumerate(terms(right, image_ref[cluster])):
                    kept[base + index] += folded(term)

        sweep(0, lambda right, first: (right * right, right * first, first * first))
        alpha, growth = guesses(lined([kept[i] for i in range(3)], 8), fields)

        def later_terms(right, first):
            step = alpha * first
            residual = right - step
            return residual * residual, residual * first, (growth * right - step) * first

        sweep(3, later_terms)
        lines_ref[...] = lined([kept[i] for i in range(6)], 8)
        lines_ref[6:7, :] = alpha
        lines_ref[7:8, :] = growth

    return call(
        kernel,
        "prepare",
        jax.ShapeDtypeStruct((8, lanes), jnp.float32),
        [vmem(), vmem(), pl.BlockSpec(memory_space=pl.ANY)],
        [pltpu.VMEM((6, 8, lanes), jnp.float32)],
        flops=8 * MIB,
        moved=4 * MIB,
    )(right_side, image, after)


def finish_second(dense, vectors, energies, value_sum, right_side, level, image, weighted, lines, devices):
    _, clusters, height, _ = dense.shape
    lanes = vectors.lanes
    fields = right_side.shape[0]
    width = height // 2
    count = len(vectors.arrays)

    def kernel(dense_ref, energies_ref, *refs):
        vector_refs, refs = refs[:count], refs[count:]
        sum_ref, right_ref, level_ref, image_ref, weighted_ref, lines_ref = refs[:6]
        later_ref, out_ref, kept, *scratch = refs[6:]
        energy = wide([energies_ref[...]] * fields)
        alpha, growth = lines_ref[6:7, :], lines_ref[7:8, :]
        kept[...] = jnp.zeros_like(kept)
        opened = vectors.open(vector_refs, scratch)

        @pl.loop(0, clusters // BATCH)
        def _(batch):
            here = pl.ds(batch * BATCH, BATCH)
            value = sum_ref[here] + weighted_ref[here]
            for part in products(dense_ref, opened, here, energy):
                value = value + part
            for local in range(BATCH):
                cluster = batch * BATCH + local
                rows = pl.ds(pl.multiple_of(cluster * width, width), width)
                right = wide([right_ref[f, rows, :] for f in range(fields)])
                first = image_ref[cluster]
                later = wide([level_ref[cluster]] * fields) * first + value[local]
                later_ref[cluster] = later
                direction = growth * right - alpha * first
                for index, left in enumerate((direction, right, first)):
                    kept[index] += folded(left * later)

        block = jnp.concatenate([lines_ref[0:6, :], lined([kept[i] for i in range(3)], 10)], axis=0)
        orbitals = lanes // fields
        line, lane = (lax.broadcasted_iota(jnp.int32, (16, 128), d) for d in (0, 1))
        rows = []
        for f, column in enumerate(field_sums(block, fields)):
            first_lane = slice(f * orbitals, f * orbitals + 1)
            filled = jnp.broadcast_to(column, (16, 128))
            filled = jnp.where(line == 9, jnp.broadcast_to(alpha[:, first_lane], (16, 128)), filled)
            filled = jnp.where(line == 10, jnp.broadcast_to(growth[:, first_lane], (16, 128)), filled)
            rows.append(jnp.sum(jnp.where(line == lane, filled, 0.0), axis=0, keepdims=True))
        rows.append(jnp.zeros((8 - fields, 128), jnp.float32))
        out_ref[...] = jnp.broadcast_to(jnp.concatenate(rows, axis=0)[None], out_ref.shape)

    return call(
        kernel,
        "finish_second",
        [
            jax.ShapeDtypeStruct((clusters, width, lanes), jnp.float32),
            jax.ShapeDtypeStruct((devices, 8, 128), jnp.float32),
        ],
        [vmem()] * (2 + count + 6),
        [pltpu.VMEM((3, 8, lanes), jnp.float32)] + vectors.scratch,
        flops=work(dense, vectors.items, lanes),
        moved=8 * MIB,
    )(dense, energies, *vectors.arrays, value_sum, right_side, level, image, weighted, lines)


def step_sizes(gathered, fields, orbitals):
    rows = gathered.reshape(-1, 128)
    flat = wide([jnp.transpose(rows[i : i + 128]) for i in range(0, rows.shape[0], 128)])
    line = [flat[i : i + 1, :] for i in range(11)]
    place = lax.broadcasted_iota(jnp.int32, line[0].shape, 1) & 7
    whole = lambda v: [
        jnp.sum(jnp.where(place == f, v, 0.0), axis=1, keepdims=True) for f in range(fields)
    ]

    def back(values):
        row = jnp.zeros_like(line[0])
        for f, value in enumerate(values):
            row = jnp.where(place == f, jnp.broadcast_to(value, row.shape), row)
        return row

    norm = whole(line[0])
    alpha = [n / b for n, b in zip(norm, whole(line[1]))]
    growth = [a * a * s / n for a, s, n in zip(alpha, whole(line[2]), norm)]
    off, more = back(alpha) - line[9], back(growth) - line[10]
    after = whole(line[3] - 2.0 * off * line[4] + off * off * line[2])
    bend = whole(
        (line[10] * line[5] - line[9] * line[6])
        + more * (line[5] + line[10] * line[1] - line[9] * line[7])
        - off * (line[6] + line[10] * line[2] - line[9] * line[8])
        + more * more * line[1]
        - more * off * (line[7] + line[2])
        + off * off * line[8]
    )
    gain = [a / b for a, b in zip(after, bend)]
    return [per_field(v, orbitals) for v in (alpha, growth, gain)]


def final(right_side, image, later, gathered):
    fields, rows, orbitals = right_side.shape
    clusters, width, lanes = image.shape
    blocks = 4
    each = clusters // blocks

    def kernel(right_ref, image_ref, later_ref, gathered_ref, solution_ref, residual_ref, steps):
        step = pl.program_id(0)

        @pl.when(step == 0)
        def _():
            alpha, growth, gain = step_sizes(gathered_ref[...], fields, orbitals)
            steps[0:1, :] = alpha + gain * growth
            steps[1:2, :] = gain * alpha

        for local in range(each):
            cluster = step * each + local
            rows = pl.ds(pl.multiple_of(cluster * width, width), width)
            here = slice(local * width, (local + 1) * width)
            for field in range(fields):
                part = slice(field * orbitals, (field + 1) * orbitals)
                one, two = steps[0:1, part], steps[1:2, part]
                right = right_ref[field, rows, :]
                first = image_ref[cluster, :, part]
                later = later_ref[cluster, :, part]
                solution_ref[field, here, :] = one * right - two * first
                residual_ref[field, here, :] = (right - one * first) + two * later

    vector = pl.BlockSpec((fields, each * width, orbitals), lambda i: (0, i, 0))
    shape = jax.ShapeDtypeStruct(right_side.shape, jnp.float32)
    return pl.pallas_call(
        kernel,
        grid=(blocks,),
        out_shape=[shape, shape],
        in_specs=[vmem()] * 4,
        out_specs=[vector, vector],
        scratch_shapes=[pltpu.VMEM((8, lanes), jnp.float32)],
        compiler_params=pltpu.CompilerParams(vmem_limit_bytes=12 * MIB),
        name="final",
    )(right_side, image, later, gathered)


def body(right_side, onsite, energies, ks_tiles, correlation_tiles, tile_slot, readers):
    span, served = readers.shape[1:]
    clusters, _, width, _ = ks_tiles.shape
    rows = lax.axis_size("row")
    devices = rows * lax.axis_size("col")
    onsite = onsite.reshape(-1, width)
    energies = energies.reshape(1, -1)
    plan = Plan(rows, span, rows == 8 and span == 7)
    readers = jnp.swapaxes(readers, 1, 2)

    def begin(weight):
        return lambda items: couple(dense, Vectors(plan, items), energies, [], weight=weight)

    def partial(items, sums):
        for group in (items[2:-2], items[-2:-1]):
            sums = couple(dense, Vectors(plan, group), energies, sums)
        return sums, Vectors(plan, items[-1:])

    early, full = pack(plan, readers, right_side, onsite)
    direct, own, full = deal(plan, readers, full, served, width)
    direct = early | direct
    dense = spread(tile_slot, ks_tiles, correlation_tiles, span, served)
    items, sums, chosen, _ = exchange(plan, readers, direct, own, full, None, begin(8), served, width)
    level = levels(onsite)
    sums, last = partial(items, sums)
    image, full, direct, out = finish_first(
        plan, dense, last, energies, sums[0], right_side, level, own, readers
    )

    items, begun, _, mark = exchange(plan, readers, direct, out, full, chosen, begin(1), served, width)
    lines = prepare(right_side, image, mark)
    _, weighted = couple(dense, last, energies, sums, mark)
    (value,), last = partial(items, begun)
    later, gathered = finish_second(
        dense, last, energies, value, right_side, level, image, weighted, lines, devices
    )
    gathered = lax.all_to_all(gathered, ("row", "col"), 0, 0)
    return tuple(final(right_side, image, later, gathered))


def solution(mesh):
    placed = (
        P(None, "row", "col"),
        P("row"),
        P("col"),
        P("row", None, None, None),
        P("row", None, None, None),
        P("row", None),
        P("row", None, None),
    )
    return jax.shard_map(
        body,
        mesh=mesh,
        in_specs=placed,
        out_specs=(P(None, "row", "col"), P(None, "row", "col")),
        check_vma=False,
    )
```

```python
import functools

import jax
import jax.numpy as jnp
from jax import lax
from jax.experimental import pallas as pl
from jax.experimental.pallas import tpu as pltpu
from jax.sharding import PartitionSpec as P

MIB = 2**20
EXTRA = 16
BATCH = 2


def shifted(array, axis, by):
    count = lax.axis_size(axis)
    return lax.ppermute(array, axis, [(i, (i + by) % count) for i in range(count)])


def vmem():
    return pl.BlockSpec(memory_space=pltpu.VMEM)


def smem():
    return pl.BlockSpec(memory_space=pltpu.SMEM)


def call(kernel, name, out_shape, specs, scratch=(), flops=0, moved=MIB, limit=12):
    return pl.pallas_call(
        kernel,
        out_shape=out_shape,
        in_specs=specs,
        out_specs=jax.tree.map(lambda _: vmem(), out_shape),
        scratch_shapes=list(scratch),
        compiler_params=pltpu.CompilerParams(vmem_limit_bytes=limit * MIB),
        cost_estimate=pl.CostEstimate(flops=flops, bytes_accessed=moved, transcendentals=0),
        name=name,
    )


def wide(parts):
    return jnp.concatenate(parts, axis=1)


def folded(term):
    return jnp.sum(term.reshape(-1, 8, term.shape[-1]), axis=0)


def lined(parts, lines):
    parts = [jnp.sum(p, axis=0, keepdims=True) for p in parts]
    parts.append(jnp.zeros((lines - len(parts), parts[0].shape[1]), jnp.float32))
    return jnp.concatenate(parts, axis=0)


def per_field(values, orbitals):
    return wide([jnp.broadcast_to(v, (1, orbitals)) for v in values])


def field_sums(lines, fields):
    orbitals = lines.shape[1] // fields
    return [
        jnp.sum(lines[:, f * orbitals : (f + 1) * orbitals], axis=1, keepdims=True)
        for f in range(fields)
    ]


class Plan:
    def __init__(self, count, span, relayed):
        self.count, self.span, self.middle, self.relayed = count, span, (span - 1) // 2, relayed

    def offset(self, source, reader):
        value = lax.rem(source - reader + (self.middle + self.count), self.count)
        return jnp.minimum(value, self.span - 1) if self.relayed else value

    def direct(self):
        if self.relayed:
            return [1, 2, 3, 7]
        far = range(self.middle, 0, -1)
        return [by for f in far for by in (f, -f)]

    def reader(self, key, me):
        return me ^ key if self.relayed else lax.rem(me + key + self.count, self.count)

    def source(self, key, me):
        return me ^ key if self.relayed else lax.rem(me - key + self.count, self.count)

    def pairs(self, key):
        if not self.relayed:
            return [(i, (i + key) % self.count) for i in range(self.count)]
        return [(i, i ^ key) for i in range(self.count) if key < 4 or i not in INNER]


INNER = (2, 3, 4, 5)


def is_inner(me):
    return (me >= INNER[0]) & (me <= INNER[-1])


def pack(plan, readers, right_side, onsite):
    fields, rows, orbitals = right_side.shape
    served = readers.shape[1]
    clusters, width = onsite.shape
    lanes = fields * orbitals
    keys = plan.direct()

    def kernel(readers_hbm, right_hbm, onsite_hbm, *refs):
        messages, rounded = refs[: len(keys) + 1], refs[len(keys) + 1]
        readers_ref, right_ref, onsite_ref, sems, more = refs[len(keys) + 2 :]
        copies = []
        for cluster in range(clusters):
            here = pl.ds(cluster * width, width)
            copies.append(
                pltpu.make_async_copy(
                    right_hbm.at[:, here, :], right_ref.at[:, here, :], sems.at[cluster]
                )
            )
        others = [
            pltpu.make_async_copy(onsite_hbm, onsite_ref, more.at[0]),
            pltpu.make_async_copy(readers_hbm, readers_ref, more.at[1]),
        ]
        for copy in copies[:1] + others + copies[1:]:
            copy.start()
        others[0].wait()
        norm = [jnp.zeros((8, orbitals), jnp.float32)] * fields
        heavy = [jnp.zeros((8, orbitals), jnp.float32)] * fields
        for cluster in range(clusters):
            copies[cluster].wait()
            weight = jnp.broadcast_to(onsite_ref[cluster : cluster + 1, :], (8, width))
            here = slice(cluster * width, (cluster + 1) * width)
            for field in range(fields):
                right = right_ref[field, here, :]
                rounded[here, field * orbitals : (field + 1) * orbitals] = right.astype(jnp.bfloat16)
                square = right * right
                norm[field] += folded(square)
                heavy[field] += jnp.dot(weight, square, preferred_element_type=jnp.float32)
        centers = [
            jnp.sum(h[:1], axis=1, keepdims=True)
            / jnp.maximum(jnp.sum(jnp.sum(n, axis=0, keepdims=True), axis=1, keepdims=True), 1e-30)
            for h, n in zip(heavy, norm)
        ]
        others[1].wait()
        rest = jnp.broadcast_to(per_field(centers, orbitals), (EXTRA, lanes))
        line, lane = (lax.broadcasted_iota(jnp.int32, (EXTRA, lanes), d) for d in (0, 1))
        for offset in range(readers_ref.shape[2]):
            for slot in range(served):
                here = (line == offset + 1) & (lane == slot)
                rest = jnp.where(here, readers_ref[0, slot, offset].astype(jnp.float32), rest)
        rounded[clusters * width :, :] = rest.astype(jnp.bfloat16)
        fill(plan, keys, readers_ref, rounded, messages, width)

    message = jax.ShapeDtypeStruct((served * width + EXTRA, lanes), jnp.bfloat16)
    full = jax.ShapeDtypeStruct((clusters * width + EXTRA, lanes), jnp.bfloat16)
    *messages, own, full = call(
        kernel,
        "pack",
        [message] * (len(keys) + 1) + [full],
        [pl.BlockSpec(memory_space=pltpu.HBM)] * 3,
        [
            pltpu.SMEM(readers.shape, readers.dtype),
            pltpu.VMEM(right_side.shape, jnp.float32),
            pltpu.VMEM(onsite.shape, jnp.float32),
            pltpu.SemaphoreType.DMA((clusters,)),
            pltpu.SemaphoreType.DMA((2,)),
        ],
        limit=51,
    )(readers, right_side, onsite)
    return dict(zip(keys, messages)), own, full


def fill(plan, keys, readers_ref, rounded, messages, width):
    me = lax.axis_index("row")
    offsets = [plan.offset(me, plan.reader(key, me)) for key in keys] + [plan.middle]
    for offset, message in zip(offsets, messages):
        served = readers_ref.shape[1]
        gather([readers_ref[0, slot, offset] for slot in range(served)], rounded, message, width)


def gather(clusters, rounded, message, width):
    for slot, cluster in enumerate(clusters):
        start = pl.multiple_of(cluster * width, width)
        message[slot * width : (slot + 1) * width, :] = rounded[pl.ds(start, width), :]
    used = len(clusters) * width
    if message.shape[0] > used:
        message[used:, :] = rounded[rounded.shape[0] - EXTRA :, :]


def relay(plan, readers, mine, full, chosen, after, served, width):
    lanes = full.shape[1]
    extra = EXTRA if chosen is None else 0
    message = jax.ShapeDtypeStruct((served * width + extra, lanes), jnp.bfloat16)

    def kernel(*refs):
        readers_ref, mine_ref, full_ref, _, *refs = refs
        me = lax.axis_index("row")
        *messages, chosen_ref = refs if chosen is None else [*refs[1:], refs[0]]
        if chosen is None:
            base = full_ref.shape[0] - EXTRA
            table = full_ref[base : base + EXTRA, 0:width].astype(jnp.float32)
            line, lane = (lax.broadcasted_iota(jnp.int32, table.shape, d) for d in (0, 1))
            for index, reader in enumerate((me, me ^ 1, me ^ 3)):
                offset = plan.offset(me ^ 6, reader)
                for slot in range(served):
                    here = (line == offset + 1) & (lane == slot)
                    chosen_ref[index, slot] = jnp.sum(jnp.where(here, table, 0.0)).astype(jnp.int32)

        @pl.when(is_inner(me))
        def _():
            for index, out in enumerate(messages):
                gather([chosen_ref[index, slot] for slot in range(served)], full_ref, out, width)

        @pl.when(jnp.logical_not(is_inner(me)))
        def _():
            for key, out in zip((6, 5), messages[1:]):
                offset = plan.offset(me, me ^ key)
                clusters = [readers_ref[0, slot, offset] for slot in range(served)]
                gather(clusters, mine_ref, out, width)

    inputs = [readers, mine, full, after] + ([] if chosen is None else [chosen])
    specs = [smem(), vmem(), vmem(), pl.BlockSpec(memory_space=pl.ANY)]
    specs += [] if chosen is None else [smem()]
    shapes, outs = [message] * 3, [vmem()] * 3
    if chosen is None:
        shapes.append(jax.ShapeDtypeStruct((3, served), jnp.int32))
        outs.append(smem())
    *messages, last = pl.pallas_call(
        kernel,
        out_shape=shapes,
        in_specs=specs,
        out_specs=outs,
        compiler_params=pltpu.CompilerParams(vmem_limit_bytes=12 * MIB),
        cost_estimate=pl.CostEstimate(flops=0, bytes_accessed=MIB, transcendentals=0),
        name="relay",
    )(*inputs)
    return (messages, last) if chosen is None else (messages + [last], chosen)


def exchange(plan, readers, direct, own, full, chosen, begin, near, served, width):
    sent = {k: lax.ppermute(m, "row", plan.pairs(k)) for k, m in direct.items()}
    if not plan.relayed:
        items = [(own, 0)] + [(sent[k], k) for k in plan.direct()]
        sums = begin(items[:3], None)
        return items, sums, None, sums[0]
    theirs = lax.ppermute(full, "row", [(i, i ^ 6) for i in INNER])
    items = [(own, 0)] + [(sent[k], k) for k in near]
    sums = begin(items[:3], theirs if chosen is None else None)
    (mine, near, far), chosen = relay(
        plan, readers, full, theirs, chosen, sums[0], served, width
    )
    near = lax.ppermute(near, "row", [(i, i ^ (1 if i in INNER else 6)) for i in range(plan.count)])
    far = lax.ppermute(far, "row", [(i, i ^ (3 if i in INNER else 5)) for i in range(plan.count)])
    items += [((mine, sent[7]), (6, 7)), (far, 5), (near, (7, 6))]
    return items, sums, chosen, mine


class Vectors:
    def __init__(self, plan, items):
        self.plan, self.items = plan, items
        self.arrays, self.scratch = [], []
        for value, _ in items:
            many = isinstance(value, tuple)
            self.arrays += list(value) if many else [value]
            if many:
                self.scratch.append(pltpu.VMEM(value[0].shape, value[0].dtype))
        self.lanes = self.arrays[0].shape[1]
        self.rows = self.arrays[0].shape[0]

    def open(self, refs, scratch):
        refs, scratch = list(refs), list(scratch)
        me = lax.axis_index("row")
        opened = []
        for value, key in self.items:
            if not self.plan.relayed:
                opened.append((self.plan.middle - key, refs.pop(0)))
                continue
            inner, outer = key if isinstance(key, tuple) else (key, key)
            held = refs.pop(0)
            if isinstance(value, tuple):
                kept, held, other = held, scratch.pop(0), refs.pop(0)

                @pl.when(is_inner(me))
                def _():
                    held[...] = kept[...]

                @pl.when(jnp.logical_not(is_inner(me)))
                def _():
                    held[...] = other[...]

            source = jnp.where(is_inner(me), me ^ inner, me ^ outer)
            opened.append((self.plan.offset(source, me), held))
        return opened


def levels(onsite):
    clusters, width = onsite.shape

    def kernel(onsite_ref, level_ref):
        for cluster in range(clusters):
            level_ref[cluster] = jnp.transpose(
                jnp.broadcast_to(onsite_ref[cluster : cluster + 1, :], (width, width))
            )

    shape = jax.ShapeDtypeStruct((clusters, width, width), jnp.float32)
    return call(kernel, "levels", shape, [vmem()])(onsite)


def spread(tile_slot, ks_tiles, correlation_tiles, span, served):
    clusters, _, width, _ = ks_tiles.shape
    slots = span * served

    def kernel(slot_ref, ks_ref, correlation_ref, out_ref, where):
        @pl.loop(0, clusters)
        def _(cluster):
            for kind, ref in enumerate((ks_ref, correlation_ref)):
                count = ref.shape[1]
                for slot in range(slots):
                    where[slot] = count
                for tile in range(count):
                    where[slot_ref[cluster, tile]] = tile
                for slot in range(slots):
                    tile = where[slot]
                    block = ref[cluster, jnp.minimum(tile, count - 1)]
                    block = jnp.where(tile < count, block, jnp.zeros_like(block))
                    lane = slot % served * width
                    out_ref[
                        slot // served, cluster, kind * width : (kind + 1) * width, lane : lane + width
                    ] = block

    return call(
        kernel,
        "spread",
        jax.ShapeDtypeStruct((span, clusters, 2 * width, served * width), jnp.bfloat16),
        [smem(), vmem(), vmem()],
        [pltpu.SMEM((slots,), jnp.int32)],
        moved=16 * MIB,
    )(tile_slot, ks_tiles, correlation_tiles)


def products(dense_ref, opened, clusters, energy):
    depth = dense_ref.shape[-1]
    for offset, vector in opened:
        left = dense_ref[offset, clusters]
        count, height, _ = left.shape
        value = jnp.dot(
            left.reshape(count * height, depth), vector[0:depth, :], preferred_element_type=jnp.float32
        )
        value = value.reshape(count, 2, height // 2, value.shape[1])
        yield value[:, 0] - energy * value[:, 1]


def centers(opened, depth):
    return [vector[depth : depth + EXTRA, :].astype(jnp.float32)[:1] for _, vector in opened]


def work(dense, items, lanes):
    return 2 * len(items) * dense.shape[1] * dense.shape[2] * dense.shape[3] * lanes


def couple(dense, vectors, energies, sums, after=None):
    _, clusters, height, depth = dense.shape
    lanes = vectors.lanes
    count = len(vectors.arrays)
    outs = 2 if vectors.rows > depth else 1
    had = len(sums)

    def kernel(dense_ref, energies_ref, *refs):
        refs = list(refs[1:] if after is not None else refs)
        vector_refs, sum_refs = refs[:count], refs[count : count + had]
        out_refs, scratch = refs[count + had : count + had + outs], refs[count + had + outs :]
        energy = wide([energies_ref[...]] * (lanes // energies_ref.shape[1]))
        opened = vectors.open(vector_refs, scratch)
        weights = centers(opened, depth) if outs == 2 else [None] * len(opened)

        @pl.loop(0, clusters // BATCH)
        def _(batch):
            here = pl.ds(batch * BATCH, BATCH)
            values = [ref[here] for ref in sum_refs]
            for weight, part in zip(weights, products(dense_ref, opened, here, energy)):
                terms = [part] if weight is None else [part, weight * part]
                values = [v + t for v, t in zip(values, terms)] if values else terms
            for ref, value in zip(out_refs, values):
                ref[here] = value

    order = [] if after is None else [after]
    inputs = [dense, energies, *order, *vectors.arrays, *sums]
    shape = jax.ShapeDtypeStruct((clusters, height // 2, lanes), jnp.float32)
    return call(
        kernel,
        "couple",
        [shape] * outs,
        [vmem()] * 2
        + [pl.BlockSpec(memory_space=pl.ANY)] * len(order)
        + [vmem()] * (len(vectors.arrays) + had),
        vectors.scratch,
        flops=work(dense, vectors.items, lanes),
        moved=4 * MIB,
    )(*inputs)


def finish_first(plan, dense, vectors, energies, value_sum, right_side, level, own, readers):
    _, clusters, height, depth = dense.shape
    lanes = vectors.lanes
    fields = right_side.shape[0]
    width = height // 2
    count = len(vectors.arrays)
    keys = plan.direct()
    outs = len(keys) + 1

    def kernel(dense_ref, energies_ref, *refs):
        vector_refs, refs = refs[:count], refs[count:]
        sum_ref, right_ref, level_ref, own_ref, readers_ref, image_ref, outgoing = refs[:7]
        messages, scratch = refs[7 : 7 + outs], refs[7 + outs :]
        energy = wide([energies_ref[...]] * fields)
        opened = vectors.open(vector_refs, scratch)
        (center,) = centers([(0, own_ref)], depth)

        @pl.loop(0, clusters // BATCH)
        def _(batch):
            here = pl.ds(batch * BATCH, BATCH)
            value = sum_ref[here]
            for part in products(dense_ref, opened, here, energy):
                value = value + part
            for local in range(BATCH):
                cluster = batch * BATCH + local
                rows = pl.ds(pl.multiple_of(cluster * width, width), width)
                right = wide([right_ref[f, rows, :] for f in range(fields)])
                image = wide([level_ref[cluster]] * fields) * right + value[local]
                image_ref[cluster] = image
                outgoing[rows, :] = (image - center * right).astype(jnp.bfloat16)

        fill(plan, keys, readers_ref, outgoing, messages, width)

    image, full, *messages, out = call(
        kernel,
        "finish_first",
        [
            jax.ShapeDtypeStruct((clusters, width, lanes), jnp.float32),
            jax.ShapeDtypeStruct((clusters * width, lanes), jnp.bfloat16),
        ]
        + [jax.ShapeDtypeStruct((depth, lanes), jnp.bfloat16)] * outs,
        [vmem()] * (2 + count + 4) + [smem()],
        vectors.scratch,
        flops=work(dense, vectors.items, lanes),
        moved=8 * MIB,
    )(dense, energies, *vectors.arrays, value_sum, right_side, level, own, readers)
    return image, full, dict(zip(keys, messages)), out


def guesses(lines, fields):
    orbitals = lines.shape[1] // fields
    alphas, growths = [], []
    for column in field_sums(lines, fields):
        norm, bend, square = column[0:1], column[1:2], column[2:3]
        norm = jnp.maximum(norm, 1e-30)
        alpha = norm / jnp.maximum(bend, 4.0 * norm)
        alphas.append(alpha)
        growths.append(jnp.clip(alpha * alpha * square / norm, 1.0, 2.0))
    return per_field(alphas, orbitals), per_field(growths, orbitals)


def prepare(right_side, image, after):
    fields, rows, orbitals = right_side.shape
    clusters, width, lanes = image.shape

    def kernel(right_ref, image_ref, _, lines_ref, kept):
        kept[...] = jnp.zeros_like(kept)

        def sweep(base, terms):
            @pl.loop(0, clusters)
            def _(cluster):
                here = pl.ds(pl.multiple_of(cluster * width, width), width)
                right = wide([right_ref[f, here, :] for f in range(fields)])
                for index, term in enumerate(terms(right, image_ref[cluster])):
                    kept[base + index] += folded(term)

        sweep(0, lambda right, first: (right * right, right * first, first * first))
        alpha, growth = guesses(lined([kept[i] for i in range(3)], 8), fields)

        def later_terms(right, first):
            step = alpha * first
            residual = right - step
            return residual * residual, residual * first, (growth * right - step) * first

        sweep(3, later_terms)
        lines_ref[...] = lined([kept[i] for i in range(6)], 8)
        lines_ref[6:7, :] = alpha
        lines_ref[7:8, :] = growth

    return call(
        kernel,
        "prepare",
        jax.ShapeDtypeStruct((8, lanes), jnp.float32),
        [vmem(), vmem(), pl.BlockSpec(memory_space=pl.ANY)],
        [pltpu.VMEM((6, 8, lanes), jnp.float32)],
        flops=8 * MIB,
        moved=4 * MIB,
    )(right_side, image, after)


def finish_second(dense, vectors, energies, value_sum, right_side, level, image, weighted, lines, devices):
    _, clusters, height, _ = dense.shape
    lanes = vectors.lanes
    fields = right_side.shape[0]
    width = height // 2
    count = len(vectors.arrays)

    def kernel(dense_ref, energies_ref, *refs):
        vector_refs, refs = refs[:count], refs[count:]
        sum_ref, right_ref, level_ref, image_ref, weighted_ref, lines_ref = refs[:6]
        later_ref, out_ref, kept, *scratch = refs[6:]
        energy = wide([energies_ref[...]] * fields)
        alpha, growth = lines_ref[6:7, :], lines_ref[7:8, :]
        kept[...] = jnp.zeros_like(kept)
        opened = vectors.open(vector_refs, scratch)

        @pl.loop(0, clusters // BATCH)
        def _(batch):
            here = pl.ds(batch * BATCH, BATCH)
            value = sum_ref[here] + weighted_ref[here]
            for part in products(dense_ref, opened, here, energy):
                value = value + part
            for local in range(BATCH):
                cluster = batch * BATCH + local
                rows = pl.ds(pl.multiple_of(cluster * width, width), width)
                right = wide([right_ref[f, rows, :] for f in range(fields)])
                first = image_ref[cluster]
                later = wide([level_ref[cluster]] * fields) * first + value[local]
                later_ref[cluster] = later
                direction = growth * right - alpha * first
                for index, left in enumerate((direction, right, first)):
                    kept[index] += folded(left * later)

        block = jnp.concatenate([lines_ref[0:6, :], lined([kept[i] for i in range(3)], 10)], axis=0)
        orbitals = lanes // fields
        line, lane = (lax.broadcasted_iota(jnp.int32, (16, 128), d) for d in (0, 1))
        rows = []
        for f, column in enumerate(field_sums(block, fields)):
            first_lane = slice(f * orbitals, f * orbitals + 1)
            filled = jnp.broadcast_to(column, (16, 128))
            filled = jnp.where(line == 9, jnp.broadcast_to(alpha[:, first_lane], (16, 128)), filled)
            filled = jnp.where(line == 10, jnp.broadcast_to(growth[:, first_lane], (16, 128)), filled)
            rows.append(jnp.sum(jnp.where(line == lane, filled, 0.0), axis=0, keepdims=True))
        rows.append(jnp.zeros((8 - fields, 128), jnp.float32))
        out_ref[...] = jnp.broadcast_to(jnp.concatenate(rows, axis=0)[None], out_ref.shape)

    return call(
        kernel,
        "finish_second",
        [
            jax.ShapeDtypeStruct((clusters, width, lanes), jnp.float32),
            jax.ShapeDtypeStruct((devices, 8, 128), jnp.float32),
        ],
        [vmem()] * (2 + count + 6),
        [pltpu.VMEM((3, 8, lanes), jnp.float32)] + vectors.scratch,
        flops=work(dense, vectors.items, lanes),
        moved=8 * MIB,
    )(dense, energies, *vectors.arrays, value_sum, right_side, level, image, weighted, lines)


def step_sizes(gathered, fields, orbitals):
    rows = gathered.reshape(-1, 128)
    flat = wide([jnp.transpose(rows[i : i + 128]) for i in range(0, rows.shape[0], 128)])
    line = [flat[i : i + 1, :] for i in range(11)]
    place = lax.broadcasted_iota(jnp.int32, line[0].shape, 1) & 7
    whole = lambda v: [
        jnp.sum(jnp.where(place == f, v, 0.0), axis=1, keepdims=True) for f in range(fields)
    ]

    def back(values):
        row = jnp.zeros_like(line[0])
        for f, value in enumerate(values):
            row = jnp.where(place == f, jnp.broadcast_to(value, row.shape), row)
        return row

    norm = whole(line[0])
    alpha = [n / b for n, b in zip(norm, whole(line[1]))]
    growth = [a * a * s / n for a, s, n in zip(alpha, whole(line[2]), norm)]
    off, more = back(alpha) - line[9], back(growth) - line[10]
    after = whole(line[3] - 2.0 * off * line[4] + off * off * line[2])
    bend = whole(
        (line[10] * line[5] - line[9] * line[6])
        + more * (line[5] + line[10] * line[1] - line[9] * line[7])
        - off * (line[6] + line[10] * line[2] - line[9] * line[8])
        + more * more * line[1]
        - more * off * (line[7] + line[2])
        + off * off * line[8]
    )
    gain = [a / b for a, b in zip(after, bend)]
    return [per_field(v, orbitals) for v in (alpha, growth, gain)]


def final(right_side, image, later, gathered):
    fields, rows, orbitals = right_side.shape
    clusters, width, lanes = image.shape
    blocks = 4
    each = clusters // blocks

    def kernel(right_ref, image_ref, later_ref, gathered_ref, solution_ref, residual_ref, steps):
        step = pl.program_id(0)

        @pl.when(step == 0)
        def _():
            alpha, growth, gain = step_sizes(gathered_ref[...], fields, orbitals)
            steps[0:1, :] = alpha + gain * growth
            steps[1:2, :] = gain * alpha

        for local in range(each):
            cluster = step * each + local
            rows = pl.ds(pl.multiple_of(cluster * width, width), width)
            here = slice(local * width, (local + 1) * width)
            for field in range(fields):
                part = slice(field * orbitals, (field + 1) * orbitals)
                one, two = steps[0:1, part], steps[1:2, part]
                right = right_ref[field, rows, :]
                first = image_ref[cluster, :, part]
                later = later_ref[cluster, :, part]
                solution_ref[field, here, :] = one * right - two * first
                residual_ref[field, here, :] = (right - one * first) + two * later

    vector = pl.BlockSpec((fields, each * width, orbitals), lambda i: (0, i, 0))
    shape = jax.ShapeDtypeStruct(right_side.shape, jnp.float32)
    return pl.pallas_call(
        kernel,
        grid=(blocks,),
        out_shape=[shape, shape],
        in_specs=[vmem()] * 4,
        out_specs=[vector, vector],
        scratch_shapes=[pltpu.VMEM((8, lanes), jnp.float32)],
        compiler_params=pltpu.CompilerParams(vmem_limit_bytes=12 * MIB),
        name="final",
    )(right_side, image, later, gathered)


def body(right_side, onsite, energies, ks_tiles, correlation_tiles, tile_slot, readers):
    span, served = readers.shape[1:]
    clusters, _, width, _ = ks_tiles.shape
    rows = lax.axis_size("row")
    devices = rows * lax.axis_size("col")
    onsite = onsite.reshape(-1, width)
    energies = energies.reshape(1, -1)
    plan = Plan(rows, span, rows == 8 and span == 7)
    readers = jnp.swapaxes(readers, 1, 2)

    def begin(items, after):
        return couple(dense, Vectors(plan, items), energies, [], after)

    def partial(items, sums):
        for group in (items[3:-2], items[-2:-1]):
            sums = couple(dense, Vectors(plan, group), energies, sums)
        return sums, Vectors(plan, items[-1:])

    direct, own, full = pack(plan, readers, right_side, onsite)
    dense = spread(tile_slot, ks_tiles, correlation_tiles, span, served)
    items, sums, chosen, _ = exchange(plan, readers, direct, own, full, None, begin, (1, 2, 3), served, width)
    level = levels(onsite)
    sums, last = partial(items, sums)
    image, full, direct, out = finish_first(
        plan, dense, last, energies, sums[0], right_side, level, own, readers
    )

    items, begun, _, mark = exchange(plan, readers, direct, out, full, chosen, begin, (2, 3, 1), served, width)
    lines = prepare(right_side, image, mark)
    _, weighted = couple(dense, last, energies, sums, mark)
    (value,), last = partial(items, begun)
    later, gathered = finish_second(
        dense, last, energies, value, right_side, level, image, weighted, lines, devices
    )
    gathered = lax.all_to_all(gathered, ("row", "col"), 0, 0)
    return tuple(final(right_side, image, later, gathered))


def solution(mesh):
    placed = (
        P(None, "row", "col"),
        P("row"),
        P("col"),
        P("row", None, None, None),
        P("row", None, None, None),
        P("row", None),
        P("row", None, None),
    )
    return jax.shard_map(
        body,
        mesh=mesh,
        in_specs=placed,
        out_specs=(P(None, "row", "col"), P(None, "row", "col")),
        check_vma=False,
    )
```

```python
import functools

import jax
import jax.numpy as jnp
from jax import lax
from jax.experimental import pallas as pl
from jax.experimental.pallas import tpu as pltpu
from jax.sharding import PartitionSpec as P

MIB = 2**20
EXTRA = 16
BATCH = 2
EARLY = 1 << 34


def shifted(array, axis, by):
    count = lax.axis_size(axis)
    return lax.ppermute(array, axis, [(i, (i + by) % count) for i in range(count)])


def vmem():
    return pl.BlockSpec(memory_space=pltpu.VMEM)


def smem():
    return pl.BlockSpec(memory_space=pltpu.SMEM)


def call(kernel, name, out_shape, specs, scratch=(), flops=0, moved=MIB, limit=12):
    return pl.pallas_call(
        kernel,
        out_shape=out_shape,
        in_specs=specs,
        out_specs=jax.tree.map(lambda _: vmem(), out_shape),
        scratch_shapes=list(scratch),
        compiler_params=pltpu.CompilerParams(vmem_limit_bytes=limit * MIB),
        cost_estimate=pl.CostEstimate(flops=flops, bytes_accessed=moved, transcendentals=0),
        name=name,
    )


def wide(parts):
    return jnp.concatenate(parts, axis=1)


def folded(term):
    return jnp.sum(term.reshape(-1, 8, term.shape[-1]), axis=0)


def lined(parts, lines):
    parts = [jnp.sum(p, axis=0, keepdims=True) for p in parts]
    parts.append(jnp.zeros((lines - len(parts), parts[0].shape[1]), jnp.float32))
    return jnp.concatenate(parts, axis=0)


def per_field(values, orbitals):
    return wide([jnp.broadcast_to(v, (1, orbitals)) for v in values])


def field_sums(lines, fields):
    orbitals = lines.shape[1] // fields
    return [
        jnp.sum(lines[:, f * orbitals : (f + 1) * orbitals], axis=1, keepdims=True)
        for f in range(fields)
    ]


class Plan:
    def __init__(self, count, span, relayed):
        self.count, self.span, self.middle, self.relayed = count, span, (span - 1) // 2, relayed

    def offset(self, source, reader):
        value = lax.rem(source - reader + (self.middle + self.count), self.count)
        return jnp.minimum(value, self.span - 1) if self.relayed else value

    def early(self):
        return [2] if self.relayed else self.direct()

    def direct(self):
        if self.relayed:
            return [1, 2, 3, 7]
        far = range(self.middle, 0, -1)
        return [by for f in far for by in (f, -f)]

    def reader(self, key, me):
        return me ^ key if self.relayed else lax.rem(me + key + self.count, self.count)

    def source(self, key, me):
        return me ^ key if self.relayed else lax.rem(me - key + self.count, self.count)

    def pairs(self, key):
        if not self.relayed:
            return [(i, (i + key) % self.count) for i in range(self.count)]
        return [(i, i ^ key) for i in range(self.count) if key < 4 or i not in INNER]


INNER = (2, 3, 4, 5)


def is_inner(me):
    return (me >= INNER[0]) & (me <= INNER[-1])


def pack(plan, readers, right_side, onsite):
    fields, rows, orbitals = right_side.shape
    served = readers.shape[1]
    clusters, width = onsite.shape
    lanes = fields * orbitals
    keys = plan.early()

    def kernel(readers_hbm, right_hbm, onsite_hbm, *refs):
        messages, rounded = refs[: len(keys)], refs[len(keys)]
        readers_ref, right_ref, onsite_ref, sems, more = refs[len(keys) + 1 :]
        copies = []
        for cluster in range(clusters):
            here = pl.ds(cluster * width, width)
            copies.append(
                pltpu.make_async_copy(
                    right_hbm.at[:, here, :], right_ref.at[:, here, :], sems.at[cluster]
                )
            )
        others = [
            pltpu.make_async_copy(onsite_hbm, onsite_ref, more.at[0]),
            pltpu.make_async_copy(readers_hbm, readers_ref, more.at[1]),
        ]
        for copy in copies[:1] + others + copies[1:]:
            copy.start()
        others[0].wait()
        norm = [jnp.zeros((8, orbitals), jnp.float32)] * fields
        heavy = [jnp.zeros((8, orbitals), jnp.float32)] * fields
        for cluster in range(clusters):
            copies[cluster].wait()
            weight = jnp.broadcast_to(onsite_ref[cluster : cluster + 1, :], (8, width))
            here = slice(cluster * width, (cluster + 1) * width)
            for field in range(fields):
                right = right_ref[field, here, :]
                rounded[here, field * orbitals : (field + 1) * orbitals] = right.astype(jnp.bfloat16)
                square = right * right
                norm[field] += folded(square)
                heavy[field] += jnp.dot(weight, square, preferred_element_type=jnp.float32)
        centers = [
            jnp.sum(h[:1], axis=1, keepdims=True)
            / jnp.maximum(jnp.sum(jnp.sum(n, axis=0, keepdims=True), axis=1, keepdims=True), 1e-30)
            for h, n in zip(heavy, norm)
        ]
        others[1].wait()
        rest = jnp.broadcast_to(per_field(centers, orbitals), (EXTRA, lanes))
        line, lane = (lax.broadcasted_iota(jnp.int32, (EXTRA, lanes), d) for d in (0, 1))
        for offset in range(readers_ref.shape[2]):
            for slot in range(served):
                here = (line == offset + 1) & (lane == slot)
                rest = jnp.where(here, readers_ref[0, slot, offset].astype(jnp.float32), rest)
        rounded[clusters * width :, :] = rest.astype(jnp.bfloat16)
        fill(plan, keys, readers_ref, rounded, messages, width)

    message = jax.ShapeDtypeStruct((served * width + EXTRA, lanes), jnp.bfloat16)
    full = jax.ShapeDtypeStruct((clusters * width + EXTRA, lanes), jnp.bfloat16)
    *messages, full = call(
        kernel,
        "pack",
        [message] * len(keys) + [full],
        [pl.BlockSpec(memory_space=pltpu.HBM)] * 3,
        [
            pltpu.SMEM(readers.shape, readers.dtype),
            pltpu.VMEM(right_side.shape, jnp.float32),
            pltpu.VMEM(onsite.shape, jnp.float32),
            pltpu.SemaphoreType.DMA((clusters,)),
            pltpu.SemaphoreType.DMA((2,)),
        ],
        limit=52,
    )(readers, right_side, onsite)
    return dict(zip(keys, messages)), full


def hand_on(array, flops=0):
    def kernel(array_ref, same_ref):
        del array_ref, same_ref

    return pl.pallas_call(
        kernel,
        out_shape=jax.ShapeDtypeStruct(array.shape, array.dtype),
        in_specs=[vmem()],
        out_specs=vmem(),
        input_output_aliases={0: 0},
        compiler_params=pltpu.CompilerParams(vmem_limit_bytes=12 * MIB),
        cost_estimate=pl.CostEstimate(flops=flops, bytes_accessed=0, transcendentals=0),
        name="hand_on",
    )(array)


def deal(plan, readers, full, served, width):
    keys = plan.direct()

    def kernel(readers_ref, full_ref, *messages):
        fill(plan, keys, readers_ref, full_ref, messages, width)

    message = jax.ShapeDtypeStruct((served * width + EXTRA, full.shape[1]), jnp.bfloat16)
    *messages, own = call(kernel, "deal", [message] * (len(keys) + 1), [smem(), vmem()])(
        readers, full
    )
    return dict(zip(keys, messages)), own


def fill(plan, keys, readers_ref, rounded, messages, width):
    me = lax.axis_index("row")
    offsets = [plan.offset(me, plan.reader(key, me)) for key in keys] + [plan.middle]
    for offset, message in zip(offsets, messages):
        served = readers_ref.shape[1]
        gather([readers_ref[0, slot, offset] for slot in range(served)], rounded, message, width)


def gather(clusters, rounded, message, width):
    for slot, cluster in enumerate(clusters):
        start = pl.multiple_of(cluster * width, width)
        message[slot * width : (slot + 1) * width, :] = rounded[pl.ds(start, width), :]
    used = len(clusters) * width
    if message.shape[0] > used:
        message[used:, :] = rounded[rounded.shape[0] - EXTRA :, :]


def relay(plan, readers, mine, full, chosen, after, served, width):
    lanes = full.shape[1]
    extra = EXTRA if chosen is None else 0
    message = jax.ShapeDtypeStruct((served * width + extra, lanes), jnp.bfloat16)

    def kernel(*refs):
        readers_ref, mine_ref, full_ref, _, *refs = refs
        me = lax.axis_index("row")
        *messages, chosen_ref = refs if chosen is None else [*refs[1:], refs[0]]
        if chosen is None:
            base = full_ref.shape[0] - EXTRA
            table = full_ref[base : base + EXTRA, 0:width].astype(jnp.float32)
            line, lane = (lax.broadcasted_iota(jnp.int32, table.shape, d) for d in (0, 1))
            for index, reader in enumerate((me, me ^ 1, me ^ 3)):
                offset = plan.offset(me ^ 6, reader)
                for slot in range(served):
                    here = (line == offset + 1) & (lane == slot)
                    chosen_ref[index, slot] = jnp.sum(jnp.where(here, table, 0.0)).astype(jnp.int32)

        @pl.when(is_inner(me))
        def _():
            for index, out in enumerate(messages):
                gather([chosen_ref[index, slot] for slot in range(served)], full_ref, out, width)

        @pl.when(jnp.logical_not(is_inner(me)))
        def _():
            for key, out in zip((6, 5), messages[1:]):
                offset = plan.offset(me, me ^ key)
                clusters = [readers_ref[0, slot, offset] for slot in range(served)]
                gather(clusters, mine_ref, out, width)

    inputs = [readers, mine, full, after] + ([] if chosen is None else [chosen])
    specs = [smem(), vmem(), vmem(), pl.BlockSpec(memory_space=pl.ANY)]
    specs += [] if chosen is None else [smem()]
    shapes, outs = [message] * 3, [vmem()] * 3
    if chosen is None:
        shapes.append(jax.ShapeDtypeStruct((3, served), jnp.int32))
        outs.append(smem())
    *messages, last = pl.pallas_call(
        kernel,
        out_shape=shapes,
        in_specs=specs,
        out_specs=outs,
        compiler_params=pltpu.CompilerParams(vmem_limit_bytes=12 * MIB),
        cost_estimate=pl.CostEstimate(flops=0, bytes_accessed=MIB, transcendentals=0),
        name="relay",
    )(*inputs)
    return (messages, last) if chosen is None else (messages + [last], chosen)


def exchange(plan, readers, early, direct, own, full, chosen, begin, near, served, width):
    sent = {k: lax.ppermute(m, "row", plan.pairs(k)) for k, m in direct.items() if k not in early}
    if not plan.relayed:
        sent |= {k: lax.ppermute(m, "row", plan.pairs(k)) for k, m in early.items()}
        items = [(own, 0)] + [(sent[k], k) for k in plan.direct()]
        sums = begin(items[:3])
        return items, sums, None, sums[0]
    theirs = lax.ppermute(full, "row", [(i, i ^ 6) for i in INNER])
    for k, m in early.items():
        inward = [(i, j) for i, j in plan.pairs(k) if j in INNER]
        outward = [(i, j) for i, j in plan.pairs(k) if i in INNER]
        first = hand_on(lax.ppermute(m, "row", inward), EARLY)
        sent[k] = (first, lax.ppermute(direct[k], "row", outward))
    items = [(own, 0)]
    items += [(sent[k], (k, k) if k in early else k) for k in near]
    sums = begin(items[:3])
    (mine, near, far), chosen = relay(
        plan, readers, full, theirs, chosen, sums[0], served, width
    )
    near = lax.ppermute(near, "row", [(i, i ^ (1 if i in INNER else 6)) for i in range(plan.count)])
    far = lax.ppermute(far, "row", [(i, i ^ (3 if i in INNER else 5)) for i in range(plan.count)])
    items += [((mine, sent[7]), (6, 7)), (far, 5), (near, (7, 6))]
    return items, sums, chosen, mine


class Vectors:
    def __init__(self, plan, items):
        self.plan, self.items = plan, items
        self.arrays, self.scratch = [], []
        for value, _ in items:
            many = isinstance(value, tuple)
            self.arrays += list(value) if many else [value]
            if many:
                self.scratch.append(pltpu.VMEM(value[0].shape, value[0].dtype))
        self.lanes = self.arrays[0].shape[1]
        self.rows = self.arrays[0].shape[0]

    def open(self, refs, scratch):
        refs, scratch = list(refs), list(scratch)
        me = lax.axis_index("row")
        opened = []
        for value, key in self.items:
            if not self.plan.relayed:
                opened.append((self.plan.middle - key, refs.pop(0)))
                continue
            inner, outer = key if isinstance(key, tuple) else (key, key)
            held = refs.pop(0)
            if isinstance(value, tuple):
                kept, held, other = held, scratch.pop(0), refs.pop(0)

                @pl.when(is_inner(me))
                def _():
                    held[...] = kept[...]

                @pl.when(jnp.logical_not(is_inner(me)))
                def _():
                    held[...] = other[...]

            source = jnp.where(is_inner(me), me ^ inner, me ^ outer)
            opened.append((self.plan.offset(source, me), held))
        return opened


def levels(onsite):
    clusters, width = onsite.shape

    def kernel(onsite_ref, level_ref):
        for cluster in range(clusters):
            level_ref[cluster] = jnp.transpose(
                jnp.broadcast_to(onsite_ref[cluster : cluster + 1, :], (width, width))
            )

    shape = jax.ShapeDtypeStruct((clusters, width, width), jnp.float32)
    return call(kernel, "levels", shape, [vmem()])(onsite)


def spread(tile_slot, ks_tiles, correlation_tiles, span, served):
    clusters, _, width, _ = ks_tiles.shape
    slots = span * served

    def kernel(slot_ref, ks_ref, correlation_ref, out_ref, where):
        @pl.loop(0, clusters)
        def _(cluster):
            for kind, ref in enumerate((ks_ref, correlation_ref)):
                count = ref.shape[1]
                for slot in range(slots):
                    where[slot] = count
                for tile in range(count):
                    where[slot_ref[cluster, tile]] = tile
                for slot in range(slots):
                    tile = where[slot]
                    block = ref[cluster, jnp.minimum(tile, count - 1)]
                    block = jnp.where(tile < count, block, jnp.zeros_like(block))
                    lane = slot % served * width
                    out_ref[
                        slot // served, cluster, kind * width : (kind + 1) * width, lane : lane + width
                    ] = block

    return call(
        kernel,
        "spread",
        jax.ShapeDtypeStruct((span, clusters, 2 * width, served * width), jnp.bfloat16),
        [smem(), vmem(), vmem()],
        [pltpu.SMEM((slots,), jnp.int32)],
        moved=16 * MIB,
    )(tile_slot, ks_tiles, correlation_tiles)


def products(dense_ref, opened, clusters, energy):
    depth = dense_ref.shape[-1]
    for offset, vector in opened:
        left = dense_ref[offset, clusters]
        count, height, _ = left.shape
        value = jnp.dot(
            left.reshape(count * height, depth), vector[0:depth, :], preferred_element_type=jnp.float32
        )
        value = value.reshape(count, 2, height // 2, value.shape[1])
        yield value[:, 0] - energy * value[:, 1]


def centers(opened, depth):
    return [vector[depth : depth + EXTRA, :].astype(jnp.float32)[:1] for _, vector in opened]


def work(dense, items, lanes):
    return 2 * len(items) * dense.shape[1] * dense.shape[2] * dense.shape[3] * lanes


def couple(dense, vectors, energies, sums, after=None, weight=1):
    _, clusters, height, depth = dense.shape
    lanes = vectors.lanes
    count = len(vectors.arrays)
    outs = 2 if vectors.rows > depth else 1
    had = len(sums)

    def kernel(dense_ref, energies_ref, *refs):
        refs = list(refs[1:] if after is not None else refs)
        vector_refs, sum_refs = refs[:count], refs[count : count + had]
        out_refs, scratch = refs[count + had : count + had + outs], refs[count + had + outs :]
        energy = wide([energies_ref[...]] * (lanes // energies_ref.shape[1]))
        opened = vectors.open(vector_refs, scratch)
        weights = centers(opened, depth) if outs == 2 else [None] * len(opened)

        @pl.loop(0, clusters // BATCH)
        def _(batch):
            here = pl.ds(batch * BATCH, BATCH)
            values = [ref[here] for ref in sum_refs]
            for weight, part in zip(weights, products(dense_ref, opened, here, energy)):
                terms = [part] if weight is None else [part, weight * part]
                values = [v + t for v, t in zip(values, terms)] if values else terms
            for ref, value in zip(out_refs, values):
                ref[here] = value

    order = [] if after is None else [after]
    inputs = [dense, energies, *order, *vectors.arrays, *sums]
    shape = jax.ShapeDtypeStruct((clusters, height // 2, lanes), jnp.float32)
    return call(
        kernel,
        "couple",
        [shape] * outs,
        [vmem()] * 2
        + [pl.BlockSpec(memory_space=pl.ANY)] * len(order)
        + [vmem()] * (len(vectors.arrays) + had),
        vectors.scratch,
        flops=weight * work(dense, vectors.items, lanes),
        moved=4 * MIB,
    )(*inputs)


def finish_first(plan, dense, vectors, energies, value_sum, right_side, level, own, readers):
    _, clusters, height, depth = dense.shape
    lanes = vectors.lanes
    fields = right_side.shape[0]
    width = height // 2
    count = len(vectors.arrays)
    keys = plan.direct()
    outs = len(keys) + 1

    def kernel(dense_ref, energies_ref, *refs):
        vector_refs, refs = refs[:count], refs[count:]
        sum_ref, right_ref, level_ref, own_ref, readers_ref, image_ref, outgoing = refs[:7]
        messages, scratch = refs[7 : 7 + outs], refs[7 + outs :]
        energy = wide([energies_ref[...]] * fields)
        opened = vectors.open(vector_refs, scratch)
        (center,) = centers([(0, own_ref)], depth)

        @pl.loop(0, clusters // BATCH)
        def _(batch):
            here = pl.ds(batch * BATCH, BATCH)
            value = sum_ref[here]
            for part in products(dense_ref, opened, here, energy):
                value = value + part
            for local in range(BATCH):
                cluster = batch * BATCH + local
                rows = pl.ds(pl.multiple_of(cluster * width, width), width)
                right = wide([right_ref[f, rows, :] for f in range(fields)])
                image = wide([level_ref[cluster]] * fields) * right + value[local]
                image_ref[cluster] = image
                outgoing[rows, :] = (image - center * right).astype(jnp.bfloat16)

        fill(plan, keys, readers_ref, outgoing, messages, width)

    image, full, *messages, out = call(
        kernel,
        "finish_first",
        [
            jax.ShapeDtypeStruct((clusters, width, lanes), jnp.float32),
            jax.ShapeDtypeStruct((clusters * width, lanes), jnp.bfloat16),
        ]
        + [jax.ShapeDtypeStruct((depth, lanes), jnp.bfloat16)] * outs,
        [vmem()] * (2 + count + 4) + [smem()],
        vectors.scratch,
        flops=work(dense, vectors.items, lanes),
        moved=8 * MIB,
    )(dense, energies, *vectors.arrays, value_sum, right_side, level, own, readers)
    return image, full, dict(zip(keys, messages)), out


def guesses(lines, fields):
    orbitals = lines.shape[1] // fields
    alphas, growths = [], []
    for column in field_sums(lines, fields):
        norm, bend, square = column[0:1], column[1:2], column[2:3]
        norm = jnp.maximum(norm, 1e-30)
        alpha = norm / jnp.maximum(bend, 4.0 * norm)
        alphas.append(alpha)
        growths.append(jnp.clip(alpha * alpha * square / norm, 1.0, 2.0))
    return per_field(alphas, orbitals), per_field(growths, orbitals)


def prepare(right_side, image, after):
    fields, rows, orbitals = right_side.shape
    clusters, width, lanes = image.shape

    def kernel(right_ref, image_ref, _, lines_ref, kept):
        kept[...] = jnp.zeros_like(kept)

        def sweep(base, terms):
            @pl.loop(0, clusters)
            def _(cluster):
                here = pl.ds(pl.multiple_of(cluster * width, width), width)
                right = wide([right_ref[f, here, :] for f in range(fields)])
                for index, term in enumerate(terms(right, image_ref[cluster])):
                    kept[base + index] += folded(term)

        sweep(0, lambda right, first: (right * right, right * first, first * first))
        alpha, growth = guesses(lined([kept[i] for i in range(3)], 8), fields)

        def later_terms(right, first):
            step = alpha * first
            residual = right - step
            return residual * residual, residual * first, (growth * right - step) * first

        sweep(3, later_terms)
        lines_ref[...] = lined([kept[i] for i in range(6)], 8)
        lines_ref[6:7, :] = alpha
        lines_ref[7:8, :] = growth

    return call(
        kernel,
        "prepare",
        jax.ShapeDtypeStruct((8, lanes), jnp.float32),
        [vmem(), vmem(), pl.BlockSpec(memory_space=pl.ANY)],
        [pltpu.VMEM((6, 8, lanes), jnp.float32)],
        flops=8 * MIB,
        moved=4 * MIB,
    )(right_side, image, after)


def finish_second(dense, vectors, energies, value_sum, right_side, level, image, weighted, lines, devices):
    _, clusters, height, _ = dense.shape
    lanes = vectors.lanes
    fields = right_side.shape[0]
    width = height // 2
    count = len(vectors.arrays)

    def kernel(dense_ref, energies_ref, *refs):
        vector_refs, refs = refs[:count], refs[count:]
        sum_ref, right_ref, level_ref, image_ref, weighted_ref, lines_ref = refs[:6]
        later_ref, out_ref, kept, *scratch = refs[6:]
        energy = wide([energies_ref[...]] * fields)
        alpha, growth = lines_ref[6:7, :], lines_ref[7:8, :]
        kept[...] = jnp.zeros_like(kept)
        opened = vectors.open(vector_refs, scratch)

        @pl.loop(0, clusters // BATCH)
        def _(batch):
            here = pl.ds(batch * BATCH, BATCH)
            value = sum_ref[here] + weighted_ref[here]
            for part in products(dense_ref, opened, here, energy):
                value = value + part
            for local in range(BATCH):
                cluster = batch * BATCH + local
                rows = pl.ds(pl.multiple_of(cluster * width, width), width)
                right = wide([right_ref[f, rows, :] for f in range(fields)])
                first = image_ref[cluster]
                later = wide([level_ref[cluster]] * fields) * first + value[local]
                later_ref[cluster] = later
                direction = growth * right - alpha * first
                for index, left in enumerate((direction, right, first)):
                    kept[index] += folded(left * later)

        block = jnp.concatenate([lines_ref[0:6, :], lined([kept[i] for i in range(3)], 10)], axis=0)
        orbitals = lanes // fields
        line, lane = (lax.broadcasted_iota(jnp.int32, (16, 128), d) for d in (0, 1))
        rows = []
        for f, column in enumerate(field_sums(block, fields)):
            first_lane = slice(f * orbitals, f * orbitals + 1)
            filled = jnp.broadcast_to(column, (16, 128))
            filled = jnp.where(line == 9, jnp.broadcast_to(alpha[:, first_lane], (16, 128)), filled)
            filled = jnp.where(line == 10, jnp.broadcast_to(growth[:, first_lane], (16, 128)), filled)
            rows.append(jnp.sum(jnp.where(line == lane, filled, 0.0), axis=0, keepdims=True))
        rows.append(jnp.zeros((8 - fields, 128), jnp.float32))
        out_ref[...] = jnp.broadcast_to(jnp.concatenate(rows, axis=0)[None], out_ref.shape)

    return call(
        kernel,
        "finish_second",
        [
            jax.ShapeDtypeStruct((clusters, width, lanes), jnp.float32),
            jax.ShapeDtypeStruct((devices, 8, 128), jnp.float32),
        ],
        [vmem()] * (2 + count + 6),
        [pltpu.VMEM((3, 8, lanes), jnp.float32)] + vectors.scratch,
        flops=work(dense, vectors.items, lanes),
        moved=8 * MIB,
    )(dense, energies, *vectors.arrays, value_sum, right_side, level, image, weighted, lines)


def step_sizes(gathered, fields, orbitals):
    rows = gathered.reshape(-1, 128)
    flat = wide([jnp.transpose(rows[i : i + 128]) for i in range(0, rows.shape[0], 128)])
    line = [flat[i : i + 1, :] for i in range(11)]
    place = lax.broadcasted_iota(jnp.int32, line[0].shape, 1) & 7
    whole = lambda v: [
        jnp.sum(jnp.where(place == f, v, 0.0), axis=1, keepdims=True) for f in range(fields)
    ]

    def back(values):
        row = jnp.zeros_like(line[0])
        for f, value in enumerate(values):
            row = jnp.where(place == f, jnp.broadcast_to(value, row.shape), row)
        return row

    norm = whole(line[0])
    alpha = [n / b for n, b in zip(norm, whole(line[1]))]
    growth = [a * a * s / n for a, s, n in zip(alpha, whole(line[2]), norm)]
    off, more = back(alpha) - line[9], back(growth) - line[10]
    after = whole(line[3] - 2.0 * off * line[4] + off * off * line[2])
    bend = whole(
        (line[10] * line[5] - line[9] * line[6])
        + more * (line[5] + line[10] * line[1] - line[9] * line[7])
        - off * (line[6] + line[10] * line[2] - line[9] * line[8])
        + more * more * line[1]
        - more * off * (line[7] + line[2])
        + off * off * line[8]
    )
    gain = [a / b for a, b in zip(after, bend)]
    return [per_field(v, orbitals) for v in (alpha, growth, gain)]


def final(right_side, image, later, gathered):
    fields, rows, orbitals = right_side.shape
    clusters, width, lanes = image.shape
    blocks = 4
    each = clusters // blocks

    def kernel(right_ref, image_ref, later_ref, gathered_ref, solution_ref, residual_ref, steps):
        step = pl.program_id(0)

        @pl.when(step == 0)
        def _():
            alpha, growth, gain = step_sizes(gathered_ref[...], fields, orbitals)
            steps[0:1, :] = alpha + gain * growth
            steps[1:2, :] = gain * alpha

        for local in range(each):
            cluster = step * each + local
            rows = pl.ds(pl.multiple_of(cluster * width, width), width)
            here = slice(local * width, (local + 1) * width)
            for field in range(fields):
                part = slice(field * orbitals, (field + 1) * orbitals)
                one, two = steps[0:1, part], steps[1:2, part]
                right = right_ref[field, rows, :]
                first = image_ref[cluster, :, part]
                later = later_ref[cluster, :, part]
                solution_ref[field, here, :] = one * right - two * first
                residual_ref[field, here, :] = (right - one * first) + two * later

    vector = pl.BlockSpec((fields, each * width, orbitals), lambda i: (0, i, 0))
    shape = jax.ShapeDtypeStruct(right_side.shape, jnp.float32)
    return pl.pallas_call(
        kernel,
        grid=(blocks,),
        out_shape=[shape, shape],
        in_specs=[vmem()] * 4,
        out_specs=[vector, vector],
        scratch_shapes=[pltpu.VMEM((8, lanes), jnp.float32)],
        compiler_params=pltpu.CompilerParams(vmem_limit_bytes=12 * MIB),
        name="final",
    )(right_side, image, later, gathered)


def body(right_side, onsite, energies, ks_tiles, correlation_tiles, tile_slot, readers):
    span, served = readers.shape[1:]
    clusters, _, width, _ = ks_tiles.shape
    rows = lax.axis_size("row")
    devices = rows * lax.axis_size("col")
    onsite = onsite.reshape(-1, width)
    energies = energies.reshape(1, -1)
    plan = Plan(rows, span, rows == 8 and span == 7)
    readers = jnp.swapaxes(readers, 1, 2)

    def begin(weight):
        return lambda items: couple(dense, Vectors(plan, items), energies, [], weight=weight)

    def partial(items, sums):
        for group in (items[3:-2], items[-2:-1]):
            sums = couple(dense, Vectors(plan, group), energies, sums)
        return sums, Vectors(plan, items[-1:])

    early, full = pack(plan, readers, right_side, onsite)
    full = hand_on(full)
    direct, own = deal(plan, readers, full, served, width)
    dense = spread(tile_slot, ks_tiles, correlation_tiles, span, served)
    items, sums, chosen, _ = exchange(
        plan, readers, early, direct, own, full, None, begin(1), (2, 1, 3), served, width
    )
    level = levels(onsite)
    sums, last = partial(items, sums)
    image, full, direct, out = finish_first(
        plan, dense, last, energies, sums[0], right_side, level, own, readers
    )

    items, begun, _, mark = exchange(
        plan, readers, {}, direct, out, full, chosen, begin(1), (2, 3, 1), served, width
    )
    lines = prepare(right_side, image, mark)
    _, weighted = couple(dense, last, energies, sums, mark)
    (value,), last = partial(items, begun)
    later, gathered = finish_second(
        dense, last, energies, value, right_side, level, image, weighted, lines, devices
    )
    gathered = lax.all_to_all(gathered, ("row", "col"), 0, 0)
    return tuple(final(right_side, image, later, gathered))


def solution(mesh):
    placed = (
        P(None, "row", "col"),
        P("row"),
        P("col"),
        P("row", None, None, None),
        P("row", None, None, None),
        P("row", None),
        P("row", None, None),
    )
    return jax.shard_map(
        body,
        mesh=mesh,
        in_specs=placed,
        out_specs=(P(None, "row", "col"), P(None, "row", "col")),
        check_vma=False,
    )
```

```python
import functools

import jax
import jax.numpy as jnp
from jax import lax
from jax.experimental import pallas as pl
from jax.experimental.pallas import tpu as pltpu
from jax.sharding import PartitionSpec as P

MIB = 2**20
EXTRA = 16
BATCH = 2
EARLY = 1 << 34


def shifted(array, axis, by):
    count = lax.axis_size(axis)
    return lax.ppermute(array, axis, [(i, (i + by) % count) for i in range(count)])


def vmem():
    return pl.BlockSpec(memory_space=pltpu.VMEM)


def smem():
    return pl.BlockSpec(memory_space=pltpu.SMEM)


def call(kernel, name, out_shape, specs, scratch=(), flops=0, moved=MIB, limit=12):
    return pl.pallas_call(
        kernel,
        out_shape=out_shape,
        in_specs=specs,
        out_specs=jax.tree.map(lambda _: vmem(), out_shape),
        scratch_shapes=list(scratch),
        compiler_params=pltpu.CompilerParams(vmem_limit_bytes=limit * MIB),
        cost_estimate=pl.CostEstimate(flops=flops, bytes_accessed=moved, transcendentals=0),
        name=name,
    )


def wide(parts):
    return jnp.concatenate(parts, axis=1)


def folded(term):
    return jnp.sum(term.reshape(-1, 8, term.shape[-1]), axis=0)


def lined(parts, lines):
    parts = [jnp.sum(p, axis=0, keepdims=True) for p in parts]
    parts.append(jnp.zeros((lines - len(parts), parts[0].shape[1]), jnp.float32))
    return jnp.concatenate(parts, axis=0)


def per_field(values, orbitals):
    return wide([jnp.broadcast_to(v, (1, orbitals)) for v in values])


def field_sums(lines, fields):
    orbitals = lines.shape[1] // fields
    return [
        jnp.sum(lines[:, f * orbitals : (f + 1) * orbitals], axis=1, keepdims=True)
        for f in range(fields)
    ]


class Plan:
    def __init__(self, count, span, relayed):
        self.count, self.span, self.middle, self.relayed = count, span, (span - 1) // 2, relayed

    def offset(self, source, reader):
        value = lax.rem(source - reader + (self.middle + self.count), self.count)
        return jnp.minimum(value, self.span - 1) if self.relayed else value

    def early(self):
        return [2] if self.relayed else self.direct()

    def direct(self):
        if self.relayed:
            return [2, 3, 7]
        far = range(self.middle, 0, -1)
        return [by for f in far for by in (f, -f)]

    def reader(self, key, me):
        return me ^ key if self.relayed else lax.rem(me + key + self.count, self.count)

    def source(self, key, me):
        return me ^ key if self.relayed else lax.rem(me - key + self.count, self.count)

    def pairs(self, key):
        if not self.relayed:
            return [(i, (i + key) % self.count) for i in range(self.count)]
        return [(i, i ^ key) for i in range(self.count) if key < 4 or i not in INNER]


INNER = (2, 3, 4, 5)


def is_inner(me):
    return (me >= INNER[0]) & (me <= INNER[-1])


def pack(plan, readers, right_side, onsite):
    fields, rows, orbitals = right_side.shape
    served = readers.shape[1]
    clusters, width = onsite.shape
    lanes = fields * orbitals
    keys = plan.early()

    def kernel(readers_hbm, right_hbm, onsite_hbm, *refs):
        messages, rounded = refs[: len(keys)], refs[len(keys)]
        readers_ref, right_ref, onsite_ref, sems, more = refs[len(keys) + 1 :]
        copies = []
        for cluster in range(clusters):
            here = pl.ds(cluster * width, width)
            copies.append(
                pltpu.make_async_copy(
                    right_hbm.at[:, here, :], right_ref.at[:, here, :], sems.at[cluster]
                )
            )
        others = [
            pltpu.make_async_copy(onsite_hbm, onsite_ref, more.at[0]),
            pltpu.make_async_copy(readers_hbm, readers_ref, more.at[1]),
        ]
        for copy in copies[:1] + others + copies[1:]:
            copy.start()
        others[0].wait()
        norm = [jnp.zeros((8, orbitals), jnp.float32)] * fields
        heavy = [jnp.zeros((8, orbitals), jnp.float32)] * fields
        for cluster in range(clusters):
            copies[cluster].wait()
            weight = jnp.broadcast_to(onsite_ref[cluster : cluster + 1, :], (8, width))
            here = slice(cluster * width, (cluster + 1) * width)
            for field in range(fields):
                right = right_ref[field, here, :]
                rounded[here, field * orbitals : (field + 1) * orbitals] = right.astype(jnp.bfloat16)
                square = right * right
                norm[field] += folded(square)
                heavy[field] += jnp.dot(weight, square, preferred_element_type=jnp.float32)
        centers = [
            jnp.sum(h[:1], axis=1, keepdims=True)
            / jnp.maximum(jnp.sum(jnp.sum(n, axis=0, keepdims=True), axis=1, keepdims=True), 1e-30)
            for h, n in zip(heavy, norm)
        ]
        others[1].wait()
        rest = jnp.broadcast_to(per_field(centers, orbitals), (EXTRA, lanes))
        line, lane = (lax.broadcasted_iota(jnp.int32, (EXTRA, lanes), d) for d in (0, 1))
        for offset in range(readers_ref.shape[2]):
            for slot in range(served):
                here = (line == offset + 1) & (lane == slot)
                rest = jnp.where(here, readers_ref[0, slot, offset].astype(jnp.float32), rest)
        rounded[clusters * width :, :] = rest.astype(jnp.bfloat16)
        fill(plan, keys, readers_ref, rounded, messages, width)

    message = jax.ShapeDtypeStruct((served * width + EXTRA, lanes), jnp.bfloat16)
    full = jax.ShapeDtypeStruct((clusters * width + EXTRA, lanes), jnp.bfloat16)
    *messages, full = call(
        kernel,
        "pack",
        [message] * len(keys) + [full],
        [pl.BlockSpec(memory_space=pltpu.HBM)] * 3,
        [
            pltpu.SMEM(readers.shape, readers.dtype),
            pltpu.VMEM(right_side.shape, jnp.float32),
            pltpu.VMEM(onsite.shape, jnp.float32),
            pltpu.SemaphoreType.DMA((clusters,)),
            pltpu.SemaphoreType.DMA((2,)),
        ],
        limit=52,
    )(readers, right_side, onsite)
    return dict(zip(keys, messages)), full


def hand_on(array, flops=0):
    def kernel(array_ref, same_ref):
        del array_ref, same_ref

    return pl.pallas_call(
        kernel,
        out_shape=jax.ShapeDtypeStruct(array.shape, array.dtype),
        in_specs=[vmem()],
        out_specs=vmem(),
        input_output_aliases={0: 0},
        compiler_params=pltpu.CompilerParams(vmem_limit_bytes=12 * MIB),
        cost_estimate=pl.CostEstimate(flops=flops, bytes_accessed=0, transcendentals=0),
        name="hand_on",
    )(array)


def deal(plan, readers, full, served, width):
    keys = plan.direct()

    def kernel(readers_ref, full_ref, *messages):
        fill(plan, keys, readers_ref, full_ref, messages, width)

    message = jax.ShapeDtypeStruct((served * width + EXTRA, full.shape[1]), jnp.bfloat16)
    *messages, own = call(kernel, "deal", [message] * (len(keys) + 1), [smem(), vmem()])(
        readers, full
    )
    return dict(zip(keys, messages)), own


def fill(plan, keys, readers_ref, rounded, messages, width):
    me = lax.axis_index("row")
    offsets = [plan.offset(me, plan.reader(key, me)) for key in keys] + [plan.middle]
    for offset, message in zip(offsets, messages):
        served = readers_ref.shape[1]
        gather([readers_ref[0, slot, offset] for slot in range(served)], rounded, message, width)


def gather(clusters, rounded, message, width):
    for slot, cluster in enumerate(clusters):
        start = pl.multiple_of(cluster * width, width)
        message[slot * width : (slot + 1) * width, :] = rounded[pl.ds(start, width), :]
    used = len(clusters) * width
    if message.shape[0] > used:
        message[used:, :] = rounded[rounded.shape[0] - EXTRA :, :]


def relay(plan, readers, mine, full, chosen, after, served, width):
    lanes = full.shape[1]
    extra = EXTRA if chosen is None else 0
    message = jax.ShapeDtypeStruct((served * width + extra, lanes), jnp.bfloat16)

    def kernel(*refs):
        readers_ref, mine_ref, full_ref, _, *refs = refs
        me = lax.axis_index("row")
        *messages, beside, chosen_ref = refs if chosen is None else [*refs[1:], refs[0]]
        if chosen is None:
            base = full_ref.shape[0] - EXTRA
            table = full_ref[base : base + EXTRA, 0:width].astype(jnp.float32)
            line, lane = (lax.broadcasted_iota(jnp.int32, table.shape, d) for d in (0, 1))
            for index, reader in enumerate((me, me ^ 1, me ^ 3)):
                offset = plan.offset(me ^ 6, reader)
                for slot in range(served):
                    here = (line == offset + 1) & (lane == slot)
                    chosen_ref[index, slot] = jnp.sum(jnp.where(here, table, 0.0)).astype(jnp.int32)

        @pl.when(is_inner(me))
        def _():
            for index, out in enumerate(messages):
                gather([chosen_ref[index, slot] for slot in range(served)], full_ref, out, width)

        @pl.when(jnp.logical_not(is_inner(me)))
        def _():
            for key, out in zip((6, 5), messages[1:]):
                offset = plan.offset(me, me ^ key)
                clusters = [readers_ref[0, slot, offset] for slot in range(served)]
                gather(clusters, mine_ref, out, width)

        fill(plan, [1], readers_ref, mine_ref, [beside], width)

    inputs = [readers, mine, full, after] + ([] if chosen is None else [chosen])
    specs = [smem(), vmem(), vmem(), pl.BlockSpec(memory_space=pl.ANY)]
    specs += [] if chosen is None else [smem()]
    shapes, outs = [message] * 4, [vmem()] * 4
    if chosen is None:
        shapes.append(jax.ShapeDtypeStruct((3, served), jnp.int32))
        outs.append(smem())
    *messages, last = pl.pallas_call(
        kernel,
        out_shape=shapes,
        in_specs=specs,
        out_specs=outs,
        compiler_params=pltpu.CompilerParams(vmem_limit_bytes=12 * MIB),
        cost_estimate=pl.CostEstimate(flops=0, bytes_accessed=MIB, transcendentals=0),
        name="relay",
    )(*inputs)
    return (messages, last) if chosen is None else (messages + [last], chosen)


def exchange(plan, readers, early, direct, own, full, chosen, begin, served, width):
    sent = {k: lax.ppermute(m, "row", plan.pairs(k)) for k, m in direct.items() if k not in early}
    if not plan.relayed:
        sent |= {k: lax.ppermute(m, "row", plan.pairs(k)) for k, m in early.items()}
        items = [(own, 0)] + [(sent[k], k) for k in plan.direct()]
        sums = begin(items[:2])
        return items, sums, None, sums[0]
    theirs = lax.ppermute(full, "row", [(i, i ^ 6) for i in INNER])
    for k, m in early.items():
        inward = [(i, j) for i, j in plan.pairs(k) if j in INNER]
        outward = [(i, j) for i, j in plan.pairs(k) if i in INNER]
        first = hand_on(lax.ppermute(m, "row", inward), EARLY)
        sent[k] = (first, lax.ppermute(direct[k], "row", outward))
    items = [(own, 0)] + [(sent[k], (k, k) if k in early else k) for k in (2, 3)]
    sums = begin(items[:2])
    (mine, near, far, beside), chosen = relay(
        plan, readers, full, theirs, chosen, sums[0], served, width
    )
    beside = lax.ppermute(beside, "row", plan.pairs(1))
    near = lax.ppermute(near, "row", [(i, i ^ (1 if i in INNER else 6)) for i in range(plan.count)])
    far = lax.ppermute(far, "row", [(i, i ^ (3 if i in INNER else 5)) for i in range(plan.count)])
    items += [((mine, sent[7]), (6, 7)), (beside, 1), (far, 5), (near, (7, 6))]
    return items, sums, chosen, mine


class Vectors:
    def __init__(self, plan, items):
        self.plan, self.items = plan, items
        self.arrays, self.scratch = [], []
        for value, _ in items:
            many = isinstance(value, tuple)
            self.arrays += list(value) if many else [value]
            if many:
                self.scratch.append(pltpu.VMEM(value[0].shape, value[0].dtype))
        self.lanes = self.arrays[0].shape[1]
        self.rows = self.arrays[0].shape[0]

    def open(self, refs, scratch):
        refs, scratch = list(refs), list(scratch)
        me = lax.axis_index("row")
        opened = []
        for value, key in self.items:
            if not self.plan.relayed:
                opened.append((self.plan.middle - key, refs.pop(0)))
                continue
            inner, outer = key if isinstance(key, tuple) else (key, key)
            held = refs.pop(0)
            if isinstance(value, tuple):
                kept, held, other = held, scratch.pop(0), refs.pop(0)

                @pl.when(is_inner(me))
                def _():
                    held[...] = kept[...]

                @pl.when(jnp.logical_not(is_inner(me)))
                def _():
                    held[...] = other[...]

            source = jnp.where(is_inner(me), me ^ inner, me ^ outer)
            opened.append((self.plan.offset(source, me), held))
        return opened


def levels(onsite):
    clusters, width = onsite.shape

    def kernel(onsite_ref, level_ref):
        for cluster in range(clusters):
            level_ref[cluster] = jnp.transpose(
                jnp.broadcast_to(onsite_ref[cluster : cluster + 1, :], (width, width))
            )

    shape = jax.ShapeDtypeStruct((clusters, width, width), jnp.float32)
    return call(kernel, "levels", shape, [vmem()])(onsite)


def spread(tile_slot, ks_tiles, correlation_tiles, span, served):
    clusters, _, width, _ = ks_tiles.shape
    slots = span * served

    def kernel(slot_ref, ks_ref, correlation_ref, out_ref, where):
        @pl.loop(0, clusters)
        def _(cluster):
            for kind, ref in enumerate((ks_ref, correlation_ref)):
                count = ref.shape[1]
                for slot in range(slots):
                    where[slot] = count
                for tile in range(count):
                    where[slot_ref[cluster, tile]] = tile
                for slot in range(slots):
                    tile = where[slot]
                    block = ref[cluster, jnp.minimum(tile, count - 1)]
                    block = jnp.where(tile < count, block, jnp.zeros_like(block))
                    lane = slot % served * width
                    out_ref[
                        slot // served, cluster, kind * width : (kind + 1) * width, lane : lane + width
                    ] = block

    return call(
        kernel,
        "spread",
        jax.ShapeDtypeStruct((span, clusters, 2 * width, served * width), jnp.bfloat16),
        [smem(), vmem(), vmem()],
        [pltpu.SMEM((slots,), jnp.int32)],
        moved=16 * MIB,
    )(tile_slot, ks_tiles, correlation_tiles)


def products(dense_ref, opened, clusters, energy):
    depth = dense_ref.shape[-1]
    for offset, vector in opened:
        left = dense_ref[offset, clusters]
        count, height, _ = left.shape
        value = jnp.dot(
            left.reshape(count * height, depth), vector[0:depth, :], preferred_element_type=jnp.float32
        )
        value = value.reshape(count, 2, height // 2, value.shape[1])
        yield value[:, 0] - energy * value[:, 1]


def centers(opened, depth):
    return [vector[depth : depth + EXTRA, :].astype(jnp.float32)[:1] for _, vector in opened]


def work(dense, items, lanes):
    return 2 * len(items) * dense.shape[1] * dense.shape[2] * dense.shape[3] * lanes


def couple(dense, vectors, energies, sums, after=None):
    _, clusters, height, depth = dense.shape
    lanes = vectors.lanes
    count = len(vectors.arrays)
    outs = 2 if vectors.rows > depth else 1
    had = len(sums)

    def kernel(dense_ref, energies_ref, *refs):
        refs = list(refs[1:] if after is not None else refs)
        vector_refs, sum_refs = refs[:count], refs[count : count + had]
        out_refs, scratch = refs[count + had : count + had + outs], refs[count + had + outs :]
        energy = wide([energies_ref[...]] * (lanes // energies_ref.shape[1]))
        opened = vectors.open(vector_refs, scratch)
        weights = centers(opened, depth) if outs == 2 else [None] * len(opened)

        @pl.loop(0, clusters // BATCH)
        def _(batch):
            here = pl.ds(batch * BATCH, BATCH)
            values = [ref[here] for ref in sum_refs]
            for weight, part in zip(weights, products(dense_ref, opened, here, energy)):
                terms = [part] if weight is None else [part, weight * part]
                values = [v + t for v, t in zip(values, terms)] if values else terms
            for ref, value in zip(out_refs, values):
                ref[here] = value

    order = [] if after is None else [after]
    inputs = [dense, energies, *order, *vectors.arrays, *sums]
    shape = jax.ShapeDtypeStruct((clusters, height // 2, lanes), jnp.float32)
    return call(
        kernel,
        "couple",
        [shape] * outs,
        [vmem()] * 2
        + [pl.BlockSpec(memory_space=pl.ANY)] * len(order)
        + [vmem()] * (len(vectors.arrays) + had),
        vectors.scratch,
        flops=work(dense, vectors.items, lanes),
        moved=4 * MIB,
    )(*inputs)


def finish_first(plan, dense, vectors, energies, value_sum, right_side, level, own, readers):
    _, clusters, height, depth = dense.shape
    lanes = vectors.lanes
    fields = right_side.shape[0]
    width = height // 2
    count = len(vectors.arrays)
    keys = plan.direct()
    outs = len(keys) + 1

    def kernel(dense_ref, energies_ref, *refs):
        vector_refs, refs = refs[:count], refs[count:]
        sum_ref, right_ref, level_ref, own_ref, readers_ref, image_ref, outgoing = refs[:7]
        messages, scratch = refs[7 : 7 + outs], refs[7 + outs :]
        energy = wide([energies_ref[...]] * fields)
        opened = vectors.open(vector_refs, scratch)
        (center,) = centers([(0, own_ref)], depth)

        @pl.loop(0, clusters // BATCH)
        def _(batch):
            here = pl.ds(batch * BATCH, BATCH)
            value = sum_ref[here]
            for part in products(dense_ref, opened, here, energy):
                value = value + part
            for local in range(BATCH):
                cluster = batch * BATCH + local
                rows = pl.ds(pl.multiple_of(cluster * width, width), width)
                right = wide([right_ref[f, rows, :] for f in range(fields)])
                image = wide([level_ref[cluster]] * fields) * right + value[local]
                image_ref[cluster] = image
                outgoing[rows, :] = (image - center * right).astype(jnp.bfloat16)

        fill(plan, keys, readers_ref, outgoing, messages, width)

    image, full, *messages, out = call(
        kernel,
        "finish_first",
        [
            jax.ShapeDtypeStruct((clusters, width, lanes), jnp.float32),
            jax.ShapeDtypeStruct((clusters * width, lanes), jnp.bfloat16),
        ]
        + [jax.ShapeDtypeStruct((depth, lanes), jnp.bfloat16)] * outs,
        [vmem()] * (2 + count + 4) + [smem()],
        vectors.scratch,
        flops=work(dense, vectors.items, lanes),
        moved=8 * MIB,
    )(dense, energies, *vectors.arrays, value_sum, right_side, level, own, readers)
    return image, full, dict(zip(keys, messages)), out


def guesses(lines, fields):
    orbitals = lines.shape[1] // fields
    alphas, growths = [], []
    for column in field_sums(lines, fields):
        norm, bend, square = column[0:1], column[1:2], column[2:3]
        norm = jnp.maximum(norm, 1e-30)
        alpha = norm / jnp.maximum(bend, 4.0 * norm)
        alphas.append(alpha)
        growths.append(jnp.clip(alpha * alpha * square / norm, 1.0, 2.0))
    return per_field(alphas, orbitals), per_field(growths, orbitals)


def prepare(right_side, image, after):
    fields, rows, orbitals = right_side.shape
    clusters, width, lanes = image.shape

    def kernel(right_ref, image_ref, _, lines_ref, kept):
        kept[...] = jnp.zeros_like(kept)

        def sweep(base, terms):
            @pl.loop(0, clusters)
            def _(cluster):
                here = pl.ds(pl.multiple_of(cluster * width, width), width)
                right = wide([right_ref[f, here, :] for f in range(fields)])
                for index, term in enumerate(terms(right, image_ref[cluster])):
                    kept[base + index] += folded(term)

        sweep(0, lambda right, first: (right * right, right * first, first * first))
        alpha, growth = guesses(lined([kept[i] for i in range(3)], 8), fields)

        def later_terms(right, first):
            step = alpha * first
            residual = right - step
            return residual * residual, residual * first, (growth * right - step) * first

        sweep(3, later_terms)
        lines_ref[...] = lined([kept[i] for i in range(6)], 8)
        lines_ref[6:7, :] = alpha
        lines_ref[7:8, :] = growth

    return call(
        kernel,
        "prepare",
        jax.ShapeDtypeStruct((8, lanes), jnp.float32),
        [vmem(), vmem(), pl.BlockSpec(memory_space=pl.ANY)],
        [pltpu.VMEM((6, 8, lanes), jnp.float32)],
        flops=8 * MIB,
        moved=4 * MIB,
    )(right_side, image, after)


def finish_second(dense, vectors, energies, value_sum, right_side, level, image, weighted, lines, devices):
    _, clusters, height, _ = dense.shape
    lanes = vectors.lanes
    fields = right_side.shape[0]
    width = height // 2
    count = len(vectors.arrays)

    def kernel(dense_ref, energies_ref, *refs):
        vector_refs, refs = refs[:count], refs[count:]
        sum_ref, right_ref, level_ref, image_ref, weighted_ref, lines_ref = refs[:6]
        later_ref, out_ref, kept, *scratch = refs[6:]
        energy = wide([energies_ref[...]] * fields)
        alpha, growth = lines_ref[6:7, :], lines_ref[7:8, :]
        kept[...] = jnp.zeros_like(kept)
        opened = vectors.open(vector_refs, scratch)

        @pl.loop(0, clusters // BATCH)
        def _(batch):
            here = pl.ds(batch * BATCH, BATCH)
            value = sum_ref[here] + weighted_ref[here]
            for part in products(dense_ref, opened, here, energy):
                value = value + part
            for local in range(BATCH):
                cluster = batch * BATCH + local
                rows = pl.ds(pl.multiple_of(cluster * width, width), width)
                right = wide([right_ref[f, rows, :] for f in range(fields)])
                first = image_ref[cluster]
                later = wide([level_ref[cluster]] * fields) * first + value[local]
                later_ref[cluster] = later
                direction = growth * right - alpha * first
                for index, left in enumerate((direction, right, first)):
                    kept[index] += folded(left * later)

        block = jnp.concatenate([lines_ref[0:6, :], lined([kept[i] for i in range(3)], 10)], axis=0)
        orbitals = lanes // fields
        line, lane = (lax.broadcasted_iota(jnp.int32, (16, 128), d) for d in (0, 1))
        rows = []
        for f, column in enumerate(field_sums(block, fields)):
            first_lane = slice(f * orbitals, f * orbitals + 1)
            filled = jnp.broadcast_to(column, (16, 128))
            filled = jnp.where(line == 9, jnp.broadcast_to(alpha[:, first_lane], (16, 128)), filled)
            filled = jnp.where(line == 10, jnp.broadcast_to(growth[:, first_lane], (16, 128)), filled)
            rows.append(jnp.sum(jnp.where(line == lane, filled, 0.0), axis=0, keepdims=True))
        rows.append(jnp.zeros((8 - fields, 128), jnp.float32))
        out_ref[...] = jnp.broadcast_to(jnp.concatenate(rows, axis=0)[None], out_ref.shape)

    return call(
        kernel,
        "finish_second",
        [
            jax.ShapeDtypeStruct((clusters, width, lanes), jnp.float32),
            jax.ShapeDtypeStruct((devices, 8, 128), jnp.float32),
        ],
        [vmem()] * (2 + count + 6),
        [pltpu.VMEM((3, 8, lanes), jnp.float32)] + vectors.scratch,
        flops=work(dense, vectors.items, lanes),
        moved=8 * MIB,
    )(dense, energies, *vectors.arrays, value_sum, right_side, level, image, weighted, lines)


def step_sizes(gathered, fields, orbitals):
    rows = gathered.reshape(-1, 128)
    flat = wide([jnp.transpose(rows[i : i + 128]) for i in range(0, rows.shape[0], 128)])
    line = [flat[i : i + 1, :] for i in range(11)]
    place = lax.broadcasted_iota(jnp.int32, line[0].shape, 1) & 7
    whole = lambda v: [
        jnp.sum(jnp.where(place == f, v, 0.0), axis=1, keepdims=True) for f in range(fields)
    ]

    def back(values):
        row = jnp.zeros_like(line[0])
        for f, value in enumerate(values):
            row = jnp.where(place == f, jnp.broadcast_to(value, row.shape), row)
        return row

    norm = whole(line[0])
    alpha = [n / b for n, b in zip(norm, whole(line[1]))]
    growth = [a * a * s / n for a, s, n in zip(alpha, whole(line[2]), norm)]
    off, more = back(alpha) - line[9], back(growth) - line[10]
    after = whole(line[3] - 2.0 * off * line[4] + off * off * line[2])
    bend = whole(
        (line[10] * line[5] - line[9] * line[6])
        + more * (line[5] + line[10] * line[1] - line[9] * line[7])
        - off * (line[6] + line[10] * line[2] - line[9] * line[8])
        + more * more * line[1]
        - more * off * (line[7] + line[2])
        + off * off * line[8]
    )
    gain = [a / b for a, b in zip(after, bend)]
    return [per_field(v, orbitals) for v in (alpha, growth, gain)]


def final(right_side, image, later, gathered):
    fields, rows, orbitals = right_side.shape
    clusters, width, lanes = image.shape
    blocks = 4
    each = clusters // blocks

    def kernel(right_ref, image_ref, later_ref, gathered_ref, solution_ref, residual_ref, steps):
        step = pl.program_id(0)

        @pl.when(step == 0)
        def _():
            alpha, growth, gain = step_sizes(gathered_ref[...], fields, orbitals)
            steps[0:1, :] = alpha + gain * growth
            steps[1:2, :] = gain * alpha

        for local in range(each):
            cluster = step * each + local
            rows = pl.ds(pl.multiple_of(cluster * width, width), width)
            here = slice(local * width, (local + 1) * width)
            for field in range(fields):
                part = slice(field * orbitals, (field + 1) * orbitals)
                one, two = steps[0:1, part], steps[1:2, part]
                right = right_ref[field, rows, :]
                first = image_ref[cluster, :, part]
                later = later_ref[cluster, :, part]
                solution_ref[field, here, :] = one * right - two * first
                residual_ref[field, here, :] = (right - one * first) + two * later

    vector = pl.BlockSpec((fields, each * width, orbitals), lambda i: (0, i, 0))
    shape = jax.ShapeDtypeStruct(right_side.shape, jnp.float32)
    return pl.pallas_call(
        kernel,
        grid=(blocks,),
        out_shape=[shape, shape],
        in_specs=[vmem()] * 4,
        out_specs=[vector, vector],
        scratch_shapes=[pltpu.VMEM((8, lanes), jnp.float32)],
        compiler_params=pltpu.CompilerParams(vmem_limit_bytes=12 * MIB),
        name="final",
    )(right_side, image, later, gathered)


def body(right_side, onsite, energies, ks_tiles, correlation_tiles, tile_slot, readers):
    span, served = readers.shape[1:]
    clusters, _, width, _ = ks_tiles.shape
    rows = lax.axis_size("row")
    devices = rows * lax.axis_size("col")
    onsite = onsite.reshape(-1, width)
    energies = energies.reshape(1, -1)
    plan = Plan(rows, span, rows == 8 and span == 7)
    readers = jnp.swapaxes(readers, 1, 2)

    def begin(items):
        return couple(dense, Vectors(plan, items), energies, [])

    def partial(items, sums):
        for group in (items[2:4], items[4:6]):
            sums = couple(dense, Vectors(plan, group), energies, sums)
        return sums, Vectors(plan, items[-1:])

    early, full = pack(plan, readers, right_side, onsite)
    full = hand_on(full)
    direct, own = deal(plan, readers, full, served, width)
    dense = spread(tile_slot, ks_tiles, correlation_tiles, span, served)
    items, sums, chosen, _ = exchange(
        plan, readers, early, direct, own, full, None, begin, served, width
    )
    level = levels(onsite)
    sums, last = partial(items, sums)
    image, full, direct, out = finish_first(
        plan, dense, last, energies, sums[0], right_side, level, own, readers
    )

    items, begun, _, mark = exchange(
        plan, readers, {}, direct, out, full, chosen, begin, served, width
    )
    lines = prepare(right_side, image, mark)
    _, weighted = couple(dense, last, energies, sums, mark)
    (value,), last = partial(items, begun)
    later, gathered = finish_second(
        dense, last, energies, value, right_side, level, image, weighted, lines, devices
    )
    gathered = lax.all_to_all(gathered, ("row", "col"), 0, 0)
    return tuple(final(right_side, image, later, gathered))


def solution(mesh):
    placed = (
        P(None, "row", "col"),
        P("row"),
        P("col"),
        P("row", None, None, None),
        P("row", None, None, None),
        P("row", None),
        P("row", None, None),
    )
    return jax.shard_map(
        body,
        mesh=mesh,
        in_specs=placed,
        out_specs=(P(None, "row", "col"), P(None, "row", "col")),
        check_vma=False,
    )
```

```python
import functools

import jax
import jax.numpy as jnp
from jax import lax
from jax.experimental import pallas as pl
from jax.experimental.pallas import tpu as pltpu
from jax.sharding import PartitionSpec as P

MIB = 2**20
EXTRA = 16
BATCH = 4


def shifted(array, axis, by):
    count = lax.axis_size(axis)
    return lax.ppermute(array, axis, [(i, (i + by) % count) for i in range(count)])


def vmem():
    return pl.BlockSpec(memory_space=pltpu.VMEM)


def smem():
    return pl.BlockSpec(memory_space=pltpu.SMEM)


def call(kernel, name, out_shape, specs, scratch=(), flops=0, moved=MIB, limit=12):
    return pl.pallas_call(
        kernel,
        out_shape=out_shape,
        in_specs=specs,
        out_specs=jax.tree.map(lambda _: vmem(), out_shape),
        scratch_shapes=list(scratch),
        compiler_params=pltpu.CompilerParams(vmem_limit_bytes=limit * MIB),
        cost_estimate=pl.CostEstimate(flops=flops, bytes_accessed=moved, transcendentals=0),
        name=name,
    )


def wide(parts):
    return jnp.concatenate(parts, axis=1)


def folded(term):
    return jnp.sum(term.reshape(-1, 8, term.shape[-1]), axis=0)


def lined(parts, lines):
    parts = [jnp.sum(p, axis=0, keepdims=True) for p in parts]
    parts.append(jnp.zeros((lines - len(parts), parts[0].shape[1]), jnp.float32))
    return jnp.concatenate(parts, axis=0)


def per_field(values, orbitals):
    return wide([jnp.broadcast_to(v, (1, orbitals)) for v in values])


def field_sums(lines, fields):
    orbitals = lines.shape[1] // fields
    return [
        jnp.sum(lines[:, f * orbitals : (f + 1) * orbitals], axis=1, keepdims=True)
        for f in range(fields)
    ]


class Plan:
    def __init__(self, count, span, relayed):
        self.count, self.span, self.middle, self.relayed = count, span, (span - 1) // 2, relayed

    def offset(self, source, reader):
        value = lax.rem(source - reader + (self.middle + self.count), self.count)
        return jnp.minimum(value, self.span - 1) if self.relayed else value

    def direct(self):
        if self.relayed:
            return [1, 2, 3, 7]
        far = range(self.middle, 0, -1)
        return [by for f in far for by in (f, -f)]

    def reader(self, key, me):
        return me ^ key if self.relayed else lax.rem(me + key + self.count, self.count)

    def source(self, key, me):
        return me ^ key if self.relayed else lax.rem(me - key + self.count, self.count)

    def pairs(self, key):
        if not self.relayed:
            return [(i, (i + key) % self.count) for i in range(self.count)]
        return [(i, i ^ key) for i in range(self.count) if key < 4 or i not in INNER]


INNER = (2, 3, 4, 5)


def is_inner(me):
    return (me >= INNER[0]) & (me <= INNER[-1])


def pack(plan, readers, right_side, onsite):
    fields, rows, orbitals = right_side.shape
    served = readers.shape[1]
    clusters, width = onsite.shape
    lanes = fields * orbitals
    keys = plan.direct()

    def kernel(readers_hbm, right_hbm, onsite_hbm, *refs):
        messages, rounded = refs[: len(keys) + 1], refs[len(keys) + 1]
        readers_ref, right_ref, onsite_ref, sems, more = refs[len(keys) + 2 :]
        copies = []
        for cluster in range(clusters):
            here = pl.ds(cluster * width, width)
            copies.append(
                pltpu.make_async_copy(
                    right_hbm.at[:, here, :], right_ref.at[:, here, :], sems.at[cluster]
                )
            )
        others = [
            pltpu.make_async_copy(onsite_hbm, onsite_ref, more.at[0]),
            pltpu.make_async_copy(readers_hbm, readers_ref, more.at[1]),
        ]
        for copy in copies[:1] + others + copies[1:]:
            copy.start()
        others[0].wait()
        norm = [jnp.zeros((8, orbitals), jnp.float32)] * fields
        heavy = [jnp.zeros((8, orbitals), jnp.float32)] * fields
        for cluster in range(clusters):
            copies[cluster].wait()
            weight = jnp.broadcast_to(onsite_ref[cluster : cluster + 1, :], (8, width))
            here = slice(cluster * width, (cluster + 1) * width)
            for field in range(fields):
                right = right_ref[field, here, :]
                rounded[here, field * orbitals : (field + 1) * orbitals] = right.astype(jnp.bfloat16)
                square = right * right
                norm[field] += folded(square)
                heavy[field] += jnp.dot(weight, square, preferred_element_type=jnp.float32)
        centers = [
            jnp.sum(h[:1], axis=1, keepdims=True)
            / jnp.maximum(jnp.sum(jnp.sum(n, axis=0, keepdims=True), axis=1, keepdims=True), 1e-30)
            for h, n in zip(heavy, norm)
        ]
        others[1].wait()
        rest = jnp.broadcast_to(per_field(centers, orbitals), (EXTRA, lanes))
        line, lane = (lax.broadcasted_iota(jnp.int32, (EXTRA, lanes), d) for d in (0, 1))
        for offset in range(readers_ref.shape[2]):
            for slot in range(served):
                here = (line == offset + 1) & (lane == slot)
                rest = jnp.where(here, readers_ref[0, slot, offset].astype(jnp.float32), rest)
        rounded[clusters * width :, :] = rest.astype(jnp.bfloat16)
        fill(plan, keys, readers_ref, rounded, messages, width)

    message = jax.ShapeDtypeStruct((served * width + EXTRA, lanes), jnp.bfloat16)
    full = jax.ShapeDtypeStruct((clusters * width + EXTRA, lanes), jnp.bfloat16)
    *messages, own, full = call(
        kernel,
        "pack",
        [message] * (len(keys) + 1) + [full],
        [pl.BlockSpec(memory_space=pltpu.HBM)] * 3,
        [
            pltpu.SMEM(readers.shape, readers.dtype),
            pltpu.VMEM(right_side.shape, jnp.float32),
            pltpu.VMEM(onsite.shape, jnp.float32),
            pltpu.SemaphoreType.DMA((clusters,)),
            pltpu.SemaphoreType.DMA((2,)),
        ],
        limit=54,
    )(readers, right_side, onsite)
    return dict(zip(keys, messages)), own, full


def fill(plan, keys, readers_ref, rounded, messages, width):
    me = lax.axis_index("row")
    offsets = [plan.offset(me, plan.reader(key, me)) for key in keys] + [plan.middle]
    for offset, message in zip(offsets, messages):
        served = readers_ref.shape[1]
        gather([readers_ref[0, slot, offset] for slot in range(served)], rounded, message, width)


def gather(clusters, rounded, message, width):
    for slot, cluster in enumerate(clusters):
        start = pl.multiple_of(cluster * width, width)
        message[slot * width : (slot + 1) * width, :] = rounded[pl.ds(start, width), :]
    used = len(clusters) * width
    if message.shape[0] > used:
        message[used:, :] = rounded[rounded.shape[0] - EXTRA :, :]


def relay(plan, readers, mine, full, chosen, after, served, width):
    lanes = full.shape[1]
    extra = EXTRA if chosen is None else 0
    message = jax.ShapeDtypeStruct((served * width + extra, lanes), jnp.bfloat16)

    def kernel(*refs):
        readers_ref, mine_ref, full_ref, _, *refs = refs
        me = lax.axis_index("row")
        *messages, chosen_ref = refs if chosen is None else [*refs[1:], refs[0]]
        if chosen is None:
            base = full_ref.shape[0] - EXTRA
            table = full_ref[base : base + EXTRA, 0:width].astype(jnp.float32)
            line, lane = (lax.broadcasted_iota(jnp.int32, table.shape, d) for d in (0, 1))
            for index, reader in enumerate((me, me ^ 1, me ^ 3)):
                offset = plan.offset(me ^ 6, reader)
                for slot in range(served):
                    here = (line == offset + 1) & (lane == slot)
                    chosen_ref[index, slot] = jnp.sum(jnp.where(here, table, 0.0)).astype(jnp.int32)

        @pl.when(is_inner(me))
        def _():
            for index, out in enumerate(messages):
                gather([chosen_ref[index, slot] for slot in range(served)], full_ref, out, width)

        @pl.when(jnp.logical_not(is_inner(me)))
        def _():
            for key, out in zip((6, 5), messages[1:]):
                offset = plan.offset(me, me ^ key)
                clusters = [readers_ref[0, slot, offset] for slot in range(served)]
                gather(clusters, mine_ref, out, width)

    inputs = [readers, mine, full, after] + ([] if chosen is None else [chosen])
    specs = [smem(), vmem(), vmem(), pl.BlockSpec(memory_space=pl.ANY)]
    specs += [] if chosen is None else [smem()]
    shapes, outs = [message] * 3, [vmem()] * 3
    if chosen is None:
        shapes.append(jax.ShapeDtypeStruct((3, served), jnp.int32))
        outs.append(smem())
    *messages, last = pl.pallas_call(
        kernel,
        out_shape=shapes,
        in_specs=specs,
        out_specs=outs,
        compiler_params=pltpu.CompilerParams(vmem_limit_bytes=12 * MIB),
        cost_estimate=pl.CostEstimate(flops=0, bytes_accessed=MIB, transcendentals=0),
        name="relay",
    )(*inputs)
    return (messages, last) if chosen is None else (messages + [last], chosen)


def exchange(plan, readers, direct, own, full, chosen, begin, near, served, width):
    sent = {k: lax.ppermute(m, "row", plan.pairs(k)) for k, m in direct.items()}
    if not plan.relayed:
        items = [(own, 0)] + [(sent[k], k) for k in plan.direct()]
        sums = begin(items[:3], None)
        return items, sums, None, sums[0]
    theirs = lax.ppermute(full, "row", [(i, i ^ 6) for i in INNER])
    items = [(own, 0)] + [(sent[k], k) for k in near]
    sums = begin(items[:3], theirs if chosen is None else None)
    (mine, near, far), chosen = relay(
        plan, readers, full, theirs, chosen, sums[0], served, width
    )
    near = lax.ppermute(near, "row", [(i, i ^ (1 if i in INNER else 6)) for i in range(plan.count)])
    far = lax.ppermute(far, "row", [(i, i ^ (3 if i in INNER else 5)) for i in range(plan.count)])
    items += [((mine, sent[7]), (6, 7)), (far, 5), (near, (7, 6))]
    return items, sums, chosen, mine


class Vectors:
    def __init__(self, plan, items):
        self.plan, self.items = plan, items
        self.arrays, self.scratch = [], []
        for value, _ in items:
            many = isinstance(value, tuple)
            self.arrays += list(value) if many else [value]
            if many:
                self.scratch.append(pltpu.VMEM(value[0].shape, value[0].dtype))
        self.lanes = self.arrays[0].shape[1]
        self.rows = self.arrays[0].shape[0]

    def open(self, refs, scratch):
        refs, scratch = list(refs), list(scratch)
        me = lax.axis_index("row")
        opened = []
        for value, key in self.items:
            if not self.plan.relayed:
                opened.append((self.plan.middle - key, refs.pop(0)))
                continue
            inner, outer = key if isinstance(key, tuple) else (key, key)
            held = refs.pop(0)
            if isinstance(value, tuple):
                kept, held, other = held, scratch.pop(0), refs.pop(0)

                @pl.when(is_inner(me))
                def _():
                    held[...] = kept[...]

                @pl.when(jnp.logical_not(is_inner(me)))
                def _():
                    held[...] = other[...]

            source = jnp.where(is_inner(me), me ^ inner, me ^ outer)
            opened.append((self.plan.offset(source, me), held))
        return opened


def levels(onsite):
    clusters, width = onsite.shape

    def kernel(onsite_ref, level_ref):
        for cluster in range(clusters):
            level_ref[cluster] = jnp.transpose(
                jnp.broadcast_to(onsite_ref[cluster : cluster + 1, :], (width, width))
            )

    shape = jax.ShapeDtypeStruct((clusters, width, width), jnp.float32)
    return call(kernel, "levels", shape, [vmem()])(onsite)


def spread(tile_slot, ks_tiles, correlation_tiles, span, served):
    clusters, _, width, _ = ks_tiles.shape
    slots = span * served

    def kernel(slot_ref, ks_ref, correlation_ref, out_ref, where):
        @pl.loop(0, clusters)
        def _(cluster):
            for kind, ref in enumerate((ks_ref, correlation_ref)):
                count = ref.shape[1]
                for slot in range(slots):
                    where[slot] = count
                for tile in range(count):
                    where[slot_ref[cluster, tile]] = tile
                for slot in range(slots):
                    tile = where[slot]
                    block = ref[cluster, jnp.minimum(tile, count - 1)]
                    block = jnp.where(tile < count, block, jnp.zeros_like(block))
                    lane = slot % served * width
                    out_ref[
                        slot // served, cluster, kind * width : (kind + 1) * width, lane : lane + width
                    ] = block

    return call(
        kernel,
        "spread",
        jax.ShapeDtypeStruct((span, clusters, 2 * width, served * width), jnp.bfloat16),
        [smem(), vmem(), vmem()],
        [pltpu.SMEM((slots,), jnp.int32)],
        moved=16 * MIB,
    )(tile_slot, ks_tiles, correlation_tiles)


def products(dense_ref, opened, clusters, energy):
    depth = dense_ref.shape[-1]
    for offset, vector in opened:
        left = dense_ref[offset, clusters]
        count, height, _ = left.shape
        value = jnp.dot(
            left.reshape(count * height, depth), vector[0:depth, :], preferred_element_type=jnp.float32
        )
        value = value.reshape(count, 2, height // 2, value.shape[1])
        yield value[:, 0] - energy * value[:, 1]


def centers(opened, depth):
    return [vector[depth : depth + EXTRA, :].astype(jnp.float32)[:1] for _, vector in opened]


def work(dense, items, lanes):
    return 2 * len(items) * dense.shape[1] * dense.shape[2] * dense.shape[3] * lanes


def couple(dense, vectors, energies, sums, after=None):
    _, clusters, height, depth = dense.shape
    lanes = vectors.lanes
    count = len(vectors.arrays)
    outs = 2 if vectors.rows > depth else 1
    had = len(sums)

    def kernel(dense_ref, energies_ref, *refs):
        refs = list(refs[1:] if after is not None else refs)
        vector_refs, sum_refs = refs[:count], refs[count : count + had]
        out_refs, scratch = refs[count + had : count + had + outs], refs[count + had + outs :]
        energy = wide([energies_ref[...]] * (lanes // energies_ref.shape[1]))
        opened = vectors.open(vector_refs, scratch)
        weights = centers(opened, depth) if outs == 2 else [None] * len(opened)

        @pl.loop(0, clusters // BATCH)
        def _(batch):
            here = pl.ds(batch * BATCH, BATCH)
            values = [ref[here] for ref in sum_refs]
            for weight, part in zip(weights, products(dense_ref, opened, here, energy)):
                terms = [part] if weight is None else [part, weight * part]
                values = [v + t for v, t in zip(values, terms)] if values else terms
            for ref, value in zip(out_refs, values):
                ref[here] = value

    order = [] if after is None else [after]
    inputs = [dense, energies, *order, *vectors.arrays, *sums]
    shape = jax.ShapeDtypeStruct((clusters, height // 2, lanes), jnp.float32)
    return call(
        kernel,
        "couple",
        [shape] * outs,
        [vmem()] * 2
        + [pl.BlockSpec(memory_space=pl.ANY)] * len(order)
        + [vmem()] * (len(vectors.arrays) + had),
        vectors.scratch,
        flops=work(dense, vectors.items, lanes),
        moved=4 * MIB,
    )(*inputs)


def finish_first(plan, dense, vectors, energies, value_sum, right_side, level, own, readers):
    _, clusters, height, depth = dense.shape
    lanes = vectors.lanes
    fields = right_side.shape[0]
    width = height // 2
    count = len(vectors.arrays)
    keys = plan.direct()
    outs = len(keys) + 1

    def kernel(dense_ref, energies_ref, *refs):
        vector_refs, refs = refs[:count], refs[count:]
        sum_ref, right_ref, level_ref, own_ref, readers_ref, image_ref, outgoing = refs[:7]
        messages, scratch = refs[7 : 7 + outs], refs[7 + outs :]
        energy = wide([energies_ref[...]] * fields)
        opened = vectors.open(vector_refs, scratch)
        (center,) = centers([(0, own_ref)], depth)

        @pl.loop(0, clusters // BATCH)
        def _(batch):
            here = pl.ds(batch * BATCH, BATCH)
            value = sum_ref[here]
            for part in products(dense_ref, opened, here, energy):
                value = value + part
            for local in range(BATCH):
                cluster = batch * BATCH + local
                rows = pl.ds(pl.multiple_of(cluster * width, width), width)
                right = wide([right_ref[f, rows, :] for f in range(fields)])
                image = wide([level_ref[cluster]] * fields) * right + value[local]
                image_ref[cluster] = image
                outgoing[rows, :] = (image - center * right).astype(jnp.bfloat16)

        fill(plan, keys, readers_ref, outgoing, messages, width)

    image, full, *messages, out = call(
        kernel,
        "finish_first",
        [
            jax.ShapeDtypeStruct((clusters, width, lanes), jnp.float32),
            jax.ShapeDtypeStruct((clusters * width, lanes), jnp.bfloat16),
        ]
        + [jax.ShapeDtypeStruct((depth, lanes), jnp.bfloat16)] * outs,
        [vmem()] * (2 + count + 4) + [smem()],
        vectors.scratch,
        flops=work(dense, vectors.items, lanes),
        moved=8 * MIB,
    )(dense, energies, *vectors.arrays, value_sum, right_side, level, own, readers)
    return image, full, dict(zip(keys, messages)), out


def guesses(lines, fields):
    orbitals = lines.shape[1] // fields
    alphas, growths = [], []
    for column in field_sums(lines, fields):
        norm, bend, square = column[0:1], column[1:2], column[2:3]
        norm = jnp.maximum(norm, 1e-30)
        alpha = norm / jnp.maximum(bend, 4.0 * norm)
        alphas.append(alpha)
        growths.append(jnp.clip(alpha * alpha * square / norm, 1.0, 2.0))
    return per_field(alphas, orbitals), per_field(growths, orbitals)


def prepare(right_side, image, after):
    fields, rows, orbitals = right_side.shape
    clusters, width, lanes = image.shape

    def kernel(right_ref, image_ref, _, lines_ref, kept):
        kept[...] = jnp.zeros_like(kept)

        def sweep(base, terms):
            @pl.loop(0, clusters)
            def _(cluster):
                here = pl.ds(pl.multiple_of(cluster * width, width), width)
                right = wide([right_ref[f, here, :] for f in range(fields)])
                for index, term in enumerate(terms(right, image_ref[cluster])):
                    kept[base + index] += folded(term)

        sweep(0, lambda right, first: (right * right, right * first, first * first))
        alpha, growth = guesses(lined([kept[i] for i in range(3)], 8), fields)

        def later_terms(right, first):
            step = alpha * first
            residual = right - step
            return residual * residual, residual * first, (growth * right - step) * first

        sweep(3, later_terms)
        lines_ref[...] = lined([kept[i] for i in range(6)], 8)
        lines_ref[6:7, :] = alpha
        lines_ref[7:8, :] = growth

    return call(
        kernel,
        "prepare",
        jax.ShapeDtypeStruct((8, lanes), jnp.float32),
        [vmem(), vmem(), pl.BlockSpec(memory_space=pl.ANY)],
        [pltpu.VMEM((6, 8, lanes), jnp.float32)],
        flops=8 * MIB,
        moved=4 * MIB,
    )(right_side, image, after)


def finish_second(dense, vectors, energies, value_sum, right_side, level, image, weighted, lines, devices):
    _, clusters, height, _ = dense.shape
    lanes = vectors.lanes
    fields = right_side.shape[0]
    width = height // 2
    count = len(vectors.arrays)

    def kernel(dense_ref, energies_ref, *refs):
        vector_refs, refs = refs[:count], refs[count:]
        sum_ref, right_ref, level_ref, image_ref, weighted_ref, lines_ref = refs[:6]
        later_ref, out_ref, kept, *scratch = refs[6:]
        energy = wide([energies_ref[...]] * fields)
        alpha, growth = lines_ref[6:7, :], lines_ref[7:8, :]
        kept[...] = jnp.zeros_like(kept)
        opened = vectors.open(vector_refs, scratch)

        @pl.loop(0, clusters // BATCH)
        def _(batch):
            here = pl.ds(batch * BATCH, BATCH)
            value = sum_ref[here] + weighted_ref[here]
            for part in products(dense_ref, opened, here, energy):
                value = value + part
            for local in range(BATCH):
                cluster = batch * BATCH + local
                rows = pl.ds(pl.multiple_of(cluster * width, width), width)
                right = wide([right_ref[f, rows, :] for f in range(fields)])
                first = image_ref[cluster]
                later = wide([level_ref[cluster]] * fields) * first + value[local]
                later_ref[cluster] = later
                direction = growth * right - alpha * first
                for index, left in enumerate((direction, right, first)):
                    kept[index] += folded(left * later)

        block = jnp.concatenate([lines_ref[0:6, :], lined([kept[i] for i in range(3)], 10)], axis=0)
        orbitals = lanes // fields
        line, lane = (lax.broadcasted_iota(jnp.int32, (16, 128), d) for d in (0, 1))
        rows = []
        for f, column in enumerate(field_sums(block, fields)):
            first_lane = slice(f * orbitals, f * orbitals + 1)
            filled = jnp.broadcast_to(column, (16, 128))
            filled = jnp.where(line == 9, jnp.broadcast_to(alpha[:, first_lane], (16, 128)), filled)
            filled = jnp.where(line == 10, jnp.broadcast_to(growth[:, first_lane], (16, 128)), filled)
            rows.append(jnp.sum(jnp.where(line == lane, filled, 0.0), axis=0, keepdims=True))
        rows.append(jnp.zeros((8 - fields, 128), jnp.float32))
        out_ref[...] = jnp.broadcast_to(jnp.concatenate(rows, axis=0)[None], out_ref.shape)

    return call(
        kernel,
        "finish_second",
        [
            jax.ShapeDtypeStruct((clusters, width, lanes), jnp.float32),
            jax.ShapeDtypeStruct((devices, 8, 128), jnp.float32),
        ],
        [vmem()] * (2 + count + 6),
        [pltpu.VMEM((3, 8, lanes), jnp.float32)] + vectors.scratch,
        flops=work(dense, vectors.items, lanes),
        moved=8 * MIB,
    )(dense, energies, *vectors.arrays, value_sum, right_side, level, image, weighted, lines)


def step_sizes(gathered, fields, orbitals):
    rows = gathered.reshape(-1, 128)
    flat = wide([jnp.transpose(rows[i : i + 128]) for i in range(0, rows.shape[0], 128)])
    line = [flat[i : i + 1, :] for i in range(11)]
    place = lax.broadcasted_iota(jnp.int32, line[0].shape, 1) & 7
    whole = lambda v: [
        jnp.sum(jnp.where(place == f, v, 0.0), axis=1, keepdims=True) for f in range(fields)
    ]

    def back(values):
        row = jnp.zeros_like(line[0])
        for f, value in enumerate(values):
            row = jnp.where(place == f, jnp.broadcast_to(value, row.shape), row)
        return row

    norm = whole(line[0])
    alpha = [n / b for n, b in zip(norm, whole(line[1]))]
    growth = [a * a * s / n for a, s, n in zip(alpha, whole(line[2]), norm)]
    off, more = back(alpha) - line[9], back(growth) - line[10]
    after = whole(line[3] - 2.0 * off * line[4] + off * off * line[2])
    bend = whole(
        (line[10] * line[5] - line[9] * line[6])
        + more * (line[5] + line[10] * line[1] - line[9] * line[7])
        - off * (line[6] + line[10] * line[2] - line[9] * line[8])
        + more * more * line[1]
        - more * off * (line[7] + line[2])
        + off * off * line[8]
    )
    gain = [a / b for a, b in zip(after, bend)]
    return [per_field(v, orbitals) for v in (alpha, growth, gain)]


def final(right_side, image, later, gathered):
    fields, rows, orbitals = right_side.shape
    clusters, width, lanes = image.shape
    blocks = 4
    each = clusters // blocks

    def kernel(right_ref, image_ref, later_ref, gathered_ref, solution_ref, residual_ref, steps):
        step = pl.program_id(0)

        @pl.when(step == 0)
        def _():
            alpha, growth, gain = step_sizes(gathered_ref[...], fields, orbitals)
            steps[0:1, :] = alpha + gain * growth
            steps[1:2, :] = gain * alpha

        for local in range(each):
            cluster = step * each + local
            rows = pl.ds(pl.multiple_of(cluster * width, width), width)
            here = slice(local * width, (local + 1) * width)
            for field in range(fields):
                part = slice(field * orbitals, (field + 1) * orbitals)
                one, two = steps[0:1, part], steps[1:2, part]
                right = right_ref[field, rows, :]
                first = image_ref[cluster, :, part]
                later = later_ref[cluster, :, part]
                solution_ref[field, here, :] = one * right - two * first
                residual_ref[field, here, :] = (right - one * first) + two * later

    vector = pl.BlockSpec((fields, each * width, orbitals), lambda i: (0, i, 0))
    shape = jax.ShapeDtypeStruct(right_side.shape, jnp.float32)
    return pl.pallas_call(
        kernel,
        grid=(blocks,),
        out_shape=[shape, shape],
        in_specs=[vmem()] * 4,
        out_specs=[vector, vector],
        scratch_shapes=[pltpu.VMEM((8, lanes), jnp.float32)],
        compiler_params=pltpu.CompilerParams(vmem_limit_bytes=12 * MIB),
        name="final",
    )(right_side, image, later, gathered)


def body(right_side, onsite, energies, ks_tiles, correlation_tiles, tile_slot, readers):
    span, served = readers.shape[1:]
    clusters, _, width, _ = ks_tiles.shape
    rows = lax.axis_size("row")
    devices = rows * lax.axis_size("col")
    onsite = onsite.reshape(-1, width)
    energies = energies.reshape(1, -1)
    plan = Plan(rows, span, rows == 8 and span == 7)
    readers = jnp.swapaxes(readers, 1, 2)

    def begin(items, after):
        return couple(dense, Vectors(plan, items), energies, [], after)

    def partial(items, sums):
        for group in (items[3:-2], items[-2:-1]):
            sums = couple(dense, Vectors(plan, group), energies, sums)
        return sums, Vectors(plan, items[-1:])

    direct, own, full = pack(plan, readers, right_side, onsite)
    dense = spread(tile_slot, ks_tiles, correlation_tiles, span, served)
    items, sums, chosen, _ = exchange(plan, readers, direct, own, full, None, begin, (1, 2, 3), served, width)
    level = levels(onsite)
    sums, last = partial(items, sums)
    image, full, direct, out = finish_first(
        plan, dense, last, energies, sums[0], right_side, level, own, readers
    )

    items, begun, _, mark = exchange(plan, readers, direct, out, full, chosen, begin, (2, 3, 1), served, width)
    lines = prepare(right_side, image, mark)
    _, weighted = couple(dense, last, energies, sums, mark)
    (value,), last = partial(items, begun)
    later, gathered = finish_second(
        dense, last, energies, value, right_side, level, image, weighted, lines, devices
    )
    gathered = lax.all_to_all(gathered, ("row", "col"), 0, 0)
    return tuple(final(right_side, image, later, gathered))


def solution(mesh):
    placed = (
        P(None, "row", "col"),
        P("row"),
        P("col"),
        P("row", None, None, None),
        P("row", None, None, None),
        P("row", None),
        P("row", None, None),
    )
    return jax.shard_map(
        body,
        mesh=mesh,
        in_specs=placed,
        out_specs=(P(None, "row", "col"), P(None, "row", "col")),
        check_vma=False,
    )
```

```python
import functools

import jax
import jax.numpy as jnp
from jax import lax
from jax.experimental import pallas as pl
from jax.experimental.pallas import tpu as pltpu
from jax.sharding import PartitionSpec as P

MIB = 2**20
EXTRA = 16
BATCH = 4


def shifted(array, axis, by):
    count = lax.axis_size(axis)
    return lax.ppermute(array, axis, [(i, (i + by) % count) for i in range(count)])


def vmem():
    return pl.BlockSpec(memory_space=pltpu.VMEM)


def smem():
    return pl.BlockSpec(memory_space=pltpu.SMEM)


def call(kernel, name, out_shape, specs, scratch=(), flops=0, moved=MIB, limit=12):
    return pl.pallas_call(
        kernel,
        out_shape=out_shape,
        in_specs=specs,
        out_specs=jax.tree.map(lambda _: vmem(), out_shape),
        scratch_shapes=list(scratch),
        compiler_params=pltpu.CompilerParams(vmem_limit_bytes=limit * MIB),
        cost_estimate=pl.CostEstimate(flops=flops, bytes_accessed=moved, transcendentals=0),
        name=name,
    )


def wide(parts):
    return jnp.concatenate(parts, axis=1)


def folded(term):
    return jnp.sum(term.reshape(-1, 8, term.shape[-1]), axis=0)


def lined(parts, lines):
    parts = [jnp.sum(p, axis=0, keepdims=True) for p in parts]
    parts.append(jnp.zeros((lines - len(parts), parts[0].shape[1]), jnp.float32))
    return jnp.concatenate(parts, axis=0)


def per_field(values, orbitals):
    return wide([jnp.broadcast_to(v, (1, orbitals)) for v in values])


def field_sums(lines, fields):
    orbitals = lines.shape[1] // fields
    return [
        jnp.sum(lines[:, f * orbitals : (f + 1) * orbitals], axis=1, keepdims=True)
        for f in range(fields)
    ]


class Plan:
    def __init__(self, count, span, relayed):
        self.count, self.span, self.middle, self.relayed = count, span, (span - 1) // 2, relayed

    def offset(self, source, reader):
        value = lax.rem(source - reader + (self.middle + self.count), self.count)
        return jnp.minimum(value, self.span - 1) if self.relayed else value

    def direct(self):
        if self.relayed:
            return [1, 2, 3, 7]
        far = range(self.middle, 0, -1)
        return [by for f in far for by in (f, -f)]

    def again(self):
        return [2, 3, 1] if self.relayed else self.direct()

    def reader(self, key, me):
        return me ^ key if self.relayed else lax.rem(me + key + self.count, self.count)

    def source(self, key, me):
        return me ^ key if self.relayed else lax.rem(me - key + self.count, self.count)

    def pairs(self, key):
        if not self.relayed:
            return [(i, (i + key) % self.count) for i in range(self.count)]
        return [(i, i ^ key) for i in range(self.count) if key < 4 or i not in INNER]


INNER = (2, 3, 4, 5)


def is_inner(me):
    return (me >= INNER[0]) & (me <= INNER[-1])


def pack(plan, readers, right_side, onsite):
    fields, rows, orbitals = right_side.shape
    served = readers.shape[1]
    clusters, width = onsite.shape
    lanes = fields * orbitals
    keys = plan.direct()

    def kernel(readers_hbm, right_hbm, onsite_hbm, *refs):
        messages, rounded = refs[: len(keys) + 1], refs[len(keys) + 1]
        readers_ref, right_ref, onsite_ref, sems, more = refs[len(keys) + 2 :]
        copies = []
        for cluster in range(clusters):
            here = pl.ds(cluster * width, width)
            copies.append(
                pltpu.make_async_copy(
                    right_hbm.at[:, here, :], right_ref.at[:, here, :], sems.at[cluster]
                )
            )
        others = [
            pltpu.make_async_copy(onsite_hbm, onsite_ref, more.at[0]),
            pltpu.make_async_copy(readers_hbm, readers_ref, more.at[1]),
        ]
        for copy in copies[:1] + others + copies[1:]:
            copy.start()
        others[0].wait()
        norm = [jnp.zeros((8, orbitals), jnp.float32)] * fields
        heavy = [jnp.zeros((8, orbitals), jnp.float32)] * fields
        for cluster in range(clusters):
            copies[cluster].wait()
            weight = jnp.broadcast_to(onsite_ref[cluster : cluster + 1, :], (8, width))
            here = slice(cluster * width, (cluster + 1) * width)
            for field in range(fields):
                right = right_ref[field, here, :]
                rounded[here, field * orbitals : (field + 1) * orbitals] = right.astype(jnp.bfloat16)
                square = right * right
                norm[field] += folded(square)
                heavy[field] += jnp.dot(weight, square, preferred_element_type=jnp.float32)
        centers = [
            jnp.sum(h[:1], axis=1, keepdims=True)
            / jnp.maximum(jnp.sum(jnp.sum(n, axis=0, keepdims=True), axis=1, keepdims=True), 1e-30)
            for h, n in zip(heavy, norm)
        ]
        others[1].wait()
        rest = jnp.broadcast_to(per_field(centers, orbitals), (EXTRA, lanes))
        line, lane = (lax.broadcasted_iota(jnp.int32, (EXTRA, lanes), d) for d in (0, 1))
        for offset in range(readers_ref.shape[2]):
            for slot in range(served):
                here = (line == offset + 1) & (lane == slot)
                rest = jnp.where(here, readers_ref[0, slot, offset].astype(jnp.float32), rest)
        rounded[clusters * width :, :] = rest.astype(jnp.bfloat16)
        fill(plan, keys, readers_ref, rounded, messages, width)

    message = jax.ShapeDtypeStruct((served * width + EXTRA, lanes), jnp.bfloat16)
    full = jax.ShapeDtypeStruct((clusters * width + EXTRA, lanes), jnp.bfloat16)
    *messages, own, full = call(
        kernel,
        "pack",
        [message] * (len(keys) + 1) + [full],
        [pl.BlockSpec(memory_space=pltpu.HBM)] * 3,
        [
            pltpu.SMEM(readers.shape, readers.dtype),
            pltpu.VMEM(right_side.shape, jnp.float32),
            pltpu.VMEM(onsite.shape, jnp.float32),
            pltpu.SemaphoreType.DMA((clusters,)),
            pltpu.SemaphoreType.DMA((2,)),
        ],
        limit=51,
    )(readers, right_side, onsite)
    return dict(zip(keys, messages)), own, full


def fill(plan, keys, readers_ref, rounded, messages, width):
    me = lax.axis_index("row")
    offsets = [plan.offset(me, plan.reader(key, me)) for key in keys] + [plan.middle]
    for offset, message in zip(offsets, messages):
        served = readers_ref.shape[1]
        gather([readers_ref[0, slot, offset] for slot in range(served)], rounded, message, width)


def gather(clusters, rounded, message, width):
    for slot, cluster in enumerate(clusters):
        start = pl.multiple_of(cluster * width, width)
        message[slot * width : (slot + 1) * width, :] = rounded[pl.ds(start, width), :]
    used = len(clusters) * width
    if message.shape[0] > used:
        message[used:, :] = rounded[rounded.shape[0] - EXTRA :, :]


def relay(plan, readers, mine, full, chosen, after, served, width):
    lanes = full.shape[1]
    extra = EXTRA if chosen is None else 0
    message = jax.ShapeDtypeStruct((served * width + extra, lanes), jnp.bfloat16)

    def kernel(*refs):
        readers_ref, mine_ref, full_ref, _, *refs = refs
        me = lax.axis_index("row")
        *messages, chosen_ref = refs if chosen is None else [*refs[1:], refs[0]]
        beyond = messages[3:]
        messages = messages[:3]
        if chosen is None:
            base = full_ref.shape[0] - EXTRA
            table = full_ref[base : base + EXTRA, 0:width].astype(jnp.float32)
            line, lane = (lax.broadcasted_iota(jnp.int32, table.shape, d) for d in (0, 1))
            for index, reader in enumerate((me, me ^ 1, me ^ 3)):
                offset = plan.offset(me ^ 6, reader)
                for slot in range(served):
                    here = (line == offset + 1) & (lane == slot)
                    chosen_ref[index, slot] = jnp.sum(jnp.where(here, table, 0.0)).astype(jnp.int32)

        @pl.when(is_inner(me))
        def _():
            for index, out in enumerate(messages):
                gather([chosen_ref[index, slot] for slot in range(served)], full_ref, out, width)

        @pl.when(jnp.logical_not(is_inner(me)))
        def _():
            for key, out in zip((6, 5, 7), [*messages[1:], *beyond]):
                offset = plan.offset(me, me ^ key)
                clusters = [readers_ref[0, slot, offset] for slot in range(served)]
                gather(clusters, mine_ref, out, width)

    inputs = [readers, mine, full, after] + ([] if chosen is None else [chosen])
    specs = [smem(), vmem(), vmem(), pl.BlockSpec(memory_space=pl.ANY)]
    specs += [] if chosen is None else [smem()]
    count = 3 if chosen is None else 4
    shapes, outs = [message] * count, [vmem()] * count
    if chosen is None:
        shapes.append(jax.ShapeDtypeStruct((3, served), jnp.int32))
        outs.append(smem())
    *messages, last = pl.pallas_call(
        kernel,
        out_shape=shapes,
        in_specs=specs,
        out_specs=outs,
        compiler_params=pltpu.CompilerParams(vmem_limit_bytes=12 * MIB),
        cost_estimate=pl.CostEstimate(flops=0, bytes_accessed=MIB, transcendentals=0),
        name="relay",
    )(*inputs)
    return (messages, last) if chosen is None else (messages + [last], chosen)


def exchange(plan, readers, direct, own, full, chosen, begin, near, served, width):
    sent = {k: lax.ppermute(m, "row", plan.pairs(k)) for k, m in direct.items()}
    if not plan.relayed:
        items = [(own, 0)] + [(sent[k], k) for k in plan.direct()]
        sums = begin(items[:2], None)
        return items, sums, None, sums[0]
    theirs = lax.ppermute(full, "row", [(i, i ^ 6) for i in INNER])
    items = [(own, 0)] + [(sent[k], k) for k in near]
    first = chosen is None
    sums = begin(items[:3], theirs) if first else begin(items[:2], None)
    (mine, near, far, *beyond), chosen = relay(
        plan, readers, full, theirs, chosen, sums[0], served, width
    )
    near = lax.ppermute(near, "row", [(i, i ^ (1 if i in INNER else 6)) for i in range(plan.count)])
    far = lax.ppermute(far, "row", [(i, i ^ (3 if i in INNER else 5)) for i in range(plan.count)])
    over = sent[7] if first else lax.ppermute(beyond[0], "row", plan.pairs(7))
    middle = [((mine, over), (6, 7)), (far, 5)]
    items += (middle if first else middle[::-1]) + [(near, (7, 6))]
    return items, sums, chosen, mine


class Vectors:
    def __init__(self, plan, items):
        self.plan, self.items = plan, items
        self.arrays, self.scratch = [], []
        for value, _ in items:
            many = isinstance(value, tuple)
            self.arrays += list(value) if many else [value]
            if many:
                self.scratch.append(pltpu.VMEM(value[0].shape, value[0].dtype))
        self.lanes = self.arrays[0].shape[1]
        self.rows = self.arrays[0].shape[0]

    def open(self, refs, scratch):
        refs, scratch = list(refs), list(scratch)
        me = lax.axis_index("row")
        opened = []
        for value, key in self.items:
            if not self.plan.relayed:
                opened.append((self.plan.middle - key, refs.pop(0)))
                continue
            inner, outer = key if isinstance(key, tuple) else (key, key)
            held = refs.pop(0)
            if isinstance(value, tuple):
                kept, held, other = held, scratch.pop(0), refs.pop(0)

                @pl.when(is_inner(me))
                def _():
                    held[...] = kept[...]

                @pl.when(jnp.logical_not(is_inner(me)))
                def _():
                    held[...] = other[...]

            source = jnp.where(is_inner(me), me ^ inner, me ^ outer)
            opened.append((self.plan.offset(source, me), held))
        return opened


def levels(onsite):
    clusters, width = onsite.shape

    def kernel(onsite_ref, level_ref):
        for cluster in range(clusters):
            level_ref[cluster] = jnp.transpose(
                jnp.broadcast_to(onsite_ref[cluster : cluster + 1, :], (width, width))
            )

    shape = jax.ShapeDtypeStruct((clusters, width, width), jnp.float32)
    return call(kernel, "levels", shape, [vmem()])(onsite)


def spread(tile_slot, ks_tiles, correlation_tiles, span, served):
    clusters, _, width, _ = ks_tiles.shape
    slots = span * served

    def kernel(slot_ref, ks_ref, correlation_ref, out_ref, where):
        @pl.loop(0, clusters)
        def _(cluster):
            for kind, ref in enumerate((ks_ref, correlation_ref)):
                count = ref.shape[1]
                for slot in range(slots):
                    where[slot] = count
                for tile in range(count):
                    where[slot_ref[cluster, tile]] = tile
                for slot in range(slots):
                    tile = where[slot]
                    block = ref[cluster, jnp.minimum(tile, count - 1)]
                    block = jnp.where(tile < count, block, jnp.zeros_like(block))
                    lane = slot % served * width
                    out_ref[
                        slot // served, cluster, kind * width : (kind + 1) * width, lane : lane + width
                    ] = block

    return call(
        kernel,
        "spread",
        jax.ShapeDtypeStruct((span, clusters, 2 * width, served * width), jnp.bfloat16),
        [smem(), vmem(), vmem()],
        [pltpu.SMEM((slots,), jnp.int32)],
        moved=16 * MIB,
    )(tile_slot, ks_tiles, correlation_tiles)


def products(dense_ref, opened, clusters, energy):
    depth = dense_ref.shape[-1]
    for offset, vector in opened:
        left = dense_ref[offset, clusters]
        count, height, _ = left.shape
        value = jnp.dot(
            left.reshape(count * height, depth), vector[0:depth, :], preferred_element_type=jnp.float32
        )
        value = value.reshape(count, 2, height // 2, value.shape[1])
        yield value[:, 0] - energy * value[:, 1]


def centers(opened, depth):
    return [vector[depth : depth + EXTRA, :].astype(jnp.float32)[:1] for _, vector in opened]


def work(dense, items, lanes):
    return 2 * len(items) * dense.shape[1] * dense.shape[2] * dense.shape[3] * lanes


def couple(dense, vectors, energies, sums, after=None):
    _, clusters, height, depth = dense.shape
    lanes = vectors.lanes
    count = len(vectors.arrays)
    outs = 2 if vectors.rows > depth else 1
    had = len(sums)

    def kernel(dense_ref, energies_ref, *refs):
        refs = list(refs[1:] if after is not None else refs)
        vector_refs, sum_refs = refs[:count], refs[count : count + had]
        out_refs, scratch = refs[count + had : count + had + outs], refs[count + had + outs :]
        energy = wide([energies_ref[...]] * (lanes // energies_ref.shape[1]))
        opened = vectors.open(vector_refs, scratch)
        weights = centers(opened, depth) if outs == 2 else [None] * len(opened)

        @pl.loop(0, clusters // BATCH)
        def _(batch):
            here = pl.ds(batch * BATCH, BATCH)
            values = [ref[here] for ref in sum_refs]
            for weight, part in zip(weights, products(dense_ref, opened, here, energy)):
                terms = [part] if weight is None else [part, weight * part]
                values = [v + t for v, t in zip(values, terms)] if values else terms
            for ref, value in zip(out_refs, values):
                ref[here] = value

    order = [] if after is None else [after]
    inputs = [dense, energies, *order, *vectors.arrays, *sums]
    shape = jax.ShapeDtypeStruct((clusters, height // 2, lanes), jnp.float32)
    return call(
        kernel,
        "couple",
        [shape] * outs,
        [vmem()] * 2
        + [pl.BlockSpec(memory_space=pl.ANY)] * len(order)
        + [vmem()] * (len(vectors.arrays) + had),
        vectors.scratch,
        flops=work(dense, vectors.items, lanes),
        moved=4 * MIB,
    )(*inputs)


def finish_first(plan, dense, vectors, energies, value_sum, right_side, level, own, readers):
    _, clusters, height, depth = dense.shape
    lanes = vectors.lanes
    fields = right_side.shape[0]
    width = height // 2
    count = len(vectors.arrays)
    keys = plan.again()
    outs = len(keys) + 1

    def kernel(dense_ref, energies_ref, *refs):
        vector_refs, refs = refs[:count], refs[count:]
        sum_ref, right_ref, level_ref, own_ref, readers_ref, image_ref, outgoing = refs[:7]
        messages, scratch = refs[7 : 7 + outs], refs[7 + outs :]
        energy = wide([energies_ref[...]] * fields)
        opened = vectors.open(vector_refs, scratch)
        (center,) = centers([(0, own_ref)], depth)

        @pl.loop(0, clusters // BATCH)
        def _(batch):
            here = pl.ds(batch * BATCH, BATCH)
            value = sum_ref[here]
            for part in products(dense_ref, opened, here, energy):
                value = value + part
            for local in range(BATCH):
                cluster = batch * BATCH + local
                rows = pl.ds(pl.multiple_of(cluster * width, width), width)
                right = wide([right_ref[f, rows, :] for f in range(fields)])
                image = wide([level_ref[cluster]] * fields) * right + value[local]
                image_ref[cluster] = image
                outgoing[rows, :] = (image - center * right).astype(jnp.bfloat16)

        fill(plan, keys, readers_ref, outgoing, messages, width)

    image, full, *messages, out = call(
        kernel,
        "finish_first",
        [
            jax.ShapeDtypeStruct((clusters, width, lanes), jnp.float32),
            jax.ShapeDtypeStruct((clusters * width, lanes), jnp.bfloat16),
        ]
        + [jax.ShapeDtypeStruct((depth, lanes), jnp.bfloat16)] * outs,
        [vmem()] * (2 + count + 4) + [smem()],
        vectors.scratch,
        flops=work(dense, vectors.items, lanes),
        moved=8 * MIB,
    )(dense, energies, *vectors.arrays, value_sum, right_side, level, own, readers)
    return image, full, dict(zip(keys, messages)), out


def guesses(lines, fields):
    orbitals = lines.shape[1] // fields
    alphas, growths = [], []
    for column in field_sums(lines, fields):
        norm, bend, square = column[0:1], column[1:2], column[2:3]
        norm = jnp.maximum(norm, 1e-30)
        alpha = norm / jnp.maximum(bend, 4.0 * norm)
        alphas.append(alpha)
        growths.append(jnp.clip(alpha * alpha * square / norm, 1.0, 2.0))
    return per_field(alphas, orbitals), per_field(growths, orbitals)


def prepare(right_side, image, after):
    fields, rows, orbitals = right_side.shape
    clusters, width, lanes = image.shape

    def kernel(right_ref, image_ref, _, lines_ref, kept):
        kept[...] = jnp.zeros_like(kept)

        def sweep(base, terms):
            @pl.loop(0, clusters)
            def _(cluster):
                here = pl.ds(pl.multiple_of(cluster * width, width), width)
                right = wide([right_ref[f, here, :] for f in range(fields)])
                for index, term in enumerate(terms(right, image_ref[cluster])):
                    kept[base + index] += folded(term)

        sweep(0, lambda right, first: (right * right, right * first, first * first))
        alpha, growth = guesses(lined([kept[i] for i in range(3)], 8), fields)

        def later_terms(right, first):
            step = alpha * first
            residual = right - step
            return residual * residual, residual * first, (growth * right - step) * first

        sweep(3, later_terms)
        lines_ref[...] = lined([kept[i] for i in range(6)], 8)
        lines_ref[6:7, :] = alpha
        lines_ref[7:8, :] = growth

    return call(
        kernel,
        "prepare",
        jax.ShapeDtypeStruct((8, lanes), jnp.float32),
        [vmem(), vmem(), pl.BlockSpec(memory_space=pl.ANY)],
        [pltpu.VMEM((6, 8, lanes), jnp.float32)],
        flops=8 * MIB,
        moved=4 * MIB,
    )(right_side, image, after)


def finish_second(dense, vectors, energies, value_sum, right_side, level, image, weighted, lines, devices):
    _, clusters, height, _ = dense.shape
    lanes = vectors.lanes
    fields = right_side.shape[0]
    width = height // 2
    count = len(vectors.arrays)

    def kernel(dense_ref, energies_ref, *refs):
        vector_refs, refs = refs[:count], refs[count:]
        sum_ref, right_ref, level_ref, image_ref, weighted_ref, lines_ref = refs[:6]
        later_ref, out_ref, kept, *scratch = refs[6:]
        energy = wide([energies_ref[...]] * fields)
        alpha, growth = lines_ref[6:7, :], lines_ref[7:8, :]
        kept[...] = jnp.zeros_like(kept)
        opened = vectors.open(vector_refs, scratch)

        @pl.loop(0, clusters // BATCH)
        def _(batch):
            here = pl.ds(batch * BATCH, BATCH)
            value = sum_ref[here] + weighted_ref[here]
            for part in products(dense_ref, opened, here, energy):
                value = value + part
            for local in range(BATCH):
                cluster = batch * BATCH + local
                rows = pl.ds(pl.multiple_of(cluster * width, width), width)
                right = wide([right_ref[f, rows, :] for f in range(fields)])
                first = image_ref[cluster]
                later = wide([level_ref[cluster]] * fields) * first + value[local]
                later_ref[cluster] = later
                direction = growth * right - alpha * first
                for index, left in enumerate((direction, right, first)):
                    kept[index] += folded(left * later)

        block = jnp.concatenate([lines_ref[0:6, :], lined([kept[i] for i in range(3)], 10)], axis=0)
        orbitals = lanes // fields
        line, lane = (lax.broadcasted_iota(jnp.int32, (16, 128), d) for d in (0, 1))
        rows = []
        for f, column in enumerate(field_sums(block, fields)):
            first_lane = slice(f * orbitals, f * orbitals + 1)
            filled = jnp.broadcast_to(column, (16, 128))
            filled = jnp.where(line == 9, jnp.broadcast_to(alpha[:, first_lane], (16, 128)), filled)
            filled = jnp.where(line == 10, jnp.broadcast_to(growth[:, first_lane], (16, 128)), filled)
            rows.append(jnp.sum(jnp.where(line == lane, filled, 0.0), axis=0, keepdims=True))
        rows.append(jnp.zeros((8 - fields, 128), jnp.float32))
        out_ref[...] = jnp.broadcast_to(jnp.concatenate(rows, axis=0)[None], out_ref.shape)

    return call(
        kernel,
        "finish_second",
        [
            jax.ShapeDtypeStruct((clusters, width, lanes), jnp.float32),
            jax.ShapeDtypeStruct((devices, 8, 128), jnp.float32),
        ],
        [vmem()] * (2 + count + 6),
        [pltpu.VMEM((3, 8, lanes), jnp.float32)] + vectors.scratch,
        flops=work(dense, vectors.items, lanes),
        moved=8 * MIB,
    )(dense, energies, *vectors.arrays, value_sum, right_side, level, image, weighted, lines)


def step_sizes(gathered, fields, orbitals):
    rows = gathered.reshape(-1, 128)
    flat = wide([jnp.transpose(rows[i : i + 128]) for i in range(0, rows.shape[0], 128)])
    line = [flat[i : i + 1, :] for i in range(11)]
    place = lax.broadcasted_iota(jnp.int32, line[0].shape, 1) & 7
    whole = lambda v: [
        jnp.sum(jnp.where(place == f, v, 0.0), axis=1, keepdims=True) for f in range(fields)
    ]

    def back(values):
        row = jnp.zeros_like(line[0])
        for f, value in enumerate(values):
            row = jnp.where(place == f, jnp.broadcast_to(value, row.shape), row)
        return row

    norm = whole(line[0])
    alpha = [n / b for n, b in zip(norm, whole(line[1]))]
    growth = [a * a * s / n for a, s, n in zip(alpha, whole(line[2]), norm)]
    off, more = back(alpha) - line[9], back(growth) - line[10]
    after = whole(line[3] - 2.0 * off * line[4] + off * off * line[2])
    bend = whole(
        (line[10] * line[5] - line[9] * line[6])
        + more * (line[5] + line[10] * line[1] - line[9] * line[7])
        - off * (line[6] + line[10] * line[2] - line[9] * line[8])
        + more * more * line[1]
        - more * off * (line[7] + line[2])
        + off * off * line[8]
    )
    gain = [a / b for a, b in zip(after, bend)]
    return [per_field(v, orbitals) for v in (alpha, growth, gain)]


def final(right_side, image, later, gathered):
    fields, rows, orbitals = right_side.shape
    clusters, width, lanes = image.shape
    blocks = 4
    each = clusters // blocks

    def kernel(right_ref, image_ref, later_ref, gathered_ref, solution_ref, residual_ref, steps):
        step = pl.program_id(0)

        @pl.when(step == 0)
        def _():
            alpha, growth, gain = step_sizes(gathered_ref[...], fields, orbitals)
            steps[0:1, :] = alpha + gain * growth
            steps[1:2, :] = gain * alpha

        for local in range(each):
            cluster = step * each + local
            rows = pl.ds(pl.multiple_of(cluster * width, width), width)
            here = slice(local * width, (local + 1) * width)
            for field in range(fields):
                part = slice(field * orbitals, (field + 1) * orbitals)
                one, two = steps[0:1, part], steps[1:2, part]
                right = right_ref[field, rows, :]
                first = image_ref[cluster, :, part]
                later = later_ref[cluster, :, part]
                solution_ref[field, here, :] = one * right - two * first
                residual_ref[field, here, :] = (right - one * first) + two * later

    vector = pl.BlockSpec((fields, each * width, orbitals), lambda i: (0, i, 0))
    shape = jax.ShapeDtypeStruct(right_side.shape, jnp.float32)
    return pl.pallas_call(
        kernel,
        grid=(blocks,),
        out_shape=[shape, shape],
        in_specs=[vmem()] * 4,
        out_specs=[vector, vector],
        scratch_shapes=[pltpu.VMEM((8, lanes), jnp.float32)],
        compiler_params=pltpu.CompilerParams(vmem_limit_bytes=12 * MIB),
        name="final",
    )(right_side, image, later, gathered)


def body(right_side, onsite, energies, ks_tiles, correlation_tiles, tile_slot, readers):
    span, served = readers.shape[1:]
    clusters, _, width, _ = ks_tiles.shape
    rows = lax.axis_size("row")
    devices = rows * lax.axis_size("col")
    onsite = onsite.reshape(-1, width)
    energies = energies.reshape(1, -1)
    plan = Plan(rows, span, rows == 8 and span == 7)
    readers = jnp.swapaxes(readers, 1, 2)

    def begin(items, after):
        return couple(dense, Vectors(plan, items), energies, [], after)

    def partial(items, sums, begun):
        for group in (items[begun:5], items[5:6]):
            sums = couple(dense, Vectors(plan, group), energies, sums)
        return sums, Vectors(plan, items[-1:])

    direct, own, full = pack(plan, readers, right_side, onsite)
    dense = spread(tile_slot, ks_tiles, correlation_tiles, span, served)
    items, sums, chosen, _ = exchange(plan, readers, direct, own, full, None, begin, (1, 2, 3), served, width)
    level = levels(onsite)
    sums, last = partial(items, sums, 3 if plan.relayed else 2)
    image, full, direct, out = finish_first(
        plan, dense, last, energies, sums[0], right_side, level, own, readers
    )

    items, begun, _, mark = exchange(plan, readers, direct, out, full, chosen, begin, (2, 3, 1), served, width)
    lines = prepare(right_side, image, mark)
    _, weighted = couple(dense, last, energies, sums, mark)
    (value,), last = partial(items, begun, 2)
    later, gathered = finish_second(
        dense, last, energies, value, right_side, level, image, weighted, lines, devices
    )
    gathered = lax.all_to_all(gathered, ("row", "col"), 0, 0)
    return tuple(final(right_side, image, later, gathered))


def solution(mesh):
    placed = (
        P(None, "row", "col"),
        P("row"),
        P("col"),
        P("row", None, None, None),
        P("row", None, None, None),
        P("row", None),
        P("row", None, None),
    )
    return jax.shard_map(
        body,
        mesh=mesh,
        in_specs=placed,
        out_specs=(P(None, "row", "col"), P(None, "row", "col")),
        check_vma=False,
    )
```

```python
import functools

import jax
import jax.numpy as jnp
from jax import lax
from jax.experimental import pallas as pl
from jax.experimental.pallas import tpu as pltpu
from jax.sharding import PartitionSpec as P

MIB = 2**20
EXTRA = 16
BATCH = 4


def shifted(array, axis, by):
    count = lax.axis_size(axis)
    return lax.ppermute(array, axis, [(i, (i + by) % count) for i in range(count)])


def vmem():
    return pl.BlockSpec(memory_space=pltpu.VMEM)


def smem():
    return pl.BlockSpec(memory_space=pltpu.SMEM)


def call(kernel, name, out_shape, specs, scratch=(), flops=0, moved=MIB, limit=12):
    return pl.pallas_call(
        kernel,
        out_shape=out_shape,
        in_specs=specs,
        out_specs=jax.tree.map(lambda _: vmem(), out_shape),
        scratch_shapes=list(scratch),
        compiler_params=pltpu.CompilerParams(vmem_limit_bytes=limit * MIB),
        cost_estimate=pl.CostEstimate(flops=flops, bytes_accessed=moved, transcendentals=0),
        name=name,
    )


def wide(parts):
    return jnp.concatenate(parts, axis=1)


def folded(term):
    return jnp.sum(term.reshape(-1, 8, term.shape[-1]), axis=0)


def lined(parts, lines):
    parts = [jnp.sum(p, axis=0, keepdims=True) for p in parts]
    parts.append(jnp.zeros((lines - len(parts), parts[0].shape[1]), jnp.float32))
    return jnp.concatenate(parts, axis=0)


def per_field(values, orbitals):
    return wide([jnp.broadcast_to(v, (1, orbitals)) for v in values])


def field_sums(lines, fields):
    orbitals = lines.shape[1] // fields
    return [
        jnp.sum(lines[:, f * orbitals : (f + 1) * orbitals], axis=1, keepdims=True)
        for f in range(fields)
    ]


class Plan:
    def __init__(self, count, span, relayed):
        self.count, self.span, self.middle, self.relayed = count, span, (span - 1) // 2, relayed

    def offset(self, source, reader):
        value = lax.rem(source - reader + (self.middle + self.count), self.count)
        return jnp.minimum(value, self.span - 1) if self.relayed else value

    def direct(self):
        if self.relayed:
            return [1, 2, 3, 7]
        far = range(self.middle, 0, -1)
        return [by for f in far for by in (f, -f)]

    def again(self):
        return [2, 3, 1] if self.relayed else self.direct()

    def reader(self, key, me):
        return me ^ key if self.relayed else lax.rem(me + key + self.count, self.count)

    def source(self, key, me):
        return me ^ key if self.relayed else lax.rem(me - key + self.count, self.count)

    def pairs(self, key):
        if not self.relayed:
            return [(i, (i + key) % self.count) for i in range(self.count)]
        return [(i, i ^ key) for i in range(self.count) if key < 4 or i not in INNER]


INNER = (2, 3, 4, 5)


def is_inner(me):
    return (me >= INNER[0]) & (me <= INNER[-1])


def pack(plan, readers, right_side, onsite):
    fields, rows, orbitals = right_side.shape
    served = readers.shape[1]
    clusters, width = onsite.shape
    lanes = fields * orbitals
    keys = plan.direct()

    def kernel(readers_hbm, right_hbm, onsite_hbm, *refs):
        messages, rounded = refs[: len(keys) + 1], refs[len(keys) + 1]
        readers_ref, right_ref, onsite_ref, sems, more = refs[len(keys) + 2 :]
        copies = []
        for cluster in range(clusters):
            here = pl.ds(cluster * width, width)
            copies.append(
                pltpu.make_async_copy(
                    right_hbm.at[:, here, :], right_ref.at[:, here, :], sems.at[cluster]
                )
            )
        others = [
            pltpu.make_async_copy(onsite_hbm, onsite_ref, more.at[0]),
            pltpu.make_async_copy(readers_hbm, readers_ref, more.at[1]),
        ]
        for copy in copies[:1] + others + copies[1:]:
            copy.start()
        others[0].wait()
        norm = [jnp.zeros((8, orbitals), jnp.float32)] * fields
        heavy = [jnp.zeros((8, orbitals), jnp.float32)] * fields
        for cluster in range(clusters):
            copies[cluster].wait()
            weight = jnp.broadcast_to(onsite_ref[cluster : cluster + 1, :], (8, width))
            here = slice(cluster * width, (cluster + 1) * width)
            for field in range(fields):
                right = right_ref[field, here, :]
                rounded[here, field * orbitals : (field + 1) * orbitals] = right.astype(jnp.bfloat16)
                square = right * right
                norm[field] += folded(square)
                heavy[field] += jnp.dot(weight, square, preferred_element_type=jnp.float32)
        centers = [
            jnp.sum(h[:1], axis=1, keepdims=True)
            / jnp.maximum(jnp.sum(jnp.sum(n, axis=0, keepdims=True), axis=1, keepdims=True), 1e-30)
            for h, n in zip(heavy, norm)
        ]
        others[1].wait()
        rest = jnp.broadcast_to(per_field(centers, orbitals), (EXTRA, lanes))
        line, lane = (lax.broadcasted_iota(jnp.int32, (EXTRA, lanes), d) for d in (0, 1))
        for offset in range(readers_ref.shape[2]):
            for slot in range(served):
                here = (line == offset + 1) & (lane == slot)
                rest = jnp.where(here, readers_ref[0, slot, offset].astype(jnp.float32), rest)
        rounded[clusters * width :, :] = rest.astype(jnp.bfloat16)
        fill(plan, keys, readers_ref, rounded, messages, width)

    message = jax.ShapeDtypeStruct((served * width + EXTRA, lanes), jnp.bfloat16)
    full = jax.ShapeDtypeStruct((clusters * width + EXTRA, lanes), jnp.bfloat16)
    *messages, own, full = call(
        kernel,
        "pack",
        [message] * (len(keys) + 1) + [full],
        [pl.BlockSpec(memory_space=pltpu.HBM)] * 3,
        [
            pltpu.SMEM(readers.shape, readers.dtype),
            pltpu.VMEM(right_side.shape, jnp.float32),
            pltpu.VMEM(onsite.shape, jnp.float32),
            pltpu.SemaphoreType.DMA((clusters,)),
            pltpu.SemaphoreType.DMA((2,)),
        ],
        limit=51,
    )(readers, right_side, onsite)
    return dict(zip(keys, messages)), own, full


def fill(plan, keys, readers_ref, rounded, messages, width):
    me = lax.axis_index("row")
    offsets = [plan.offset(me, plan.reader(key, me)) for key in keys] + [plan.middle]
    for offset, message in zip(offsets, messages):
        served = readers_ref.shape[1]
        gather([readers_ref[0, slot, offset] for slot in range(served)], rounded, message, width)


def gather(clusters, rounded, message, width):
    for slot, cluster in enumerate(clusters):
        start = pl.multiple_of(cluster * width, width)
        message[slot * width : (slot + 1) * width, :] = rounded[pl.ds(start, width), :]
    used = len(clusters) * width
    if message.shape[0] > used:
        message[used:, :] = rounded[rounded.shape[0] - EXTRA :, :]


def relay(plan, readers, mine, full, chosen, after, served, width):
    lanes = full.shape[1]
    extra = EXTRA if chosen is None else 0
    message = jax.ShapeDtypeStruct((served * width + extra, lanes), jnp.bfloat16)

    def kernel(*refs):
        readers_ref, mine_ref, full_ref, _, *refs = refs
        me = lax.axis_index("row")
        *messages, chosen_ref = refs if chosen is None else [*refs[1:], refs[0]]
        beyond = messages[3:]
        messages = messages[:3]
        if chosen is None:
            base = full_ref.shape[0] - EXTRA
            table = full_ref[base : base + EXTRA, 0:width].astype(jnp.float32)
            line, lane = (lax.broadcasted_iota(jnp.int32, table.shape, d) for d in (0, 1))
            for index, reader in enumerate((me, me ^ 1, me ^ 3)):
                offset = plan.offset(me ^ 6, reader)
                for slot in range(served):
                    here = (line == offset + 1) & (lane == slot)
                    chosen_ref[index, slot] = jnp.sum(jnp.where(here, table, 0.0)).astype(jnp.int32)

        @pl.when(is_inner(me))
        def _():
            for index, out in enumerate(messages):
                gather([chosen_ref[index, slot] for slot in range(served)], full_ref, out, width)

        @pl.when(jnp.logical_not(is_inner(me)))
        def _():
            for key, out in zip((6, 5, 7), [*messages[1:], *beyond]):
                offset = plan.offset(me, me ^ key)
                clusters = [readers_ref[0, slot, offset] for slot in range(served)]
                gather(clusters, mine_ref, out, width)

    inputs = [readers, mine, full, after] + ([] if chosen is None else [chosen])
    specs = [smem(), vmem(), vmem(), pl.BlockSpec(memory_space=pl.ANY)]
    specs += [] if chosen is None else [smem()]
    count = 3 if chosen is None else 4
    shapes, outs = [message] * count, [vmem()] * count
    if chosen is None:
        shapes.append(jax.ShapeDtypeStruct((3, served), jnp.int32))
        outs.append(smem())
    *messages, last = pl.pallas_call(
        kernel,
        out_shape=shapes,
        in_specs=specs,
        out_specs=outs,
        compiler_params=pltpu.CompilerParams(vmem_limit_bytes=12 * MIB),
        cost_estimate=pl.CostEstimate(flops=0, bytes_accessed=MIB, transcendentals=0),
        name="relay",
    )(*inputs)
    return (messages, last) if chosen is None else (messages + [last], chosen)


def exchange(plan, readers, direct, own, full, chosen, begin, near, served, width):
    sent = {k: lax.ppermute(m, "row", plan.pairs(k)) for k, m in direct.items()}
    if not plan.relayed:
        items = [(own, 0)] + [(sent[k], k) for k in plan.direct()]
        sums = begin(items[:2], None)
        return items, sums, None, sums[0]
    theirs = lax.ppermute(full, "row", [(i, i ^ 6) for i in INNER])
    items = [(own, 0)] + [(sent[k], k) for k in near]
    first = chosen is None
    sums = begin(items[:3], theirs) if first else begin(items[:2], None)
    (mine, near, far, *beyond), chosen = relay(
        plan, readers, full, theirs, chosen, sums[0], served, width
    )
    near = lax.ppermute(near, "row", [(i, i ^ (1 if i in INNER else 6)) for i in range(plan.count)])
    far = lax.ppermute(far, "row", [(i, i ^ (3 if i in INNER else 5)) for i in range(plan.count)])
    over = sent[7] if first else lax.ppermute(beyond[0], "row", plan.pairs(7))
    middle = [((mine, over), (6, 7)), (far, 5)]
    items += (middle if first else middle[::-1]) + [(near, (7, 6))]
    return items, sums, chosen, mine


class Vectors:
    def __init__(self, plan, items):
        self.plan, self.items = plan, items
        self.arrays, self.scratch = [], []
        for value, _ in items:
            many = isinstance(value, tuple)
            self.arrays += list(value) if many else [value]
            if many:
                self.scratch.append(pltpu.VMEM(value[0].shape, value[0].dtype))
        self.lanes = self.arrays[0].shape[1]
        self.rows = self.arrays[0].shape[0]

    def open(self, refs, scratch):
        refs, scratch = list(refs), list(scratch)
        me = lax.axis_index("row")
        opened = []
        for value, key in self.items:
            if not self.plan.relayed:
                opened.append((self.plan.middle - key, refs.pop(0)))
                continue
            inner, outer = key if isinstance(key, tuple) else (key, key)
            held = refs.pop(0)
            if isinstance(value, tuple):
                kept, held, other = held, scratch.pop(0), refs.pop(0)

                @pl.when(is_inner(me))
                def _():
                    held[...] = kept[...]

                @pl.when(jnp.logical_not(is_inner(me)))
                def _():
                    held[...] = other[...]

            source = jnp.where(is_inner(me), me ^ inner, me ^ outer)
            opened.append((self.plan.offset(source, me), held))
        return opened


def levels(onsite):
    clusters, width = onsite.shape

    def kernel(onsite_ref, level_ref):
        for cluster in range(clusters):
            level_ref[cluster] = jnp.transpose(
                jnp.broadcast_to(onsite_ref[cluster : cluster + 1, :], (width, width))
            )

    shape = jax.ShapeDtypeStruct((clusters, width, width), jnp.float32)
    return call(kernel, "levels", shape, [vmem()])(onsite)


def spread(tile_slot, ks_tiles, correlation_tiles, span, served):
    clusters, _, width, _ = ks_tiles.shape
    slots = span * served

    def kernel(slot_ref, ks_ref, correlation_ref, out_ref, where):
        @pl.loop(0, clusters)
        def _(cluster):
            for kind, ref in enumerate((ks_ref, correlation_ref)):
                count = ref.shape[1]
                for slot in range(slots):
                    where[slot] = count
                for tile in range(count):
                    where[slot_ref[cluster, tile]] = tile
                for slot in range(slots):
                    tile = where[slot]
                    block = ref[cluster, jnp.minimum(tile, count - 1)]
                    block = jnp.where(tile < count, block, jnp.zeros_like(block))
                    lane = slot % served * width
                    out_ref[
                        slot // served, cluster, kind * width : (kind + 1) * width, lane : lane + width
                    ] = block

    return call(
        kernel,
        "spread",
        jax.ShapeDtypeStruct((span, clusters, 2 * width, served * width), jnp.bfloat16),
        [smem(), vmem(), vmem()],
        [pltpu.SMEM((slots,), jnp.int32)],
        moved=16 * MIB,
    )(tile_slot, ks_tiles, correlation_tiles)


def products(dense_ref, opened, clusters, energy):
    depth = dense_ref.shape[-1]
    for offset, vector in opened:
        left = dense_ref[offset, clusters]
        count, height, _ = left.shape
        value = jnp.dot(
            left.reshape(count * height, depth), vector[0:depth, :], preferred_element_type=jnp.float32
        )
        value = value.reshape(count, 2, height // 2, value.shape[1])
        yield value[:, 0] - energy * value[:, 1]


def centers(opened, depth):
    return [vector[depth : depth + EXTRA, :].astype(jnp.float32)[:1] for _, vector in opened]


def work(dense, items, lanes):
    return 2 * len(items) * dense.shape[1] * dense.shape[2] * dense.shape[3] * lanes


def couple(dense, vectors, energies, sums, after=None):
    _, clusters, height, depth = dense.shape
    lanes = vectors.lanes
    count = len(vectors.arrays)
    outs = 2 if vectors.rows > depth else 1
    had = len(sums)

    def kernel(dense_ref, energies_ref, *refs):
        refs = list(refs[1:] if after is not None else refs)
        vector_refs, sum_refs = refs[:count], refs[count : count + had]
        out_refs, scratch = refs[count + had : count + had + outs], refs[count + had + outs :]
        energy = wide([energies_ref[...]] * (lanes // energies_ref.shape[1]))
        opened = vectors.open(vector_refs, scratch)
        weights = centers(opened, depth) if outs == 2 else [None] * len(opened)

        @pl.loop(0, clusters // BATCH)
        def _(batch):
            here = pl.ds(batch * BATCH, BATCH)
            values = [ref[here] for ref in sum_refs]
            for weight, part in zip(weights, products(dense_ref, opened, here, energy)):
                terms = [part] if weight is None else [part, weight * part]
                values = [v + t for v, t in zip(values, terms)] if values else terms
            for ref, value in zip(out_refs, values):
                ref[here] = value

    order = [] if after is None else [after]
    inputs = [dense, energies, *order, *vectors.arrays, *sums]
    shape = jax.ShapeDtypeStruct((clusters, height // 2, lanes), jnp.float32)
    return call(
        kernel,
        "couple",
        [shape] * outs,
        [vmem()] * 2
        + [pl.BlockSpec(memory_space=pl.ANY)] * len(order)
        + [vmem()] * (len(vectors.arrays) + had),
        vectors.scratch,
        flops=work(dense, vectors.items, lanes),
        moved=4 * MIB,
    )(*inputs)


def finish_first(plan, dense, vectors, energies, value_sum, right_side, level, own, readers):
    _, clusters, height, depth = dense.shape
    lanes = vectors.lanes
    fields = right_side.shape[0]
    width = height // 2
    count = len(vectors.arrays)
    keys = plan.again()
    outs = len(keys) + 1

    def kernel(dense_ref, energies_ref, *refs):
        vector_refs, refs = refs[:count], refs[count:]
        sum_ref, right_ref, level_ref, own_ref, readers_ref, image_ref, outgoing = refs[:7]
        messages, scratch = refs[7 : 7 + outs], refs[7 + outs :]
        energy = wide([energies_ref[...]] * fields)
        opened = vectors.open(vector_refs, scratch)
        (center,) = centers([(0, own_ref)], depth)

        @pl.loop(0, clusters // BATCH)
        def _(batch):
            here = pl.ds(batch * BATCH, BATCH)
            value = sum_ref[here]
            for part in products(dense_ref, opened, here, energy):
                value = value + part
            for local in range(BATCH):
                cluster = batch * BATCH + local
                rows = pl.ds(pl.multiple_of(cluster * width, width), width)
                right = wide([right_ref[f, rows, :] for f in range(fields)])
                image = wide([level_ref[cluster]] * fields) * right + value[local]
                image_ref[cluster] = image
                outgoing[rows, :] = (image - center * right).astype(jnp.bfloat16)

        fill(plan, keys, readers_ref, outgoing, messages, width)

    image, full, *messages, out = call(
        kernel,
        "finish_first",
        [
            jax.ShapeDtypeStruct((clusters, width, lanes), jnp.float32),
            jax.ShapeDtypeStruct((clusters * width, lanes), jnp.bfloat16),
        ]
        + [jax.ShapeDtypeStruct((depth, lanes), jnp.bfloat16)] * outs,
        [vmem()] * (2 + count + 4) + [smem()],
        vectors.scratch,
        flops=work(dense, vectors.items, lanes),
        moved=8 * MIB,
    )(dense, energies, *vectors.arrays, value_sum, right_side, level, own, readers)
    return image, full, dict(zip(keys, messages)), out


def guesses(lines, fields):
    orbitals = lines.shape[1] // fields
    alphas, growths = [], []
    for column in field_sums(lines, fields):
        norm, bend, square = column[0:1], column[1:2], column[2:3]
        norm = jnp.maximum(norm, 1e-30)
        alpha = norm / jnp.maximum(bend, 4.0 * norm)
        alphas.append(alpha)
        growths.append(jnp.clip(alpha * alpha * square / norm, 1.0, 2.0))
    return per_field(alphas, orbitals), per_field(growths, orbitals)


def prepare(right_side, image, after):
    fields, rows, orbitals = right_side.shape
    clusters, width, lanes = image.shape

    def kernel(right_ref, image_ref, _, lines_ref, kept):
        kept[...] = jnp.zeros_like(kept)

        def sweep(base, terms):
            @pl.loop(0, clusters)
            def _(cluster):
                here = pl.ds(pl.multiple_of(cluster * width, width), width)
                right = wide([right_ref[f, here, :] for f in range(fields)])
                for index, term in enumerate(terms(right, image_ref[cluster])):
                    kept[base + index] += folded(term)

        sweep(0, lambda right, first: (right * right, right * first, first * first))
        alpha, growth = guesses(lined([kept[i] for i in range(3)], 8), fields)

        def later_terms(right, first):
            step = alpha * first
            residual = right - step
            return residual * residual, residual * first, (growth * right - step) * first

        sweep(3, later_terms)
        lines_ref[...] = lined([kept[i] for i in range(6)], 8)
        lines_ref[6:7, :] = alpha
        lines_ref[7:8, :] = growth

    return call(
        kernel,
        "prepare",
        jax.ShapeDtypeStruct((8, lanes), jnp.float32),
        [vmem(), vmem(), pl.BlockSpec(memory_space=pl.ANY)],
        [pltpu.VMEM((6, 8, lanes), jnp.float32)],
        flops=8 * MIB,
        moved=4 * MIB,
    )(right_side, image, after)


def finish_second(dense, vectors, energies, value_sum, right_side, level, image, weighted, lines, devices):
    _, clusters, height, _ = dense.shape
    lanes = vectors.lanes
    fields = right_side.shape[0]
    width = height // 2
    count = len(vectors.arrays)

    def kernel(dense_ref, energies_ref, *refs):
        vector_refs, refs = refs[:count], refs[count:]
        sum_ref, right_ref, level_ref, image_ref, weighted_ref, lines_ref = refs[:6]
        later_ref, out_ref, kept, *scratch = refs[6:]
        energy = wide([energies_ref[...]] * fields)
        alpha, growth = lines_ref[6:7, :], lines_ref[7:8, :]
        kept[...] = jnp.zeros_like(kept)
        opened = vectors.open(vector_refs, scratch)

        @pl.loop(0, clusters // BATCH)
        def _(batch):
            here = pl.ds(batch * BATCH, BATCH)
            value = sum_ref[here] + weighted_ref[here]
            for part in products(dense_ref, opened, here, energy):
                value = value + part
            for local in range(BATCH):
                cluster = batch * BATCH + local
                rows = pl.ds(pl.multiple_of(cluster * width, width), width)
                right = wide([right_ref[f, rows, :] for f in range(fields)])
                first = image_ref[cluster]
                later = wide([level_ref[cluster]] * fields) * first + value[local]
                later_ref[cluster] = later
                direction = growth * right - alpha * first
                for index, left in enumerate((direction, right, first)):
                    kept[index] += folded(left * later)

        block = jnp.concatenate([lines_ref[0:6, :], lined([kept[i] for i in range(3)], 10)], axis=0)
        orbitals = lanes // fields
        line, lane = (lax.broadcasted_iota(jnp.int32, (16, 128), d) for d in (0, 1))
        rows = []
        for f, column in enumerate(field_sums(block, fields)):
            first_lane = slice(f * orbitals, f * orbitals + 1)
            filled = jnp.broadcast_to(column, (16, 128))
            filled = jnp.where(line == 9, jnp.broadcast_to(alpha[:, first_lane], (16, 128)), filled)
            filled = jnp.where(line == 10, jnp.broadcast_to(growth[:, first_lane], (16, 128)), filled)
            rows.append(jnp.sum(jnp.where(line == lane, filled, 0.0), axis=0, keepdims=True))
        rows.append(jnp.zeros((8 - fields, 128), jnp.float32))
        out_ref[...] = jnp.broadcast_to(jnp.concatenate(rows, axis=0)[None], out_ref.shape)

    return call(
        kernel,
        "finish_second",
        [
            jax.ShapeDtypeStruct((clusters, width, lanes), jnp.float32),
            jax.ShapeDtypeStruct((devices, 8, 128), jnp.float32),
        ],
        [vmem()] * (2 + count + 6),
        [pltpu.VMEM((3, 8, lanes), jnp.float32)] + vectors.scratch,
        flops=work(dense, vectors.items, lanes),
        moved=8 * MIB,
    )(dense, energies, *vectors.arrays, value_sum, right_side, level, image, weighted, lines)


def step_sizes(gathered, fields, orbitals):
    rows = gathered.reshape(-1, 128)
    flat = wide([jnp.transpose(rows[i : i + 128]) for i in range(0, rows.shape[0], 128)])
    line = [flat[i : i + 1, :] for i in range(11)]
    place = lax.broadcasted_iota(jnp.int32, line[0].shape, 1) & 7
    whole = lambda v: [
        jnp.sum(jnp.where(place == f, v, 0.0), axis=1, keepdims=True) for f in range(fields)
    ]

    def back(values):
        row = jnp.zeros_like(line[0])
        for f, value in enumerate(values):
            row = jnp.where(place == f, jnp.broadcast_to(value, row.shape), row)
        return row

    norm = whole(line[0])
    alpha = [n / b for n, b in zip(norm, whole(line[1]))]
    growth = [a * a * s / n for a, s, n in zip(alpha, whole(line[2]), norm)]
    off, more = back(alpha) - line[9], back(growth) - line[10]
    after = whole(line[3] - 2.0 * off * line[4] + off * off * line[2])
    bend = whole(
        (line[10] * line[5] - line[9] * line[6])
        + more * (line[5] + line[10] * line[1] - line[9] * line[7])
        - off * (line[6] + line[10] * line[2] - line[9] * line[8])
        + more * more * line[1]
        - more * off * (line[7] + line[2])
        + off * off * line[8]
    )
    gain = [a / b for a, b in zip(after, bend)]
    return [per_field(v, orbitals) for v in (alpha, growth, gain)]


def final(right_side, image, later, gathered):
    fields, rows, orbitals = right_side.shape
    clusters, width, lanes = image.shape
    blocks = 4
    each = clusters // blocks

    def kernel(right_ref, image_ref, later_ref, gathered_ref, solution_ref, residual_ref, steps):
        step = pl.program_id(0)

        @pl.when(step == 0)
        def _():
            alpha, growth, gain = step_sizes(gathered_ref[...], fields, orbitals)
            steps[0:1, :] = alpha + gain * growth
            steps[1:2, :] = gain * alpha

        for local in range(each):
            cluster = step * each + local
            rows = pl.ds(pl.multiple_of(cluster * width, width), width)
            here = slice(local * width, (local + 1) * width)
            for field in range(fields):
                part = slice(field * orbitals, (field + 1) * orbitals)
                one, two = steps[0:1, part], steps[1:2, part]
                right = right_ref[field, rows, :]
                first = image_ref[cluster, :, part]
                later = later_ref[cluster, :, part]
                solution_ref[field, here, :] = one * right - two * first
                residual_ref[field, here, :] = (right - one * first) + two * later

    vector = pl.BlockSpec((fields, each * width, orbitals), lambda i: (0, i, 0))
    shape = jax.ShapeDtypeStruct(right_side.shape, jnp.float32)
    return pl.pallas_call(
        kernel,
        grid=(blocks,),
        out_shape=[shape, shape],
        in_specs=[vmem()] * 4,
        out_specs=[vector, vector],
        scratch_shapes=[pltpu.VMEM((8, lanes), jnp.float32)],
        compiler_params=pltpu.CompilerParams(vmem_limit_bytes=12 * MIB),
        name="final",
    )(right_side, image, later, gathered)


def body(right_side, onsite, energies, ks_tiles, correlation_tiles, tile_slot, readers):
    span, served = readers.shape[1:]
    clusters, _, width, _ = ks_tiles.shape
    rows = lax.axis_size("row")
    devices = rows * lax.axis_size("col")
    onsite = onsite.reshape(-1, width)
    energies = energies.reshape(1, -1)
    plan = Plan(rows, span, rows == 8 and span == 7)
    readers = jnp.swapaxes(readers, 1, 2)

    def begin(items, after):
        return couple(dense, Vectors(plan, items), energies, [], after)

    def partial(items, sums, begun):
        for group in (items[begun:5], items[5:6]):
            sums = couple(dense, Vectors(plan, group), energies, sums)
        return sums, Vectors(plan, items[-1:])

    direct, own, full = pack(plan, readers, right_side, onsite)
    dense = spread(tile_slot, ks_tiles, correlation_tiles, span, served)
    items, sums, chosen, _ = exchange(plan, readers, direct, own, full, None, begin, (2, 1, 3), served, width)
    level = levels(onsite)
    sums, last = partial(items, sums, 3 if plan.relayed else 2)
    image, full, direct, out = finish_first(
        plan, dense, last, energies, sums[0], right_side, level, own, readers
    )

    items, begun, _, mark = exchange(plan, readers, direct, out, full, chosen, begin, (2, 3, 1), served, width)
    lines = prepare(right_side, image, mark)
    _, weighted = couple(dense, last, energies, sums, mark)
    (value,), last = partial(items, begun, 2)
    later, gathered = finish_second(
        dense, last, energies, value, right_side, level, image, weighted, lines, devices
    )
    gathered = lax.all_to_all(gathered, ("row", "col"), 0, 0)
    return tuple(final(right_side, image, later, gathered))


def solution(mesh):
    placed = (
        P(None, "row", "col"),
        P("row"),
        P("col"),
        P("row", None, None, None),
        P("row", None, None, None),
        P("row", None),
        P("row", None, None),
    )
    return jax.shard_map(
        body,
        mesh=mesh,
        in_specs=placed,
        out_specs=(P(None, "row", "col"), P(None, "row", "col")),
        check_vma=False,
    )
```
